32 devices in a mesh: wide: 8 (over y, x, core), narrow: 4 (over z).
Axes of the slice: x: 2, y: 2, z: 4, core: 2. Of those that a mesh axis runs over, the one named last changes fastest.
Arguments:
- patches: bfloat16 [8192, 1536], P('wide'), may hold values from -6 to 6
- cotangent: bfloat16 [8192, 1536], P('wide'), may hold values from -6 to 6
- conditioning: bfloat16 [8, 1024], P('wide'), may hold values from -6 to 6
- captions: bfloat16 [2048, 4096], P('wide'), may hold values from -6 to 6
- item_lengths: int32 [8], replicated, may hold values from 0 to 4096, as said below
- grid_widths: int32 [8], replicated, may hold values from 16 to 64, as said below
- w_ada: bfloat16 [1024, 4, 1536], P(None, None, 'narrow'), may hold values from -0.1875 to 0.1875
- norm_gains: float32 [4, 1536], replicated, may hold values from 0.25 to 1.75
- w_qkv: bfloat16 [3, 1536, 1536], P(None, None, 'narrow'), may hold values from -0.15625 to 0.15625
- head_gains: float32 [3, 64], replicated, may hold values from 0.25 to 1.75
- cross_gate: float32 [24], P('narrow'), may hold values from -1.5 to 1.5
- w_caption: bfloat16 [2, 4096, 1536], P(None, None, 'narrow'), may hold values from -0.09375 to 0.09375
- w_out: bfloat16 [1536, 1536], P('narrow'), may hold values from -0.15625 to 0.15625
- w_gate_up: bfloat16 [2, 1536, 4096], P(None, None, 'narrow'), may hold values from -0.15625 to 0.15625
- w_down: bfloat16 [4096, 1536], P('narrow'), may hold values from -0.09375 to 0.09375
Outputs:
- output: bfloat16 [8192, 1536], P('wide')
- grad_patches: bfloat16 [8192, 1536], P('wide')
- grad_conditioning: float32 [8, 1024], P('wide')
- grad_captions: bfloat16 [2048, 4096], P('wide')
- grad_ada: float32 [1024, 4, 1536], P('wide', None, 'narrow')
- grad_norm_gains: float32 [4, 1536], P(None, 'wide')
- grad_qkv: float32 [3, 1536, 1536], P(None, 'wide', 'narrow')
- grad_head_gains: float32 [3, 64], replicated
- grad_cross_gate: float32 [24], replicated
- grad_caption_w: float32 [2, 4096, 1536], P(None, 'wide', 'narrow')
- grad_out_w: float32 [1536, 1536], P('narrow', 'wide')
- grad_gate_up: float32 [2, 1536, 4096], P(None, 'wide', 'narrow')
- grad_down: float32 [4096, 1536], P('narrow', 'wide')
The draws below stay inside these ranges and needn't reach their ends.
Inputs may be any that keep to these rules, and one draw needn't show every extreme that they name: `item_lengths`: each length is a multiple of 1024, items fill all 8192 tokens in order with zeros after the last, and in every draw some item has exactly 4096 tokens. `grid_widths`: each is a power of two.
All inputs are finite; a program needn't handle non-finite values.
Results may differ from the reference program's by a relative error of at most 0.019.
Values may be sent and summed in bfloat16 or wider, within the bound.
No kernel may reach another device: no remote copies, remote signals or barrier semaphores. Data moves between devices by JAX's collectives and lax.ppermute only.
A program may use at most 384 MiB of HBM per device.

```python
import jax
import jax.numpy as jnp
from jax import lax

D = 1536
H = 24
HD = 64
FF = 4096
DT = 4096
CD = 1024
LTXT = 256
TOK_DEV = 1024
SPAN = 4
ITEM_SLOTS = 8
TOKENS = 8192


def draw_item_lengths(key, part):
    key = jax.random.fold_in(key, 5)
    first_key, second_key = jax.random.split(key)
    item_spans = jax.random.randint(first_key, (ITEM_SLOTS,), 1, SPAN + 1)
    forced = jax.random.randint(second_key, (), 0, 2)
    item_spans = jnp.where(jnp.arange(ITEM_SLOTS) == forced, SPAN, item_spans)
    closing = jnp.cumsum(item_spans)
    opening = closing - item_spans
    kept_spans = jnp.clip(jnp.minimum(item_spans, ITEM_SLOTS - opening), 0, SPAN)
    return (kept_spans * TOK_DEV).astype(jnp.int32)


def draw_grid_widths(key, part):
    key = jax.random.fold_in(key, 9)
    powers = jax.random.randint(key, (ITEM_SLOTS,), 4, 7)
    return (jnp.int32(2) ** powers).astype(jnp.int32)


def block_levels(own_key, extent, cuts, smallest, largest):
    def one(dim, shards_of):
        steps = jax.random.uniform(jax.random.fold_in(jax.random.fold_in(own_key, 6), dim), (shards_of,), jnp.float32, smallest / len(cuts), largest / len(cuts))
        return jnp.repeat(jnp.exp(steps), extent[dim] // shards_of).reshape((-1,) + (1,) * (len(extent) - dim - 1))

    level = one(*cuts[0])
    for cut in cuts[1:]:
        level = level * one(*cut)
    return level


def bell_draw(own_key, dims, spread, most, pieces=(), kind=jnp.bfloat16):
    level = block_levels(own_key, dims, pieces, -0.22, 0.18) if pieces else 1.0
    values = jax.random.normal(own_key, dims, jnp.float32) * spread * level
    return jnp.minimum(jnp.maximum(values, -most), most).astype(kind)


def setup_inputs(seed: int = 0) -> dict:
    seeds = jax.random.split(jax.random.key(seed), 16)
    patches = bell_draw(seeds[0], (TOKENS, D), 1.0, 6.0, ((0, 8),))
    cotangent = bell_draw(seeds[1], (TOKENS, D), 1.0, 6.0, ((0, 8),))
    conditioning = bell_draw(seeds[2], (ITEM_SLOTS, CD), 1.0, 6.0, ((0, 8),))
    captions = bell_draw(seeds[3], (ITEM_SLOTS * LTXT, DT), 1.0, 6.0, ((0, 8),))
    item_lengths = draw_item_lengths(jax.random.fold_in(seeds[15], 71), 0)
    grid_widths = draw_grid_widths(jax.random.fold_in(seeds[15], 71), 0)
    w_ada = bell_draw(seeds[6], (CD, 4, D), CD ** -0.5, 0.1875, ((2, 4),))
    norm_gains = jnp.clip(1.0 + 0.15 * jax.random.normal(seeds[7], (4, D), jnp.float32), 0.25, 1.75)
    w_qkv = bell_draw(seeds[8], (3, D, D), D ** -0.5, 0.15625, ((2, 4),))
    head_gains = jnp.clip(1.0 + 0.15 * jax.random.normal(seeds[9], (3, HD), jnp.float32), 0.25, 1.75)
    cross_gate = jnp.clip(jax.random.uniform(seeds[10], (H,), jnp.float32, -1.5, 1.5) * block_levels(seeds[10], (H,), ((0, 4),), -0.4, 0.0), -1.5, 1.5)
    w_caption = bell_draw(seeds[11], (2, DT, D), DT ** -0.5, 0.09375, ((2, 4),))
    w_out = bell_draw(seeds[12], (D, D), D ** -0.5, 0.15625, ((0, 4),))
    w_gate_up = bell_draw(seeds[13], (2, D, FF), D ** -0.5, 0.15625, ((2, 4),))
    w_down = bell_draw(seeds[14], (FF, D), FF ** -0.5, 0.09375, ((0, 4),))
    return dict(patches=patches, cotangent=cotangent, conditioning=conditioning, captions=captions, item_lengths=item_lengths, grid_widths=grid_widths, w_ada=w_ada, norm_gains=norm_gains, w_qkv=w_qkv, head_gains=head_gains, cross_gate=cross_gate, w_caption=w_caption, w_out=w_out, w_gate_up=w_gate_up, w_down=w_down)


@jax.custom_vjp
def low(v):
    return lax.optimization_barrier(v.astype(jnp.bfloat16)).astype(jnp.float32)

@jax.custom_vjp
def low_back(v):
    return v

def low_keep(v):
    return (low(v), None)

def low_pass(kept, grad):
    return (grad,)

def back_keep(v):
    return (v, None)

def back_low(kept, grad):
    return (low(grad),)
low.defvjp(low_keep, low_pass)
low_back.defvjp(back_keep, back_low)
epsilon = 1e-05
scaling = 0.125
masked_score = -1e+30
highest = lax.Precision.HIGHEST

def matmul(left, right):
    return jnp.dot(left, right, precision=highest, preferred_element_type=jnp.float32)

def rms(values, gain_vec):
    return values * lax.rsqrt(lax.optimization_barrier(jnp.mean(values * values, -1, keepdims=True)) + epsilon) * gain_vec

def rotate(values, cos_tab, sin_tab):
    halfway = values.shape[-1] // 2
    former = values[..., :halfway]
    latter = values[..., halfway:]
    cos_tab = cos_tab[..., None, :]
    sin_tab = sin_tab[..., None, :]
    return jnp.concatenate([former * cos_tab - latter * sin_tab, latter * cos_tab + former * sin_tab], -1)

def rotary(values, tables):
    halfway = values.shape[-1] // 2
    return jnp.concatenate([rotate(values[..., :halfway], tables[0], tables[1]), rotate(values[..., halfway:], tables[2], tables[3])], -1)

def rope_tables(row_pos, col_pos, quarter):
    frequency = 10000.0 ** (-jnp.arange(quarter, dtype=jnp.float32) / quarter)
    row_angle = row_pos.astype(jnp.float32)[..., None] * frequency
    col_angle = col_pos.astype(jnp.float32)[..., None] * frequency
    return (jnp.cos(row_angle), jnp.sin(row_angle), jnp.cos(col_angle), jnp.sin(col_angle))

def attention(query_low, key_heads, value_heads, cap_keys, cap_values, cross_gate, block_item):
    reach_blocks = SPAN - 1
    window = 2 * SPAN - 1
    pad_spec = ((0, 0), (reach_blocks, reach_blocks), (0, 0), (0, 0))
    query_h = jnp.transpose(query_low, (2, 0, 1, 3))
    key_pad = jnp.pad(jnp.transpose(key_heads, (2, 0, 1, 3)), pad_spec)
    value_pad = jnp.pad(jnp.transpose(value_heads, (2, 0, 1, 3)), pad_spec)
    cap_key_h = jnp.transpose(cap_keys, (2, 0, 1, 3))
    cap_value_h = jnp.transpose(cap_values, (2, 0, 1, 3))
    item_pad = jnp.pad(block_item, (reach_blocks, reach_blocks), constant_values=-1)

    def one_head(operands):
        query_one, key_one, value_one, cap_key_one, cap_value_one, gate_one = operands

        def one_block(block_idx):
            rows_q = query_one[block_idx]
            key_rows = lax.dynamic_slice_in_dim(key_one, block_idx, window, 0).reshape(window * TOK_DEV, HD)
            value_rows = lax.dynamic_slice_in_dim(value_one, block_idx, window, 0).reshape(window * TOK_DEV, HD)
            near_items = lax.dynamic_slice_in_dim(item_pad, block_idx, window, 0)
            live_keys = jnp.repeat(near_items == block_item[block_idx], TOK_DEV)
            scores = low_back(matmul(rows_q, key_rows.T) * scaling)
            scores = jnp.where(live_keys[None, :], scores, masked_score)
            row_top = lax.optimization_barrier(jnp.max(scores, -1, keepdims=True))
            log_total = row_top + jnp.log(lax.optimization_barrier(jnp.sum(jnp.exp(scores - row_top), -1, keepdims=True)))
            attn_prob = low(jnp.exp(scores - log_total))
            self_out = matmul(attn_prob, value_rows)
            cross_scores = low_back(matmul(rows_q, cap_key_one[block_idx].T) * scaling)
            cross_top = lax.optimization_barrier(jnp.max(cross_scores, -1, keepdims=True))
            cross_log = cross_top + jnp.log(lax.optimization_barrier(jnp.sum(jnp.exp(cross_scores - cross_top), -1, keepdims=True)))
            cross_prob = low(jnp.exp(cross_scores - cross_log))
            cross_out = low_back(matmul(cross_prob, cap_value_one[block_idx]))
            return self_out + jnp.tanh(gate_one) * cross_out
        return lax.map(jax.checkpoint(one_block), jnp.arange(ITEM_SLOTS, dtype=jnp.int32))
    mixed_heads = lax.map(jax.checkpoint(one_head), (query_h, key_pad, value_pad, cap_key_h, cap_value_h, cross_gate))
    return jnp.transpose(mixed_heads, (1, 2, 0, 3))

def layer(patches, conditioning, captions, w_ada, norm_gains, w_qkv, head_gains, cross_gate, w_caption, w_out, w_gate_up, w_down, tables, block_item, block_source):
    mod_slots = matmul(low(jax.nn.silu(conditioning)), w_ada.reshape(CD, 4 * D))
    mod_slots = low_back(mod_slots).reshape(ITEM_SLOTS, 4, D)
    mod_block = mod_slots[block_source]
    scale_one = mod_block[:, 0][:, None, :]
    gate_one = mod_block[:, 1][:, None, :]
    scale_two = mod_block[:, 2][:, None, :]
    gate_two = mod_block[:, 3][:, None, :]
    residual = patches.reshape(ITEM_SLOTS, TOK_DEV, D)
    attn_in = low(rms(residual, norm_gains[0]) * (1.0 + scale_one))
    projected = low_back(jnp.einsum('std,jde->jste', attn_in, w_qkv, precision=highest))
    heads_view = projected.reshape(3, ITEM_SLOTS, TOK_DEV, H, HD)
    query_low = low(rotary(rms(heads_view[0], head_gains[0]), tables))
    key_low = low(rotary(rms(heads_view[1], head_gains[1]), tables))
    value_low = low(heads_view[2])
    cap_raw = low_back(jnp.einsum('skd,jde->jske', captions.reshape(ITEM_SLOTS, LTXT, DT), w_caption, precision=highest))
    cap_keys = low(rms(cap_raw[0].reshape(ITEM_SLOTS, LTXT, H, HD), head_gains[2]))[block_source]
    cap_values = low(cap_raw[1].reshape(ITEM_SLOTS, LTXT, H, HD))[block_source]
    mixed_heads = attention(query_low, key_low, value_low, cap_keys, cap_values, cross_gate, block_item)
    mixed_low = low(low_back(mixed_heads)).reshape(ITEM_SLOTS, TOK_DEV, D)
    attn_full = low_back(jnp.einsum('ste,ed->std', mixed_low, w_out, precision=highest))
    middle = residual + jnp.tanh(gate_one) * rms(attn_full, norm_gains[1])
    ffn_in = low(rms(middle, norm_gains[2]) * (1.0 + scale_two))
    gate_up = low_back(jnp.einsum('std,jdf->jstf', ffn_in, w_gate_up, precision=highest))
    hidden = low(jax.nn.silu(gate_up[0]) * gate_up[1])
    ffn_full = low_back(jnp.einsum('stf,fd->std', hidden, w_down, precision=highest))
    result = middle + jnp.tanh(gate_two) * rms(ffn_full, norm_gains[3])
    return result.reshape(TOKENS, D)

def reference(patches, cotangent, conditioning, captions, item_lengths, grid_widths, w_ada, norm_gains, w_qkv, head_gains, cross_gate, w_caption, w_out, w_gate_up, w_down):
    item_ends = jnp.cumsum(item_lengths).astype(jnp.int32)
    token_ids = jnp.arange(TOKENS, dtype=jnp.int32)
    token_item = lax.optimization_barrier(jnp.sum((token_ids[:, None] >= item_ends[None, :]).astype(jnp.int32), 1)).astype(jnp.int32)
    is_item = token_item[:, None] == jnp.arange(ITEM_SLOTS, dtype=jnp.int32)[None, :]
    item_starts = (item_ends - item_lengths).astype(jnp.int32)
    token_start = lax.optimization_barrier(jnp.sum(jnp.where(is_item, item_starts[None, :], 0), 1)).astype(jnp.int32)
    token_grid = lax.optimization_barrier(jnp.sum(jnp.where(is_item, grid_widths[None, :], 0), 1)).astype(jnp.int32)
    offsets = token_ids - token_start
    tables = tuple((table.reshape(ITEM_SLOTS, TOK_DEV, HD // 4) for table in rope_tables(offsets // token_grid, offsets % token_grid, HD // 4)))
    block_item = token_item[::TOK_DEV]
    block_source = (token_start[::TOK_DEV] // TOK_DEV).astype(jnp.int32)
    floats = tuple((array.astype(jnp.float32) for array in (patches, conditioning, captions, w_ada, norm_gains, w_qkv, head_gains, cross_gate, w_caption, w_out, w_gate_up, w_down)))

    def forward(*inputs):
        return layer(*inputs, tables, block_item, block_source)
    result, pull_back = jax.vjp(forward, *floats)
    gradients = pull_back(cotangent.astype(jnp.float32))
    return (result.astype(jnp.bfloat16), gradients[0].astype(jnp.bfloat16), gradients[1], gradients[2].astype(jnp.bfloat16), gradients[3], gradients[4], gradients[5], gradients[6], gradients[7], gradients[8], gradients[9], gradients[10], gradients[11])
```

```python
import functools

import jax
import jax.numpy as jnp
from jax import lax
from jax.experimental import pallas as pl
from jax.experimental.pallas import tpu as pltpu
from jax.sharding import PartitionSpec as P

HD = 64
SPAN = 4
EPS = 1e-05
LOG2E = 1.4426950408889634
f32 = jnp.float32
bf16 = jnp.bfloat16
VMEM = 56 * 1024 * 1024
NT = (((1,), (1,)), ((), ()))
TN = (((0,), (0,)), ((), ()))


def params(n):
    return pltpu.CompilerParams(
        dimension_semantics=("arbitrary",) * n, vmem_limit_bytes=VMEM
    )


def sds(shape, dtype):
    return jax.ShapeDtypeStruct(shape, dtype)


def mm(a, b):
    return jnp.dot(a, b, preferred_element_type=f32)


def mm_nt(a, b):
    return lax.dot_general(a, b, NT, preferred_element_type=f32)


def mm_tn(a, b):
    return lax.dot_general(a, b, TN, preferred_element_type=f32)


def split(x):
    hi = x.astype(bf16)
    return hi, (x - hi.astype(f32)).astype(bf16)


def head_sum(x, ones):
    hi, lo = split(x)
    return mm(hi, ones) + mm(lo, ones)


def head_ones(n):
    a = lax.broadcasted_iota(jnp.int32, (n, n), 0) // HD
    b = lax.broadcasted_iota(jnp.int32, (n, n), 1) // HD
    return (a == b).astype(bf16)


def halves(n):
    lane = lax.broadcasted_iota(jnp.int32, (1, n), 1)
    return (lane < HD, lane >= HD)


def keep(x, mask):
    return jnp.where(mask, x, jnp.zeros_like(x))


def inv_rms(x):
    return lax.rsqrt(jnp.mean(x * x, -1, keepdims=True) + EPS)


def row(ref, k):
    return ref[k : k + 1, :]


def whole(shape):
    zeros = (0,) * len(shape)
    return pl.BlockSpec(shape, lambda *_: zeros, pipeline_mode=pl.Buffered(1))


def rows_of(br, width, first=0):
    return pl.BlockSpec((br, width), lambda i, *_: (i, first))


def accumulate(ref, value, first):
    @pl.when(first)
    def _():
        ref[...] = value

    @pl.when(jnp.logical_not(first))
    def _():
        ref[...] += value


def col_sum(x):
    return jnp.sum(x, 0, keepdims=True)


def tile3(t, n):
    return jnp.concatenate([t] * (n // t.shape[1]), 1)


def qkv_kernel(p_ref, v_ref, w_ref, c_ref, s1_ref, s2_ref, hg_ref, a_ref, qr_ref, kr_ref, q_ref, k_ref, vv_ref):
    x = p_ref[...].astype(f32)
    a = (x * inv_rms(x) * row(v_ref, 0)).astype(bf16)
    a_ref[...] = a
    n = q_ref.shape[1]
    ones = head_ones(n)
    cos, s1, s2 = (tile3(t[...], n) for t in (c_ref, s1_ref, s2_ref))

    def turned(y, gain):
        z = y * lax.rsqrt(head_sum(y * y, ones) * (1.0 / HD) + EPS) * gain
        return z * cos + pltpu.roll(z, n - 16, 1) * s1 + pltpu.roll(z, 16, 1) * s2

    q = mm(a, w_ref[0])
    qr_ref[...] = q
    q_ref[...] = (turned(q, row(hg_ref, 0)) * (0.125 * LOG2E)).astype(bf16)
    k = mm(a, w_ref[1])
    kr_ref[...] = k
    k_ref[...] = turned(k, row(hg_ref, 1)).astype(bf16)
    vv_ref[...] = mm(a, w_ref[2]).astype(bf16)


def qkv_call(patches, vec, w, tabs, hg, br=256):
    t, d = patches.shape
    n = w.shape[2]
    return pl.pallas_call(
        qkv_kernel,
        grid=(t // br,),
        in_specs=[rows_of(br, d), whole(vec.shape), whole(w.shape)]
        + [rows_of(br, 128)] * 3
        + [whole(hg.shape)],
        out_specs=[rows_of(br, d)] + [rows_of(br, n)] * 5,
        out_shape=[sds((t, d), bf16), sds((t, n), f32), sds((t, n), f32)] + [sds((t, n), bf16)] * 3,
        compiler_params=params(1),
        name="qkv",
    )(patches, vec, w, *tabs, hg)


def dqkv_kernel(dq_ref, dk_ref, dv_ref, qr_ref, kr_ref, c_ref, s1_ref, s2_ref, hg_ref, w_ref, p_ref, g_ref, sc_ref, d_ref, da_ref, hs_ref, cs_ref):
    n = dq_ref.shape[1]
    first = pl.program_id(0) == 0
    ones = head_ones(n)
    cos, s1, s2 = (tile3(t[...], n) for t in (c_ref, s1_ref, s2_ref))

    def back(dy, x, gain):
        dz = dy * cos - pltpu.roll(dy, 16, 1) * s2 - pltpu.roll(dy, n - 16, 1) * s1
        r = lax.rsqrt(head_sum(x * x, ones) * (1.0 / HD) + EPS)
        xh = x * r
        g = dz * gain
        return r * (g - xh * (head_sum(g * xh, ones) * (1.0 / HD))), col_sum(dz * xh)

    dq, hq = back(dq_ref[...], qr_ref[...], row(hg_ref, 0))
    dk, hk = back(dk_ref[...], kr_ref[...], row(hg_ref, 1))
    dql, dkl, dvl = dq.astype(bf16), dk.astype(bf16), dv_ref[...].astype(bf16)
    d_ref[:, :n] = dql
    d_ref[:, n : 2 * n] = dkl
    d_ref[:, 2 * n :] = dvl
    da = mm_nt(dql, w_ref[0]) + mm_nt(dkl, w_ref[1]) + mm_nt(dvl, w_ref[2])
    da_ref[...] = da.astype(bf16)
    x = p_ref[...].astype(f32)
    accumulate(cs_ref, col_sum(da * (x * inv_rms(x))), first)
    accumulate(hs_ref, jnp.concatenate([hq, hk], 0), first)


def dqkv_call(dq, dk, dv, qr, kr, tabs, hg, w, patches, g, sc, br=256):
    t, n = dq.shape
    d = patches.shape[1]
    return pl.pallas_call(
        dqkv_kernel,
        grid=(t // br,),
        in_specs=[rows_of(br, n)] * 5
        + [rows_of(br, 128)] * 3
        + [whole(hg.shape), whole(w.shape), rows_of(br, d), whole(g.shape), whole(sc.shape)],
        out_specs=[rows_of(br, 3 * n), rows_of(br, d), pl.BlockSpec((2, n), lambda i: (0, 0)), pl.BlockSpec((1, d), lambda i: (0, 0))],
        out_shape=[sds((t, 3 * n), bf16), sds((t, d), bf16), sds((2, n), f32), sds((1, d), f32)],
        compiler_params=params(1),
        name="dqkv",
    )(dq, dk, dv, qr, kr, *tabs, hg, w, patches, g, sc)


def soft_sums(q, k, v, mask):
    e = jnp.exp2(mm_nt(q, keep(k, mask))).astype(bf16)
    return mm(e, jnp.where(mask, v, jnp.ones_like(v)))


def attend_kernel(sc, q_ref, k_ref, v_ref, ck_ref, cv_ref, tg_ref, mix_ref, o_ref, li_ref, acc):
    j = pl.program_id(2)
    masks = halves(128)
    keys = 512

    @pl.when(j == 0)
    def _():
        acc[...] = jnp.zeros_like(acc)

    @pl.when(j < sc[0])
    def _():
        q = q_ref[...]
        for h in range(2):
            total = acc[h]
            for c in range(k_ref.shape[0] // keys):
                at = slice(c * keys, (c + 1) * keys)
                total = total + soft_sums(q, k_ref[at, :], v_ref[at, :], masks[h])
            acc[h] = total

    @pl.when(j == SPAN - 1)
    def _():
        q = q_ref[...]

        def finish(a0, a1):
            inverse = 1.0 / jnp.where(masks[0], pltpu.roll(a0, HD, 1), pltpu.roll(a1, HD, 1))
            return jnp.where(masks[0], a0, a1) * inverse, inverse

        o, li = finish(acc[0], acc[1])
        c0, c1 = (soft_sums(q, ck_ref[...], cv_ref[...], m) for m in masks)
        mix_ref[...] = (o + tg_ref[...] * finish(c0, c1)[0]).astype(bf16)
        o_ref[...] = o.astype(bf16)
        li_ref[...] = li


def attend_call(sc, q, k, v, cap, tg, block, bq=512):
    t, n = q.shape
    pairs = n // 128
    text = 256
    mine = lambda p, i, j, s: (i, p)
    return pl.pallas_call(
        attend_kernel,
        grid_spec=pltpu.PrefetchScalarGridSpec(
            num_scalar_prefetch=1,
            grid=(pairs, t // bq, SPAN),
            in_specs=[
                pl.BlockSpec((bq, 128), mine),
                pl.BlockSpec((block, 128), lambda p, i, j, s: (s[2 + j], p)),
                pl.BlockSpec((block, 128), lambda p, i, j, s: (s[2 + j], p)),
                pl.BlockSpec((text, 128), lambda p, i, j, s: (s[1], p)),
                pl.BlockSpec((text, 128), lambda p, i, j, s: (s[1], pairs + p)),
                pl.BlockSpec((1, 128), lambda p, i, j, s: (0, p)),
            ],
            out_specs=[pl.BlockSpec((bq, 128), mine)] * 3,
            scratch_shapes=[pltpu.VMEM((2, bq, 128), f32)],
        ),
        out_shape=[sds((t, n), bf16), sds((t, n), bf16), sds((t, n), f32)],
        compiler_params=params(3),
        name="attend",
    )(sc, q, k, v, cap, cap, tg)


def caption_back_kernel(sc, q_ref, d_ref, ck_ref, cv_ref, tg_ref, dq_ref, dk_ref, dv_ref, gs_ref):
    first = pl.program_id(1) == 0
    masks = halves(128)
    q, d = q_ref[...], d_ref[...]
    dq = jnp.zeros(q.shape, f32)
    dk = jnp.zeros(ck_ref.shape, f32)
    dv = jnp.zeros(ck_ref.shape, f32)
    sums = []
    for h in range(2):
        ck, cv = keep(ck_ref[...], masks[h]), keep(cv_ref[...], masks[h])
        gate = tg_ref[:, h * HD : h * HD + 1]
        e = jnp.exp2(mm_nt(q, ck))
        prob = e * (1.0 / jnp.sum(e, -1, keepdims=True))
        dp = mm_nt(d, cv)
        m = jnp.sum(prob * dp, -1, keepdims=True)
        dc = (prob * (dp - m) * gate).astype(bf16)
        dq = dq + mm(dc, ck)
        dk = dk + mm_tn(dc, keep(q, masks[h]))
        dv = dv + mm_tn(prob.astype(bf16), keep(d, masks[h]))
        sums.append(jnp.sum(m, 0, keepdims=True))
    dq_ref[...] = dq * 0.125
    accumulate(dk_ref, dk * (1.0 / LOG2E), first)
    accumulate(dv_ref, dv * tg_ref[...], first)
    accumulate(gs_ref, jnp.where(masks[0], sums[0], sums[1]), first)


def caption_back_call(sc, q, d, cap, tg, bq=512):
    t, n = q.shape
    pairs = n // 128
    text = 256
    mine = lambda p, i, s: (i, p)
    held = lambda p, i, s: (0, p)
    return pl.pallas_call(
        caption_back_kernel,
        grid_spec=pltpu.PrefetchScalarGridSpec(
            num_scalar_prefetch=1,
            grid=(pairs, t // bq),
            in_specs=[
                pl.BlockSpec((bq, 128), mine),
                pl.BlockSpec((bq, 128), mine),
                pl.BlockSpec((text, 128), lambda p, i, s: (s[1], p)),
                pl.BlockSpec((text, 128), lambda p, i, s: (s[1], pairs + p)),
                pl.BlockSpec((1, 128), held),
            ],
            out_specs=[
                pl.BlockSpec((bq, 128), mine),
                pl.BlockSpec((text, 128), held),
                pl.BlockSpec((text, 128), held),
                pl.BlockSpec((1, 128), held),
            ],
        ),
        out_shape=[sds((t, n), f32), sds((text, n), f32), sds((text, n), f32), sds((1, n), f32)],
        compiler_params=params(2),
        name="caption_back",
    )(sc, q, d, cap, cap, tg)


def dq_kernel(sc, q_ref, d_ref, dl_ref, k_ref, v_ref, c_ref, dq_ref, acc):
    j = pl.program_id(2)
    masks = halves(128)
    keys = 512

    @pl.when(j == 0)
    def _():
        acc[...] = jnp.zeros_like(acc)

    @pl.when(j < sc[0])
    def _():
        q, d = q_ref[...], d_ref[...]
        total = acc[...]
        for c in range(k_ref.shape[0] // keys):
            at = slice(c * keys, (c + 1) * keys)
            for h in range(2):
                k = keep(k_ref[at, :], masks[h])
                e = jnp.exp2(mm_nt(q, k))
                dp = mm_nt(d, keep(v_ref[at, :], masks[h]))
                ds = (e * (dp - dl_ref[:, h * HD : h * HD + 1])).astype(bf16)
                total = total + mm(ds, k)
        acc[...] = total

    @pl.when(j == SPAN - 1)
    def _():
        dq_ref[...] = acc[...] * 0.125 + c_ref[...]


def dq_call(sc, q, d, dl, k, v, cap_dq, block, bq=512):
    t, n = q.shape
    pairs = n // 128
    mine = lambda p, i, j, s: (i, p)
    other = lambda p, i, j, s: (s[2 + j], p)
    return pl.pallas_call(
        dq_kernel,
        grid_spec=pltpu.PrefetchScalarGridSpec(
            num_scalar_prefetch=1,
            grid=(pairs, t // bq, SPAN),
            in_specs=[pl.BlockSpec((bq, 128), mine)] * 3
            + [pl.BlockSpec((block, 128), other)] * 2
            + [pl.BlockSpec((bq, 128), mine)],
            out_specs=pl.BlockSpec((bq, 128), mine),
            scratch_shapes=[pltpu.VMEM((bq, 128), f32)],
        ),
        out_shape=sds((t, n), f32),
        compiler_params=params(3),
        name="dq",
    )(sc, q, d, dl, k, v, cap_dq)


def dkv_kernel(sc, k_ref, v_ref, q_ref, d_ref, dl_ref, dk_ref, dv_ref, acc):
    pair = pl.program_id(0)
    j = pl.program_id(2)
    masks = halves(128)
    queries = 512

    @pl.when(j == 0)
    def _():
        acc[...] = jnp.zeros_like(acc)

    @pl.when(j < sc[0])
    def _():
        k, v = k_ref[...], v_ref[...]
        dk, dv = acc[0], acc[1]
        for h in range(2):
            km, vm = keep(k, masks[h]), keep(v, masks[h])
            delta = dl_ref[0, pl.ds(2 * pair + h, 1), :]
            for c in range(q_ref.shape[0] // queries):
                at = slice(c * queries, (c + 1) * queries)
                q, d = q_ref[at, :], d_ref[at, :]
                e = jnp.exp2(mm_nt(km, q))
                ds = (e * (mm_nt(vm, d) - delta[:, at])).astype(bf16)
                dv = dv + mm(e.astype(bf16), keep(d, masks[h]))
                dk = dk + mm(ds, keep(q, masks[h]))
        acc[0] = dk
        acc[1] = dv

    @pl.when(j == SPAN - 1)
    def _():
        dk_ref[...] = acc[0] * (1.0 / LOG2E)
        dv_ref[...] = acc[1]


def dkv_call(sc, k, v, q, d, dl, block, bk=512):
    t, n = k.shape
    pairs = n // 128
    mine = lambda p, i, j, s: (i, p)
    other = lambda p, i, j, s: (s[2 + j], p)
    return pl.pallas_call(
        dkv_kernel,
        grid_spec=pltpu.PrefetchScalarGridSpec(
            num_scalar_prefetch=1,
            grid=(pairs, t // bk, SPAN),
            in_specs=[pl.BlockSpec((bk, 128), mine)] * 2
            + [pl.BlockSpec((block, 128), other)] * 2
            + [pl.BlockSpec((1, dl.shape[1], block), lambda p, i, j, s: (s[2 + j], 0, 0))],
            out_specs=[pl.BlockSpec((bk, 128), mine)] * 2,
            scratch_shapes=[pltpu.VMEM((2, bk, 128), f32)],
        ),
        out_shape=[sds((t, n), f32)] * 2,
        compiler_params=params(3),
        name="dkv",
    )(sc, k, v, q, d, dl)


def ffn_kernel(p_ref, at_ref, v_ref, wg_ref, wd_ref, mid_ref, a_ref, gu_ref, h_ref, f_ref):
    at = at_ref[...].astype(f32)
    mid = p_ref[...].astype(f32) + row(v_ref, 1) * (at * inv_rms(at))
    mid_ref[...] = mid
    a = (mid * inv_rms(mid) * row(v_ref, 2)).astype(bf16)
    a_ref[...] = a
    g = mm(a, wg_ref[0])
    u = mm(a, wg_ref[1])
    n = g.shape[1]
    gu_ref[:, :n] = g.astype(bf16)
    gu_ref[:, n:] = u.astype(bf16)
    h = (g * jax.nn.sigmoid(g) * u).astype(bf16)
    h_ref[...] = h
    f_ref[...] = mm(h, wd_ref[...]).astype(bf16)


def ffn_call(patches, at, vec, wg, wd, br=256):
    t, d = patches.shape
    n = wd.shape[0]
    return pl.pallas_call(
        ffn_kernel,
        grid=(t // br,),
        in_specs=[rows_of(br, d), rows_of(br, d), whole(vec.shape), whole(wg.shape), whole(wd.shape)],
        out_specs=[rows_of(br, d), rows_of(br, d), rows_of(br, 2 * n), rows_of(br, n), rows_of(br, d)],
        out_shape=[sds((t, d), f32), sds((t, d), bf16), sds((t, 2 * n), bf16), sds((t, n), bf16), sds((t, d), bf16)],
        compiler_params=params(1),
        name="ffn",
    )(patches, at, vec, wg, wd)


def ffn_back_kernel(f_ref, mid_ref, c_ref, gu_ref, v_ref, wg_ref, wd_ref, y_ref, df_ref, dgu_ref, da_ref, cs_ref):
    f = f_ref[...].astype(f32)
    cot = c_ref[...].astype(f32)
    r = inv_rms(f)
    fh = f * r
    y_ref[...] = (mid_ref[...] + row(v_ref, 3) * fh).astype(bf16)
    z = cot * row(v_ref, 3)
    df = (r * (z - fh * jnp.mean(z * fh, -1, keepdims=True))).astype(bf16)
    df_ref[...] = df
    accumulate(cs_ref, col_sum(cot * fh), pl.program_id(0) == 0)
    dh = mm_nt(df, wd_ref[...])
    n = dh.shape[1]
    g = gu_ref[:, :n].astype(f32)
    u = gu_ref[:, n:].astype(f32)
    s = jax.nn.sigmoid(g)
    gs = g * s
    dg = (dh * u * (s + gs * (1.0 - s))).astype(bf16)
    du = (dh * gs).astype(bf16)
    dgu_ref[:, :n] = dg
    dgu_ref[:, n:] = du
    da_ref[...] = (mm_nt(dg, wg_ref[0]) + mm_nt(du, wg_ref[1])).astype(bf16)


def ffn_back_call(f, mid, cot, gu, vec, wg, wd, br=256):
    t, d = f.shape
    n = wd.shape[0]
    return pl.pallas_call(
        ffn_back_kernel,
        grid=(t // br,),
        in_specs=[rows_of(br, d), rows_of(br, d), rows_of(br, d), rows_of(br, 2 * n), whole(vec.shape), whole(wg.shape), whole(wd.shape)],
        out_specs=[rows_of(br, d), rows_of(br, d), rows_of(br, 2 * n), rows_of(br, d), pl.BlockSpec((1, d), lambda i: (0, 0))],
        out_shape=[sds((t, d), bf16), sds((t, d), bf16), sds((t, 2 * n), bf16), sds((t, d), bf16), sds((1, d), f32)],
        compiler_params=params(1),
        name="ffn_back",
    )(f, mid, cot, gu, vec, wg, wd)


def out_back_kernel(da_ref, mid_ref, at_ref, c_ref, v_ref, w_ref, o_ref, li_ref, dm_ref, dat_ref, dx_ref, ds_ref, dc_ref, dr_ref, c3_ref, c2_ref):
    first = pl.program_id(0) == 0
    da = da_ref[...].astype(f32)
    mid = mid_ref[...]
    r = inv_rms(mid)
    mh = mid * r
    z = da * row(v_ref, 2)
    dm = c_ref[...].astype(f32) + r * (z - mh * jnp.mean(z * mh, -1, keepdims=True))
    dm_ref[...] = dm
    accumulate(c3_ref, col_sum(da * mh), first)
    at = at_ref[...].astype(f32)
    ra = inv_rms(at)
    ah = at * ra
    accumulate(c2_ref, col_sum(dm * ah), first)
    z = dm * row(v_ref, 1)
    dat = (ra * (z - ah * jnp.mean(z * ah, -1, keepdims=True))).astype(bf16)
    dat_ref[...] = dat
    dx = mm_nt(dat, w_ref[...]).astype(bf16)
    dx_ref[...] = dx
    n = dx.shape[1]
    ds = dx.astype(f32) * li_ref[...]
    ds_ref[...] = ds.astype(bf16)
    prod = ds * o_ref[...].astype(f32)
    dc_ref[...] = head_sum(prod, head_ones(n))
    hi, lo = split(prod)
    a = lax.broadcasted_iota(jnp.int32, (8, n), 0)
    b = lax.broadcasted_iota(jnp.int32, (8, n), 1) // HD
    sel = (a == b).astype(bf16)
    dr_ref[...] = mm_nt(sel, hi) + mm_nt(sel, lo)


def out_back_call(da, mid, at, cot, vec, w, o, li, br=256):
    t, d = da.shape
    n = w.shape[0]
    one = pl.BlockSpec((1, d), lambda i: (0, 0))
    return pl.pallas_call(
        out_back_kernel,
        grid=(t // br,),
        in_specs=[rows_of(br, d)] * 4 + [whole(vec.shape), whole(w.shape), rows_of(br, n), rows_of(br, n)],
        out_specs=[rows_of(br, d), rows_of(br, d), rows_of(br, n), rows_of(br, n), rows_of(br, n), pl.BlockSpec((8, br), lambda i: (0, i)), one, one],
        out_shape=[sds((t, d), f32), sds((t, d), bf16), sds((t, n), bf16), sds((t, n), bf16), sds((t, n), f32), sds((8, t), f32), sds((1, d), f32), sds((1, d), f32)],
        compiler_params=params(1),
        name="out_back",
    )(da, mid, at, cot, vec, w, o, li)


def last_kernel(da_ref, p_ref, dm_ref, v_ref, o_ref):
    x = p_ref[...].astype(f32)
    r = inv_rms(x)
    xh = x * r
    z = da_ref[...].astype(f32) * row(v_ref, 0)
    o_ref[...] = (dm_ref[...] + r * (z - xh * jnp.mean(z * xh, -1, keepdims=True))).astype(bf16)


def last_call(da, patches, dm, vec, br=256):
    t, d = da.shape
    return pl.pallas_call(
        last_kernel,
        grid=(t // br,),
        in_specs=[rows_of(br, d)] * 3 + [whole(vec.shape)],
        out_specs=rows_of(br, d),
        out_shape=sds((t, d), bf16),
        compiler_params=params(1),
        name="last",
    )(da, patches, dm, vec)


def caption_grad_kernel(dk_ref, dv_ref, kr_ref, hg_ref, d_ref, hs_ref):
    n = dk_ref.shape[1]
    ones = head_ones(n)
    x = kr_ref[...]
    r = lax.rsqrt(head_sum(x * x, ones) * (1.0 / HD) + EPS)
    xh = x * r
    dy = dk_ref[...]
    g = dy * row(hg_ref, 2)
    d_ref[:, :n] = (r * (g - xh * (head_sum(g * xh, ones) * (1.0 / HD)))).astype(bf16)
    d_ref[:, n:] = dv_ref[...].astype(bf16)
    hs_ref[...] = col_sum(dy * xh)


def caption_norm_kernel(kr_ref, v_ref, hg_ref, o_ref):
    n = kr_ref.shape[1]
    x = kr_ref[...]
    r = lax.rsqrt(head_sum(x * x, head_ones(n)) * (1.0 / HD) + EPS)
    o_ref[:, :n] = (x * r * row(hg_ref, 2)).astype(bf16)
    o_ref[:, n:] = v_ref[...].astype(bf16)


def xor_gather(x):
    half = x.shape[0] // 2
    swap = lambda a, m: lax.ppermute(a, "wide", [(i, i ^ m) for i in range(8)])
    a, b = x[:half], x[half:]
    ra, rb = swap(a, 2), swap(b, 4)
    a4, a6 = swap(a, 4), swap(ra, 4)
    b2, b6 = swap(b, 2), swap(rb, 2)
    parts = [x, None, jnp.concatenate([ra, b2]), None, jnp.concatenate([a4, rb]), None, jnp.concatenate([a6, b6]), None]
    for m in (0, 2, 4, 6):
        parts[m + 1] = swap(parts[m], 1)
    return jnp.concatenate(parts)


def gather_wide(x, place):
    if lax.axis_size("wide") == 8:
        return xor_gather(x)
    return lax.all_gather(x, "wide", axis=0, tiled=True)


def narrow_sum(x):
    return lax.psum(x, "narrow")


def scatter_rows(x):
    return lax.psum_scatter(x.astype(bf16), "wide", scatter_dimension=0, tiled=True)


def rope_tables(position, width):
    lane = jnp.arange(128, dtype=jnp.int32)
    within = lane % HD
    quarter = HD // 4
    frequency = 10000.0 ** (-(within % quarter).astype(f32) / quarter)
    by_row = within < HD // 2
    where = jnp.where(by_row[None, :], (position // width)[:, None], (position % width)[:, None])
    angle = where.astype(f32) * frequency[None, :]
    cos, sin = jnp.cos(angle), jnp.sin(angle)
    former = (within % (HD // 2) < quarter)[None, :]
    return cos, jnp.where(former, -sin, 0.0), jnp.where(former, 0.0, sin)


def local(
    patches,
    cotangent,
    conditioning,
    captions,
    item_lengths,
    grid_widths,
    w_ada,
    norm_gains,
    w_qkv,
    head_gains,
    cross_gate,
    w_caption,
    w_out,
    w_gate_up,
    w_down,
):
    t, d = patches.shape
    n = w_qkv.shape[2]
    heads = n // HD
    ada = w_ada.shape[2]
    ff = w_down.shape[0]
    text = captions.shape[0]
    cd = conditioning.shape[1]
    count = lax.axis_size("wide")
    deep = lax.axis_size("narrow")
    me = lax.axis_index("wide")
    mz = lax.axis_index("narrow")

    slots = item_lengths.shape[0]
    spans = item_lengths // t
    order = jnp.arange(slots, dtype=jnp.int32)
    ends = jnp.sum(jnp.where(order[None, :] <= order[:, None], spans[None, :], 0), 1)
    blocks = jnp.arange(count, dtype=jnp.int32)
    item = jnp.sum((ends[None, :] <= blocks[:, None]).astype(jnp.int32), 1)
    is_item = item[:, None] == order[None, :]
    pick = lambda values: jnp.sum(jnp.where(is_item, values[None, :], 0), 1)
    firsts = pick(ends - spans)
    mine = blocks == me
    of_me = lambda values: jnp.sum(jnp.where(mine, values, 0))
    first = of_me(firsts)
    length = of_me(pick(spans))
    width = of_me(pick(grid_widths))
    position = (me - first) * t + jnp.arange(t, dtype=jnp.int32)
    tabs = rope_tables(position, width)
    steps = first + jnp.minimum(jnp.arange(SPAN, dtype=jnp.int32), length - 1)
    if count == 8:
        steps = steps ^ me
    sc = jnp.concatenate([jnp.stack([length, first]), steps]).astype(jnp.int32)

    cond = conditioning.astype(f32)[0]
    silu_low = jax.nn.silu(cond).astype(bf16)
    mod = jnp.sum(silu_low.astype(f32)[:, None, None] * w_ada.astype(f32), 0)
    share = cd // deep
    sent = jnp.concatenate([mod.reshape(-1), lax.dynamic_slice_in_dim(cond, mz * share, share)])
    got = lax.all_gather(lax.all_gather(sent, "narrow"), "wide")
    mods = got[:, :, : 4 * ada].reshape(count, deep, 4, ada).transpose(0, 2, 1, 3).reshape(count, 4, d)
    conds = got[:, :, 4 * ada :].reshape(count, cd)
    my_mod = lax.dynamic_index_in_dim(mods, first, 0, False)
    of_block = jnp.sum(jnp.where((firsts[:, None] == blocks[None, :])[:, :, None, None], mods[None], 0.0), 1)
    scales = 1.0 + of_block
    gates = jnp.tanh(of_block)
    factor = jnp.stack([1.0 + my_mod[0], jnp.tanh(my_mod[1]), 1.0 + my_mod[2], jnp.tanh(my_mod[3])])
    vec = norm_gains * factor
    hg = jnp.tile(head_gains, (1, heads))
    tg_heads = jnp.tanh(cross_gate)
    tg = jnp.repeat(tg_heads, HD)[None, :]

    cap_raw = jnp.einsum("kd,jde->jke", captions, w_caption, preferred_element_type=f32)
    cap_own = pl.pallas_call(
        caption_norm_kernel,
        out_shape=sds((text, 2 * n), bf16),
        compiler_params=params(0),
        name="caption_norm",
    )(cap_raw[0], cap_raw[1], hg)
    cap = lax.all_gather(cap_own, "wide", axis=0, tiled=True)

    a1, q_raw, k_raw, q, k, v = qkv_call(patches, vec, w_qkv, tabs, hg)
    k_all = gather_wide(k, me)
    v_all = gather_wide(v, me)
    q_all = gather_wide(q, me)
    mixed, o_self, linv = attend_call(sc, q, k_all, v_all, cap, tg, t)
    attn = narrow_sum(mm(mixed, w_out).astype(bf16))

    mid, a3, gu, hidden, ffn_part = ffn_call(patches, attn, vec, w_gate_up, w_down)
    ffn = narrow_sum(ffn_part)
    output, d_ffn, d_gu, da3_part, c4 = ffn_back_call(ffn, mid, cotangent, gu, vec, w_gate_up, w_down)
    da3 = narrow_sum(da3_part)
    g_down = scatter_rows(mm_tn(d_ffn, hidden))
    g_gu = scatter_rows(mm_tn(a3, d_gu))

    d_mid, d_attn, d_mixed, d_scaled, delta, delta_row, c3, c2 = out_back_call(
        da3, mid, attn, cotangent, vec, w_out, o_self, linv
    )
    d_all = gather_wide(d_scaled, me)
    if count == 8:
        delta_all = lax.all_gather(delta_row, "wide")
        delta_all = jnp.stack([lax.dynamic_index_in_dim(delta_all, me ^ m, 0, False) for m in range(8)])
    else:
        delta_all = lax.all_gather(delta_row, "wide")
    dq_cap, dck, dcv, gate_sum = caption_back_call(sc, q, d_mixed, cap, tg)
    cap_sent = jnp.concatenate([dck, dcv], 1).astype(bf16)
    cap_got = lax.all_gather(cap_sent, "wide")
    cap_total = jnp.sum(jnp.where((firsts == me)[:, None, None], cap_got.astype(f32), 0.0), 0)
    dq = dq_call(sc, q, d_scaled, delta, k_all, v_all, dq_cap, t)
    dk, dv = dkv_call(sc, k, v, q_all, d_all, delta_all, t)
    d_qkv, da1_part, hs_qk, c1 = dqkv_call(dq, dk, dv, q_raw, k_raw, tabs, hg, w_qkv, patches, vec, vec)
    da1 = narrow_sum(da1_part)
    grad_patches = last_call(da1, patches, d_mid, vec)
    g_out = scatter_rows(mm_tn(d_attn, mixed))
    g_qkv = scatter_rows(mm_tn(a1, d_qkv))

    d_cap, hs_c = pl.pallas_call(
        caption_grad_kernel,
        out_shape=[sds((text, 2 * n), bf16), sds((1, n), f32)],
        compiler_params=params(0),
        name="caption_grad",
    )(cap_total[:, :n], cap_total[:, n:], cap_raw[0], hg)
    g_cap = scatter_rows(mm_tn(captions, d_cap))
    d_text = mm_nt(d_cap[:, :n], w_caption[0]) + mm_nt(d_cap[:, n:], w_caption[1])
    grad_captions = narrow_sum(d_text.astype(bf16))

    head_part = jnp.concatenate([hs_qk, hs_c]).reshape(3, heads, HD).sum(1)
    gate_part = gate_sum[0, ::HD] * (1.0 - tg_heads * tg_heads)
    sent = jnp.concatenate([c1[0], head_part.reshape(-1), gate_part])
    got = lax.all_gather(sent, "narrow")
    summed = jnp.sum(got[:, : d + 3 * HD], 0)
    sent = jnp.concatenate([summed, got[:, d + 3 * HD :].reshape(-1), c2[0], c3[0], c4[0]])
    got = lax.all_gather(sent, "wide")
    one, rest = got[:, :d], got[:, d:]
    grad_head_gains = jnp.sum(rest[:, : 3 * HD], 0).reshape(3, HD)
    grad_cross_gate = jnp.sum(rest[:, 3 * HD : 3 * HD + deep * heads], 0)
    two, three, four = (rest[:, 3 * HD + deep * heads + k * d :][:, :d] for k in range(3))
    cols = jnp.stack([one, two, three, four], 1)
    gain_factor = jnp.stack([scales[:, 0], gates[:, 1], scales[:, 2], gates[:, 3]], 1)
    gain_grads = jnp.sum(gain_factor * cols, 0)
    wide_cols = d // count
    grad_norm_gains = lax.dynamic_slice_in_dim(gain_grads, me * wide_cols, wide_cols, 1)
    ones = jnp.ones_like(one)
    slope = jnp.stack([ones, 1.0 - gates[:, 1] ** 2, ones, 1.0 - gates[:, 3] ** 2], 1)
    d_mod = lax.dynamic_slice_in_dim(slope * norm_gains[None] * cols, mz * ada, ada, 2)
    at_slot = (firsts[None, :] == blocks[:, None]).astype(f32)
    d_slots = jnp.sum(at_slot[:, :, None, None] * d_mod[None], 1).astype(bf16).astype(f32)
    cond_rows = cd // count
    silu_mine = lax.dynamic_slice_in_dim(jax.nn.silu(conds).astype(bf16).astype(f32), me * cond_rows, cond_rows, 1)
    grad_ada = jnp.sum(silu_mine[:, :, None, None] * d_slots[:, None], 0)
    d_mine = lax.dynamic_index_in_dim(d_slots, me, 0, False)
    cond_part = jnp.sum(d_mine[None] * w_ada.astype(f32), (1, 2))
    cond_total = jnp.sum(lax.all_gather(cond_part, "narrow"), 0)
    pull_silu = jax.vjp(jax.nn.silu, cond)[1]
    grad_conditioning = pull_silu(cond_total)[0].reshape(1, -1)

    rows = d // count
    return (
        output,
        grad_patches,
        grad_conditioning,
        grad_captions,
        grad_ada,
        grad_norm_gains,
        g_qkv.astype(f32).reshape(rows, 3, n).transpose(1, 0, 2),
        grad_head_gains,
        grad_cross_gate,
        g_cap.astype(f32).reshape(-1, 2, n).transpose(1, 0, 2),
        g_out.astype(f32).T,
        g_gu.astype(f32).reshape(rows, 2, ff).transpose(1, 0, 2),
        g_down.astype(f32).T,
    )


def solution(mesh):
    placed = (
        P("wide", None),
        P("wide", None),
        P("wide", None),
        P("wide", None),
        P(),
        P(),
        P(None, None, "narrow"),
        P(),
        P(None, None, "narrow"),
        P(),
        P("narrow"),
        P(None, None, "narrow"),
        P("narrow", None),
        P(None, None, "narrow"),
        P("narrow", None),
    )
    return jax.shard_map(
        local,
        mesh=mesh,
        in_specs=placed,
        out_specs=(
            P("wide", None),
            P("wide", None),
            P("wide", None),
            P("wide", None),
            P("wide", None, "narrow"),
            P(None, "wide"),
            P(None, "wide", "narrow"),
            P(),
            P(),
            P(None, "wide", "narrow"),
            P("narrow", "wide"),
            P(None, "wide", "narrow"),
            P("narrow", "wide"),
        ),
        check_vma=False,
    )
```

```python
import functools

import jax
import jax.numpy as jnp
from jax import lax
from jax.experimental import pallas as pl
from jax.experimental.pallas import tpu as pltpu
from jax.sharding import PartitionSpec as P

HD = 64
SPAN = 4
EPS = 1e-05
LOG2E = 1.4426950408889634
f32 = jnp.float32
bf16 = jnp.bfloat16
VMEM = 56 * 1024 * 1024
BR = 256
NT = (((1,), (1,)), ((), ()))
TN = (((0,), (0,)), ((), ()))


def params(n):
    return pltpu.CompilerParams(
        dimension_semantics=("arbitrary",) * n, vmem_limit_bytes=VMEM
    )


def sds(shape, dtype):
    return jax.ShapeDtypeStruct(shape, dtype)


def mm(a, b):
    return jnp.dot(a, b, preferred_element_type=f32)


def mm_nt(a, b):
    return lax.dot_general(a, b, NT, preferred_element_type=f32)


def mm_tn(a, b):
    return lax.dot_general(a, b, TN, preferred_element_type=f32)


def split(x):
    hi = x.astype(bf16)
    return hi, (x - hi.astype(f32)).astype(bf16)


def head_sum(x, ones):
    hi, lo = split(x)
    return mm(hi, ones) + mm(lo, ones)


def head_ones(n):
    a = lax.broadcasted_iota(jnp.int32, (n, n), 0) // HD
    b = lax.broadcasted_iota(jnp.int32, (n, n), 1) // HD
    return (a == b).astype(bf16)


def halves(n):
    lane = lax.broadcasted_iota(jnp.int32, (1, n), 1)
    return (lane < HD, lane >= HD)


def keep(x, mask):
    return jnp.where(mask, x, jnp.zeros_like(x))


def inv_rms(x):
    return lax.rsqrt(jnp.mean(x * x, -1, keepdims=True) + EPS)


def row(ref, k):
    return ref[k : k + 1, :]


def whole(shape):
    zeros = (0,) * len(shape)
    return pl.BlockSpec(shape, lambda *_: zeros, pipeline_mode=pl.Buffered(1))


def rows_of(br, width, first=0):
    return pl.BlockSpec((br, width), lambda i, *_: (i, first))


def accumulate(ref, value, first):
    @pl.when(first)
    def _():
        ref[...] = value

    @pl.when(jnp.logical_not(first))
    def _():
        ref[...] += value


def col_sum(x):
    return jnp.sum(x, 0, keepdims=True)


def tile3(t, n):
    return jnp.concatenate([t] * (n // t.shape[1]), 1)


def qkv_kernel(p_ref, v_ref, w_ref, c_ref, s1_ref, s2_ref, hg_ref, a_ref, qr_ref, kr_ref, q_ref, k_ref, vv_ref):
    x = p_ref[...].astype(f32)
    a = (x * inv_rms(x) * row(v_ref, 0)).astype(bf16)
    a_ref[...] = a
    n = q_ref.shape[1]
    ones = head_ones(n)
    cos, s1, s2 = (tile3(t[...], n) for t in (c_ref, s1_ref, s2_ref))

    def turned(y, gain):
        z = y * lax.rsqrt(head_sum(y * y, ones) * (1.0 / HD) + EPS) * gain
        return z * cos + pltpu.roll(z, n - 16, 1) * s1 + pltpu.roll(z, 16, 1) * s2

    q = mm(a, w_ref[0])
    qr_ref[...] = q
    q_ref[...] = (turned(q, row(hg_ref, 0)) * (0.125 * LOG2E)).astype(bf16)
    k = mm(a, w_ref[1])
    kr_ref[...] = k
    k_ref[...] = turned(k, row(hg_ref, 1)).astype(bf16)
    vv_ref[...] = mm(a, w_ref[2]).astype(bf16)


def qkv_call(patches, vec, w, tabs, hg, br=256):
    t, d = patches.shape
    n = w.shape[2]
    return pl.pallas_call(
        qkv_kernel,
        grid=(t // br,),
        in_specs=[rows_of(br, d), whole(vec.shape), whole(w.shape)]
        + [rows_of(br, 128)] * 3
        + [whole(hg.shape)],
        out_specs=[rows_of(br, d)] + [rows_of(br, n)] * 5,
        out_shape=[sds((t, d), bf16), sds((t, n), f32), sds((t, n), f32)] + [sds((t, n), bf16)] * 3,
        compiler_params=params(1),
        name="qkv",
    )(patches, vec, w, *tabs, hg)


def soft_sums(q, k, v, mask):
    e = jnp.exp2(mm_nt(q, keep(k, mask))).astype(bf16)
    return mm(e, jnp.where(mask, v, jnp.ones_like(v)))


def attend_kernel(sc, q_ref, k_ref, v_ref, ck_ref, cv_ref, tg_ref, mix_ref, o_ref, li_ref, acc):
    j = pl.program_id(1)
    masks = halves(128)
    keys = 512

    @pl.when(j == 0)
    def _():
        acc[...] = jnp.zeros_like(acc)

    @pl.when(j < sc[0])
    def _():
        q = q_ref[...]
        for h in range(2):
            total = acc[h]
            for c in range(k_ref.shape[0] // keys):
                at = slice(c * keys, (c + 1) * keys)
                total = total + soft_sums(q, k_ref[at, :], v_ref[at, :], masks[h])
            acc[h] = total

    @pl.when(j == SPAN - 1)
    def _():
        q = q_ref[...]

        def finish(a0, a1):
            inverse = 1.0 / jnp.where(masks[0], pltpu.roll(a0, HD, 1), pltpu.roll(a1, HD, 1))
            return jnp.where(masks[0], a0, a1) * inverse, inverse

        o, li = finish(acc[0], acc[1])
        c0, c1 = (soft_sums(q, ck_ref[...], cv_ref[...], m) for m in masks)
        mix_ref[...] = (o + tg_ref[...] * finish(c0, c1)[0]).astype(bf16)
        o_ref[...] = o.astype(bf16)
        li_ref[...] = li


def attend_call(sc, q, k, v, cap, tg, c, block):
    n = q.shape[1]
    pairs = n // 128
    text = cap.shape[0] * block // k.shape[0]
    mine = lambda p, j, s: (0, p)
    return pl.pallas_call(
        attend_kernel,
        grid_spec=pltpu.PrefetchScalarGridSpec(
            num_scalar_prefetch=1,
            grid=(pairs, SPAN),
            in_specs=[
                pl.BlockSpec((BR, 128), lambda p, j, s: (c, p)),
                pl.BlockSpec((block, 128), lambda p, j, s: (s[2 + j], p)),
                pl.BlockSpec((block, 128), lambda p, j, s: (s[2 + j], p)),
                pl.BlockSpec((text, 128), lambda p, j, s: (s[1], p)),
                pl.BlockSpec((text, 128), lambda p, j, s: (s[1], pairs + p)),
                pl.BlockSpec((1, 128), mine),
            ],
            out_specs=[pl.BlockSpec((BR, 128), mine)] * 3,
            scratch_shapes=[pltpu.VMEM((2, BR, 128), f32)],
        ),
        out_shape=[sds((BR, n), bf16), sds((BR, n), bf16), sds((BR, n), f32)],
        compiler_params=params(2),
        name="attend",
    )(sc, q, k, v, cap, cap, tg)


def caption_back_kernel(sc, q_ref, d_ref, ck_ref, cv_ref, tg_ref, dq_ref, dk_ref, dv_ref, gs_ref):
    masks = halves(128)
    q, d = q_ref[...], d_ref[...]
    dq = jnp.zeros(q.shape, f32)
    dk = jnp.zeros(ck_ref.shape, f32)
    dv = jnp.zeros(ck_ref.shape, f32)
    sums = []
    for h in range(2):
        ck, cv = keep(ck_ref[...], masks[h]), keep(cv_ref[...], masks[h])
        gate = tg_ref[:, h * HD : h * HD + 1]
        e = jnp.exp2(mm_nt(q, ck))
        prob = e * (1.0 / jnp.sum(e, -1, keepdims=True))
        dp = mm_nt(d, cv)
        m = jnp.sum(prob * dp, -1, keepdims=True)
        dc = (prob * (dp - m) * gate).astype(bf16)
        dq = dq + mm(dc, ck)
        dk = dk + mm_tn(dc, keep(q, masks[h]))
        dv = dv + mm_tn(prob.astype(bf16), keep(d, masks[h]))
        sums.append(jnp.sum(m, 0, keepdims=True))
    dq_ref[...] = dq * 0.125
    dk_ref[...] = dk * (1.0 / LOG2E)
    dv_ref[...] = dv * tg_ref[...]
    gs_ref[...] = jnp.where(masks[0], sums[0], sums[1])


def caption_back_call(sc, q, d, cap, tg, c, text):
    n = q.shape[1]
    pairs = n // 128
    mine = lambda p, s: (0, p)
    return pl.pallas_call(
        caption_back_kernel,
        grid_spec=pltpu.PrefetchScalarGridSpec(
            num_scalar_prefetch=1,
            grid=(pairs,),
            in_specs=[
                pl.BlockSpec((BR, 128), lambda p, s: (c, p)),
                pl.BlockSpec((BR, 128), mine),
                pl.BlockSpec((text, 128), lambda p, s: (s[1], p)),
                pl.BlockSpec((text, 128), lambda p, s: (s[1], pairs + p)),
                pl.BlockSpec((1, 128), mine),
            ],
            out_specs=[
                pl.BlockSpec((BR, 128), mine),
                pl.BlockSpec((text, 128), mine),
                pl.BlockSpec((text, 128), mine),
                pl.BlockSpec((1, 128), mine),
            ],
        ),
        out_shape=[sds((BR, n), f32), sds((text, n), f32), sds((text, n), f32), sds((1, n), f32)],
        compiler_params=params(1),
        name="caption_back",
    )(sc, q, d, cap, cap, tg)


def minus_delta(rows, head):
    lane = lax.broadcasted_iota(jnp.int32, (rows, 128), 1)
    return jnp.where((lane >= 3 * head) & (lane < 3 * head + 3), -1.0, 0.0).astype(bf16)


def dq_kernel(sc, q_ref, d_ref, x_ref, k_ref, v_ref, c_ref, dq_ref, acc):
    pair = pl.program_id(0)
    j = pl.program_id(1)
    masks = halves(128)
    keys = 512

    @pl.when(j == 0)
    def _():
        acc[...] = jnp.zeros_like(acc)

    @pl.when(j < sc[0])
    def _():
        q = q_ref[...]
        dx = jnp.concatenate([d_ref[...], x_ref[...]], 1)
        total = acc[...]
        for h in range(2):
            off = minus_delta(keys, 2 * pair + h)
            for c in range(k_ref.shape[0] // keys):
                at = slice(c * keys, (c + 1) * keys)
                k = keep(k_ref[at, :], masks[h])
                e = jnp.exp2(mm_nt(q, k))
                dp = mm_nt(dx, jnp.concatenate([keep(v_ref[at, :], masks[h]), off], 1))
                total = total + mm((e * dp).astype(bf16), k)
        acc[...] = total

    @pl.when(j == SPAN - 1)
    def _():
        dq_ref[...] = acc[...] * 0.125 + c_ref[...]


def dq_call(sc, q, d, k, v, cap_dq, c, block):
    n = q.shape[1]
    pairs = n // 128
    mine = lambda p, j, s: (0, p)
    other = lambda p, j, s: (s[2 + j], p)
    return pl.pallas_call(
        dq_kernel,
        grid_spec=pltpu.PrefetchScalarGridSpec(
            num_scalar_prefetch=1,
            grid=(pairs, SPAN),
            in_specs=[
                pl.BlockSpec((BR, 128), lambda p, j, s: (c, p)),
                pl.BlockSpec((BR, 128), mine),
                pl.BlockSpec((BR, 128), lambda p, j, s: (0, pairs)),
                pl.BlockSpec((block, 128), other),
                pl.BlockSpec((block, 128), other),
                pl.BlockSpec((BR, 128), mine),
            ],
            out_specs=pl.BlockSpec((BR, 128), mine),
            scratch_shapes=[pltpu.VMEM((BR, 128), f32)],
        ),
        out_shape=sds((BR, n), f32),
        compiler_params=params(2),
        name="dq",
    )(sc, q, d, d, k, v, cap_dq)


def dkv_kernel(start, sc, k_ref, v_ref, q_ref, d_ref, x_ref, *rest):
    dk_ref, dv_ref = rest[-2:]
    pair = pl.program_id(0)
    j = pl.program_id(1)
    masks = halves(128)
    keys = 512

    @pl.when(j == 0)
    def _():
        if start:
            dk_ref[...] = jnp.zeros_like(dk_ref)
            dv_ref[...] = jnp.zeros_like(dv_ref)
        else:
            dk_ref[...] = rest[0][...]
            dv_ref[...] = rest[1][...]

    @pl.when(j < sc[0])
    def _():
        q, d = q_ref[...], d_ref[...]
        dx = jnp.concatenate([d, x_ref[...]], 1)
        qs = [keep(q, m) for m in masks]
        ds = [keep(d, m) for m in masks]
        for c in range(k_ref.shape[0] // keys):
            at = slice(c * keys, (c + 1) * keys)
            dk, dv = dk_ref[at, :], dv_ref[at, :]
            for h in range(2):
                off = minus_delta(keys, 2 * pair + h)
                e = jnp.exp2(mm_nt(k_ref[at, :], qs[h]))
                dp = mm_nt(jnp.concatenate([keep(v_ref[at, :], masks[h]), off], 1), dx)
                dv = dv + mm(e.astype(bf16), ds[h])
                dk = dk + mm((e * dp).astype(bf16), qs[h])
            dk_ref[at, :] = dk
            dv_ref[at, :] = dv


def dkv_call(sc, k, v, q_all, d_all, before, c):
    t, n = k.shape
    pairs = n // 128
    chunks = t // BR
    mine = pl.BlockSpec((t, 128), lambda p, j, s: (0, p))
    return pl.pallas_call(
        functools.partial(dkv_kernel, not before),
        grid_spec=pltpu.PrefetchScalarGridSpec(
            num_scalar_prefetch=1,
            grid=(pairs, SPAN),
            in_specs=[
                mine,
                mine,
                pl.BlockSpec((BR, 128), lambda p, j, s: (s[2 + SPAN + j] * chunks + c, p)),
                pl.BlockSpec((BR, 128), lambda p, j, s: (s[2 + j], p)),
                pl.BlockSpec((BR, 128), lambda p, j, s: (s[2 + j], pairs)),
            ]
            + [mine] * len(before),
            out_specs=[mine, mine],
        ),
        out_shape=[sds((t, n), f32)] * 2,
        input_output_aliases={6: 0, 7: 1} if before else {},
        compiler_params=params(2),
        name="dkv",
    )(sc, k, v, q_all, d_all, d_all, *before)


def chunk_call(kernel, name, c, ins, specs, chunk_outs, sum_outs, whole_outs, before):
    one = lambda r, w: pl.BlockSpec((r, w), lambda i: (0, 0))
    loose = chunk_outs + sum_outs
    into = [pl.BlockSpec((BR, w), lambda i: (c, 0)) for _, w, _ in whole_outs]
    held = list(before)
    body = kernel
    if held:

        def body(*refs):
            kernel(*refs[: len(ins)], *refs[len(ins) + len(held) :])

    return pl.pallas_call(
        body,
        grid=(1,),
        in_specs=specs + [pl.BlockSpec(memory_space=pl.ANY)] * len(held),
        out_specs=[one(r, w) for r, w, _ in loose] + into,
        out_shape=[sds((r, w), k) for r, w, k in loose + whole_outs],
        input_output_aliases={len(ins) + k: len(loose) + k for k in range(len(held))},
        compiler_params=params(1),
        name=name,
    )(*ins, *held)


def part(c, width):
    return pl.BlockSpec((BR, width), lambda i: (c, 0))


def alone(width):
    return pl.BlockSpec((BR, width), lambda i: (0, 0))


def ffn_kernel(p_ref, at_ref, v_ref, wg_ref, wd_ref, mid_ref, gu_ref, f_ref, a_ref, h_ref):
    at = at_ref[...].astype(f32)
    mid = p_ref[...].astype(f32) + row(v_ref, 1) * (at * inv_rms(at))
    mid_ref[...] = mid
    a = (mid * inv_rms(mid) * row(v_ref, 2)).astype(bf16)
    a_ref[...] = a
    g = mm(a, wg_ref[0])
    u = mm(a, wg_ref[1])
    n = g.shape[1]
    gu_ref[:, :n] = g.astype(bf16)
    gu_ref[:, n:] = u.astype(bf16)
    h = (g * jax.nn.sigmoid(g) * u).astype(bf16)
    h_ref[...] = h
    f_ref[...] = mm(h, wd_ref[...]).astype(bf16)


def ffn_call(c, patches, at, vec, wg, wd, before):
    t, d = patches.shape
    n = wd.shape[0]
    return chunk_call(
        ffn_kernel,
        "ffn",
        c,
        (patches, at, vec, wg, wd),
        [part(c, d), alone(d), whole(vec.shape), whole(wg.shape), whole(wd.shape)],
        [(BR, d, f32), (BR, 2 * n, bf16), (BR, d, bf16)],
        [],
        [(t, d, bf16), (t, n, bf16)],
        before,
    )


def ffn_back_kernel(f_ref, mid_ref, c_ref, gu_ref, v_ref, wg_ref, wd_ref, da_ref, cs_ref, y_ref, df_ref, dgu_ref):
    f = f_ref[...].astype(f32)
    cot = c_ref[...].astype(f32)
    r = inv_rms(f)
    fh = f * r
    y_ref[...] = (mid_ref[...] + row(v_ref, 3) * fh).astype(bf16)
    z = cot * row(v_ref, 3)
    df = (r * (z - fh * jnp.mean(z * fh, -1, keepdims=True))).astype(bf16)
    df_ref[...] = df
    cs_ref[...] = col_sum(cot * fh)
    dh = mm_nt(df, wd_ref[...])
    n = dh.shape[1]
    g = gu_ref[:, :n].astype(f32)
    u = gu_ref[:, n:].astype(f32)
    s = jax.nn.sigmoid(g)
    gs = g * s
    dg = (dh * u * (s + gs * (1.0 - s))).astype(bf16)
    du = (dh * gs).astype(bf16)
    dgu_ref[:, :n] = dg
    dgu_ref[:, n:] = du
    da_ref[...] = (mm_nt(dg, wg_ref[0]) + mm_nt(du, wg_ref[1])).astype(bf16)


def ffn_back_call(c, f, mid, cot, gu, vec, wg, wd, before):
    t, d = cot.shape
    n = wd.shape[0]
    return chunk_call(
        ffn_back_kernel,
        "ffn_back",
        c,
        (f, mid, cot, gu, vec, wg, wd),
        [alone(d), alone(d), part(c, d), alone(2 * n), whole(vec.shape), whole(wg.shape), whole(wd.shape)],
        [(BR, d, bf16)],
        [(1, d, f32)],
        [(t, d, bf16), (t, d, bf16), (t, 2 * n, bf16)],
        before,
    )


def out_back_kernel(da_ref, mid_ref, at_ref, c_ref, v_ref, w_ref, o_ref, li_ref, dm_ref, dx_ref, ds_ref, c3_ref, c2_ref, dat_ref):
    da = da_ref[...].astype(f32)
    mid = mid_ref[...]
    r = inv_rms(mid)
    mh = mid * r
    z = da * row(v_ref, 2)
    dm = c_ref[...].astype(f32) + r * (z - mh * jnp.mean(z * mh, -1, keepdims=True))
    dm_ref[...] = dm
    c3_ref[...] = col_sum(da * mh)
    at = at_ref[...].astype(f32)
    ra = inv_rms(at)
    ah = at * ra
    c2_ref[...] = col_sum(dm * ah)
    z = dm * row(v_ref, 1)
    dat = (ra * (z - ah * jnp.mean(z * ah, -1, keepdims=True))).astype(bf16)
    dat_ref[...] = dat
    dx = mm_nt(dat, w_ref[...]).astype(bf16)
    dx_ref[...] = dx
    n = dx.shape[1]
    ds = dx.astype(f32) * li_ref[...]
    ds_ref[:, :n] = ds.astype(bf16)
    hi, lo = split(ds * o_ref[...].astype(f32))
    head = lax.broadcasted_iota(jnp.int32, (n, 128), 0) // HD
    lane = lax.broadcasted_iota(jnp.int32, (n, 128), 1)
    to_lanes = (lane // 3 == head).astype(bf16)
    delta = mm(hi, to_lanes) + mm(lo, to_lanes)
    one = delta.astype(bf16).astype(f32)
    two = (delta - one).astype(bf16).astype(f32)
    which = lax.broadcasted_iota(jnp.int32, (1, 128), 1) % 3
    ds_ref[:, n:] = jnp.where(which == 0, one, jnp.where(which == 1, two, delta - one - two)).astype(bf16)


def out_back_call(c, da, mid, at, cot, vec, w, o, li, before):
    t, d = cot.shape
    n = w.shape[0]
    return chunk_call(
        out_back_kernel,
        "out_back",
        c,
        (da, mid, at, cot, vec, w, o, li),
        [alone(d), alone(d), alone(d), part(c, d), whole(vec.shape), whole(w.shape), alone(n), alone(n)],
        [(BR, d, f32), (BR, n, bf16), (BR, n + 128, bf16)],
        [(1, d, f32), (1, d, f32)],
        [(t, d, bf16)],
        before,
    )


def dqkv_kernel(dq_ref, dk_ref, dv_ref, qr_ref, kr_ref, c_ref, s1_ref, s2_ref, hg_ref, w_ref, p_ref, da_ref, hs_ref, cs_ref, d_ref):
    n = dq_ref.shape[1]
    ones = head_ones(n)
    cos, s1, s2 = (tile3(t[...], n) for t in (c_ref, s1_ref, s2_ref))

    def back(dy, x, gain):
        dz = dy * cos - pltpu.roll(dy, 16, 1) * s2 - pltpu.roll(dy, n - 16, 1) * s1
        r = lax.rsqrt(head_sum(x * x, ones) * (1.0 / HD) + EPS)
        xh = x * r
        g = dz * gain
        return r * (g - xh * (head_sum(g * xh, ones) * (1.0 / HD))), col_sum(dz * xh)

    dq, hq = back(dq_ref[...], qr_ref[...], row(hg_ref, 0))
    dk, hk = back(dk_ref[...] * (1.0 / LOG2E), kr_ref[...], row(hg_ref, 1))
    dql, dkl, dvl = dq.astype(bf16), dk.astype(bf16), dv_ref[...].astype(bf16)
    d_ref[:, :n] = dql
    d_ref[:, n : 2 * n] = dkl
    d_ref[:, 2 * n :] = dvl
    da = mm_nt(dql, w_ref[0]) + mm_nt(dkl, w_ref[1]) + mm_nt(dvl, w_ref[2])
    da_ref[...] = da.astype(bf16)
    x = p_ref[...].astype(f32)
    cs_ref[...] = col_sum(da * (x * inv_rms(x)))
    hs_ref[0:1, :] = hq
    hs_ref[1:2, :] = hk


def dqkv_call(c, dq, dk, dv, qr, kr, tabs, hg, w, patches, before):
    t, d = patches.shape
    n = dq.shape[1]
    return chunk_call(
        dqkv_kernel,
        "dqkv",
        c,
        (dq, dk, dv, qr, kr, *tabs, hg, w, patches),
        [alone(n)] + [part(c, n)] * 4 + [part(c, 128)] * 3 + [whole(hg.shape), whole(w.shape), part(c, d)],
        [(BR, d, bf16)],
        [(2, n, f32), (1, d, f32)],
        [(t, 3 * n, bf16)],
        before,
    )


def last_kernel(da_ref, p_ref, dm_ref, v_ref, o_ref):
    x = p_ref[...].astype(f32)
    r = inv_rms(x)
    xh = x * r
    z = da_ref[...].astype(f32) * row(v_ref, 0)
    o_ref[...] = (dm_ref[...] + r * (z - xh * jnp.mean(z * xh, -1, keepdims=True))).astype(bf16)


def last_call(c, da, patches, dm, vec, before):
    t, d = patches.shape
    return chunk_call(
        last_kernel,
        "last",
        c,
        (da, patches, dm, vec),
        [alone(d), part(c, d), alone(d), whole(vec.shape)],
        [],
        [],
        [(t, d, bf16)],
        before,
    )


def caption_grad_kernel(dk_ref, dv_ref, kr_ref, hg_ref, d_ref, hs_ref):
    n = dk_ref.shape[1]
    ones = head_ones(n)
    x = kr_ref[...]
    r = lax.rsqrt(head_sum(x * x, ones) * (1.0 / HD) + EPS)
    xh = x * r
    dy = dk_ref[...]
    g = dy * row(hg_ref, 2)
    d_ref[:, :n] = (r * (g - xh * (head_sum(g * xh, ones) * (1.0 / HD)))).astype(bf16)
    d_ref[:, n:] = dv_ref[...].astype(bf16)
    hs_ref[...] = col_sum(dy * xh)


def caption_norm_kernel(kr_ref, v_ref, hg_ref, o_ref):
    n = kr_ref.shape[1]
    x = kr_ref[...]
    r = lax.rsqrt(head_sum(x * x, head_ones(n)) * (1.0 / HD) + EPS)
    o_ref[:, :n] = (x * r * row(hg_ref, 2)).astype(bf16)
    o_ref[:, n:] = v_ref[...].astype(bf16)


def xor_gather(x):
    half = x.shape[0] // 2
    swap = lambda a, m: lax.ppermute(a, "wide", [(i, i ^ m) for i in range(8)])
    a, b = x[:half], x[half:]
    ra, rb = swap(a, 2), swap(b, 4)
    a4, b2 = swap(jnp.concatenate([a, ra]), 4), swap(jnp.concatenate([b, rb]), 2)
    parts = [x, None, jnp.concatenate([ra, b2[:half]]), None, jnp.concatenate([a4[:half], rb]), None, jnp.concatenate([a4[half:], b2[half:]]), None]
    for m in (0, 2, 4, 6):
        parts[m + 1] = swap(parts[m], 1)
    return jnp.concatenate(parts)


def gather_wide(x):
    if lax.axis_size("wide") == 8:
        return xor_gather(x)
    return lax.all_gather(x, "wide", axis=0, tiled=True)


def gather_small(x, axis):
    size = x.shape[0]
    wide = -(-size // 1024) * 1024
    padded = jnp.pad(x, (0, wide - size)).reshape(1, 8, wide // 8)
    return lax.all_gather(padded, axis, axis=0, tiled=True).reshape(-1, wide)[:, :size]


class Line:
    def __init__(self, place):
        self.end = (place == 0) | (place == 3)
        self.second = self.third = None

    def step(self, x):
        send = functools.partial(lax.ppermute, axis_name="narrow")
        inwards, out = [(0, 1), (3, 2)], [(1, 0), (2, 3)]
        second, third = self.second, self.third
        got_in = got_out = None
        if x is not None and third is not None and x.shape == third.shape:
            got_in = got_out = send(jnp.where(self.end, x, third), perm=inwards + out)
        else:
            if x is not None:
                got_in = send(x, perm=inwards)
            if third is not None:
                got_out = send(third, perm=out)
        total = None if third is None else jnp.where(self.end, got_out, third)
        self.third = None if second is None else second + send(second, perm=[(1, 2), (2, 1)])
        self.second = None if x is None else x + got_in
        return total


class Sums:
    def __init__(self, size, place):
        self.line = Line(place) if size == 4 else None
        self.names, self.done = [], {}

    def add(self, name, x):
        if self.line is None:
            self.done[name] = lax.psum(x, "narrow")
            return
        self._step(name, x)

    def _step(self, name, x):
        total = self.line.step(x)
        self.names.append(name)
        if total is not None:
            self.done[self.names[-3]] = total

    def get(self, name):
        while name not in self.done:
            self._step(None, None)
        return self.done[name]


def scatter_rows(x):
    return lax.psum_scatter(x.astype(bf16), "wide", scatter_dimension=0, tiled=True)


def rope_tables(position, width):
    lane = jnp.arange(128, dtype=jnp.int32)
    within = lane % HD
    quarter = HD // 4
    frequency = 10000.0 ** (-(within % quarter).astype(f32) / quarter)
    by_row = within < HD // 2
    where = jnp.where(by_row[None, :], (position // width)[:, None], (position % width)[:, None])
    angle = where.astype(f32) * frequency[None, :]
    cos, sin = jnp.cos(angle), jnp.sin(angle)
    former = (within % (HD // 2) < quarter)[None, :]
    return cos, jnp.where(former, -sin, 0.0), jnp.where(former, 0.0, sin)


def local(
    patches,
    cotangent,
    conditioning,
    captions,
    item_lengths,
    grid_widths,
    w_ada,
    norm_gains,
    w_qkv,
    head_gains,
    cross_gate,
    w_caption,
    w_out,
    w_gate_up,
    w_down,
):
    t, d = patches.shape
    n = w_qkv.shape[2]
    heads = n // HD
    ada = w_ada.shape[2]
    ff = w_down.shape[0]
    text = captions.shape[0]
    cd = conditioning.shape[1]
    count = lax.axis_size("wide")
    deep = lax.axis_size("narrow")
    me = lax.axis_index("wide")
    mz = lax.axis_index("narrow")

    slots = item_lengths.shape[0]
    spans = item_lengths // t
    order = jnp.arange(slots, dtype=jnp.int32)
    ends = jnp.sum(jnp.where(order[None, :] <= order[:, None], spans[None, :], 0), 1)
    blocks = jnp.arange(count, dtype=jnp.int32)
    item = jnp.sum((ends[None, :] <= blocks[:, None]).astype(jnp.int32), 1)
    is_item = item[:, None] == order[None, :]
    pick = lambda values: jnp.sum(jnp.where(is_item, values[None, :], 0), 1)
    firsts = pick(ends - spans)
    mine = blocks == me
    of_me = lambda values: jnp.sum(jnp.where(mine, values, 0))
    first = of_me(firsts)
    length = of_me(pick(spans))
    width = of_me(pick(grid_widths))
    position = (me - first) * t + jnp.arange(t, dtype=jnp.int32)
    tabs = rope_tables(position, width)
    steps = first + jnp.minimum(jnp.arange(SPAN, dtype=jnp.int32), length - 1)
    places = steps ^ me if count == 8 else steps
    sc = jnp.concatenate([jnp.stack([length, first]), places, steps]).astype(jnp.int32)

    cond = conditioning.astype(f32)[0]
    silu_low = jax.nn.silu(cond).astype(bf16)
    mod = jnp.sum(silu_low.astype(f32)[:, None, None] * w_ada.astype(f32), 0)
    share = cd // deep
    sent = jnp.concatenate([mod.reshape(-1), lax.dynamic_slice_in_dim(cond, mz * share, share)])
    got = gather_small(sent, "narrow").reshape(-1)
    got = gather_small(got, "wide").reshape(count, deep, -1)
    mods = got[:, :, : 4 * ada].reshape(count, deep, 4, ada).transpose(0, 2, 1, 3).reshape(count, 4, d)
    conds = got[:, :, 4 * ada :].reshape(count, cd)
    my_mod = lax.dynamic_index_in_dim(mods, first, 0, False)
    of_block = jnp.sum(jnp.where((firsts[:, None] == blocks[None, :])[:, :, None, None], mods[None], 0.0), 1)
    scales = 1.0 + of_block
    gates = jnp.tanh(of_block)
    factor = jnp.stack([1.0 + my_mod[0], jnp.tanh(my_mod[1]), 1.0 + my_mod[2], jnp.tanh(my_mod[3])])
    vec = norm_gains * factor
    hg = jnp.tile(head_gains, (1, heads))
    tg_heads = jnp.tanh(cross_gate)
    tg = jnp.repeat(tg_heads, HD)[None, :]

    cap_raw = jnp.einsum("kd,jde->jke", captions, w_caption, preferred_element_type=f32)
    cap_own = pl.pallas_call(
        caption_norm_kernel,
        out_shape=sds((text, 2 * n), bf16),
        compiler_params=params(0),
        name="caption_norm",
    )(cap_raw[0], cap_raw[1], hg)
    cap = lax.all_gather(cap_own, "wide", axis=0, tiled=True)

    chunks = range(t // BR)
    sums = Sums(deep, mz)
    a1, q_raw, k_raw, q, k, v = qkv_call(patches, vec, w_qkv, tabs, hg)
    k_all = gather_wide(k)
    v_all = gather_wide(v)
    q_all = lax.all_gather(q, "wide", axis=0, tiled=True)
    heads_out = [None for _ in chunks]
    for c in chunks:
        heads_out[c] = attend_call(sc, q, k_all, v_all, cap, tg, c, t)
        sums.add(("attn", c), mm(heads_out[c][0], w_out).astype(bf16))

    mids, gus = {}, {}
    whole_out = ()
    for c in chunks:
        mids[c], gus[c], ffn_part, *whole_out = ffn_call(c, patches, sums.get(("attn", c)), vec, w_gate_up, w_down, whole_out)
        sums.add(("ffn", c), ffn_part)
    a3, hidden = whole_out
    whole_out = ()
    c4 = 0.0
    for c in chunks:
        da3_part, part_sum, *whole_out = ffn_back_call(
            c, sums.get(("ffn", c)), mids[c], cotangent, gus[c], vec, w_gate_up, w_down, whole_out
        )
        sums.add(("da3", c), da3_part)
        c4 = c4 + part_sum
    output, d_ffn, d_gu = whole_out
    g_down = scatter_rows(mm_tn(d_ffn, hidden))
    g_gu = scatter_rows(mm_tn(a3, d_gu))

    d_mids, dqs = {}, {}
    whole_out, dkv = (), ()
    c2 = c3 = dck = dcv = gate_sum = 0.0
    for c in chunks:
        mixed, o_self, linv = heads_out[c]
        d_mids[c], d_mixed, d_scaled, p3, p2, *whole_out = out_back_call(
            c, sums.get(("da3", c)), mids[c], sums.get(("attn", c)), cotangent, vec, w_out, o_self, linv, whole_out
        )
        c2, c3 = c2 + p2, c3 + p3
        d_all = gather_wide(d_scaled)
        dq_cap, pk, pv, pg = caption_back_call(sc, q, d_mixed, cap, tg, c, text)
        dck, dcv, gate_sum = dck + pk, dcv + pv, gate_sum + pg
        dqs[c] = dq_call(sc, q, d_scaled, k_all, v_all, dq_cap, c, t)
        dkv = dkv_call(sc, k, v, q_all, d_all, dkv, c)
    (d_attn,) = whole_out
    mixed = jnp.concatenate([heads_out[c][0] for c in chunks])
    g_out = scatter_rows(mm_tn(d_attn, mixed))
    whole_out = ()
    c1 = hs_qk = 0.0
    for c in chunks:
        da1_part, p_hs, p1, *whole_out = dqkv_call(c, dqs[c], *dkv, q_raw, k_raw, tabs, hg, w_qkv, patches, whole_out)
        sums.add(("da1", c), da1_part)
        hs_qk, c1 = hs_qk + p_hs, c1 + p1
    (d_qkv,) = whole_out
    g_qkv = scatter_rows(mm_tn(a1, d_qkv))

    cap_got = gather_wide(jnp.concatenate([dck, dcv], 1).astype(bf16)).reshape(count, text, 2 * n)
    from_block = blocks ^ me if count == 8 else blocks
    in_slot = jnp.sum(jnp.where(from_block[:, None] == blocks[None, :], (firsts == me)[None, :], False), 1) > 0
    cap_total = jnp.sum(jnp.where(in_slot[:, None, None], cap_got.astype(f32), 0.0), 0)
    d_cap, hs_c = pl.pallas_call(
        caption_grad_kernel,
        out_shape=[sds((text, 2 * n), bf16), sds((1, n), f32)],
        compiler_params=params(0),
        name="caption_grad",
    )(cap_total[:, :n], cap_total[:, n:], cap_raw[0], hg)
    g_cap = scatter_rows(mm_tn(captions, d_cap))
    d_text = (mm_nt(d_cap[:, :n], w_caption[0]) + mm_nt(d_cap[:, n:], w_caption[1])).astype(bf16)
    pieces = 4
    cut = d_text.shape[1] // pieces
    for k in range(pieces):
        sums.add(("text", k), d_text[:, k * cut : (k + 1) * cut])
    whole_out = ()
    for c in chunks:
        whole_out = last_call(c, sums.get(("da1", c)), patches, d_mids[c], vec, whole_out)
    (grad_patches,) = whole_out
    grad_captions = jnp.concatenate([sums.get(("text", k)) for k in range(pieces)], 1)

    head_part = jnp.concatenate([hs_qk, hs_c]).reshape(3, heads, HD).sum(1)
    gate_part = gate_sum[0, ::HD] * (1.0 - tg_heads * tg_heads)
    sent = jnp.concatenate([c1[0], head_part.reshape(-1), gate_part])
    got = gather_small(sent, "narrow")
    summed = jnp.sum(got[:, : d + 3 * HD], 0)
    sent = jnp.concatenate([summed, got[:, d + 3 * HD :].reshape(-1), c2[0], c3[0], c4[0]])
    got = gather_small(sent, "wide")
    one, rest = got[:, :d], got[:, d:]
    grad_head_gains = jnp.sum(rest[:, : 3 * HD], 0).reshape(3, HD)
    grad_cross_gate = jnp.sum(rest[:, 3 * HD : 3 * HD + deep * heads], 0)
    two, three, four = (rest[:, 3 * HD + deep * heads + k * d :][:, :d] for k in range(3))
    cols = jnp.stack([one, two, three, four], 1)
    gain_factor = jnp.stack([scales[:, 0], gates[:, 1], scales[:, 2], gates[:, 3]], 1)
    gain_grads = jnp.sum(gain_factor * cols, 0)
    wide_cols = d // count
    grad_norm_gains = lax.dynamic_slice_in_dim(gain_grads, me * wide_cols, wide_cols, 1)
    ones = jnp.ones_like(one)
    slope = jnp.stack([ones, 1.0 - gates[:, 1] ** 2, ones, 1.0 - gates[:, 3] ** 2], 1)
    d_mod = lax.dynamic_slice_in_dim(slope * norm_gains[None] * cols, mz * ada, ada, 2)
    at_slot = (firsts[None, :] == blocks[:, None]).astype(f32)
    d_slots = jnp.sum(at_slot[:, :, None, None] * d_mod[None], 1).astype(bf16).astype(f32)
    cond_rows = cd // count
    silu_mine = lax.dynamic_slice_in_dim(jax.nn.silu(conds).astype(bf16).astype(f32), me * cond_rows, cond_rows, 1)
    grad_ada = jnp.sum(silu_mine[:, :, None, None] * d_slots[:, None], 0)
    d_mine = lax.dynamic_index_in_dim(d_slots, me, 0, False)
    cond_part = jnp.sum(d_mine[None] * w_ada.astype(f32), (1, 2))
    cond_total = jnp.sum(gather_small(cond_part, "narrow"), 0)
    pull_silu = jax.vjp(jax.nn.silu, cond)[1]
    grad_conditioning = pull_silu(cond_total)[0].reshape(1, -1)

    rows = d // count
    return (
        output,
        grad_patches,
        grad_conditioning,
        grad_captions,
        grad_ada,
        grad_norm_gains,
        g_qkv.astype(f32).reshape(rows, 3, n).transpose(1, 0, 2),
        grad_head_gains,
        grad_cross_gate,
        g_cap.astype(f32).reshape(-1, 2, n).transpose(1, 0, 2),
        g_out.astype(f32).T,
        g_gu.astype(f32).reshape(rows, 2, ff).transpose(1, 0, 2),
        g_down.astype(f32).T,
    )


def solution(mesh):
    placed = (
        P("wide", None),
        P("wide", None),
        P("wide", None),
        P("wide", None),
        P(),
        P(),
        P(None, None, "narrow"),
        P(),
        P(None, None, "narrow"),
        P(),
        P("narrow"),
        P(None, None, "narrow"),
        P("narrow", None),
        P(None, None, "narrow"),
        P("narrow", None),
    )
    return jax.shard_map(
        local,
        mesh=mesh,
        in_specs=placed,
        out_specs=(
            P("wide", None),
            P("wide", None),
            P("wide", None),
            P("wide", None),
            P("wide", None, "narrow"),
            P(None, "wide"),
            P(None, "wide", "narrow"),
            P(),
            P(),
            P(None, "wide", "narrow"),
            P("narrow", "wide"),
            P(None, "wide", "narrow"),
            P("narrow", "wide"),
        ),
        check_vma=False,
    )
```

```python
import functools

import jax
import jax.numpy as jnp
from jax import lax
from jax.experimental import pallas as pl
from jax.experimental.pallas import tpu as pltpu
from jax.sharding import PartitionSpec as P

HD = 64
SPAN = 4
EPS = 1e-05
LOG2E = 1.4426950408889634
f32 = jnp.float32
bf16 = jnp.bfloat16
VMEM = 56 * 1024 * 1024
BR = 256
NT = (((1,), (1,)), ((), ()))
TN = (((0,), (0,)), ((), ()))


def params(n):
    return pltpu.CompilerParams(
        dimension_semantics=("arbitrary",) * n, vmem_limit_bytes=VMEM
    )


def sds(shape, dtype):
    return jax.ShapeDtypeStruct(shape, dtype)


def mm(a, b):
    return jnp.dot(a, b, preferred_element_type=f32)


def mm_nt(a, b):
    return lax.dot_general(a, b, NT, preferred_element_type=f32)


def mm_tn(a, b):
    return lax.dot_general(a, b, TN, preferred_element_type=f32)


def split(x):
    hi = x.astype(bf16)
    return hi, (x - hi.astype(f32)).astype(bf16)


def head_sum(x, ones):
    hi, lo = split(x)
    return mm(hi, ones) + mm(lo, ones)


def head_ones(n):
    a = lax.broadcasted_iota(jnp.int32, (n, n), 0) // HD
    b = lax.broadcasted_iota(jnp.int32, (n, n), 1) // HD
    return (a == b).astype(bf16)


def halves(n):
    lane = lax.broadcasted_iota(jnp.int32, (1, n), 1)
    return (lane < HD, lane >= HD)


def keep(x, mask):
    return jnp.where(mask, x, jnp.zeros_like(x))


def inv_rms(x):
    return lax.rsqrt(jnp.mean(x * x, -1, keepdims=True) + EPS)


def row(ref, k):
    return ref[k : k + 1, :]


def whole(shape):
    zeros = (0,) * len(shape)
    return pl.BlockSpec(shape, lambda *_: zeros, pipeline_mode=pl.Buffered(1))


def rows_of(br, width, first=0):
    return pl.BlockSpec((br, width), lambda i, *_: (i, first))


def accumulate(ref, value, first):
    @pl.when(first)
    def _():
        ref[...] = value

    @pl.when(jnp.logical_not(first))
    def _():
        ref[...] += value


def col_sum(x):
    return jnp.sum(x, 0, keepdims=True)


def tile3(t, n):
    return jnp.concatenate([t] * (n // t.shape[1]), 1)


def qkv_kernel(p_ref, v_ref, w_ref, c_ref, s1_ref, s2_ref, hg_ref, a_ref, qr_ref, kr_ref, q_ref, k_ref, vv_ref):
    x = p_ref[...].astype(f32)
    a = (x * inv_rms(x) * row(v_ref, 0)).astype(bf16)
    a_ref[...] = a
    n = q_ref.shape[1]
    ones = head_ones(n)
    cos, s1, s2 = (tile3(t[...], n) for t in (c_ref, s1_ref, s2_ref))

    def turned(y, gain):
        z = y * lax.rsqrt(head_sum(y * y, ones) * (1.0 / HD) + EPS) * gain
        return z * cos + pltpu.roll(z, n - 16, 1) * s1 + pltpu.roll(z, 16, 1) * s2

    q = mm(a, w_ref[0])
    qr_ref[...] = q
    q_ref[...] = (turned(q, row(hg_ref, 0)) * (0.125 * LOG2E)).astype(bf16)
    k = mm(a, w_ref[1])
    kr_ref[...] = k
    k_ref[...] = turned(k, row(hg_ref, 1)).astype(bf16)
    vv_ref[...] = mm(a, w_ref[2]).astype(bf16)


def qkv_call(patches, vec, w, tabs, hg, br=256):
    t, d = patches.shape
    n = w.shape[2]
    return pl.pallas_call(
        qkv_kernel,
        grid=(t // br,),
        in_specs=[rows_of(br, d), whole(vec.shape), whole(w.shape)]
        + [rows_of(br, 128)] * 3
        + [whole(hg.shape)],
        out_specs=[rows_of(br, d)] + [rows_of(br, n)] * 5,
        out_shape=[sds((t, d), bf16), sds((t, n), f32), sds((t, n), f32)] + [sds((t, n), bf16)] * 3,
        compiler_params=params(1),
        name="qkv",
    )(patches, vec, w, *tabs, hg)


def soft_sums(q, k, v, mask):
    e = jnp.exp2(mm_nt(q, keep(k, mask))).astype(bf16)
    return mm(e, jnp.where(mask, v, jnp.ones_like(v)))


def loose(n):
    return [pl.BlockSpec(memory_space=pl.ANY)] * n


def item_block(j, s):
    return jnp.minimum(j, s[0] - 1)


def attend_kernel(sc, q_ref, k_ref, v_ref, ck_ref, cv_ref, tg_ref, mix_ref, o_ref, li_ref, acc):
    j = pl.program_id(1)
    masks = halves(128)
    keys = 512

    @pl.when(j == 0)
    def _():
        acc[...] = jnp.zeros_like(acc)

    @pl.when(j < sc[0])
    def _():
        q = q_ref[...]
        for h in range(2):
            total = acc[h]
            for c in range(k_ref.shape[0] // keys):
                at = slice(c * keys, (c + 1) * keys)
                total = total + soft_sums(q, k_ref[at, :], v_ref[at, :], masks[h])
            acc[h] = total

    @pl.when(j == SPAN - 1)
    def _():
        q = q_ref[...]

        def finish(a0, a1):
            inverse = 1.0 / jnp.where(masks[0], pltpu.roll(a0, HD, 1), pltpu.roll(a1, HD, 1))
            return jnp.where(masks[0], a0, a1) * inverse, inverse

        o, li = finish(acc[0], acc[1])
        c0, c1 = (soft_sums(q, ck_ref[...], cv_ref[...], m) for m in masks)
        mix_ref[...] = (o + tg_ref[...] * finish(c0, c1)[0]).astype(bf16)
        o_ref[...] = o.astype(bf16)
        li_ref[...] = li


def attend_call(sc, q, k, v, ck, cv, tg, h):
    n = q.shape[1]
    pairs = n // 128
    block = k.shape[0] // SPAN
    bq = 2 * BR
    text = ck.shape[0]
    mine = lambda p, j, s: (0, p)
    other = lambda p, j, s: (item_block(j, s), p)
    return pl.pallas_call(
        attend_kernel,
        grid_spec=pltpu.PrefetchScalarGridSpec(
            num_scalar_prefetch=1,
            grid=(pairs, SPAN),
            in_specs=[
                pl.BlockSpec((bq, 128), lambda p, j, s: (h, p)),
                pl.BlockSpec((block, 128), other),
                pl.BlockSpec((block, 128), other),
                pl.BlockSpec((text, 128), mine),
                pl.BlockSpec((text, 128), mine),
                pl.BlockSpec((1, 128), mine),
            ],
            out_specs=[pl.BlockSpec((bq, 128), mine)] * 3,
            scratch_shapes=[pltpu.VMEM((2, bq, 128), f32)],
        ),
        out_shape=[sds((bq, n), bf16), sds((bq, n), bf16), sds((bq, n), f32)],
        compiler_params=params(2),
        name="attend",
    )(sc, q, k, v, ck, cv, tg)


def caption_back_kernel(q_ref, da_ref, db_ref, ck_ref, cv_ref, tg_ref, dq_ref, dk_ref, dv_ref, gs_ref):
    masks = halves(128)
    q, d = q_ref[...], jnp.concatenate([da_ref[...], db_ref[...]], 0)
    dq = jnp.zeros(q.shape, f32)
    dk = jnp.zeros(ck_ref.shape, f32)
    dv = jnp.zeros(ck_ref.shape, f32)
    sums = []
    for h in range(2):
        ck, cv = keep(ck_ref[...], masks[h]), keep(cv_ref[...], masks[h])
        gate = tg_ref[:, h * HD : h * HD + 1]
        e = jnp.exp2(mm_nt(q, ck))
        prob = e * (1.0 / jnp.sum(e, -1, keepdims=True))
        dp = mm_nt(d, cv)
        m = jnp.sum(prob * dp, -1, keepdims=True)
        dc = (prob * (dp - m) * gate).astype(bf16)
        dq = dq + mm(dc, ck)
        dk = dk + mm_tn(dc, keep(q, masks[h]))
        dv = dv + mm_tn(prob.astype(bf16), keep(d, masks[h]))
        sums.append(jnp.sum(m, 0, keepdims=True))
    dq_ref[...] = dq * 0.125
    dk_ref[...] = dk * (1.0 / LOG2E)
    dv_ref[...] = dv * tg_ref[...]
    gs_ref[...] = jnp.where(masks[0], sums[0], sums[1])


def caption_back_call(q, da, db, ck, cv, tg, h):
    n = q.shape[1]
    pairs = n // 128
    bq = 2 * BR
    text = ck.shape[0]
    mine = lambda p: (0, p)
    return pl.pallas_call(
        caption_back_kernel,
        grid=(pairs,),
        in_specs=[
            pl.BlockSpec((bq, 128), lambda p: (h, p)),
            pl.BlockSpec((BR, 128), mine),
            pl.BlockSpec((BR, 128), mine),
            pl.BlockSpec((text, 128), mine),
            pl.BlockSpec((text, 128), mine),
            pl.BlockSpec((1, 128), mine),
        ],
        out_specs=[
            pl.BlockSpec((bq, 128), mine),
            pl.BlockSpec((text, 128), mine),
            pl.BlockSpec((text, 128), mine),
            pl.BlockSpec((1, 128), mine),
        ],
        out_shape=[sds((bq, n), f32), sds((text, n), f32), sds((text, n), f32), sds((1, n), f32)],
        compiler_params=params(1),
        name="caption_back",
    )(q, da, db, ck, cv, tg)


def minus_delta(rows, head):
    lane = lax.broadcasted_iota(jnp.int32, (rows, 128), 1)
    return jnp.where((lane >= 3 * head) & (lane < 3 * head + 3), -1.0, 0.0).astype(bf16)


def dq_kernel(sc, q_ref, da_ref, xa_ref, db_ref, xb_ref, k_ref, v_ref, c_ref, *rest):
    dq_ref, acc = rest[-2:]
    pair = pl.program_id(0)
    j = pl.program_id(1)
    masks = halves(128)
    keys = 512

    @pl.when(j == 0)
    def _():
        acc[...] = jnp.zeros_like(acc)

    @pl.when(j < sc[0])
    def _():
        q = q_ref[...]
        dx = jnp.concatenate(
            [jnp.concatenate([da_ref[...], xa_ref[...]], 1), jnp.concatenate([db_ref[...], xb_ref[...]], 1)], 0
        )
        total = acc[...]
        for h in range(2):
            off = minus_delta(keys, 2 * pair + h)
            for c in range(k_ref.shape[0] // keys):
                at = slice(c * keys, (c + 1) * keys)
                k = keep(k_ref[at, :], masks[h])
                e = jnp.exp2(mm_nt(q, k))
                dp = mm_nt(dx, jnp.concatenate([keep(v_ref[at, :], masks[h]), off], 1))
                total = total + mm((e * dp).astype(bf16), k)
        acc[...] = total

    @pl.when(j == SPAN - 1)
    def _():
        dq_ref[...] = acc[...] * 0.125 + c_ref[...]


def dq_call(sc, q, da, db, k, v, cap_dq, h, after):
    n = q.shape[1]
    pairs = n // 128
    block = k.shape[0] // SPAN
    bq = 2 * BR
    mine = lambda p, j, s: (0, p)
    extra = lambda p, j, s: (0, pairs)
    other = lambda p, j, s: (item_block(j, s), p)
    return pl.pallas_call(
        dq_kernel,
        grid_spec=pltpu.PrefetchScalarGridSpec(
            num_scalar_prefetch=1,
            grid=(pairs, SPAN),
            in_specs=[
                pl.BlockSpec((bq, 128), lambda p, j, s: (h, p)),
                pl.BlockSpec((BR, 128), mine),
                pl.BlockSpec((BR, 128), extra),
                pl.BlockSpec((BR, 128), mine),
                pl.BlockSpec((BR, 128), extra),
                pl.BlockSpec((block, 128), other),
                pl.BlockSpec((block, 128), other),
                pl.BlockSpec((bq, 128), mine),
            ]
            + loose(len(after)),
            out_specs=pl.BlockSpec((bq, 128), mine),
            scratch_shapes=[pltpu.VMEM((bq, 128), f32)],
        ),
        out_shape=sds((bq, n), f32),
        compiler_params=params(2),
        name="dq",
    )(sc, q, da, da, db, db, k, v, cap_dq, *after)


def dkv_kernel(start, sc, k_ref, v_ref, q_ref, da_ref, xa_ref, db_ref, xb_ref, *rest):
    dk_ref, dv_ref = rest[-2:]
    pair = pl.program_id(0)
    j = pl.program_id(1)
    masks = halves(128)
    keys = 512

    @pl.when(j == 0)
    def _():
        if start:
            dk_ref[...] = jnp.zeros_like(dk_ref)
            dv_ref[...] = jnp.zeros_like(dv_ref)
        else:
            dk_ref[...] = rest[0][...]
            dv_ref[...] = rest[1][...]

    @pl.when(j < sc[0])
    def _():
        q = q_ref[...]
        d = jnp.concatenate([da_ref[...], db_ref[...]], 0)
        dx = jnp.concatenate([d, jnp.concatenate([xa_ref[...], xb_ref[...]], 0)], 1)
        qs = [keep(q, m) for m in masks]
        ds = [keep(d, m) for m in masks]
        for c in range(k_ref.shape[0] // keys):
            at = slice(c * keys, (c + 1) * keys)
            dk, dv = dk_ref[at, :], dv_ref[at, :]
            for h in range(2):
                off = minus_delta(keys, 2 * pair + h)
                e = jnp.exp2(mm_nt(k_ref[at, :], qs[h]))
                dp = mm_nt(jnp.concatenate([keep(v_ref[at, :], masks[h]), off], 1), dx)
                dv = dv + mm(e.astype(bf16), ds[h])
                dk = dk + mm((e * dp).astype(bf16), qs[h])
            dk_ref[at, :] = dk
            dv_ref[at, :] = dv


def dkv_call(sc, k, v, q_all, da, db, h, rows, at, before, after):
    t, n = k.shape
    pairs = n // 128
    bq = 2 * BR
    per = t // bq
    mine = pl.BlockSpec((rows, 128), lambda p, j, s: (at, p))
    out = pl.BlockSpec((rows, 128), lambda p, j, s: (0, p))
    other = pl.BlockSpec((BR, 128), lambda p, j, s: (item_block(j, s), p))
    extra = pl.BlockSpec((BR, 128), lambda p, j, s: (item_block(j, s), pairs))
    return pl.pallas_call(
        functools.partial(dkv_kernel, not before),
        grid_spec=pltpu.PrefetchScalarGridSpec(
            num_scalar_prefetch=1,
            grid=(pairs, SPAN),
            in_specs=[
                mine,
                mine,
                pl.BlockSpec((bq, 128), lambda p, j, s: (s[1 + SPAN + j] * per + h, p)),
                other,
                extra,
                other,
                extra,
            ]
            + [mine] * len(before)
            + loose(len(after)),
            out_specs=[out, out],
        ),
        out_shape=[sds((rows, n), f32)] * 2,
        compiler_params=params(2),
        name="dkv",
    )(sc, k, v, q_all, da, da, db, db, *before, *after)


def chunk_call(kernel, name, c, ins, specs, chunk_outs, sum_outs, whole_outs, before):
    one = lambda r, w: pl.BlockSpec((r, w), lambda i: (0, 0))
    loose = chunk_outs + sum_outs
    into = [pl.BlockSpec((BR, w), lambda i: (c, 0)) for _, w, _ in whole_outs]
    held = list(before)
    body = kernel
    if held:

        def body(*refs):
            kernel(*refs[: len(ins)], *refs[len(ins) + len(held) :])

    return pl.pallas_call(
        body,
        grid=(1,),
        in_specs=specs + [pl.BlockSpec(memory_space=pl.ANY)] * len(held),
        out_specs=[one(r, w) for r, w, _ in loose] + into,
        out_shape=[sds((r, w), k) for r, w, k in loose + whole_outs],
        input_output_aliases={len(ins) + k: len(loose) + k for k in range(len(held))},
        compiler_params=params(1),
        name=name,
    )(*ins, *held)


def part(c, width):
    return pl.BlockSpec((BR, width), lambda i: (c, 0))


def alone(width):
    return pl.BlockSpec((BR, width), lambda i: (0, 0))


def pair_grad_kernel(a_ref, b_ref, c_ref, d_ref, o_ref):
    n = b_ref.shape[1]
    o_ref[:, :n] = mm_tn(a_ref[...], b_ref[...]).astype(bf16)
    o_ref[:, n:] = mm_tn(c_ref[...], d_ref[...]).astype(bf16)


def pair_grad_call(a, b, c, d):
    t, m = a.shape
    n, k = b.shape[1], d.shape[1]
    blk = 256
    cols = pl.BlockSpec((t, blk), lambda i: (0, i))
    return pl.pallas_call(
        pair_grad_kernel,
        grid=(m // blk,),
        in_specs=[cols, whole(b.shape), cols, whole(d.shape)],
        out_specs=pl.BlockSpec((blk, n + k), lambda i: (i, 0)),
        out_shape=sds((m, n + k), bf16),
        compiler_params=params(1),
        name="pair_grad",
    )(a, b, c, d)


def ffn_kernel(p_ref, at_ref, v_ref, wg_ref, wd_ref, mid_ref, gu_ref, f_ref, a_ref, h_ref):
    at = at_ref[...].astype(f32)
    mid = p_ref[...].astype(f32) + row(v_ref, 1) * (at * inv_rms(at))
    mid_ref[...] = mid
    a = (mid * inv_rms(mid) * row(v_ref, 2)).astype(bf16)
    a_ref[...] = a
    g = mm(a, wg_ref[0])
    u = mm(a, wg_ref[1])
    n = g.shape[1]
    gu_ref[:, :n] = g.astype(bf16)
    gu_ref[:, n:] = u.astype(bf16)
    h = (g * jax.nn.sigmoid(g) * u).astype(bf16)
    h_ref[...] = h
    f_ref[...] = mm(h, wd_ref[...]).astype(bf16)


def ffn_call(c, patches, at, vec, wg, wd, before):
    t, d = patches.shape
    n = wd.shape[0]
    return chunk_call(
        ffn_kernel,
        "ffn",
        c,
        (patches, at, vec, wg, wd),
        [part(c, d), alone(d), whole(vec.shape), whole(wg.shape), whole(wd.shape)],
        [(BR, d, f32), (BR, 2 * n, bf16), (BR, d, bf16)],
        [],
        [(t, d, bf16), (t, n, bf16)],
        before,
    )


def ffn_back_kernel(f_ref, mid_ref, c_ref, gu_ref, v_ref, wg_ref, wd_ref, da_ref, cs_ref, y_ref, df_ref, dgu_ref):
    f = f_ref[...].astype(f32)
    cot = c_ref[...].astype(f32)
    r = inv_rms(f)
    fh = f * r
    y_ref[...] = (mid_ref[...] + row(v_ref, 3) * fh).astype(bf16)
    z = cot * row(v_ref, 3)
    df = (r * (z - fh * jnp.mean(z * fh, -1, keepdims=True))).astype(bf16)
    df_ref[...] = df
    cs_ref[...] = col_sum(cot * fh)
    dh = mm_nt(df, wd_ref[...])
    n = dh.shape[1]
    g = gu_ref[:, :n].astype(f32)
    u = gu_ref[:, n:].astype(f32)
    s = jax.nn.sigmoid(g)
    gs = g * s
    dg = (dh * u * (s + gs * (1.0 - s))).astype(bf16)
    du = (dh * gs).astype(bf16)
    dgu_ref[:, :n] = dg
    dgu_ref[:, n:] = du
    da_ref[...] = (mm_nt(dg, wg_ref[0]) + mm_nt(du, wg_ref[1])).astype(bf16)


def ffn_back_call(c, f, mid, cot, gu, vec, wg, wd, before):
    t, d = cot.shape
    n = wd.shape[0]
    return chunk_call(
        ffn_back_kernel,
        "ffn_back",
        c,
        (f, mid, cot, gu, vec, wg, wd),
        [alone(d), alone(d), part(c, d), alone(2 * n), whole(vec.shape), whole(wg.shape), whole(wd.shape)],
        [(BR, d, bf16)],
        [(1, d, f32)],
        [(t, d, bf16), (t, d, bf16), (t, 2 * n, bf16)],
        before,
    )


def out_back_kernel(da_ref, mid_ref, at_ref, c_ref, v_ref, w_ref, o_ref, li_ref, dm_ref, dx_ref, ds_ref, c3_ref, c2_ref, dat_ref):
    da = da_ref[...].astype(f32)
    mid = mid_ref[...]
    r = inv_rms(mid)
    mh = mid * r
    z = da * row(v_ref, 2)
    dm = c_ref[...].astype(f32) + r * (z - mh * jnp.mean(z * mh, -1, keepdims=True))
    dm_ref[...] = dm
    c3_ref[...] = col_sum(da * mh)
    at = at_ref[...].astype(f32)
    ra = inv_rms(at)
    ah = at * ra
    c2_ref[...] = col_sum(dm * ah)
    z = dm * row(v_ref, 1)
    dat = (ra * (z - ah * jnp.mean(z * ah, -1, keepdims=True))).astype(bf16)
    dat_ref[...] = dat
    dx = mm_nt(dat, w_ref[...]).astype(bf16)
    dx_ref[...] = dx
    n = dx.shape[1]
    ds = dx.astype(f32) * li_ref[...]
    ds_ref[:, :n] = ds.astype(bf16)
    hi, lo = split(ds * o_ref[...].astype(f32))
    head = lax.broadcasted_iota(jnp.int32, (n, 128), 0) // HD
    lane = lax.broadcasted_iota(jnp.int32, (n, 128), 1)
    to_lanes = (lane // 3 == head).astype(bf16)
    delta = mm(hi, to_lanes) + mm(lo, to_lanes)
    one = delta.astype(bf16).astype(f32)
    two = (delta - one).astype(bf16).astype(f32)
    which = lax.broadcasted_iota(jnp.int32, (1, 128), 1) % 3
    ds_ref[:, n:] = jnp.where(which == 0, one, jnp.where(which == 1, two, delta - one - two)).astype(bf16)


def out_back_call(c, da, mid, at, cot, vec, w, o, li, before):
    t, d = cot.shape
    n = w.shape[0]
    return chunk_call(
        out_back_kernel,
        "out_back",
        c,
        (da, mid, at, cot, vec, w, o, li),
        [alone(d), alone(d), alone(d), part(c, d), whole(vec.shape), whole(w.shape), part(c % 2, n), part(c % 2, n)],
        [(BR, d, f32), (BR, n, bf16), (BR, n + 128, bf16)],
        [(1, d, f32), (1, d, f32)],
        [(t, d, bf16)],
        before,
    )


def dqkv_kernel(dq_ref, dk_ref, dv_ref, qr_ref, kr_ref, c_ref, s1_ref, s2_ref, hg_ref, w_ref, p_ref, da_ref, hs_ref, cs_ref, d_ref):
    n = dq_ref.shape[1]
    ones = head_ones(n)
    cos, s1, s2 = (tile3(t[...], n) for t in (c_ref, s1_ref, s2_ref))

    def back(dy, x, gain):
        dz = dy * cos - pltpu.roll(dy, 16, 1) * s2 - pltpu.roll(dy, n - 16, 1) * s1
        r = lax.rsqrt(head_sum(x * x, ones) * (1.0 / HD) + EPS)
        xh = x * r
        g = dz * gain
        return r * (g - xh * (head_sum(g * xh, ones) * (1.0 / HD))), col_sum(dz * xh)

    dq, hq = back(dq_ref[...], qr_ref[...], row(hg_ref, 0))
    dk, hk = back(dk_ref[...] * (1.0 / LOG2E), kr_ref[...], row(hg_ref, 1))
    dql, dkl, dvl = dq.astype(bf16), dk.astype(bf16), dv_ref[...].astype(bf16)
    d_ref[:, :n] = dql
    d_ref[:, n : 2 * n] = dkl
    d_ref[:, 2 * n :] = dvl
    da = mm_nt(dql, w_ref[0]) + mm_nt(dkl, w_ref[1]) + mm_nt(dvl, w_ref[2])
    da_ref[...] = da.astype(bf16)
    x = p_ref[...].astype(f32)
    cs_ref[...] = col_sum(da * (x * inv_rms(x)))
    hs_ref[0:1, :] = hq
    hs_ref[1:2, :] = hk


def dqkv_call(c, dq, dk, dv, qr, kr, tabs, hg, w, patches, before):
    t, d = patches.shape
    n = dq.shape[1]
    return chunk_call(
        dqkv_kernel,
        "dqkv",
        c,
        (dq, dk, dv, qr, kr, *tabs, hg, w, patches),
        [part(c % 2, n)] * 3 + [part(c, n)] * 2 + [part(c, 128)] * 3 + [whole(hg.shape), whole(w.shape), part(c, d)],
        [(BR, d, bf16)],
        [(2, n, f32), (1, d, f32)],
        [(t, 3 * n, bf16)],
        before,
    )


def last_kernel(da_ref, p_ref, dm_ref, v_ref, o_ref):
    x = p_ref[...].astype(f32)
    r = inv_rms(x)
    xh = x * r
    z = da_ref[...].astype(f32) * row(v_ref, 0)
    o_ref[...] = (dm_ref[...] + r * (z - xh * jnp.mean(z * xh, -1, keepdims=True))).astype(bf16)


def last_call(c, da, patches, dm, vec, before):
    t, d = patches.shape
    return chunk_call(
        last_kernel,
        "last",
        c,
        (da, patches, dm, vec),
        [alone(d), part(c, d), alone(d), whole(vec.shape)],
        [],
        [],
        [(t, d, bf16)],
        before,
    )


def caption_grad_kernel(dk_ref, dv_ref, kr_ref, hg_ref, d_ref, hs_ref):
    n = dk_ref.shape[1]
    ones = head_ones(n)
    x = kr_ref[...]
    r = lax.rsqrt(head_sum(x * x, ones) * (1.0 / HD) + EPS)
    xh = x * r
    dy = dk_ref[...]
    g = dy * row(hg_ref, 2)
    d_ref[:, :n] = (r * (g - xh * (head_sum(g * xh, ones) * (1.0 / HD)))).astype(bf16)
    d_ref[:, n:] = dv_ref[...].astype(bf16)
    hs_ref[...] = col_sum(dy * xh)


def caption_norm_kernel(kr_ref, v_ref, hg_ref, k_ref, o_ref):
    x = kr_ref[...]
    r = lax.rsqrt(head_sum(x * x, head_ones(x.shape[1])) * (1.0 / HD) + EPS)
    k_ref[...] = (x * r * row(hg_ref, 2)).astype(bf16)
    o_ref[...] = v_ref[...].astype(bf16)


def swap(x, axis, size, m):
    return lax.ppermute(x, axis, [(i, i ^ m) for i in range(size)])


def pick_kernel(count, n_pieces, sc, *refs):
    a, b = refs[:n_pieces], refs[n_pieces : 2 * n_pieces]
    outs, sem = refs[2 * n_pieces : 2 * n_pieces + 2], refs[-1]
    rows = a[0].shape[0]
    for k, (pieces, out) in enumerate(zip((a, b), outs)):
        for j in range(count):
            for m in range(n_pieces):

                @pl.when(sc[1 + j] == m)
                def _():
                    pltpu.make_async_copy(pieces[m], out.at[pl.ds(j * rows, rows)], sem.at[k, j]).start()

    for k, (pieces, out) in enumerate(zip((a, b), outs)):
        for j in range(count):
            pltpu.make_async_copy(pieces[0], out.at[pl.ds(j * rows, rows)], sem.at[k, j]).wait()


def gather_item(a, b, sc, count):
    size = lax.axis_size("wide")
    if size != 8:
        full = [lax.all_gather(x, "wide") for x in (a, b)]
        return [
            jnp.concatenate([lax.dynamic_index_in_dim(x, sc[1 + SPAN + j], 0, False) for j in range(count)]) for x in full
        ]
    go = lambda x, m: swap(x, "wide", 8, m)
    a2, b4 = go(a, 2), go(b, 4)
    a4, b2 = go(a, 4), go(b, 2)
    a6, b6 = go(a2, 4), go(b4, 2)
    pieces = []
    for four in ((a, a2, a4, a6), (b, b2, b4, b6)):
        for x in four:
            pieces += [x, go(x, 1)]
    out = [sds((count * x.shape[0], x.shape[1]), x.dtype) for x in (a, b)]
    return pl.pallas_call(
        functools.partial(pick_kernel, count, 8),
        grid_spec=pltpu.PrefetchScalarGridSpec(
            num_scalar_prefetch=1,
            grid=(1,),
            in_specs=loose(16),
            out_specs=loose(2),
            scratch_shapes=[pltpu.SemaphoreType.DMA((2, count))],
        ),
        out_shape=out,
        compiler_params=params(1),
        name="pick",
    )(sc, *pieces)


def gather_small(x, axis):
    n = x.shape[0]
    wide = -(-n // 1024) * 1024
    x = jnp.pad(x, (0, wide - n)).reshape(wide // 128, 128)
    size = lax.axis_size(axis)
    if size > 8:
        return lax.all_gather(x, axis).reshape(size, wide)[:, :n]
    got = jnp.stack([x] + [swap(x, axis, size, m) for m in range(1, size)])
    order = jnp.arange(size, dtype=jnp.int32)
    mine = (order[:, None] ^ lax.axis_index(axis)) == order[None, :]
    out = jnp.sum(jnp.where(mine[:, :, None, None], got[None], 0.0), 1)
    return out.reshape(size, wide)[:, :n]


def hop_kernel(have, sc, *refs):
    ins = dict(zip(have["in"], refs))
    outs = dict(zip(have["out"], refs[len(have["in"]) :]))
    end = sc[0] == 1
    if "total" in outs:
        outs["total"][...] = jnp.where(end, ins["r1"][...], ins["send"][...])
    third = None
    if "second" in ins:
        third = ins["second"][...] + ins["r2"][...]
    if "second" in outs:
        outs["second"][...] = ins["x"][...] + ins["r1"][...]
    if "send" in outs:
        new = ins["new"][...] if "new" in ins else third
        outs["send"][...] = new if third is None else jnp.where(end, new, third)


class Line:
    def __init__(self, place):
        self.end = ((place == 0) | (place == 3)).astype(jnp.int32).reshape(1)
        self.x = self.second = self.send = None
        self.third = False

    def step(self, new):
        if self.send is None:
            self.x = self.send = new
            return None
        go = lambda x, perm: lax.ppermute(x, "narrow", perm)
        ins = {"r1": go(self.send, [(0, 1), (3, 2), (1, 0), (2, 3)])}
        outs = []
        if self.third:
            ins["send"] = self.send
            outs.append("total")
        if self.second is not None:
            ins["r2"] = go(self.second, [(1, 2), (2, 1)])
            ins["second"] = self.second
        if self.x is not None:
            ins["x"] = self.x
            outs.append("second")
        if new is not None:
            ins["new"] = new
        if new is not None or self.second is not None:
            outs.append("send")
        like = ins["r1"]
        block = pl.BlockSpec((BR // 2, like.shape[1]), lambda i, s: (i, 0))
        got = pl.pallas_call(
            functools.partial(hop_kernel, {"in": list(ins), "out": outs}),
            grid_spec=pltpu.PrefetchScalarGridSpec(
                num_scalar_prefetch=1, grid=(2,), in_specs=[block] * len(ins), out_specs=[block] * len(outs)
            ),
            out_shape=[sds(like.shape, like.dtype)] * len(outs),
            compiler_params=params(1),
            name="hop",
        )(self.end, *ins.values())
        got = dict(zip(outs, got))
        self.third = self.second is not None
        self.x, self.second, self.send = new, got.get("second"), got.get("send")
        return got.get("total")


class Sums:
    def __init__(self, size, place):
        self.line = Line(place) if size == 4 else None
        self.names, self.done = [], {}

    def add(self, name, x):
        if self.line is None:
            self.done[name] = lax.psum(x, "narrow")
            return
        if self.line.send is None:
            self.names = [None]
        self._step(name, x)

    def _step(self, name, x):
        total = self.line.step(x)
        self.names.append(name)
        if total is not None:
            self.done[self.names[-4]] = total

    def get(self, name):
        while name not in self.done:
            self._step(None, None)
        return self.done[name]


def scatter_rows(x):
    return lax.psum_scatter(x.astype(bf16), "wide", scatter_dimension=0, tiled=True)


def rope_tables(position, width):
    lane = jnp.arange(128, dtype=jnp.int32)
    within = lane % HD
    quarter = HD // 4
    frequency = 10000.0 ** (-(within % quarter).astype(f32) / quarter)
    by_row = within < HD // 2
    where = jnp.where(by_row[None, :], (position // width)[:, None], (position % width)[:, None])
    angle = where.astype(f32) * frequency[None, :]
    cos, sin = jnp.cos(angle), jnp.sin(angle)
    former = (within % (HD // 2) < quarter)[None, :]
    return cos, jnp.where(former, -sin, 0.0), jnp.where(former, 0.0, sin)


def local(
    patches,
    cotangent,
    conditioning,
    captions,
    item_lengths,
    grid_widths,
    w_ada,
    norm_gains,
    w_qkv,
    head_gains,
    cross_gate,
    w_caption,
    w_out,
    w_gate_up,
    w_down,
):
    t, d = patches.shape
    n = w_qkv.shape[2]
    heads = n // HD
    ada = w_ada.shape[2]
    ff = w_down.shape[0]
    text = captions.shape[0]
    cd = conditioning.shape[1]
    count = lax.axis_size("wide")
    deep = lax.axis_size("narrow")
    me = lax.axis_index("wide")
    mz = lax.axis_index("narrow")

    slots = item_lengths.shape[0]
    spans = item_lengths // t
    order = jnp.arange(slots, dtype=jnp.int32)
    ends = jnp.sum(jnp.where(order[None, :] <= order[:, None], spans[None, :], 0), 1)
    blocks = jnp.arange(count, dtype=jnp.int32)
    item = jnp.sum((ends[None, :] <= blocks[:, None]).astype(jnp.int32), 1)
    is_item = item[:, None] == order[None, :]
    pick = lambda values: jnp.sum(jnp.where(is_item, values[None, :], 0), 1)
    firsts = pick(ends - spans)
    mine = blocks == me
    of_me = lambda values: jnp.sum(jnp.where(mine, values, 0))
    first = of_me(firsts)
    length = of_me(pick(spans))
    width = of_me(pick(grid_widths))
    position = (me - first) * t + jnp.arange(t, dtype=jnp.int32)
    tabs = rope_tables(position, width)
    steps = first + jnp.minimum(jnp.arange(SPAN, dtype=jnp.int32), length - 1)
    places = steps ^ me if count == 8 else steps
    sc = jnp.concatenate([length.reshape(1), places, steps]).astype(jnp.int32)

    cond = conditioning.astype(f32)[0]
    silu_low = jax.nn.silu(cond).astype(bf16)
    mod = jnp.sum(silu_low.astype(f32)[:, None, None] * w_ada.astype(f32), 0)
    share = cd // deep
    sent = jnp.concatenate([mod.reshape(-1), lax.dynamic_slice_in_dim(cond, mz * share, share)])
    got = gather_small(sent, "narrow").reshape(-1)
    got = gather_small(got, "wide").reshape(count, deep, -1)
    mods = got[:, :, : 4 * ada].reshape(count, deep, 4, ada).transpose(0, 2, 1, 3).reshape(count, 4, d)
    conds = got[:, :, 4 * ada :].reshape(count, cd)
    my_mod = lax.dynamic_index_in_dim(mods, first, 0, False)
    of_block = jnp.sum(jnp.where((firsts[:, None] == blocks[None, :])[:, :, None, None], mods[None], 0.0), 1)
    scales = 1.0 + of_block
    gates = jnp.tanh(of_block)
    factor = jnp.stack([1.0 + my_mod[0], jnp.tanh(my_mod[1]), 1.0 + my_mod[2], jnp.tanh(my_mod[3])])
    vec = norm_gains * factor
    hg = jnp.tile(head_gains, (1, heads))
    tg_heads = jnp.tanh(cross_gate)
    tg = jnp.repeat(tg_heads, HD)[None, :]

    cap_raw = jnp.einsum("kd,jde->jke", captions, w_caption, preferred_element_type=f32)
    cap_own = pl.pallas_call(
        caption_norm_kernel,
        out_shape=[sds((text, n), bf16)] * 2,
        compiler_params=params(0),
        name="caption_norm",
    )(cap_raw[0], cap_raw[1], hg)
    ck, cv = gather_item(*cap_own, sc, 1)

    chunks = range(t // BR)
    pairs_of = range(t // (2 * BR))
    sums = Sums(deep, mz)
    a1, q_raw, k_raw, q, k, v = qkv_call(patches, vec, w_qkv, tabs, hg)
    k_all, v_all = gather_item(k, v, sc, SPAN)
    q_all = lax.all_gather(q, "wide", axis=0, tiled=True)
    heads_out = {}
    for h in pairs_of:
        heads_out[h] = attend_call(sc, q, k_all, v_all, ck, cv, tg, h)
        for c in (0, 1):
            sums.add(("attn", 2 * h + c), mm(heads_out[h][0][c * BR : (c + 1) * BR], w_out).astype(bf16))

    mids, gus = {}, {}
    whole_out = ()
    for c in chunks:
        mids[c], gus[c], ffn_part, *whole_out = ffn_call(c, patches, sums.get(("attn", c)), vec, w_gate_up, w_down, whole_out)
        sums.add(("ffn", c), ffn_part)
    a3, hidden = whole_out
    whole_out = ()
    c4 = 0.0
    for c in chunks:
        da3_part, part_sum, *whole_out = ffn_back_call(
            c, sums.get(("ffn", c)), mids[c], cotangent, gus[c], vec, w_gate_up, w_down, whole_out
        )
        sums.add(("da3", c), da3_part)
        c4 = c4 + part_sum
    output, d_ffn, d_gu = whole_out
    mlp_part = pair_grad_call(a3, d_gu, d_ffn, hidden)
    g_mlp = scatter_rows(mlp_part)

    d_mids, dqs, d_item, d_mixed, d_scaled = {}, {}, {}, {}, {}
    whole_out = ()
    c2 = c3 = dck = dcv = gate_sum = 0.0
    for h in pairs_of:
        mixed, o_self, linv = heads_out[h]
        for c in (2 * h, 2 * h + 1):
            d_mids[c], d_mixed[c], d_scaled[c], p3, p2, *whole_out = out_back_call(
                c, sums.get(("da3", c)), mids[c], sums.get(("attn", c)), cotangent, vec, w_out, o_self, linv, whole_out
            )
            c2, c3 = c2 + p2, c3 + p3
        two = (d_scaled[2 * h], d_scaled[2 * h + 1])
        d_item[h] = gather_item(*two, sc, SPAN)
        dq_cap, pk, pv, pg = caption_back_call(q, d_mixed[2 * h], d_mixed[2 * h + 1], ck, cv, tg, h)
        dck, dcv, gate_sum = dck + pk, dcv + pv, gate_sum + pg
        dqs[h] = dq_call(sc, q, *two, k_all, v_all, dq_cap, h, (mlp_part,) if h == 0 else ())
    (d_attn,) = whole_out

    kept = (jnp.arange(SPAN) < length) & (first == me)
    in_slot = lambda x: jnp.sum(jnp.where(kept[:, None, None], x.reshape(SPAN, text, n).astype(f32), 0.0), 0)
    got_k, got_v = gather_item(dck.astype(bf16), dcv.astype(bf16), sc, SPAN)
    d_cap, hs_c = pl.pallas_call(
        caption_grad_kernel,
        out_shape=[sds((text, 2 * n), bf16), sds((1, n), f32)],
        compiler_params=params(0),
        name="caption_grad",
    )(in_slot(got_k), in_slot(got_v), cap_raw[0], hg)
    cap_part = mm_tn(captions, d_cap).astype(bf16)
    g_cap = scatter_rows(cap_part)
    d_text = (mm_nt(d_cap[:, :n], w_caption[0]) + mm_nt(d_cap[:, n:], w_caption[1])).astype(bf16)
    pieces = -(-d_text.shape[1] // d)
    padded = jnp.pad(d_text, ((0, 0), (0, pieces * d - d_text.shape[1])))
    for k_ in range(pieces):
        sums.add(("text", k_), padded[:, k_ * d : (k_ + 1) * d])

    last_half = len(pairs_of) - 1
    before = ()
    for h in pairs_of[:-1]:
        before = dkv_call(sc, k, v, q_all, *d_item[h], h, t, 0, before, ())
    whole_out = ()
    c1 = hs_qk = 0.0
    for h in pairs_of:
        dkv = dkv_call(sc, k, v, q_all, *d_item[last_half], last_half, 2 * BR, h, before, (d_text,))
        for c in (2 * h, 2 * h + 1):
            da1_part, p_hs, p1, *whole_out = dqkv_call(c, dqs[h], *dkv, q_raw, k_raw, tabs, hg, w_qkv, patches, whole_out)
            sums.add(("da1", c), da1_part)
            hs_qk, c1 = hs_qk + p_hs, c1 + p1
    (d_qkv,) = whole_out
    mixed = jnp.concatenate([heads_out[h][0] for h in pairs_of])
    g_attn = scatter_rows(pair_grad_call(a1, d_qkv, d_attn, mixed))
    whole_out = ()
    for c in chunks:
        whole_out = last_call(c, sums.get(("da1", c)), patches, d_mids[c], vec, whole_out)
    (grad_patches,) = whole_out
    grad_captions = jnp.concatenate([sums.get(("text", k_)) for k_ in range(pieces)], 1)[:, : d_text.shape[1]]

    head_part = jnp.concatenate([hs_qk, hs_c]).reshape(3, heads, HD).sum(1)
    gate_part = gate_sum[0, ::HD] * (1.0 - tg_heads * tg_heads)
    sent = jnp.concatenate([c1[0], head_part.reshape(-1), gate_part])
    got = gather_small(sent, "narrow")
    summed = jnp.sum(got[:, : d + 3 * HD], 0)
    sent = jnp.concatenate([summed, got[:, d + 3 * HD :].reshape(-1), c2[0], c3[0], c4[0]])
    got = gather_small(sent, "wide")
    one, rest = got[:, :d], got[:, d:]
    grad_head_gains = jnp.sum(rest[:, : 3 * HD], 0).reshape(3, HD)
    grad_cross_gate = jnp.sum(rest[:, 3 * HD : 3 * HD + deep * heads], 0)
    two, three, four = (rest[:, 3 * HD + deep * heads + k * d :][:, :d] for k in range(3))
    cols = jnp.stack([one, two, three, four], 1)
    gain_factor = jnp.stack([scales[:, 0], gates[:, 1], scales[:, 2], gates[:, 3]], 1)
    gain_grads = jnp.sum(gain_factor * cols, 0)
    wide_cols = d // count
    grad_norm_gains = lax.dynamic_slice_in_dim(gain_grads, me * wide_cols, wide_cols, 1)
    ones = jnp.ones_like(one)
    slope = jnp.stack([ones, 1.0 - gates[:, 1] ** 2, ones, 1.0 - gates[:, 3] ** 2], 1)
    d_mod = lax.dynamic_slice_in_dim(slope * norm_gains[None] * cols, mz * ada, ada, 2)
    at_slot = (firsts[None, :] == blocks[:, None]).astype(f32)
    d_slots = jnp.sum(at_slot[:, :, None, None] * d_mod[None], 1).astype(bf16).astype(f32)
    cond_rows = cd // count
    silu_mine = lax.dynamic_slice_in_dim(jax.nn.silu(conds).astype(bf16).astype(f32), me * cond_rows, cond_rows, 1)
    grad_ada = jnp.sum(silu_mine[:, :, None, None] * d_slots[:, None], 0)
    d_mine = lax.dynamic_index_in_dim(d_slots, me, 0, False)
    cond_part = jnp.sum(d_mine[None] * w_ada.astype(f32), (1, 2))
    cond_total = jnp.sum(gather_small(cond_part, "narrow"), 0)
    pull_silu = jax.vjp(jax.nn.silu, cond)[1]
    grad_conditioning = pull_silu(cond_total)[0].reshape(1, -1)

    rows = d // count
    return (
        output,
        grad_patches,
        grad_conditioning,
        grad_captions,
        grad_ada,
        grad_norm_gains,
        g_attn[:, : 3 * n].astype(f32).reshape(rows, 3, n).transpose(1, 0, 2),
        grad_head_gains,
        grad_cross_gate,
        g_cap.astype(f32).reshape(-1, 2, n).transpose(1, 0, 2),
        g_attn[:, 3 * n :].astype(f32).T,
        g_mlp[:, : 2 * ff].astype(f32).reshape(rows, 2, ff).transpose(1, 0, 2),
        g_mlp[:, 2 * ff :].astype(f32).T,
    )


def solution(mesh):
    placed = (
        P("wide", None),
        P("wide", None),
        P("wide", None),
        P("wide", None),
        P(),
        P(),
        P(None, None, "narrow"),
        P(),
        P(None, None, "narrow"),
        P(),
        P("narrow"),
        P(None, None, "narrow"),
        P("narrow", None),
        P(None, None, "narrow"),
        P("narrow", None),
    )
    return jax.shard_map(
        local,
        mesh=mesh,
        in_specs=placed,
        out_specs=(
            P("wide", None),
            P("wide", None),
            P("wide", None),
            P("wide", None),
            P("wide", None, "narrow"),
            P(None, "wide"),
            P(None, "wide", "narrow"),
            P(),
            P(),
            P(None, "wide", "narrow"),
            P("narrow", "wide"),
            P(None, "wide", "narrow"),
            P("narrow", "wide"),
        ),
        check_vma=False,
    )
```

```python
import functools

import jax
import jax.numpy as jnp
from jax import lax
from jax.experimental import pallas as pl
from jax.experimental.pallas import tpu as pltpu
from jax.sharding import PartitionSpec as P

HD = 64
SPAN = 4
EPS = 1e-05
LOG2E = 1.4426950408889634
f32 = jnp.float32
bf16 = jnp.bfloat16
VMEM = 56 * 1024 * 1024
BR = 256
NT = (((1,), (1,)), ((), ()))
TN = (((0,), (0,)), ((), ()))


def params(n):
    return pltpu.CompilerParams(
        dimension_semantics=("arbitrary",) * n, vmem_limit_bytes=VMEM
    )


def sds(shape, dtype):
    return jax.ShapeDtypeStruct(shape, dtype)


class Order:
    def __init__(self):
        self.token = ()

    def run(self, name, kernel, grid, ins, in_specs, out_specs, out_shape, scratch=(), scalar=None, held=(), first_held=0, after=()):
        pre = 0 if scalar is None else 1
        given = pre + len(ins)
        extra = [*self.token, *after, *held]

        def body(*refs):
            kernel(*refs[:given], *refs[given + len(extra) :])

        at = given + len(extra) - len(held)
        out = pl.pallas_call(
            body,
            grid_spec=pltpu.PrefetchScalarGridSpec(
                num_scalar_prefetch=pre,
                grid=grid,
                in_specs=list(in_specs) + loose(len(extra)),
                out_specs=out_specs,
                scratch_shapes=list(scratch),
            ),
            out_shape=out_shape,
            input_output_aliases={at + k: first_held + k for k in range(len(held))},
            compiler_params=params(len(grid)),
            name=name,
        )(*(() if scalar is None else (scalar,)), *ins, *extra)
        self.token = (out[0],)
        return out


def loose(n):
    return [pl.BlockSpec(memory_space=pl.ANY)] * n


def mm(a, b):
    return jnp.dot(a, b, preferred_element_type=f32)


def mm_nt(a, b):
    return lax.dot_general(a, b, NT, preferred_element_type=f32)


def mm_tn(a, b):
    return lax.dot_general(a, b, TN, preferred_element_type=f32)


def split(x):
    hi = x.astype(bf16)
    return hi, (x - hi.astype(f32)).astype(bf16)


def head_sum(x, ones):
    hi, lo = split(x)
    return mm(hi, ones) + mm(lo, ones)


def head_ones(n):
    a = lax.broadcasted_iota(jnp.int32, (n, n), 0) // HD
    b = lax.broadcasted_iota(jnp.int32, (n, n), 1) // HD
    return (a == b).astype(bf16)


def halves(n):
    lane = lax.broadcasted_iota(jnp.int32, (1, n), 1)
    return (lane < HD, lane >= HD)


def keep(x, mask):
    return jnp.where(mask, x, jnp.zeros_like(x))


def inv_rms(x):
    return lax.rsqrt(jnp.mean(x * x, -1, keepdims=True) + EPS)


def row(ref, k):
    return ref[k : k + 1, :]


def whole(shape):
    zeros = (0,) * len(shape)
    return pl.BlockSpec(shape, lambda *_: zeros, pipeline_mode=pl.Buffered(1))


def rows_of(br, width, first=0):
    return pl.BlockSpec((br, width), lambda i, *_: (i, first))


def accumulate(ref, value, first):
    @pl.when(first)
    def _():
        ref[...] = value

    @pl.when(jnp.logical_not(first))
    def _():
        ref[...] += value


def col_sum(x):
    return jnp.sum(x, 0, keepdims=True)


def tile3(t, n):
    return jnp.concatenate([t] * (n // t.shape[1]), 1)


def qkv_kernel(p_ref, v_ref, w_ref, c_ref, s1_ref, s2_ref, hg_ref, a_ref, qr_ref, kr_ref, q_ref, k_ref, vv_ref):
    x = p_ref[...].astype(f32)
    a = (x * inv_rms(x) * row(v_ref, 0)).astype(bf16)
    a_ref[...] = a
    n = q_ref.shape[1]
    ones = head_ones(n)
    cos, s1, s2 = (tile3(t[...], n) for t in (c_ref, s1_ref, s2_ref))

    def turned(y, gain):
        z = y * lax.rsqrt(head_sum(y * y, ones) * (1.0 / HD) + EPS) * gain
        return z * cos + pltpu.roll(z, n - 16, 1) * s1 + pltpu.roll(z, 16, 1) * s2

    q = mm(a, w_ref[0])
    qr_ref[...] = q
    q_ref[...] = (turned(q, row(hg_ref, 0)) * (0.125 * LOG2E)).astype(bf16)
    k = mm(a, w_ref[1])
    kr_ref[...] = k
    k_ref[...] = turned(k, row(hg_ref, 1)).astype(bf16)
    vv_ref[...] = mm(a, w_ref[2]).astype(bf16)


def qkv_call(order, patches, vec, w, tabs, hg, br=256):
    t, d = patches.shape
    n = w.shape[2]
    return order.run(
        "qkv",
        qkv_kernel,
        (t // br,),
        (patches, vec, w, *tabs, hg),
        [rows_of(br, d), whole(vec.shape), whole(w.shape)] + [rows_of(br, 128)] * 3 + [whole(hg.shape)],
        [rows_of(br, d)] + [rows_of(br, n)] * 5,
        [sds((t, d), bf16), sds((t, n), f32), sds((t, n), f32)] + [sds((t, n), bf16)] * 3,
    )


def soft_sums(q, k, v, mask):
    e = jnp.exp2(mm_nt(q, keep(k, mask))).astype(bf16)
    return mm(e, jnp.where(mask, v, jnp.ones_like(v)))


def item_block(j, s):
    return jnp.minimum(j, s[0] - 1)


def attend_kernel(sc, q_ref, k_ref, v_ref, ck_ref, cv_ref, tg_ref, mix_ref, o_ref, li_ref, acc):
    j = pl.program_id(1)
    masks = halves(128)
    keys = 512

    @pl.when(j == 0)
    def _():
        acc[...] = jnp.zeros_like(acc)

    @pl.when(j < sc[0])
    def _():
        q = q_ref[...]
        for h in range(2):
            total = acc[h]
            for c in range(k_ref.shape[0] // keys):
                at = slice(c * keys, (c + 1) * keys)
                total = total + soft_sums(q, k_ref[at, :], v_ref[at, :], masks[h])
            acc[h] = total

    @pl.when(j == SPAN - 1)
    def _():
        q = q_ref[...]

        def finish(a0, a1):
            inverse = 1.0 / jnp.where(masks[0], pltpu.roll(a0, HD, 1), pltpu.roll(a1, HD, 1))
            return jnp.where(masks[0], a0, a1) * inverse, inverse

        o, li = finish(acc[0], acc[1])
        c0, c1 = (soft_sums(q, ck_ref[...], cv_ref[...], m) for m in masks)
        mix_ref[...] = (o + tg_ref[...] * finish(c0, c1)[0]).astype(bf16)
        o_ref[...] = o.astype(bf16)
        li_ref[...] = li


def attend_call(order, sc, q, k, v, ck, cv, tg, h):
    n = q.shape[1]
    pairs = n // 128
    block = k.shape[0] // SPAN
    bq = 2 * BR
    text = ck.shape[0]
    mine = lambda p, j, s: (0, p)
    other = lambda p, j, s: (item_block(j, s), p)
    return order.run(
        "attend",
        attend_kernel,
        (pairs, SPAN),
        (q, k, v, ck, cv, tg),
        [
            pl.BlockSpec((bq, 128), lambda p, j, s: (h, p)),
            pl.BlockSpec((block, 128), other),
            pl.BlockSpec((block, 128), other),
            pl.BlockSpec((text, 128), mine),
            pl.BlockSpec((text, 128), mine),
            pl.BlockSpec((1, 128), mine),
        ],
        [pl.BlockSpec((bq, 128), mine)] * 3,
        [sds((bq, n), bf16), sds((bq, n), bf16), sds((bq, n), f32)],
        [pltpu.VMEM((2, bq, 128), f32)],
        sc,
    )


def caption_back_kernel(q_ref, da_ref, db_ref, ck_ref, cv_ref, tg_ref, dq_ref, dk_ref, dv_ref, gs_ref):
    masks = halves(128)
    q, d = q_ref[...], jnp.concatenate([da_ref[...], db_ref[...]], 0)
    dq = jnp.zeros(q.shape, f32)
    dk = jnp.zeros(ck_ref.shape, f32)
    dv = jnp.zeros(ck_ref.shape, f32)
    sums = []
    for h in range(2):
        ck, cv = keep(ck_ref[...], masks[h]), keep(cv_ref[...], masks[h])
        gate = tg_ref[:, h * HD : h * HD + 1]
        e = jnp.exp2(mm_nt(q, ck))
        prob = e * (1.0 / jnp.sum(e, -1, keepdims=True))
        dp = mm_nt(d, cv)
        m = jnp.sum(prob * dp, -1, keepdims=True)
        dc = (prob * (dp - m) * gate).astype(bf16)
        dq = dq + mm(dc, ck)
        dk = dk + mm_tn(dc, keep(q, masks[h]))
        dv = dv + mm_tn(prob.astype(bf16), keep(d, masks[h]))
        sums.append(jnp.sum(m, 0, keepdims=True))
    dq_ref[...] = dq * 0.125
    dk_ref[...] = dk * (1.0 / LOG2E)
    dv_ref[...] = dv * tg_ref[...]
    gs_ref[...] = jnp.where(masks[0], sums[0], sums[1])


def caption_back_call(order, q, da, db, ck, cv, tg, h):
    n = q.shape[1]
    pairs = n // 128
    bq = 2 * BR
    text = ck.shape[0]
    mine = lambda p: (0, p)
    return order.run(
        "caption_back",
        caption_back_kernel,
        (pairs,),
        (q, da, db, ck, cv, tg),
        [
            pl.BlockSpec((bq, 128), lambda p: (h, p)),
            pl.BlockSpec((BR, 128), mine),
            pl.BlockSpec((BR, 128), mine),
            pl.BlockSpec((text, 128), mine),
            pl.BlockSpec((text, 128), mine),
            pl.BlockSpec((1, 128), mine),
        ],
        [
            pl.BlockSpec((bq, 128), mine),
            pl.BlockSpec((text, 128), mine),
            pl.BlockSpec((text, 128), mine),
            pl.BlockSpec((1, 128), mine),
        ],
        [sds((bq, n), f32), sds((text, n), f32), sds((text, n), f32), sds((1, n), f32)],
    )


def minus_delta(rows, head):
    lane = lax.broadcasted_iota(jnp.int32, (rows, 128), 1)
    return jnp.where((lane >= 3 * head) & (lane < 3 * head + 3), -1.0, 0.0).astype(bf16)


def dq_kernel(sc, q_ref, da_ref, xa_ref, db_ref, xb_ref, k_ref, v_ref, c_ref, dq_ref, acc):
    pair = pl.program_id(0)
    j = pl.program_id(1)
    masks = halves(128)
    keys = 512

    @pl.when(j == 0)
    def _():
        acc[...] = jnp.zeros_like(acc)

    @pl.when(j < sc[0])
    def _():
        q = q_ref[...]
        dx = jnp.concatenate(
            [jnp.concatenate([da_ref[...], xa_ref[...]], 1), jnp.concatenate([db_ref[...], xb_ref[...]], 1)], 0
        )
        total = acc[...]
        for h in range(2):
            off = minus_delta(keys, 2 * pair + h)
            for c in range(k_ref.shape[0] // keys):
                at = slice(c * keys, (c + 1) * keys)
                k = keep(k_ref[at, :], masks[h])
                e = jnp.exp2(mm_nt(q, k))
                dp = mm_nt(dx, jnp.concatenate([keep(v_ref[at, :], masks[h]), off], 1))
                total = total + mm((e * dp).astype(bf16), k)
        acc[...] = total

    @pl.when(j == SPAN - 1)
    def _():
        dq_ref[...] = acc[...] * 0.125 + c_ref[...]


def dq_call(order, sc, q, da, db, k, v, cap_dq, h):
    n = q.shape[1]
    pairs = n // 128
    block = k.shape[0] // SPAN
    bq = 2 * BR
    mine = lambda p, j, s: (0, p)
    extra = lambda p, j, s: (0, pairs)
    other = lambda p, j, s: (item_block(j, s), p)
    return order.run(
        "dq",
        dq_kernel,
        (pairs, SPAN),
        (q, da, da, db, db, k, v, cap_dq),
        [
            pl.BlockSpec((bq, 128), lambda p, j, s: (h, p)),
            pl.BlockSpec((BR, 128), mine),
            pl.BlockSpec((BR, 128), extra),
            pl.BlockSpec((BR, 128), mine),
            pl.BlockSpec((BR, 128), extra),
            pl.BlockSpec((block, 128), other),
            pl.BlockSpec((block, 128), other),
            pl.BlockSpec((bq, 128), mine),
        ],
        [pl.BlockSpec((bq, 128), mine)],
        [sds((bq, n), f32)],
        [pltpu.VMEM((bq, 128), f32)],
        sc,
    )[0]


def dkv_kernel(parts, pair, sc, k_ref, v_ref, q_ref, *rest):
    d_refs, x_refs = rest[0 : 2 * parts : 2], rest[1 : 2 * parts : 2]
    dk_ref, dv_ref = rest[2 * parts :]
    j = pl.program_id(0)
    masks = halves(128)
    keys = 512
    queries = 2 * BR

    @pl.when(j == 0)
    def _():
        dk_ref[...] = jnp.zeros_like(dk_ref)
        dv_ref[...] = jnp.zeros_like(dv_ref)

    @pl.when(j < sc[0])
    def _():
        for c in range(k_ref.shape[0] // keys):
            at = slice(c * keys, (c + 1) * keys)
            dk, dv = dk_ref[at, :], dv_ref[at, :]
            for h in range(2):
                off = minus_delta(keys, 2 * pair + h)
                vx = jnp.concatenate([keep(v_ref[at, :], masks[h]), off], 1)
                for r in range(parts // 2):
                    q = keep(q_ref[r * queries : (r + 1) * queries, :], masks[h])
                    d = jnp.concatenate([d_refs[2 * r][...], d_refs[2 * r + 1][...]], 0)
                    x = jnp.concatenate([x_refs[2 * r][...], x_refs[2 * r + 1][...]], 0)
                    e = jnp.exp2(mm_nt(k_ref[at, :], q))
                    dp = mm_nt(vx, jnp.concatenate([d, x], 1))
                    dv = dv + mm(e.astype(bf16), keep(d, masks[h]))
                    dk = dk + mm((e * dp).astype(bf16), q)
            dk_ref[at, :] = dk
            dv_ref[at, :] = dv


def dkv_call(order, sc, k, v, q_all, ds, pair):
    t, n = k.shape
    pairs = n // 128
    mine = pl.BlockSpec((t, 128), lambda j, s: (0, pair))
    out = pl.BlockSpec((t, 128), lambda j, s: (0, 0))
    other = pl.BlockSpec((BR, 128), lambda j, s: (item_block(j, s), pair))
    extra = pl.BlockSpec((BR, 128), lambda j, s: (item_block(j, s), pairs))
    return order.run(
        "dkv",
        functools.partial(dkv_kernel, len(ds), pair),
        (SPAN,),
        (k, v, q_all, *(x for d in ds for x in (d, d))),
        [mine, mine, pl.BlockSpec((t, 128), lambda j, s: (s[1 + SPAN + j], pair))] + [other, extra] * len(ds),
        [out, out],
        [sds((t, 128), f32)] * 2,
        scalar=sc,
    )


def chunk_call(order, kernel, name, c, ins, specs, chunk_outs, sum_outs, whole_outs, before):
    one = lambda r, w: pl.BlockSpec((r, w), lambda i: (0, 0))
    own = chunk_outs + sum_outs
    into = [pl.BlockSpec((BR, w), lambda i: (c, 0)) for _, w, _ in whole_outs]
    return order.run(
        name,
        kernel,
        (1,),
        ins,
        specs,
        [one(r, w) for r, w, _ in own] + into,
        [sds((r, w), k) for r, w, k in own + whole_outs],
        held=tuple(before),
        first_held=len(own),
    )


def part(c, width):
    return pl.BlockSpec((BR, width), lambda i: (c, 0))


def alone(width):
    return pl.BlockSpec((BR, width), lambda i: (0, 0))


def pair_grad_kernel(a_ref, b_ref, c_ref, d_ref, o_ref):
    n = b_ref.shape[1]
    o_ref[:, :n] = mm_tn(a_ref[...], b_ref[...]).astype(bf16)
    o_ref[:, n:] = mm_tn(c_ref[...], d_ref[...]).astype(bf16)


def pair_grad_call(order, a, b, c, d, part=0, parts=1, before=()):
    t, m = a.shape
    n, k = b.shape[1], d.shape[1]
    blk = 256
    steps = m // blk // parts
    cols = pl.BlockSpec((t, blk), lambda i: (0, part * steps + i))
    return order.run(
        "pair_grad",
        pair_grad_kernel,
        (steps,),
        (a, b, c, d),
        [cols, whole(b.shape), cols, whole(d.shape)],
        [pl.BlockSpec((blk, n + k), lambda i: (part * steps + i, 0))],
        [sds((m, n + k), bf16)],
        held=before,
    )


def ffn_kernel(p_ref, at_ref, v_ref, wg_ref, wd_ref, mid_ref, gu_ref, f_ref, a_ref, h_ref):
    at = at_ref[...].astype(f32)
    mid = p_ref[...].astype(f32) + row(v_ref, 1) * (at * inv_rms(at))
    mid_ref[...] = mid
    a = (mid * inv_rms(mid) * row(v_ref, 2)).astype(bf16)
    a_ref[...] = a
    g = mm(a, wg_ref[0])
    u = mm(a, wg_ref[1])
    n = g.shape[1]
    gu_ref[:, :n] = g.astype(bf16)
    gu_ref[:, n:] = u.astype(bf16)
    h = (g * jax.nn.sigmoid(g) * u).astype(bf16)
    h_ref[...] = h
    f_ref[...] = mm(h, wd_ref[...]).astype(bf16)


def ffn_call(order, c, patches, at, vec, wg, wd, before):
    t, d = patches.shape
    n = wd.shape[0]
    return chunk_call(
        order,
        ffn_kernel,
        "ffn",
        c,
        (patches, at, vec, wg, wd),
        [part(c, d), alone(d), whole(vec.shape), whole(wg.shape), whole(wd.shape)],
        [(BR, d, f32), (BR, 2 * n, bf16), (BR, d, bf16)],
        [],
        [(t, d, bf16), (t, n, bf16)],
        before,
    )


def ffn_back_kernel(f_ref, mid_ref, c_ref, gu_ref, v_ref, wg_ref, wd_ref, da_ref, cs_ref, y_ref, df_ref, dgu_ref):
    f = f_ref[...].astype(f32)
    cot = c_ref[...].astype(f32)
    r = inv_rms(f)
    fh = f * r
    y_ref[...] = (mid_ref[...] + row(v_ref, 3) * fh).astype(bf16)
    z = cot * row(v_ref, 3)
    df = (r * (z - fh * jnp.mean(z * fh, -1, keepdims=True))).astype(bf16)
    df_ref[...] = df
    cs_ref[...] = col_sum(cot * fh)
    dh = mm_nt(df, wd_ref[...])
    n = dh.shape[1]
    g = gu_ref[:, :n].astype(f32)
    u = gu_ref[:, n:].astype(f32)
    s = jax.nn.sigmoid(g)
    gs = g * s
    dg = (dh * u * (s + gs * (1.0 - s))).astype(bf16)
    du = (dh * gs).astype(bf16)
    dgu_ref[:, :n] = dg
    dgu_ref[:, n:] = du
    da_ref[...] = (mm_nt(dg, wg_ref[0]) + mm_nt(du, wg_ref[1])).astype(bf16)


def ffn_back_call(order, c, f, mid, cot, gu, vec, wg, wd, before):
    t, d = cot.shape
    n = wd.shape[0]
    return chunk_call(
        order,
        ffn_back_kernel,
        "ffn_back",
        c,
        (f, mid, cot, gu, vec, wg, wd),
        [alone(d), alone(d), part(c, d), alone(2 * n), whole(vec.shape), whole(wg.shape), whole(wd.shape)],
        [(BR, d, bf16)],
        [(1, d, f32)],
        [(t, d, bf16), (t, d, bf16), (t, 2 * n, bf16)],
        before,
    )


def out_back_kernel(da_ref, mid_ref, at_ref, c_ref, v_ref, w_ref, o_ref, li_ref, dm_ref, dx_ref, ds_ref, c3_ref, c2_ref, dat_ref):
    da = da_ref[...].astype(f32)
    mid = mid_ref[...]
    r = inv_rms(mid)
    mh = mid * r
    z = da * row(v_ref, 2)
    dm = c_ref[...].astype(f32) + r * (z - mh * jnp.mean(z * mh, -1, keepdims=True))
    dm_ref[...] = dm
    c3_ref[...] = col_sum(da * mh)
    at = at_ref[...].astype(f32)
    ra = inv_rms(at)
    ah = at * ra
    c2_ref[...] = col_sum(dm * ah)
    z = dm * row(v_ref, 1)
    dat = (ra * (z - ah * jnp.mean(z * ah, -1, keepdims=True))).astype(bf16)
    dat_ref[...] = dat
    dx = mm_nt(dat, w_ref[...]).astype(bf16)
    dx_ref[...] = dx
    n = dx.shape[1]
    ds = dx.astype(f32) * li_ref[...]
    ds_ref[:, :n] = ds.astype(bf16)
    hi, lo = split(ds * o_ref[...].astype(f32))
    head = lax.broadcasted_iota(jnp.int32, (n, 128), 0) // HD
    lane = lax.broadcasted_iota(jnp.int32, (n, 128), 1)
    to_lanes = (lane // 3 == head).astype(bf16)
    delta = mm(hi, to_lanes) + mm(lo, to_lanes)
    one = delta.astype(bf16).astype(f32)
    two = (delta - one).astype(bf16).astype(f32)
    which = lax.broadcasted_iota(jnp.int32, (1, 128), 1) % 3
    ds_ref[:, n:] = jnp.where(which == 0, one, jnp.where(which == 1, two, delta - one - two)).astype(bf16)


def out_back_call(order, c, da, mid, at, cot, vec, w, o, li, before):
    t, d = cot.shape
    n = w.shape[0]
    return chunk_call(
        order,
        out_back_kernel,
        "out_back",
        c,
        (da, mid, at, cot, vec, w, o, li),
        [alone(d), alone(d), alone(d), part(c, d), whole(vec.shape), whole(w.shape), part(c % 2, n), part(c % 2, n)],
        [(BR, d, f32), (BR, n, bf16), (BR, n + 128, bf16)],
        [(1, d, f32), (1, d, f32)],
        [(t, d, bf16)],
        before,
    )


def dqkv_kernel(pairs, dq_ref, *refs):
    dk_refs, dv_refs = refs[0 : 2 * pairs : 2], refs[1 : 2 * pairs : 2]
    (qr_ref, kr_ref, c_ref, s1_ref, s2_ref, hg_ref, w_ref, p_ref, da_ref, hs_ref, cs_ref, d_ref) = refs[2 * pairs :]
    side = lambda parts: jnp.concatenate([x[...] for x in parts], 1)
    n = dq_ref.shape[1]
    ones = head_ones(n)
    cos, s1, s2 = (tile3(t[...], n) for t in (c_ref, s1_ref, s2_ref))

    def back(dy, x, gain):
        dz = dy * cos - pltpu.roll(dy, 16, 1) * s2 - pltpu.roll(dy, n - 16, 1) * s1
        r = lax.rsqrt(head_sum(x * x, ones) * (1.0 / HD) + EPS)
        xh = x * r
        g = dz * gain
        return r * (g - xh * (head_sum(g * xh, ones) * (1.0 / HD))), col_sum(dz * xh)

    dq, hq = back(dq_ref[...], qr_ref[...], row(hg_ref, 0))
    dk, hk = back(side(dk_refs) * (1.0 / LOG2E), kr_ref[...], row(hg_ref, 1))
    dql, dkl, dvl = dq.astype(bf16), dk.astype(bf16), side(dv_refs).astype(bf16)
    d_ref[:, :n] = dql
    d_ref[:, n : 2 * n] = dkl
    d_ref[:, 2 * n :] = dvl
    da = mm_nt(dql, w_ref[0]) + mm_nt(dkl, w_ref[1]) + mm_nt(dvl, w_ref[2])
    da_ref[...] = da.astype(bf16)
    x = p_ref[...].astype(f32)
    cs_ref[...] = col_sum(da * (x * inv_rms(x)))
    hs_ref[0:1, :] = hq
    hs_ref[1:2, :] = hk


def dqkv_call(order, c, dq, dkv, qr, kr, tabs, hg, w, patches, before):
    t, d = patches.shape
    n = dq.shape[1]
    return chunk_call(
        order,
        functools.partial(dqkv_kernel, len(dkv)),
        "dqkv",
        c,
        (dq, *(x for two in dkv for x in two), qr, kr, *tabs, hg, w, patches),
        [part(c % 2, n)] + [part(c, 128)] * (2 * len(dkv)) + [part(c, n)] * 2 + [part(c, 128)] * 3 + [whole(hg.shape), whole(w.shape), part(c, d)],
        [(BR, d, bf16)],
        [(2, n, f32), (1, d, f32)],
        [(t, 3 * n, bf16)],
        before,
    )


def last_kernel(da_ref, p_ref, dm_ref, v_ref, o_ref):
    x = p_ref[...].astype(f32)
    r = inv_rms(x)
    xh = x * r
    z = da_ref[...].astype(f32) * row(v_ref, 0)
    o_ref[...] = (dm_ref[...] + r * (z - xh * jnp.mean(z * xh, -1, keepdims=True))).astype(bf16)


def last_call(order, c, da, patches, dm, vec, before):
    t, d = patches.shape
    return chunk_call(
        order,
        last_kernel,
        "last",
        c,
        (da, patches, dm, vec),
        [alone(d), part(c, d), alone(d), whole(vec.shape)],
        [],
        [],
        [(t, d, bf16)],
        before,
    )


def caption_grad_kernel(dk_ref, dv_ref, kr_ref, hg_ref, d_ref, hs_ref):
    n = dk_ref.shape[1]
    ones = head_ones(n)
    x = kr_ref[...]
    r = lax.rsqrt(head_sum(x * x, ones) * (1.0 / HD) + EPS)
    xh = x * r
    dy = dk_ref[...]
    g = dy * row(hg_ref, 2)
    d_ref[:, :n] = (r * (g - xh * (head_sum(g * xh, ones) * (1.0 / HD)))).astype(bf16)
    d_ref[:, n:] = dv_ref[...].astype(bf16)
    hs_ref[...] = col_sum(dy * xh)


def caption_norm_kernel(kr_ref, v_ref, hg_ref, k_ref, o_ref):
    x = kr_ref[...]
    r = lax.rsqrt(head_sum(x * x, head_ones(x.shape[1])) * (1.0 / HD) + EPS)
    k_ref[...] = (x * r * row(hg_ref, 2)).astype(bf16)
    o_ref[...] = v_ref[...].astype(bf16)


def swap(x, axis, size, m):
    return lax.ppermute(x, axis, [(i, i ^ m) for i in range(size)])


def pick_kernel(count, n_pieces, sc, *refs):
    a, b = refs[:n_pieces], refs[n_pieces : 2 * n_pieces]
    outs, sem = refs[2 * n_pieces : 2 * n_pieces + 2], refs[-1]
    rows = a[0].shape[0]
    for k, (pieces, out) in enumerate(zip((a, b), outs)):
        for j in range(count):
            for m in range(n_pieces):

                @pl.when(sc[1 + j] == m)
                def _():
                    pltpu.make_async_copy(pieces[m], out.at[pl.ds(j * rows, rows)], sem.at[k, j]).start()

    for k, (pieces, out) in enumerate(zip((a, b), outs)):
        for j in range(count):
            pltpu.make_async_copy(pieces[0], out.at[pl.ds(j * rows, rows)], sem.at[k, j]).wait()


def gather_item(a, b):
    size = lax.axis_size("wide")
    if size != 8:
        return [lax.all_gather(x, "wide") for x in (a, b)]
    go = lambda x, m: swap(x, "wide", 8, m)
    a2, b4 = go(a, 2), go(b, 4)
    a4, b2 = go(a, 4), go(b, 2)
    a6, b6 = go(a2, 4), go(b4, 2)
    pieces = []
    for four in ((a, a2, a4, a6), (b, b2, b4, b6)):
        for x in four:
            pieces += [x, go(x, 1)]
    return pieces


def pick(order, sc, pieces, count):
    if len(pieces) == 2:
        one = lambda x, j: lax.dynamic_index_in_dim(x, sc[1 + SPAN + j], 0, False)
        return [jnp.concatenate([one(x, j) for j in range(count)]) for x in pieces]
    rows, width = pieces[0].shape
    return order.run(
        "pick",
        functools.partial(pick_kernel, count, 8),
        (1,),
        pieces,
        loose(16),
        [pl.BlockSpec((count * rows, width), lambda i, s: (0, 0))] * 2,
        [sds((count * rows, width), pieces[0].dtype)] * 2,
        [pltpu.SemaphoreType.DMA((2, count))],
        sc,
    )


def gather_small(x, axis):
    n = x.shape[0]
    wide = -(-n // 1024) * 1024
    x = jnp.pad(x, (0, wide - n)).reshape(wide // 128, 128)
    size = lax.axis_size(axis)
    if size > 8:
        return lax.all_gather(x, axis).reshape(size, wide)[:, :n]
    got = jnp.stack([x] + [swap(x, axis, size, m) for m in range(1, size)])
    order = jnp.arange(size, dtype=jnp.int32)
    mine = (order[:, None] ^ lax.axis_index(axis)) == order[None, :]
    out = jnp.sum(jnp.where(mine[:, :, None, None], got[None], 0.0), 1)
    return out.reshape(size, wide)[:, :n]


def gather_now(x, axis):
    n = x.shape[0]
    wide = -(-n // 1024) * 1024
    padded = jnp.pad(x, (0, wide - n)).reshape(1, 8, wide // 8)
    return lax.all_gather(padded, axis, axis=0, tiled=True).reshape(-1, wide)[:, :n]


def hop_kernel(have, sc, *refs):
    ins = dict(zip(have["in"], refs))
    outs = dict(zip(have["out"], refs[len(have["in"]) :]))
    end = sc[0] == 1
    if "total" in outs:
        outs["total"][...] = jnp.where(end, ins["r1"][...], ins["send"][...])
    third = None
    if "second" in ins:
        third = ins["second"][...] + ins["r2"][...]
    if "second" in outs:
        outs["second"][...] = ins["x"][...] + ins["r1"][...]
    if "send" in outs:
        new = ins["new"][...] if "new" in ins else third
        outs["send"][...] = new if third is None else jnp.where(end, new, third)


class Line:
    def __init__(self, order, place):
        self.order = order
        self.end = ((place == 0) | (place == 3)).astype(jnp.int32).reshape(1)
        self.x = self.second = self.send = None
        self.third = False

    def step(self, new, after=()):
        if self.send is None:
            self.x = self.send = new
            return None
        go = lambda x, perm: lax.ppermute(x, "narrow", perm)
        ins = {"r1": go(self.send, [(0, 1), (3, 2), (1, 0), (2, 3)])}
        outs = []
        if self.third:
            ins["send"] = self.send
            outs.append("total")
        if self.second is not None:
            ins["r2"] = go(self.second, [(1, 2), (2, 1)])
            ins["second"] = self.second
        if self.x is not None:
            ins["x"] = self.x
            outs.append("second")
        if new is not None:
            ins["new"] = new
        if new is not None or self.second is not None:
            outs.append("send")
        like = ins["r1"]
        block = pl.BlockSpec((BR // 2, like.shape[1]), lambda i, s: (i, 0))
        got = self.order.run(
            "hop",
            functools.partial(hop_kernel, {"in": list(ins), "out": outs}),
            (2,),
            list(ins.values()),
            [block] * len(ins),
            [block] * len(outs),
            [sds(like.shape, like.dtype)] * len(outs),
            scalar=self.end,
            after=after,
        )
        got = dict(zip(outs, got))
        self.third = self.second is not None
        self.x, self.second, self.send = new, got.get("second"), got.get("send")
        return got.get("total")


class Sums:
    def __init__(self, order, size, place):
        self.line = Line(order, place) if size == 4 else None
        self.names, self.done = [], {}

    def add(self, name, x, after=()):
        if self.line is None:
            self.done[name] = lax.psum(x, "narrow")
            return
        if self.line.send is None:
            self.names = [None]
        self._step(name, x, after)

    def _step(self, name, x, after):
        total = self.line.step(x, after)
        self.names.append(name)
        if total is not None:
            self.done[self.names[-4]] = total

    def get(self, name, after=()):
        while name not in self.done:
            self._step(None, None, after)
            after = ()
        return self.done[name]


def scatter_rows(x):
    return lax.psum_scatter(x.astype(bf16), "wide", scatter_dimension=0, tiled=True)


def rope_tables(position, width):
    lane = jnp.arange(128, dtype=jnp.int32)
    within = lane % HD
    quarter = HD // 4
    frequency = 10000.0 ** (-(within % quarter).astype(f32) / quarter)
    by_row = within < HD // 2
    where = jnp.where(by_row[None, :], (position // width)[:, None], (position % width)[:, None])
    angle = where.astype(f32) * frequency[None, :]
    cos, sin = jnp.cos(angle), jnp.sin(angle)
    former = (within % (HD // 2) < quarter)[None, :]
    return cos, jnp.where(former, -sin, 0.0), jnp.where(former, 0.0, sin)


def local(
    patches,
    cotangent,
    conditioning,
    captions,
    item_lengths,
    grid_widths,
    w_ada,
    norm_gains,
    w_qkv,
    head_gains,
    cross_gate,
    w_caption,
    w_out,
    w_gate_up,
    w_down,
):
    t, d = patches.shape
    n = w_qkv.shape[2]
    heads = n // HD
    ada = w_ada.shape[2]
    ff = w_down.shape[0]
    text = captions.shape[0]
    cd = conditioning.shape[1]
    count = lax.axis_size("wide")
    deep = lax.axis_size("narrow")
    me = lax.axis_index("wide")
    mz = lax.axis_index("narrow")

    slots = item_lengths.shape[0]
    spans = item_lengths // t
    order = jnp.arange(slots, dtype=jnp.int32)
    ends = jnp.sum(jnp.where(order[None, :] <= order[:, None], spans[None, :], 0), 1)
    blocks = jnp.arange(count, dtype=jnp.int32)
    item = jnp.sum((ends[None, :] <= blocks[:, None]).astype(jnp.int32), 1)
    is_item = item[:, None] == order[None, :]
    choose = lambda values: jnp.sum(jnp.where(is_item, values[None, :], 0), 1)
    firsts = choose(ends - spans)
    mine = blocks == me
    of_me = lambda values: jnp.sum(jnp.where(mine, values, 0))
    first = of_me(firsts)
    length = of_me(choose(spans))
    width = of_me(choose(grid_widths))
    position = (me - first) * t + jnp.arange(t, dtype=jnp.int32)
    tabs = rope_tables(position, width)
    steps = first + jnp.minimum(jnp.arange(SPAN, dtype=jnp.int32), length - 1)
    places = steps ^ me if count == 8 else steps
    sc = jnp.concatenate([length.reshape(1), places, steps]).astype(jnp.int32)

    cond = conditioning.astype(f32)[0]
    silu_low = jax.nn.silu(cond).astype(bf16)
    mod = jnp.sum(silu_low.astype(f32)[:, None, None] * w_ada.astype(f32), 0)
    share = cd // deep
    sent = jnp.concatenate([mod.reshape(-1), lax.dynamic_slice_in_dim(cond, mz * share, share)])
    got = gather_now(gather_now(sent, "narrow").reshape(-1), "wide").reshape(count, deep, -1)
    mods = got[:, :, : 4 * ada].reshape(count, deep, 4, ada).transpose(0, 2, 1, 3).reshape(count, 4, d)
    conds = got[:, :, 4 * ada :].reshape(count, cd)
    my_mod = lax.dynamic_index_in_dim(mods, first, 0, False)
    of_block = jnp.sum(jnp.where((firsts[:, None] == blocks[None, :])[:, :, None, None], mods[None], 0.0), 1)
    scales = 1.0 + of_block
    gates = jnp.tanh(of_block)
    factor = jnp.stack([1.0 + my_mod[0], jnp.tanh(my_mod[1]), 1.0 + my_mod[2], jnp.tanh(my_mod[3])])
    vec = norm_gains * factor
    hg = jnp.tile(head_gains, (1, heads))
    tg_heads = jnp.tanh(cross_gate)
    tg = jnp.repeat(tg_heads, HD)[None, :]

    order = Order()
    cap_raw = jnp.einsum("kd,jde->jke", captions, w_caption, preferred_element_type=f32)
    whole_cap = pl.BlockSpec((text, n), lambda i: (0, 0))
    cap_own = order.run(
        "caption_norm",
        caption_norm_kernel,
        (1,),
        (cap_raw[0], cap_raw[1], hg),
        [whole_cap, whole_cap, whole(hg.shape)],
        [whole_cap, whole_cap],
        [sds((text, n), bf16)] * 2,
    )
    cap_pieces = gather_item(*cap_own)

    chunks = range(t // BR)
    pairs_of = range(t // (2 * BR))
    sums = Sums(order, deep, mz)
    a1, q_raw, k_raw, q, k, v = qkv_call(order, patches, vec, w_qkv, tabs, hg)
    kv_pieces = gather_item(k, v)
    q_all = lax.all_gather(q, "wide", axis=0, tiled=True)
    ck, cv = pick(order, sc, cap_pieces, 1)
    k_all, v_all = pick(order, sc, kv_pieces, SPAN)
    heads_out = {}
    for h in pairs_of:
        heads_out[h] = attend_call(order, sc, q, k_all, v_all, ck, cv, tg, h)
        if h == 0:
            sums.add(("attn", 0), mm(heads_out[0][0][:BR], w_out).astype(bf16))
    for c in chunks[1:]:
        at = (c % 2) * BR
        sums.add(("attn", c), mm(heads_out[c // 2][0][at : at + BR], w_out).astype(bf16))

    mids, gus = {}, {}
    whole_out = ()
    for c in chunks:
        mids[c], gus[c], ffn_part, *whole_out = ffn_call(
            order, c, patches, sums.get(("attn", c)), vec, w_gate_up, w_down, whole_out
        )
        sums.add(("ffn", c), ffn_part)
    a3, hidden = whole_out
    whole_out = ()
    c4 = 0.0
    for c in chunks:
        da3_part, part_sum, *whole_out = ffn_back_call(
            order, c, sums.get(("ffn", c)), mids[c], cotangent, gus[c], vec, w_gate_up, w_down, whole_out
        )
        sums.add(("da3", c), da3_part)
        c4 = c4 + part_sum
    output, d_ffn, d_gu = whole_out

    d_mids, dqs, dq_caps, d_pieces, d_mixed, d_scaled = {}, {}, {}, {}, {}, {}
    whole_out = ()
    mlp_part = ()
    c2 = c3 = dck = dcv = gate_sum = 0.0
    for h in pairs_of:
        mixed, o_self, linv = heads_out[h]
        for c in (2 * h, 2 * h + 1):
            d_mids[c], d_mixed[c], d_scaled[c], p3, p2, *whole_out = out_back_call(
                order, c, sums.get(("da3", c)), mids[c], sums.get(("attn", c)), cotangent, vec, w_out, o_self, linv, whole_out
            )
            c2, c3 = c2 + p2, c3 + p3
            if c % 2 == 0:
                mlp_part = pair_grad_call(order, a3, d_gu, d_ffn, hidden, h, len(pairs_of), mlp_part)
        d_pieces[h] = gather_item(d_scaled[2 * h], d_scaled[2 * h + 1])
        dq_caps[h], pk, pv, pg = caption_back_call(order, q, d_mixed[2 * h], d_mixed[2 * h + 1], ck, cv, tg, h)
        dck, dcv, gate_sum = dck + pk, dcv + pv, gate_sum + pg
    (d_attn,) = whole_out
    g_mlp = scatter_rows(mlp_part[0])
    back_pieces = gather_item(dck.astype(bf16), dcv.astype(bf16))
    for h in pairs_of:
        dqs[h] = dq_call(order, sc, q, d_scaled[2 * h], d_scaled[2 * h + 1], k_all, v_all, dq_caps[h], h)

    kept = (jnp.arange(SPAN) < length) & (first == me)
    in_slot = lambda x: jnp.sum(jnp.where(kept[:, None, None], x.reshape(SPAN, text, n).astype(f32), 0.0), 0)
    got_k, got_v = pick(order, sc, back_pieces, SPAN)
    d_cap, hs_c = order.run(
        "caption_grad",
        caption_grad_kernel,
        (1,),
        (in_slot(got_k), in_slot(got_v), cap_raw[0], hg),
        [whole_cap, whole_cap, whole_cap, whole(hg.shape)],
        [pl.BlockSpec((text, 2 * n), lambda i: (0, 0)), pl.BlockSpec((1, n), lambda i: (0, 0))],
        [sds((text, 2 * n), bf16), sds((1, n), f32)],
    )
    d_text = (mm_nt(d_cap[:, :n], w_caption[0]) + mm_nt(d_cap[:, n:], w_caption[1])).astype(bf16)
    cap_part = mm_tn(captions, d_cap).astype(bf16)
    g_cap = scatter_rows(cap_part)
    pieces = -(-d_text.shape[1] // d)
    padded = jnp.pad(d_text, ((0, 0), (0, pieces * d - d_text.shape[1])))
    text_parts = [padded[:, p * d : (p + 1) * d] for p in range(pieces)]

    ds = [x for h in pairs_of for x in pick(order, sc, d_pieces[h], SPAN)]
    sums.add(("text", 0), text_parts[0])
    dkv = []
    for p in range(n // 128):
        dkv.append(dkv_call(order, sc, k, v, q_all, ds, p))
        if p + 1 < pieces:
            sums.add(("text", p + 1), text_parts[p + 1], (cap_part,) if p == 0 else ())
    for p in range(n // 128 + 1, pieces):
        sums.add(("text", p), text_parts[p])
    whole_out = ()
    c1 = hs_qk = 0.0
    mixed = jnp.concatenate([heads_out[h][0] for h in pairs_of])
    for c in chunks:
        da1_part, p_hs, p1, *whole_out = dqkv_call(order, c, dqs[c // 2], dkv, q_raw, k_raw, tabs, hg, w_qkv, patches, whole_out)
        if c == chunks[-1]:
            (d_qkv,) = whole_out
            attn_part = pair_grad_call(order, a1, d_qkv, d_attn, mixed)[0]
        sums.add(("da1", c), da1_part, (g_mlp,) if c == 0 else ())
        hs_qk, c1 = hs_qk + p_hs, c1 + p1
    g_attn = scatter_rows(attn_part)
    whole_out = ()
    for c in chunks:
        whole_out = last_call(order, c, sums.get(("da1", c), (g_cap,)), patches, d_mids[c], vec, whole_out)
    (grad_patches,) = whole_out
    grad_captions = jnp.concatenate([sums.get(("text", p)) for p in range(pieces)], 1)[:, : d_text.shape[1]]

    head_part = jnp.concatenate([hs_qk, hs_c]).reshape(3, heads, HD).sum(1)
    gate_part = gate_sum[0, ::HD] * (1.0 - tg_heads * tg_heads)
    sent = jnp.concatenate([c1[0], head_part.reshape(-1), gate_part])
    got = gather_small(sent, "narrow")
    summed = jnp.sum(got[:, : d + 3 * HD], 0)
    sent = jnp.concatenate([summed, got[:, d + 3 * HD :].reshape(-1), c2[0], c3[0], c4[0]])
    got = gather_small(sent, "wide")
    one, rest = got[:, :d], got[:, d:]
    grad_head_gains = jnp.sum(rest[:, : 3 * HD], 0).reshape(3, HD)
    grad_cross_gate = jnp.sum(rest[:, 3 * HD : 3 * HD + deep * heads], 0)
    two, three, four = (rest[:, 3 * HD + deep * heads + k * d :][:, :d] for k in range(3))
    cols = jnp.stack([one, two, three, four], 1)
    gain_factor = jnp.stack([scales[:, 0], gates[:, 1], scales[:, 2], gates[:, 3]], 1)
    gain_grads = jnp.sum(gain_factor * cols, 0)
    wide_cols = d // count
    grad_norm_gains = lax.dynamic_slice_in_dim(gain_grads, me * wide_cols, wide_cols, 1)
    ones = jnp.ones_like(one)
    slope = jnp.stack([ones, 1.0 - gates[:, 1] ** 2, ones, 1.0 - gates[:, 3] ** 2], 1)
    d_mod = lax.dynamic_slice_in_dim(slope * norm_gains[None] * cols, mz * ada, ada, 2)
    at_slot = (firsts[None, :] == blocks[:, None]).astype(f32)
    d_slots = jnp.sum(at_slot[:, :, None, None] * d_mod[None], 1).astype(bf16).astype(f32)
    cond_rows = cd // count
    silu_mine = lax.dynamic_slice_in_dim(jax.nn.silu(conds).astype(bf16).astype(f32), me * cond_rows, cond_rows, 1)
    grad_ada = jnp.sum(silu_mine[:, :, None, None] * d_slots[:, None], 0)
    d_mine = lax.dynamic_index_in_dim(d_slots, me, 0, False)
    cond_part = jnp.sum(d_mine[None] * w_ada.astype(f32), (1, 2))
    cond_total = jnp.sum(gather_small(cond_part, "narrow"), 0)
    pull_silu = jax.vjp(jax.nn.silu, cond)[1]
    grad_conditioning = pull_silu(cond_total)[0].reshape(1, -1)

    rows = d // count
    return (
        output,
        grad_patches,
        grad_conditioning,
        grad_captions,
        grad_ada,
        grad_norm_gains,
        g_attn[:, : 3 * n].astype(f32).reshape(rows, 3, n).transpose(1, 0, 2),
        grad_head_gains,
        grad_cross_gate,
        g_cap.astype(f32).reshape(-1, 2, n).transpose(1, 0, 2),
        g_attn[:, 3 * n :].astype(f32).T,
        g_mlp[:, : 2 * ff].astype(f32).reshape(rows, 2, ff).transpose(1, 0, 2),
        g_mlp[:, 2 * ff :].astype(f32).T,
    )


def solution(mesh):
    placed = (
        P("wide", None),
        P("wide", None),
        P("wide", None),
        P("wide", None),
        P(),
        P(),
        P(None, None, "narrow"),
        P(),
        P(None, None, "narrow"),
        P(),
        P("narrow"),
        P(None, None, "narrow"),
        P("narrow", None),
        P(None, None, "narrow"),
        P("narrow", None),
    )
    return jax.shard_map(
        local,
        mesh=mesh,
        in_specs=placed,
        out_specs=(
            P("wide", None),
            P("wide", None),
            P("wide", None),
            P("wide", None),
            P("wide", None, "narrow"),
            P(None, "wide"),
            P(None, "wide", "narrow"),
            P(),
            P(),
            P(None, "wide", "narrow"),
            P("narrow", "wide"),
            P(None, "wide", "narrow"),
            P("narrow", "wide"),
        ),
        check_vma=False,
    )
```

```python
import functools

import jax
import jax.numpy as jnp
from jax import lax
from jax.experimental import pallas as pl
from jax.experimental.pallas import tpu as pltpu
from jax.sharding import PartitionSpec as P

HD = 64
SPAN = 4
EPS = 1e-05
LOG2E = 1.4426950408889634
f32 = jnp.float32
bf16 = jnp.bfloat16
VMEM = 56 * 1024 * 1024
BR = 256
NT = (((1,), (1,)), ((), ()))
TN = (((0,), (0,)), ((), ()))


def params(n):
    return pltpu.CompilerParams(
        dimension_semantics=("arbitrary",) * n, vmem_limit_bytes=VMEM
    )


def sds(shape, dtype):
    return jax.ShapeDtypeStruct(shape, dtype)


class Order:
    def __init__(self):
        self.token = ()

    def run(self, name, kernel, grid, ins, in_specs, out_specs, out_shape, scratch=(), scalar=None, held=(), first_held=0, after=()):
        pre = 0 if scalar is None else 1
        given = pre + len(ins)
        extra = [*self.token, *after, *held]

        def body(*refs):
            kernel(*refs[:given], *refs[given + len(extra) :])

        at = given + len(extra) - len(held)
        out = pl.pallas_call(
            body,
            grid_spec=pltpu.PrefetchScalarGridSpec(
                num_scalar_prefetch=pre,
                grid=grid,
                in_specs=list(in_specs) + loose(len(extra)),
                out_specs=out_specs,
                scratch_shapes=list(scratch),
            ),
            out_shape=out_shape,
            input_output_aliases={at + k: first_held + k for k in range(len(held))},
            compiler_params=params(len(grid)),
            name=name,
        )(*(() if scalar is None else (scalar,)), *ins, *extra)
        self.token = (out[0],)
        return out


def loose(n):
    return [pl.BlockSpec(memory_space=pl.ANY)] * n


def mm(a, b):
    return jnp.dot(a, b, preferred_element_type=f32)


def mm_nt(a, b):
    return lax.dot_general(a, b, NT, preferred_element_type=f32)


def mm_tn(a, b):
    return lax.dot_general(a, b, TN, preferred_element_type=f32)


def split(x):
    hi = x.astype(bf16)
    return hi, (x - hi.astype(f32)).astype(bf16)


def head_sum(x, ones):
    hi, lo = split(x)
    return mm(hi, ones) + mm(lo, ones)


def head_ones(n):
    a = lax.broadcasted_iota(jnp.int32, (n, n), 0) // HD
    b = lax.broadcasted_iota(jnp.int32, (n, n), 1) // HD
    return (a == b).astype(bf16)


def halves(n):
    lane = lax.broadcasted_iota(jnp.int32, (1, n), 1)
    return (lane < HD, lane >= HD)


def keep(x, mask):
    return jnp.where(mask, x, jnp.zeros_like(x))


def inv_rms(x):
    return lax.rsqrt(jnp.mean(x * x, -1, keepdims=True) + EPS)


def row(ref, k):
    return ref[k : k + 1, :]


def whole(shape):
    zeros = (0,) * len(shape)
    return pl.BlockSpec(shape, lambda *_: zeros, pipeline_mode=pl.Buffered(1))


def rows_of(br, width, first=0):
    return pl.BlockSpec((br, width), lambda i, *_: (i, first))


def accumulate(ref, value, first):
    @pl.when(first)
    def _():
        ref[...] = value

    @pl.when(jnp.logical_not(first))
    def _():
        ref[...] += value


def col_sum(x):
    return jnp.sum(x, 0, keepdims=True)


def tile3(t, n):
    return jnp.concatenate([t] * (n // t.shape[1]), 1)


def key_kernel(p_ref, v_ref, w_ref, c_ref, s1_ref, s2_ref, hg_ref, a_ref, kr_ref, k_ref):
    x = p_ref[...].astype(f32)
    a = (x * inv_rms(x) * row(v_ref, 0)).astype(bf16)
    a_ref[...] = a
    k = mm(a, w_ref[0])
    kr_ref[...] = k
    k_ref[...] = turned(k, row(hg_ref, 1), (c_ref, s1_ref, s2_ref)).astype(bf16)


def turned(y, gain, tabs):
    n = y.shape[1]
    cos, s1, s2 = (tile3(t[...], n) for t in tabs)
    z = y * lax.rsqrt(head_sum(y * y, head_ones(n)) * (1.0 / HD) + EPS) * gain
    return z * cos + pltpu.roll(z, n - 16, 1) * s1 + pltpu.roll(z, 16, 1) * s2


def query_kernel(a_ref, wq_ref, wv_ref, c_ref, s1_ref, s2_ref, hg_ref, qr_ref, q_ref, v_ref):
    a = a_ref[...]
    v_ref[...] = mm(a, wv_ref[0]).astype(bf16)
    q = mm(a, wq_ref[0])
    qr_ref[...] = q
    q_ref[...] = (turned(q, row(hg_ref, 0), (c_ref, s1_ref, s2_ref)) * (0.125 * LOG2E)).astype(bf16)


def one_weight(w, k):
    return pl.BlockSpec((1, *w.shape[1:]), lambda *_: (k, 0, 0), pipeline_mode=pl.Buffered(1))


def key_call(order, patches, vec, w, tabs, hg, br=256):
    t, d = patches.shape
    n = w.shape[2]
    return order.run(
        "key",
        key_kernel,
        (t // br,),
        (patches, vec, w, *tabs, hg),
        [rows_of(br, d), whole(vec.shape), one_weight(w, 1)] + [rows_of(br, 128)] * 3 + [whole(hg.shape)],
        [rows_of(br, d)] + [rows_of(br, n)] * 2,
        [sds((t, d), bf16), sds((t, n), f32), sds((t, n), bf16)],
    )


def query_call(order, a, w, tabs, hg, br=256):
    t, d = a.shape
    n = w.shape[2]
    return order.run(
        "query",
        query_kernel,
        (t // br,),
        (a, w, w, *tabs, hg),
        [rows_of(br, d), one_weight(w, 0), one_weight(w, 2)] + [rows_of(br, 128)] * 3 + [whole(hg.shape)],
        [rows_of(br, n)] * 3,
        [sds((t, n), f32), sds((t, n), bf16), sds((t, n), bf16)],
    )


def soft_sums(q, k, v, mask):
    e = jnp.exp2(mm_nt(q, keep(k, mask))).astype(bf16)
    return mm(e, jnp.where(mask, v, jnp.ones_like(v)))


def item_block(j, s):
    return jnp.minimum(j, s[0] - 1)


def attend_kernel(sc, q_ref, k_ref, v_ref, ck_ref, cv_ref, tg_ref, mix_ref, o_ref, li_ref, acc):
    j = pl.program_id(1)
    masks = halves(128)
    keys = 512

    @pl.when(j == 0)
    def _():
        acc[...] = jnp.zeros_like(acc)

    @pl.when(j < sc[0])
    def _():
        q = q_ref[...]
        for h in range(2):
            total = acc[h]
            for c in range(k_ref.shape[0] // keys):
                at = slice(c * keys, (c + 1) * keys)
                total = total + soft_sums(q, k_ref[at, :], v_ref[at, :], masks[h])
            acc[h] = total

    @pl.when(j == SPAN - 1)
    def _():
        q = q_ref[...]

        def finish(a0, a1):
            inverse = 1.0 / jnp.where(masks[0], pltpu.roll(a0, HD, 1), pltpu.roll(a1, HD, 1))
            return jnp.where(masks[0], a0, a1) * inverse, inverse

        o, li = finish(acc[0], acc[1])
        c0, c1 = (soft_sums(q, ck_ref[...], cv_ref[...], m) for m in masks)
        mix_ref[...] = (o + tg_ref[...] * finish(c0, c1)[0]).astype(bf16)
        o_ref[...] = o.astype(bf16)
        li_ref[...] = li


def attend_call(order, sc, q, k, v, cap, tg, at, bq):
    n = q.shape[1]
    pairs = n // 128
    block = k.shape[0] // SPAN
    text = cap.shape[0]
    mine = lambda p, j, s: (0, p)
    other = lambda p, j, s: (item_block(j, s), p)
    return order.run(
        "attend",
        attend_kernel,
        (pairs, SPAN),
        (q, k, v, cap, cap, tg),
        [
            pl.BlockSpec((bq, 128), lambda p, j, s: (at, p)),
            pl.BlockSpec((block, 128), other),
            pl.BlockSpec((block, 128), other),
            pl.BlockSpec((text, 128), mine),
            pl.BlockSpec((text, 128), lambda p, j, s: (0, pairs + p)),
            pl.BlockSpec((1, 128), mine),
        ],
        [pl.BlockSpec((bq, 128), mine)] * 3,
        [sds((bq, n), bf16), sds((bq, n), bf16), sds((bq, n), f32)],
        [pltpu.VMEM((2, bq, 128), f32)],
        sc,
    )


def caption_back_kernel(q_ref, da_ref, db_ref, ck_ref, cv_ref, tg_ref, dq_ref, dk_ref, dv_ref, gs_ref):
    masks = halves(128)
    q, d = q_ref[...], jnp.concatenate([da_ref[...], db_ref[...]], 0)
    dq = jnp.zeros(q.shape, f32)
    dk = jnp.zeros(ck_ref.shape, f32)
    dv = jnp.zeros(ck_ref.shape, f32)
    sums = []
    for h in range(2):
        ck, cv = keep(ck_ref[...], masks[h]), keep(cv_ref[...], masks[h])
        gate = tg_ref[:, h * HD : h * HD + 1]
        e = jnp.exp2(mm_nt(q, ck))
        prob = e * (1.0 / jnp.sum(e, -1, keepdims=True))
        dp = mm_nt(d, cv)
        m = jnp.sum(prob * dp, -1, keepdims=True)
        dc = (prob * (dp - m) * gate).astype(bf16)
        dq = dq + mm(dc, ck)
        dk = dk + mm_tn(dc, keep(q, masks[h]))
        dv = dv + mm_tn(prob.astype(bf16), keep(d, masks[h]))
        sums.append(jnp.sum(m, 0, keepdims=True))
    dq_ref[...] = dq * 0.125
    dk_ref[...] = dk * (1.0 / LOG2E)
    dv_ref[...] = dv * tg_ref[...]
    gs_ref[...] = jnp.where(masks[0], sums[0], sums[1])


def caption_back_call(order, q, da, db, cap, tg, h):
    n = q.shape[1]
    pairs = n // 128
    bq = 2 * BR
    text = cap.shape[0]
    mine = lambda p: (0, p)
    return order.run(
        "caption_back",
        caption_back_kernel,
        (pairs,),
        (q, da, db, cap, cap, tg),
        [
            pl.BlockSpec((bq, 128), lambda p: (h, p)),
            pl.BlockSpec((BR, 128), mine),
            pl.BlockSpec((BR, 128), mine),
            pl.BlockSpec((text, 128), mine),
            pl.BlockSpec((text, 128), lambda p: (0, pairs + p)),
            pl.BlockSpec((1, 128), mine),
        ],
        [
            pl.BlockSpec((bq, 128), mine),
            pl.BlockSpec((text, 128), mine),
            pl.BlockSpec((text, 128), mine),
            pl.BlockSpec((1, 128), mine),
        ],
        [sds((bq, n), f32), sds((text, n), f32), sds((text, n), f32), sds((1, n), f32)],
    )


def minus_delta(rows, head):
    lane = lax.broadcasted_iota(jnp.int32, (rows, 128), 1)
    return jnp.where((lane >= 3 * head) & (lane < 3 * head + 3), -1.0, 0.0).astype(bf16)


def dq_kernel(sc, q_ref, da_ref, xa_ref, db_ref, xb_ref, k_ref, v_ref, c_ref, dq_ref, acc):
    pair = pl.program_id(0)
    j = pl.program_id(1)
    masks = halves(128)
    keys = 512

    @pl.when(j == 0)
    def _():
        acc[...] = jnp.zeros_like(acc)

    @pl.when(j < sc[0])
    def _():
        q = q_ref[...]
        dx = jnp.concatenate(
            [jnp.concatenate([da_ref[...], xa_ref[...]], 1), jnp.concatenate([db_ref[...], xb_ref[...]], 1)], 0
        )
        total = acc[...]
        for h in range(2):
            off = minus_delta(keys, 2 * pair + h)
            for c in range(k_ref.shape[0] // keys):
                at = slice(c * keys, (c + 1) * keys)
                k = keep(k_ref[at, :], masks[h])
                e = jnp.exp2(mm_nt(q, k))
                dp = mm_nt(dx, jnp.concatenate([keep(v_ref[at, :], masks[h]), off], 1))
                total = total + mm((e * dp).astype(bf16), k)
        acc[...] = total

    @pl.when(j == SPAN - 1)
    def _():
        dq_ref[...] = acc[...] * 0.125 + c_ref[...]


def dq_call(order, sc, q, da, db, k, v, cap_dq, h, after=()):
    n = q.shape[1]
    pairs = n // 128
    block = k.shape[0] // SPAN
    bq = 2 * BR
    mine = lambda p, j, s: (0, p)
    extra = lambda p, j, s: (0, pairs)
    other = lambda p, j, s: (item_block(j, s), p)
    return order.run(
        "dq",
        dq_kernel,
        (pairs, SPAN),
        (q, da, da, db, db, k, v, cap_dq),
        [
            pl.BlockSpec((bq, 128), lambda p, j, s: (h, p)),
            pl.BlockSpec((BR, 128), mine),
            pl.BlockSpec((BR, 128), extra),
            pl.BlockSpec((BR, 128), mine),
            pl.BlockSpec((BR, 128), extra),
            pl.BlockSpec((block, 128), other),
            pl.BlockSpec((block, 128), other),
            pl.BlockSpec((bq, 128), mine),
        ],
        [pl.BlockSpec((bq, 128), mine)],
        [sds((bq, n), f32)],
        [pltpu.VMEM((bq, 128), f32)],
        sc,
        after=after,
    )[0]


def dkv_kernel(parts, pair, sc, k_ref, v_ref, q_ref, *rest):
    d_refs, x_refs = rest[0 : 2 * parts : 2], rest[1 : 2 * parts : 2]
    dk_ref, dv_ref = rest[2 * parts :]
    j = pl.program_id(0)
    masks = halves(128)
    keys = 512
    queries = 2 * BR

    @pl.when(j == 0)
    def _():
        dk_ref[...] = jnp.zeros_like(dk_ref)
        dv_ref[...] = jnp.zeros_like(dv_ref)

    @pl.when(j < sc[0])
    def _():
        for c in range(k_ref.shape[0] // keys):
            at = slice(c * keys, (c + 1) * keys)
            dk, dv = dk_ref[at, :], dv_ref[at, :]
            for h in range(2):
                off = minus_delta(keys, 2 * pair + h)
                vx = jnp.concatenate([keep(v_ref[at, :], masks[h]), off], 1)
                for r in range(parts // 2):
                    q = keep(q_ref[r * queries : (r + 1) * queries, :], masks[h])
                    d = jnp.concatenate([d_refs[2 * r][...], d_refs[2 * r + 1][...]], 0)
                    x = jnp.concatenate([x_refs[2 * r][...], x_refs[2 * r + 1][...]], 0)
                    e = jnp.exp2(mm_nt(k_ref[at, :], q))
                    dp = mm_nt(vx, jnp.concatenate([d, x], 1))
                    dv = dv + mm(e.astype(bf16), keep(d, masks[h]))
                    dk = dk + mm((e * dp).astype(bf16), q)
            dk_ref[at, :] = dk
            dv_ref[at, :] = dv


def dkv_call(order, sc, k, v, q_all, ds, pair):
    t, n = k.shape
    pairs = n // 128
    mine = pl.BlockSpec((t, 128), lambda j, s: (0, pair))
    out = pl.BlockSpec((t, 128), lambda j, s: (0, 0))
    other = pl.BlockSpec((BR, 128), lambda j, s: (item_block(j, s), pair))
    extra = pl.BlockSpec((BR, 128), lambda j, s: (item_block(j, s), pairs))
    return order.run(
        "dkv",
        functools.partial(dkv_kernel, len(ds), pair),
        (SPAN,),
        (k, v, q_all, *(x for d in ds for x in (d, d))),
        [mine, mine, pl.BlockSpec((t, 128), lambda j, s: (s[1 + SPAN + j], pair))] + [other, extra] * len(ds),
        [out, out],
        [sds((t, 128), f32)] * 2,
        scalar=sc,
    )


def chunk_call(order, kernel, name, c, ins, specs, chunk_outs, sum_outs, whole_outs, before):
    one = lambda r, w: pl.BlockSpec((r, w), lambda i: (0, 0))
    own = chunk_outs + sum_outs
    into = [pl.BlockSpec((BR, w), lambda i: (c, 0)) for _, w, _ in whole_outs]
    return order.run(
        name,
        kernel,
        (1,),
        ins,
        specs,
        [one(r, w) for r, w, _ in own] + into,
        [sds((r, w), k) for r, w, k in own + whole_outs],
        held=tuple(before),
        first_held=len(own),
    )


def part(c, width):
    return pl.BlockSpec((BR, width), lambda i: (c, 0))


def alone(width):
    return pl.BlockSpec((BR, width), lambda i: (0, 0))


def pair_grad_kernel(a_ref, b_ref, c_ref, d_ref, o_ref):
    n = b_ref.shape[1]
    o_ref[:, :n] = mm_tn(a_ref[...], b_ref[...]).astype(bf16)
    o_ref[:, n:] = mm_tn(c_ref[...], d_ref[...]).astype(bf16)


def pair_grad_call(order, a, b, c, d, part=0, parts=1, before=(), after=()):
    t, m = a.shape
    n, k = b.shape[1], d.shape[1]
    blk = 256
    steps = m // blk // parts
    cols = pl.BlockSpec((t, blk), lambda i: (0, part * steps + i))
    return order.run(
        "pair_grad",
        pair_grad_kernel,
        (steps,),
        (a, b, c, d),
        [cols, whole(b.shape), cols, whole(d.shape)],
        [pl.BlockSpec((blk, n + k), lambda i: (part * steps + i, 0))],
        [sds((m, n + k), bf16)],
        held=before,
        after=after,
    )


def ffn_kernel(p_ref, at_ref, v_ref, wg_ref, wd_ref, mid_ref, gu_ref, f_ref, a_ref, h_ref):
    at = at_ref[...].astype(f32)
    mid = p_ref[...].astype(f32) + row(v_ref, 1) * (at * inv_rms(at))
    mid_ref[...] = mid
    a = (mid * inv_rms(mid) * row(v_ref, 2)).astype(bf16)
    a_ref[...] = a
    g = mm(a, wg_ref[0])
    u = mm(a, wg_ref[1])
    n = g.shape[1]
    gu_ref[:, :n] = g.astype(bf16)
    gu_ref[:, n:] = u.astype(bf16)
    h = (g * jax.nn.sigmoid(g) * u).astype(bf16)
    h_ref[...] = h
    f_ref[...] = mm(h, wd_ref[...]).astype(bf16)


def ffn_call(order, c, patches, at, vec, wg, wd, before):
    t, d = patches.shape
    n = wd.shape[0]
    return chunk_call(
        order,
        ffn_kernel,
        "ffn",
        c,
        (patches, at, vec, wg, wd),
        [part(c, d), alone(d), whole(vec.shape), whole(wg.shape), whole(wd.shape)],
        [(BR, d, f32), (BR, 2 * n, bf16), (BR, d, bf16)],
        [],
        [(t, d, bf16), (t, n, bf16)],
        before,
    )


def ffn_back_kernel(f_ref, mid_ref, c_ref, gu_ref, v_ref, wg_ref, wd_ref, da_ref, cs_ref, y_ref, df_ref, dgu_ref):
    f = f_ref[...].astype(f32)
    cot = c_ref[...].astype(f32)
    r = inv_rms(f)
    fh = f * r
    y_ref[...] = (mid_ref[...] + row(v_ref, 3) * fh).astype(bf16)
    z = cot * row(v_ref, 3)
    df = (r * (z - fh * jnp.mean(z * fh, -1, keepdims=True))).astype(bf16)
    df_ref[...] = df
    cs_ref[...] = col_sum(cot * fh)
    dh = mm_nt(df, wd_ref[...])
    n = dh.shape[1]
    g = gu_ref[:, :n].astype(f32)
    u = gu_ref[:, n:].astype(f32)
    s = jax.nn.sigmoid(g)
    gs = g * s
    dg = (dh * u * (s + gs * (1.0 - s))).astype(bf16)
    du = (dh * gs).astype(bf16)
    dgu_ref[:, :n] = dg
    dgu_ref[:, n:] = du
    da_ref[...] = (mm_nt(dg, wg_ref[0]) + mm_nt(du, wg_ref[1])).astype(bf16)


def ffn_back_call(order, c, f, mid, cot, gu, vec, wg, wd, before):
    t, d = cot.shape
    n = wd.shape[0]
    return chunk_call(
        order,
        ffn_back_kernel,
        "ffn_back",
        c,
        (f, mid, cot, gu, vec, wg, wd),
        [alone(d), alone(d), part(c, d), alone(2 * n), whole(vec.shape), whole(wg.shape), whole(wd.shape)],
        [(BR, d, bf16)],
        [(1, d, f32)],
        [(t, d, bf16), (t, d, bf16), (t, 2 * n, bf16)],
        before,
    )


def out_back_kernel(da_ref, mid_ref, at_ref, c_ref, v_ref, w_ref, o_ref, li_ref, dm_ref, dx_ref, ds_ref, c3_ref, c2_ref, dat_ref):
    da = da_ref[...].astype(f32)
    mid = mid_ref[...]
    r = inv_rms(mid)
    mh = mid * r
    z = da * row(v_ref, 2)
    dm = c_ref[...].astype(f32) + r * (z - mh * jnp.mean(z * mh, -1, keepdims=True))
    dm_ref[...] = dm
    c3_ref[...] = col_sum(da * mh)
    at = at_ref[...].astype(f32)
    ra = inv_rms(at)
    ah = at * ra
    c2_ref[...] = col_sum(dm * ah)
    z = dm * row(v_ref, 1)
    dat = (ra * (z - ah * jnp.mean(z * ah, -1, keepdims=True))).astype(bf16)
    dat_ref[...] = dat
    dx = mm_nt(dat, w_ref[...]).astype(bf16)
    dx_ref[...] = dx
    n = dx.shape[1]
    ds = dx.astype(f32) * li_ref[...]
    ds_ref[:, :n] = ds.astype(bf16)
    hi, lo = split(ds * o_ref[...].astype(f32))
    head = lax.broadcasted_iota(jnp.int32, (n, 128), 0) // HD
    lane = lax.broadcasted_iota(jnp.int32, (n, 128), 1)
    to_lanes = (lane // 3 == head).astype(bf16)
    delta = mm(hi, to_lanes) + mm(lo, to_lanes)
    one = delta.astype(bf16).astype(f32)
    two = (delta - one).astype(bf16).astype(f32)
    which = lax.broadcasted_iota(jnp.int32, (1, 128), 1) % 3
    ds_ref[:, n:] = jnp.where(which == 0, one, jnp.where(which == 1, two, delta - one - two)).astype(bf16)


def out_back_call(order, c, da, mid, at, cot, vec, w, o, li, place, before):
    t, d = cot.shape
    n = w.shape[0]
    return chunk_call(
        order,
        out_back_kernel,
        "out_back",
        c,
        (da, mid, at, cot, vec, w, o, li),
        [alone(d), alone(d), alone(d), part(c, d), whole(vec.shape), whole(w.shape), part(place, n), part(place, n)],
        [(BR, d, f32), (BR, n, bf16), (BR, n + 128, bf16)],
        [(1, d, f32), (1, d, f32)],
        [(t, d, bf16)],
        before,
    )


def dqkv_kernel(pairs, dq_ref, *refs):
    dk_refs, dv_refs = refs[0 : 2 * pairs : 2], refs[1 : 2 * pairs : 2]
    (qr_ref, kr_ref, c_ref, s1_ref, s2_ref, hg_ref, w_ref, p_ref, da_ref, hs_ref, cs_ref, d_ref) = refs[2 * pairs :]
    side = lambda parts: jnp.concatenate([x[...] for x in parts], 1)
    n = dq_ref.shape[1]
    ones = head_ones(n)
    cos, s1, s2 = (tile3(t[...], n) for t in (c_ref, s1_ref, s2_ref))

    def back(dy, x, gain):
        dz = dy * cos - pltpu.roll(dy, 16, 1) * s2 - pltpu.roll(dy, n - 16, 1) * s1
        r = lax.rsqrt(head_sum(x * x, ones) * (1.0 / HD) + EPS)
        xh = x * r
        g = dz * gain
        return r * (g - xh * (head_sum(g * xh, ones) * (1.0 / HD))), col_sum(dz * xh)

    dq, hq = back(dq_ref[...], qr_ref[...], row(hg_ref, 0))
    dk, hk = back(side(dk_refs) * (1.0 / LOG2E), kr_ref[...], row(hg_ref, 1))
    dql, dkl, dvl = dq.astype(bf16), dk.astype(bf16), side(dv_refs).astype(bf16)
    d_ref[:, :n] = dql
    d_ref[:, n : 2 * n] = dkl
    d_ref[:, 2 * n :] = dvl
    da = mm_nt(dql, w_ref[0]) + mm_nt(dkl, w_ref[1]) + mm_nt(dvl, w_ref[2])
    da_ref[...] = da.astype(bf16)
    x = p_ref[...].astype(f32)
    cs_ref[...] = col_sum(da * (x * inv_rms(x)))
    hs_ref[0:1, :] = hq
    hs_ref[1:2, :] = hk


def dqkv_call(order, c, dq, dkv, qr, kr, tabs, hg, w, patches, before):
    t, d = patches.shape
    n = dq.shape[1]
    return chunk_call(
        order,
        functools.partial(dqkv_kernel, len(dkv)),
        "dqkv",
        c,
        (dq, *(x for two in dkv for x in two), qr, kr, *tabs, hg, w, patches),
        [part(c % 2, n)] + [part(c, 128)] * (2 * len(dkv)) + [part(c, n)] * 2 + [part(c, 128)] * 3 + [whole(hg.shape), whole(w.shape), part(c, d)],
        [(BR, d, bf16)],
        [(2, n, f32), (1, d, f32)],
        [(t, 3 * n, bf16)],
        before,
    )


def last_kernel(da_ref, p_ref, dm_ref, v_ref, o_ref):
    x = p_ref[...].astype(f32)
    r = inv_rms(x)
    xh = x * r
    z = da_ref[...].astype(f32) * row(v_ref, 0)
    o_ref[...] = (dm_ref[...] + r * (z - xh * jnp.mean(z * xh, -1, keepdims=True))).astype(bf16)


def last_call(order, c, da, patches, dm, vec, before):
    t, d = patches.shape
    return chunk_call(
        order,
        last_kernel,
        "last",
        c,
        (da, patches, dm, vec),
        [alone(d), part(c, d), alone(d), whole(vec.shape)],
        [],
        [],
        [(t, d, bf16)],
        before,
    )


def caption_grad_kernel(dk_ref, dv_ref, kr_ref, hg_ref, d_ref, hs_ref):
    n = dk_ref.shape[1]
    ones = head_ones(n)
    x = kr_ref[...]
    r = lax.rsqrt(head_sum(x * x, ones) * (1.0 / HD) + EPS)
    xh = x * r
    dy = dk_ref[...]
    g = dy * row(hg_ref, 2)
    d_ref[:, :n] = (r * (g - xh * (head_sum(g * xh, ones) * (1.0 / HD)))).astype(bf16)
    d_ref[:, n:] = dv_ref[...].astype(bf16)
    hs_ref[...] = col_sum(dy * xh)


def caption_norm_kernel(kr_ref, v_ref, hg_ref, o_ref):
    n = kr_ref.shape[1]
    x = kr_ref[...]
    r = lax.rsqrt(head_sum(x * x, head_ones(n)) * (1.0 / HD) + EPS)
    o_ref[:, :n] = (x * r * row(hg_ref, 2)).astype(bf16)
    o_ref[:, n:] = v_ref[...].astype(bf16)


def swap(x, axis, size, m):
    return lax.ppermute(x, axis, [(i, i ^ m) for i in range(size)])


def pick_kernel(count, n_pieces, sc, *refs):
    a, b = refs[:n_pieces], refs[n_pieces : 2 * n_pieces]
    outs, sem = refs[2 * n_pieces : 2 * n_pieces + 2], refs[-1]
    rows = a[0].shape[0]
    for k, (pieces, out) in enumerate(zip((a, b), outs)):
        for j in range(count):
            for m in range(n_pieces):

                @pl.when(sc[1 + j] == m)
                def _():
                    pltpu.make_async_copy(pieces[m], out.at[pl.ds(j * rows, rows)], sem.at[k, j]).start()

    for k, (pieces, out) in enumerate(zip((a, b), outs)):
        for j in range(count):
            pltpu.make_async_copy(pieces[0], out.at[pl.ds(j * rows, rows)], sem.at[k, j]).wait()


class Gather:
    def __init__(self, a, b):
        self.all = None
        if lax.axis_size("wide") != 8:
            self.first = self.second = ()
            self.all = [lax.all_gather(x, "wide") for x in (a, b)]
            return
        send = lambda x, pairs: lax.ppermute(x, "wide", pairs)
        over_x = [(i, i ^ 2) for i in range(8)]
        over_y = [(1, 5), (4, 0), (3, 7), (6, 2)]
        a2, a4, b4, b2 = send(a, over_x), send(a, over_y), send(b, over_y), send(b, over_x)
        a6 = send(a2, [(0, 4), (1, 5), (6, 2), (7, 3)])
        b6x, b6y = send(b2, [(0, 4), (7, 3)]), send(b4, [(7, 5), (0, 2)])
        self.first = (a2, a4, b4, b2)
        self.second = (a6, b6x, b6y)
        self.kept = ((a, a2, a4, a6), (b, b2, b4, b6x + b6y))

    def pieces(self):
        if self.all is not None:
            return self.all
        return [y for four in self.kept for x in four for y in (x, swap(x, "wide", 8, 1))]


def shift(x, by):
    size = lax.axis_size("wide")
    return lax.ppermute(x, "wide", [(i, i + by) for i in range(size) if 0 <= i + by < size])


def pick(order, sc, pieces, count):
    if len(pieces) == 2:
        one = lambda x, j: lax.dynamic_index_in_dim(x, sc[1 + SPAN + j], 0, False)
        return [jnp.concatenate([one(x, j) for j in range(count)]) for x in pieces]
    rows, width = pieces[0].shape
    return order.run(
        "pick",
        functools.partial(pick_kernel, count, 8),
        (1,),
        pieces,
        loose(16),
        [pl.BlockSpec((count * rows, width), lambda i, s: (0, 0))] * 2,
        [sds((count * rows, width), pieces[0].dtype)] * 2,
        [pltpu.SemaphoreType.DMA((2, count))],
        sc,
    )


def gather_small(x, axis):
    n = x.shape[0]
    wide = -(-n // 1024) * 1024
    x = jnp.pad(x, (0, wide - n)).reshape(wide // 128, 128)
    size = lax.axis_size(axis)
    if size > 8:
        return lax.all_gather(x, axis).reshape(size, wide)[:, :n]
    got = jnp.stack([x] + [swap(x, axis, size, m) for m in range(1, size)])
    order = jnp.arange(size, dtype=jnp.int32)
    mine = (order[:, None] ^ lax.axis_index(axis)) == order[None, :]
    out = jnp.sum(jnp.where(mine[:, :, None, None], got[None], 0.0), 1)
    return out.reshape(size, wide)[:, :n]


def gather_now(x, axis):
    n = x.shape[0]
    wide = -(-n // 1024) * 1024
    padded = jnp.pad(x, (0, wide - n)).reshape(1, 8, wide // 8)
    return lax.all_gather(padded, axis, axis=0, tiled=True).reshape(-1, wide)[:, :n]


def hop_kernel(have, sc, *refs):
    ins = dict(zip(have["in"], refs))
    outs = dict(zip(have["out"], refs[len(have["in"]) :]))
    end = sc[0] == 1
    if "total" in outs:
        outs["total"][...] = jnp.where(end, ins["r1"][...], ins["send"][...])
    third = None
    if "second" in ins:
        third = ins["second"][...] + ins["r2"][...]
    if "second" in outs:
        outs["second"][...] = ins["x"][...] + ins["r1"][...]
    if "send" in outs:
        new = ins["new"][...] if "new" in ins else third
        outs["send"][...] = new if third is None else jnp.where(end, new, third)


class Line:
    def __init__(self, order, place):
        self.order = order
        self.end = ((place == 0) | (place == 3)).astype(jnp.int32).reshape(1)
        self.x = self.second = self.send = None
        self.third = False

    def step(self, new, after=()):
        if self.send is None:
            self.x = self.send = new
            return None
        go = lambda x, perm: lax.ppermute(x, "narrow", perm)
        ins = {"r1": go(self.send, [(0, 1), (3, 2), (1, 0), (2, 3)])}
        outs = []
        if self.third:
            ins["send"] = self.send
            outs.append("total")
        if self.second is not None:
            ins["r2"] = go(self.second, [(1, 2), (2, 1)])
            ins["second"] = self.second
        if self.x is not None:
            ins["x"] = self.x
            outs.append("second")
        if new is not None:
            ins["new"] = new
        if new is not None or self.second is not None:
            outs.append("send")
        like = ins["r1"]
        block = pl.BlockSpec((BR // 4, like.shape[1]), lambda i, s: (i, 0))
        got = self.order.run(
            "hop",
            functools.partial(hop_kernel, {"in": list(ins), "out": outs}),
            (4,),
            list(ins.values()),
            [block] * len(ins),
            [block] * len(outs),
            [sds(like.shape, like.dtype)] * len(outs),
            scalar=self.end,
            after=after,
        )
        got = dict(zip(outs, got))
        self.third = self.second is not None
        self.x, self.second, self.send = new, got.get("second"), got.get("send")
        return got.get("total")


class Sums:
    def __init__(self, order, size, place):
        self.line = Line(order, place) if size == 4 else None
        self.names, self.done = [], {}

    def add(self, name, x, after=()):
        if self.line is None:
            self.done[name] = lax.psum(x, "narrow")
            return
        if self.line.send is None:
            self.names = [None]
        self._step(name, x, after)

    def _step(self, name, x, after):
        total = self.line.step(x, after)
        self.names.append(name)
        if total is not None:
            self.done[self.names[-4]] = total

    def get(self, name, after=()):
        while name not in self.done:
            self._step(None, None, after)
            after = ()
        return self.done[name]


def scatter_rows(x):
    return lax.psum_scatter(x.astype(bf16), "wide", scatter_dimension=0, tiled=True)


def rope_tables(position, width):
    lane = jnp.arange(128, dtype=jnp.int32)
    within = lane % HD
    quarter = HD // 4
    frequency = 10000.0 ** (-(within % quarter).astype(f32) / quarter)
    by_row = within < HD // 2
    where = jnp.where(by_row[None, :], (position // width)[:, None], (position % width)[:, None])
    angle = where.astype(f32) * frequency[None, :]
    cos, sin = jnp.cos(angle), jnp.sin(angle)
    former = (within % (HD // 2) < quarter)[None, :]
    return cos, jnp.where(former, -sin, 0.0), jnp.where(former, 0.0, sin)


def local(
    patches,
    cotangent,
    conditioning,
    captions,
    item_lengths,
    grid_widths,
    w_ada,
    norm_gains,
    w_qkv,
    head_gains,
    cross_gate,
    w_caption,
    w_out,
    w_gate_up,
    w_down,
):
    t, d = patches.shape
    n = w_qkv.shape[2]
    heads = n // HD
    ada = w_ada.shape[2]
    ff = w_down.shape[0]
    text = captions.shape[0]
    cd = conditioning.shape[1]
    count = lax.axis_size("wide")
    deep = lax.axis_size("narrow")
    me = lax.axis_index("wide")
    mz = lax.axis_index("narrow")

    slots = item_lengths.shape[0]
    spans = item_lengths // t
    order = jnp.arange(slots, dtype=jnp.int32)
    ends = jnp.sum(jnp.where(order[None, :] <= order[:, None], spans[None, :], 0), 1)
    blocks = jnp.arange(count, dtype=jnp.int32)
    item = jnp.sum((ends[None, :] <= blocks[:, None]).astype(jnp.int32), 1)
    is_item = item[:, None] == order[None, :]
    choose = lambda values: jnp.sum(jnp.where(is_item, values[None, :], 0), 1)
    firsts = choose(ends - spans)
    mine = blocks == me
    of_me = lambda values: jnp.sum(jnp.where(mine, values, 0))
    first = of_me(firsts)
    length = of_me(choose(spans))
    width = of_me(choose(grid_widths))
    position = (me - first) * t + jnp.arange(t, dtype=jnp.int32)
    tabs = rope_tables(position, width)
    steps = first + jnp.minimum(jnp.arange(SPAN, dtype=jnp.int32), length - 1)
    places = steps ^ me if count == 8 else steps
    sc = jnp.concatenate([length.reshape(1), places, steps]).astype(jnp.int32)

    cond = conditioning.astype(f32)[0]
    silu_low = jax.nn.silu(cond).astype(bf16)
    mod = jnp.sum(silu_low.astype(f32)[:, None, None] * w_ada.astype(f32), 0)
    share = cd // deep
    sent = jnp.concatenate([mod.reshape(-1), lax.dynamic_slice_in_dim(cond, mz * share, share)])
    got = gather_now(gather_now(sent, "narrow").reshape(-1), "wide").reshape(count, deep, -1)
    mods = got[:, :, : 4 * ada].reshape(count, deep, 4, ada).transpose(0, 2, 1, 3).reshape(count, 4, d)
    conds = got[:, :, 4 * ada :].reshape(count, cd)
    my_mod = lax.dynamic_index_in_dim(mods, first, 0, False)
    of_block = jnp.sum(jnp.where((firsts[:, None] == blocks[None, :])[:, :, None, None], mods[None], 0.0), 1)
    scales = 1.0 + of_block
    gates = jnp.tanh(of_block)
    factor = jnp.stack([1.0 + my_mod[0], jnp.tanh(my_mod[1]), 1.0 + my_mod[2], jnp.tanh(my_mod[3])])
    vec = norm_gains * factor
    hg = jnp.tile(head_gains, (1, heads))
    tg_heads = jnp.tanh(cross_gate)
    tg = jnp.repeat(tg_heads, HD)[None, :]

    order = Order()
    chunks = range(t // BR)
    pairs_of = range(t // (2 * BR))
    sums = Sums(order, deep, mz)
    a1, k_raw, k = key_call(order, patches, vec, w_qkv, tabs, hg)
    q_raw, q, v = query_call(order, a1, w_qkv, tabs, hg)
    kv = Gather(k, v)

    cap_raw = jnp.einsum("kd,jde->jke", captions, w_caption, preferred_element_type=f32)
    whole_cap = pl.BlockSpec((text, n), lambda i: (0, 0))
    both_cap = pl.BlockSpec((text, 2 * n), lambda i: (0, 0))
    (cap,) = order.run(
        "caption_norm",
        caption_norm_kernel,
        (1,),
        (cap_raw[0], cap_raw[1], hg),
        [whole_cap, whole_cap, whole(hg.shape)],
        [both_cap],
        [sds((text, 2 * n), bf16)],
    )
    offset = me - first
    cap = jnp.where(offset == 1, shift(cap, 1), cap)
    cap = jnp.where(offset >= 2, shift(cap, 2), cap)

    q_all = lax.all_gather(q, "wide", axis=0, tiled=True)
    k_all, v_all = pick(order, sc, kv.pieces(), SPAN)
    heads_out = {}
    for c in chunks[: len(chunks) // 2]:
        heads_out[c] = (*attend_call(order, sc, q, k_all, v_all, cap, tg, c, BR), 0)
        sums.add(("attn", c), mm(heads_out[c][0], w_out).astype(bf16))
    half = (len(chunks) + 1) // 2
    later = attend_call(order, sc, q, k_all, v_all, cap, tg, 1, half * BR)
    for c in chunks[half:]:
        heads_out[c] = (*later, c - half)
        at = (c - half) * BR
        sums.add(("attn", c), mm(later[0][at : at + BR], w_out).astype(bf16))

    mids, gus = {}, {}
    whole_out = ()
    for c in chunks:
        mids[c], gus[c], ffn_part, *whole_out = ffn_call(
            order, c, patches, sums.get(("attn", c)), vec, w_gate_up, w_down, whole_out
        )
        sums.add(("ffn", c), ffn_part)
    a3, hidden = whole_out
    whole_out = ()
    c4 = 0.0
    for c in chunks:
        da3_part, part_sum, *whole_out = ffn_back_call(
            order, c, sums.get(("ffn", c)), mids[c], cotangent, gus[c], vec, w_gate_up, w_down, whole_out
        )
        sums.add(("da3", c), da3_part)
        c4 = c4 + part_sum
    output, d_ffn, d_gu = whole_out

    d_mids, dqs, dq_caps, d_got, d_mixed, d_scaled = {}, {}, {}, {}, {}, {}
    whole_out = ()
    mlp_part = ()
    behind = ()
    c2 = c3 = dck = dcv = gate_sum = 0.0
    for h in pairs_of:
        for c in (2 * h, 2 * h + 1):
            _, o_self, linv, place = heads_out[c]
            if c == 2 * h + 1 and h > 0:
                behind = d_got[h - 1].second
            da3 = sums.get(("da3", c), behind)
            d_mids[c], d_mixed[c], d_scaled[c], p3, p2, *whole_out = out_back_call(
                order, c, da3, mids[c], sums.get(("attn", c)), cotangent, vec, w_out, o_self, linv, place, whole_out
            )
            c2, c3 = c2 + p2, c3 + p3
            behind = ()
            if c == 2 * h:
                early = d_got[h - 1].first if h > 0 else ()
                mlp_part = pair_grad_call(order, a3, d_gu, d_ffn, hidden, h, len(pairs_of), mlp_part, early)
        d_got[h] = Gather(d_scaled[2 * h], d_scaled[2 * h + 1])
        dq_caps[h], pk, pv, pg = caption_back_call(order, q, d_mixed[2 * h], d_mixed[2 * h + 1], cap, tg, h)
        dck, dcv, gate_sum = dck + pk, dcv + pv, gate_sum + pg
    (d_attn,) = whole_out
    g_mlp = scatter_rows(mlp_part[0])
    cap_sum = jnp.concatenate([dck, dcv], 1)
    got_two = shift(cap_sum.astype(bf16), -2)
    cap_sum = cap_sum + jnp.where(offset + 2 < length, got_two.astype(f32), 0.0)
    got_one = shift(cap_sum.astype(bf16), -1)
    cap_sum = jnp.where(offset == 0, cap_sum + jnp.where(offset + 1 < length, got_one.astype(f32), 0.0), 0.0)
    last_half = pairs_of[-1]
    for h in pairs_of:
        after = () if h == 0 else (*d_got[last_half].first, got_two)
        dqs[h] = dq_call(order, sc, q, d_scaled[2 * h], d_scaled[2 * h + 1], k_all, v_all, dq_caps[h], h, after)

    d_cap, hs_c = order.run(
        "caption_grad",
        caption_grad_kernel,
        (1,),
        (cap_sum[:, :n], cap_sum[:, n:], cap_raw[0], hg),
        [whole_cap, whole_cap, whole_cap, whole(hg.shape)],
        [both_cap, pl.BlockSpec((1, n), lambda i: (0, 0))],
        [sds((text, 2 * n), bf16), sds((1, n), f32)],
        after=d_got[last_half].second,
    )
    d_text = (mm_nt(d_cap[:, :n], w_caption[0]) + mm_nt(d_cap[:, n:], w_caption[1])).astype(bf16)
    cap_part = mm_tn(captions, d_cap).astype(bf16)
    g_cap = scatter_rows(cap_part)
    pieces = -(-d_text.shape[1] // d)
    padded = jnp.pad(d_text, ((0, 0), (0, pieces * d - d_text.shape[1])))
    text_parts = [padded[:, p * d : (p + 1) * d] for p in range(pieces)]

    ds = [x for h in pairs_of for x in pick(order, sc, d_got[h].pieces(), SPAN)]
    sums.add(("text", 0), text_parts[0])
    dkv = []
    for p in range(n // 128):
        dkv.append(dkv_call(order, sc, k, v, q_all, ds, p))
        if p + 1 < pieces:
            sums.add(("text", p + 1), text_parts[p + 1], (cap_part,) if p == 0 else ())
    for p in range(n // 128 + 1, pieces):
        sums.add(("text", p), text_parts[p])
    whole_out = ()
    c1 = hs_qk = 0.0
    mixed = jnp.concatenate([heads_out[c][0] for c in chunks[:half]] + [later[0]])
    for c in chunks:
        da1_part, p_hs, p1, *whole_out = dqkv_call(order, c, dqs[c // 2], dkv, q_raw, k_raw, tabs, hg, w_qkv, patches, whole_out)
        if c == chunks[-1]:
            (d_qkv,) = whole_out
            attn_part = pair_grad_call(order, a1, d_qkv, d_attn, mixed)[0]
        sums.add(("da1", c), da1_part, (g_mlp,) if c == 0 else ())
        hs_qk, c1 = hs_qk + p_hs, c1 + p1
    g_attn = scatter_rows(attn_part)
    whole_out = ()
    for c in chunks:
        whole_out = last_call(order, c, sums.get(("da1", c), (g_cap,)), patches, d_mids[c], vec, whole_out)
    (grad_patches,) = whole_out
    grad_captions = jnp.concatenate([sums.get(("text", p)) for p in range(pieces)], 1)[:, : d_text.shape[1]]

    head_part = jnp.concatenate([hs_qk, hs_c]).reshape(3, heads, HD).sum(1)
    gate_part = gate_sum[0, ::HD] * (1.0 - tg_heads * tg_heads)
    sent = jnp.concatenate([c1[0], head_part.reshape(-1), gate_part])
    got = gather_small(sent, "narrow")
    summed = jnp.sum(got[:, : d + 3 * HD], 0)
    sent = jnp.concatenate([summed, got[:, d + 3 * HD :].reshape(-1), c2[0], c3[0], c4[0]])
    got = gather_small(sent, "wide")
    one, rest = got[:, :d], got[:, d:]
    grad_head_gains = jnp.sum(rest[:, : 3 * HD], 0).reshape(3, HD)
    grad_cross_gate = jnp.sum(rest[:, 3 * HD : 3 * HD + deep * heads], 0)
    two, three, four = (rest[:, 3 * HD + deep * heads + k * d :][:, :d] for k in range(3))
    cols = jnp.stack([one, two, three, four], 1)
    gain_factor = jnp.stack([scales[:, 0], gates[:, 1], scales[:, 2], gates[:, 3]], 1)
    gain_grads = jnp.sum(gain_factor * cols, 0)
    wide_cols = d // count
    grad_norm_gains = lax.dynamic_slice_in_dim(gain_grads, me * wide_cols, wide_cols, 1)
    ones = jnp.ones_like(one)
    slope = jnp.stack([ones, 1.0 - gates[:, 1] ** 2, ones, 1.0 - gates[:, 3] ** 2], 1)
    d_mod = lax.dynamic_slice_in_dim(slope * norm_gains[None] * cols, mz * ada, ada, 2)
    at_slot = (firsts[None, :] == blocks[:, None]).astype(f32)
    d_slots = jnp.sum(at_slot[:, :, None, None] * d_mod[None], 1).astype(bf16).astype(f32)
    cond_rows = cd // count
    silu_mine = lax.dynamic_slice_in_dim(jax.nn.silu(conds).astype(bf16).astype(f32), me * cond_rows, cond_rows, 1)
    grad_ada = jnp.sum(silu_mine[:, :, None, None] * d_slots[:, None], 0)
    d_mine = lax.dynamic_index_in_dim(d_slots, me, 0, False)
    cond_part = jnp.sum(d_mine[None] * w_ada.astype(f32), (1, 2))
    cond_total = jnp.sum(gather_small(cond_part, "narrow"), 0)
    pull_silu = jax.vjp(jax.nn.silu, cond)[1]
    grad_conditioning = pull_silu(cond_total)[0].reshape(1, -1)

    rows = d // count
    return (
        output,
        grad_patches,
        grad_conditioning,
        grad_captions,
        grad_ada,
        grad_norm_gains,
        g_attn[:, : 3 * n].astype(f32).reshape(rows, 3, n).transpose(1, 0, 2),
        grad_head_gains,
        grad_cross_gate,
        g_cap.astype(f32).reshape(-1, 2, n).transpose(1, 0, 2),
        g_attn[:, 3 * n :].astype(f32).T,
        g_mlp[:, : 2 * ff].astype(f32).reshape(rows, 2, ff).transpose(1, 0, 2),
        g_mlp[:, 2 * ff :].astype(f32).T,
    )


def solution(mesh):
    placed = (
        P("wide", None),
        P("wide", None),
        P("wide", None),
        P("wide", None),
        P(),
        P(),
        P(None, None, "narrow"),
        P(),
        P(None, None, "narrow"),
        P(),
        P("narrow"),
        P(None, None, "narrow"),
        P("narrow", None),
        P(None, None, "narrow"),
        P("narrow", None),
    )
    return jax.shard_map(
        local,
        mesh=mesh,
        in_specs=placed,
        out_specs=(
            P("wide", None),
            P("wide", None),
            P("wide", None),
            P("wide", None),
            P("wide", None, "narrow"),
            P(None, "wide"),
            P(None, "wide", "narrow"),
            P(),
            P(),
            P(None, "wide", "narrow"),
            P("narrow", "wide"),
            P(None, "wide", "narrow"),
            P("narrow", "wide"),
        ),
        check_vma=False,
    )
```

```python
import functools

import jax
import jax.numpy as jnp
from jax import lax
from jax.experimental import pallas as pl
from jax.experimental.pallas import tpu as pltpu
from jax.sharding import PartitionSpec as P

HD = 64
SPAN = 4
EPS = 1e-05
LOG2E = 1.4426950408889634
f32 = jnp.float32
bf16 = jnp.bfloat16
VMEM = 56 * 1024 * 1024
BR = 256
NT = (((1,), (1,)), ((), ()))
TN = (((0,), (0,)), ((), ()))


def params(n):
    return pltpu.CompilerParams(
        dimension_semantics=("arbitrary",) * n, vmem_limit_bytes=VMEM
    )


def sds(shape, dtype):
    return jax.ShapeDtypeStruct(shape, dtype)


COST = {
    "key": 8, "query": 9, "caption_norm": 2, "pick": 5, "attend": 18, "hop": 3, "ffn": 9, "ffn_back": 10, "out_back": 6,
    "pair_grad": 10, "caption_back": 6, "dq": 27, "dkv": 24, "dqkv": 7, "caption_grad": 3, "last": 3, "note": 1, "pin": 1,
}


class Order:
    def __init__(self):
        self.token = ()

    def run(self, name, kernel, grid, ins, in_specs, out_specs, out_shape, scratch=(), scalar=None, held=(), first_held=0, after=()):
        pre = 0 if scalar is None else 1
        given = pre + len(ins)
        extra = [*self.token, *after, *held]

        def body(*refs):
            kernel(*refs[:given], *refs[given + len(extra) :])

        at = given + len(extra) - len(held)
        out = pl.pallas_call(
            body,
            grid_spec=pltpu.PrefetchScalarGridSpec(
                num_scalar_prefetch=pre,
                grid=grid,
                in_specs=list(in_specs) + loose(len(extra)),
                out_specs=out_specs,
                scratch_shapes=list(scratch),
            ),
            out_shape=out_shape,
            input_output_aliases={at + k: first_held + k for k in range(len(held))},
            compiler_params=params(len(grid)),
            cost_estimate=pl.CostEstimate(
                flops=COST[name] * 250_000_000, bytes_accessed=COST[name] * 750_000, transcendentals=0
            ),
            name=name,
        )(*(() if scalar is None else (scalar,)), *ins, *extra)
        self.token = (out[0],)
        return out


def loose(n):
    return [pl.BlockSpec(memory_space=pl.ANY)] * n


def mm(a, b):
    return jnp.dot(a, b, preferred_element_type=f32)


def mm_nt(a, b):
    return lax.dot_general(a, b, NT, preferred_element_type=f32)


def mm_tn(a, b):
    return lax.dot_general(a, b, TN, preferred_element_type=f32)


def split(x):
    hi = x.astype(bf16)
    return hi, (x - hi.astype(f32)).astype(bf16)


def head_sum(x, ones):
    hi, lo = split(x)
    return mm(hi, ones) + mm(lo, ones)


def head_ones(n):
    a = lax.broadcasted_iota(jnp.int32, (n, n), 0) // HD
    b = lax.broadcasted_iota(jnp.int32, (n, n), 1) // HD
    return (a == b).astype(bf16)


def halves(n):
    lane = lax.broadcasted_iota(jnp.int32, (1, n), 1)
    return (lane < HD, lane >= HD)


def keep(x, mask):
    return jnp.where(mask, x, jnp.zeros_like(x))


def inv_rms(x):
    return lax.rsqrt(jnp.mean(x * x, -1, keepdims=True) + EPS)


def row(ref, k):
    return ref[k : k + 1, :]


def whole(shape):
    zeros = (0,) * len(shape)
    return pl.BlockSpec(shape, lambda *_: zeros, pipeline_mode=pl.Buffered(1))


def rows_of(br, width, first=0):
    return pl.BlockSpec((br, width), lambda i, *_: (i, first))


def accumulate(ref, value, first):
    @pl.when(first)
    def _():
        ref[...] = value

    @pl.when(jnp.logical_not(first))
    def _():
        ref[...] += value


def col_sum(x):
    return jnp.sum(x, 0, keepdims=True)


def tile3(t, n):
    return jnp.concatenate([t] * (n // t.shape[1]), 1)


def key_kernel(p_ref, v_ref, w_ref, wv_ref, c_ref, s1_ref, s2_ref, hg_ref, a_ref, kr_ref, k_ref, vv_ref):
    x = p_ref[...].astype(f32)
    a = (x * inv_rms(x) * row(v_ref, 0)).astype(bf16)
    a_ref[...] = a
    k = mm(a, w_ref[0])
    kr_ref[...] = k
    k_ref[...] = turned(k, row(hg_ref, 1), (c_ref, s1_ref, s2_ref)).astype(bf16)
    vv_ref[...] = mm(a, wv_ref[0]).astype(bf16)


def turned(y, gain, tabs):
    n = y.shape[1]
    cos, s1, s2 = (tile3(t[...], n) for t in tabs)
    z = y * lax.rsqrt(head_sum(y * y, head_ones(n)) * (1.0 / HD) + EPS) * gain
    return z * cos + pltpu.roll(z, n - 16, 1) * s1 + pltpu.roll(z, 16, 1) * s2


def query_kernel(a_ref, wq_ref, c_ref, s1_ref, s2_ref, hg_ref, qr_ref, q_ref):
    q = mm(a_ref[...], wq_ref[0])
    qr_ref[...] = q
    q_ref[...] = (turned(q, row(hg_ref, 0), (c_ref, s1_ref, s2_ref)) * (0.125 * LOG2E)).astype(bf16)


def one_weight(w, k):
    return pl.BlockSpec((1, *w.shape[1:]), lambda *_: (k, 0, 0), pipeline_mode=pl.Buffered(1))


def key_call(order, patches, vec, w, tabs, hg, after, br=256):
    t, d = patches.shape
    n = w.shape[2]
    return order.run(
        "key",
        key_kernel,
        (t // br,),
        (patches, vec, w, w, *tabs, hg),
        [rows_of(br, d), whole(vec.shape), one_weight(w, 1), one_weight(w, 2)] + [rows_of(br, 128)] * 3 + [whole(hg.shape)],
        [rows_of(br, d)] + [rows_of(br, n)] * 3,
        [sds((t, d), bf16), sds((t, n), f32), sds((t, n), bf16), sds((t, n), bf16)],
        after=after,
    )


def query_call(order, a, w, tabs, hg, after, br=256):
    t, d = a.shape
    n = w.shape[2]
    return order.run(
        "query",
        query_kernel,
        (t // br,),
        (a, w, *tabs, hg),
        [rows_of(br, d), one_weight(w, 0)] + [rows_of(br, 128)] * 3 + [whole(hg.shape)],
        [rows_of(br, n)] * 2,
        [sds((t, n), f32), sds((t, n), bf16)],
        after=after,
    )


def soft_sums(q, k, v, mask):
    e = jnp.exp2(mm_nt(q, keep(k, mask))).astype(bf16)
    return mm(e, jnp.where(mask, v, jnp.ones_like(v)))


def item_block(j, s):
    return jnp.minimum(j, s[0] - 1)


def attend_kernel(sc, q_ref, k_ref, v_ref, ck_ref, cv_ref, tg_ref, mix_ref, o_ref, li_ref, acc):
    j = pl.program_id(1)
    masks = halves(128)
    keys = 512

    @pl.when(j == 0)
    def _():
        acc[...] = jnp.zeros_like(acc)

    @pl.when(j < sc[0])
    def _():
        q = q_ref[...]
        for h in range(2):
            total = acc[h]
            for c in range(k_ref.shape[0] // keys):
                at = slice(c * keys, (c + 1) * keys)
                total = total + soft_sums(q, k_ref[at, :], v_ref[at, :], masks[h])
            acc[h] = total

    @pl.when(j == SPAN - 1)
    def _():
        q = q_ref[...]

        def finish(a0, a1):
            inverse = 1.0 / jnp.where(masks[0], pltpu.roll(a0, HD, 1), pltpu.roll(a1, HD, 1))
            return jnp.where(masks[0], a0, a1) * inverse, inverse

        o, li = finish(acc[0], acc[1])
        c0, c1 = (soft_sums(q, ck_ref[...], cv_ref[...], m) for m in masks)
        mix_ref[...] = (o + tg_ref[...] * finish(c0, c1)[0]).astype(bf16)
        o_ref[...] = o.astype(bf16)
        li_ref[...] = li


def attend_call(order, sc, q, k, v, cap, tg, at, bq):
    n = q.shape[1]
    pairs = n // 128
    block = k.shape[0] // SPAN
    text = cap.shape[0]
    mine = lambda p, j, s: (0, p)
    other = lambda p, j, s: (item_block(j, s), p)
    return order.run(
        "attend",
        attend_kernel,
        (pairs, SPAN),
        (q, k, v, cap, cap, tg),
        [
            pl.BlockSpec((bq, 128), lambda p, j, s: (at, p)),
            pl.BlockSpec((block, 128), other),
            pl.BlockSpec((block, 128), other),
            pl.BlockSpec((text, 128), mine),
            pl.BlockSpec((text, 128), lambda p, j, s: (0, pairs + p)),
            pl.BlockSpec((1, 128), mine),
        ],
        [pl.BlockSpec((bq, 128), mine)] * 3,
        [sds((bq, n), bf16), sds((bq, n), bf16), sds((bq, n), f32)],
        [pltpu.VMEM((2, bq, 128), f32)],
        sc,
    )


def caption_back_kernel(q_ref, da_ref, db_ref, ck_ref, cv_ref, tg_ref, dq_ref, dk_ref, dv_ref, gs_ref):
    masks = halves(128)
    q, d = q_ref[...], jnp.concatenate([da_ref[...], db_ref[...]], 0)
    dq = jnp.zeros(q.shape, f32)
    dk = jnp.zeros(ck_ref.shape, f32)
    dv = jnp.zeros(ck_ref.shape, f32)
    sums = []
    for h in range(2):
        ck, cv = keep(ck_ref[...], masks[h]), keep(cv_ref[...], masks[h])
        gate = tg_ref[:, h * HD : h * HD + 1]
        e = jnp.exp2(mm_nt(q, ck))
        prob = e * (1.0 / jnp.sum(e, -1, keepdims=True))
        dp = mm_nt(d, cv)
        m = jnp.sum(prob * dp, -1, keepdims=True)
        dc = (prob * (dp - m) * gate).astype(bf16)
        dq = dq + mm(dc, ck)
        dk = dk + mm_tn(dc, keep(q, masks[h]))
        dv = dv + mm_tn(prob.astype(bf16), keep(d, masks[h]))
        sums.append(jnp.sum(m, 0, keepdims=True))
    dq_ref[...] = dq * 0.125
    dk_ref[...] = dk * (1.0 / LOG2E)
    dv_ref[...] = dv * tg_ref[...]
    gs_ref[...] = jnp.where(masks[0], sums[0], sums[1])


def caption_back_call(order, q, da, db, cap, tg, h):
    n = q.shape[1]
    pairs = n // 128
    bq = 2 * BR
    text = cap.shape[0]
    mine = lambda p: (0, p)
    return order.run(
        "caption_back",
        caption_back_kernel,
        (pairs,),
        (q, da, db, cap, cap, tg),
        [
            pl.BlockSpec((bq, 128), lambda p: (h, p)),
            pl.BlockSpec((BR, 128), mine),
            pl.BlockSpec((BR, 128), mine),
            pl.BlockSpec((text, 128), mine),
            pl.BlockSpec((text, 128), lambda p: (0, pairs + p)),
            pl.BlockSpec((1, 128), mine),
        ],
        [
            pl.BlockSpec((bq, 128), mine),
            pl.BlockSpec((text, 128), mine),
            pl.BlockSpec((text, 128), mine),
            pl.BlockSpec((1, 128), mine),
        ],
        [sds((bq, n), f32), sds((text, n), f32), sds((text, n), f32), sds((1, n), f32)],
    )


def minus_delta(rows, head):
    lane = lax.broadcasted_iota(jnp.int32, (rows, 128), 1)
    return jnp.where((lane >= 3 * head) & (lane < 3 * head + 3), -1.0, 0.0).astype(bf16)


def dq_kernel(sc, q_ref, d_ref, x_ref, k_ref, v_ref, c_ref, dq_ref, acc):
    pair = pl.program_id(0)
    j = pl.program_id(1)
    masks = halves(128)
    keys = 512

    @pl.when(j == 0)
    def _():
        acc[...] = jnp.zeros_like(acc)

    @pl.when(j < sc[0])
    def _():
        q = q_ref[...]
        dx = jnp.concatenate([d_ref[...], x_ref[...]], 1)
        total = acc[...]
        for h in range(2):
            off = minus_delta(keys, 2 * pair + h)
            for c in range(k_ref.shape[0] // keys):
                at = slice(c * keys, (c + 1) * keys)
                k = keep(k_ref[at, :], masks[h])
                e = jnp.exp2(mm_nt(q, k))
                dp = mm_nt(dx, jnp.concatenate([keep(v_ref[at, :], masks[h]), off], 1))
                total = total + mm((e * dp).astype(bf16), k)
        acc[...] = total

    @pl.when(j == SPAN - 1)
    def _():
        dq_ref[...] = acc[...] * 0.125 + c_ref[...]


def dq_call(order, sc, q, d, k, v, cap_dq, h, after=()):
    n = q.shape[1]
    pairs = n // 128
    block = k.shape[0] // SPAN
    bq = 2 * BR
    mine = lambda p, j, s: (0, p)
    extra = lambda p, j, s: (0, pairs)
    other = lambda p, j, s: (item_block(j, s), p)
    return order.run(
        "dq",
        dq_kernel,
        (pairs, SPAN),
        (q, d, d, k, v, cap_dq),
        [
            pl.BlockSpec((bq, 128), lambda p, j, s: (h, p)),
            pl.BlockSpec((bq, 128), mine),
            pl.BlockSpec((bq, 128), extra),
            pl.BlockSpec((block, 128), other),
            pl.BlockSpec((block, 128), other),
            pl.BlockSpec((bq, 128), mine),
        ],
        [pl.BlockSpec((bq, 128), mine)],
        [sds((bq, n), f32)],
        [pltpu.VMEM((bq, 128), f32)],
        sc,
        after=after,
    )[0]


def dkv_kernel(parts, base, sc, k_ref, v_ref, q_ref, *rest):
    d_refs, x_refs = rest[0 : 2 * parts : 2], rest[1 : 2 * parts : 2]
    dk_ref, dv_ref = rest[2 * parts :]
    pair = base + pl.program_id(0)
    j = pl.program_id(1)
    masks = halves(128)
    queries = 2 * BR

    @pl.when(j == 0)
    def _():
        dk_ref[...] = jnp.zeros_like(dk_ref)
        dv_ref[...] = jnp.zeros_like(dv_ref)

    @pl.when(j < sc[0])
    def _():
        dk, dv = dk_ref[...], dv_ref[...]
        for h in range(2):
            vx = jnp.concatenate([keep(v_ref[...], masks[h]), minus_delta(v_ref.shape[0], 2 * pair + h)], 1)
            for r in range(parts):
                q = keep(q_ref[r * queries : (r + 1) * queries, :], masks[h])
                d, x = d_refs[r][...], x_refs[r][...]
                e = jnp.exp2(mm_nt(k_ref[...], q))
                dp = mm_nt(vx, jnp.concatenate([d, x], 1))
                dv = dv + mm(e.astype(bf16), keep(d, masks[h]))
                dk = dk + mm((e * dp).astype(bf16), q)
        dk_ref[...] = dk
        dv_ref[...] = dv


def dkv_call(order, sc, k, v, q_all, ds, half, base, n_pairs):
    t, n = k.shape
    pairs = n // 128
    rows = 2 * BR
    mine = pl.BlockSpec((rows, 128), lambda p, j, s: (half, base + p))
    out = pl.BlockSpec((rows, 128), lambda p, j, s: (0, p))
    other = pl.BlockSpec((rows, 128), lambda p, j, s: (item_block(j, s), base + p))
    extra = pl.BlockSpec((rows, 128), lambda p, j, s: (item_block(j, s), pairs))
    return order.run(
        "dkv",
        functools.partial(dkv_kernel, len(ds), base),
        (n_pairs, SPAN),
        (k, v, q_all, *(x for d in ds for x in (d, d))),
        [mine, mine, pl.BlockSpec((t, 128), lambda p, j, s: (s[1 + SPAN + j], base + p))] + [other, extra] * len(ds),
        [out, out],
        [sds((rows, n_pairs * 128), f32)] * 2,
        scalar=sc,
    )


def chunk_call(order, kernel, name, c, ins, specs, chunk_outs, sum_outs, whole_outs, before):
    one = lambda r, w: pl.BlockSpec((r, w), lambda i: (0, 0))
    own = chunk_outs + sum_outs
    into = [pl.BlockSpec((BR, w), lambda i, at=c % (r // BR): (at, 0)) for r, w, _ in whole_outs]
    return order.run(
        name,
        kernel,
        (1,),
        ins,
        specs,
        [one(r, w) for r, w, _ in own] + into,
        [sds((r, w), k) for r, w, k in own + whole_outs],
        held=tuple(before),
        first_held=len(own),
    )


def part(c, width):
    return pl.BlockSpec((BR, width), lambda i: (c, 0))


def alone(width):
    return pl.BlockSpec((BR, width), lambda i: (0, 0))


def pair_grad_kernel(a_ref, b_ref, c_ref, d_ref, o_ref):
    n = b_ref.shape[1]
    o_ref[:, :n] = mm_tn(a_ref[...], b_ref[...]).astype(bf16)
    o_ref[:, n:] = mm_tn(c_ref[...], d_ref[...]).astype(bf16)


def pair_grad_call(order, a, b, c, d, part=0, parts=1, before=(), after=()):
    t, m = a.shape
    n, k = b.shape[1], d.shape[1]
    blk = 256
    steps = m // blk // parts
    cols = pl.BlockSpec((t, blk), lambda i: (0, part * steps + i))
    return order.run(
        "pair_grad",
        pair_grad_kernel,
        (steps,),
        (a, b, c, d),
        [cols, whole(b.shape), cols, whole(d.shape)],
        [pl.BlockSpec((blk, n + k), lambda i: (part * steps + i, 0))],
        [sds((m, n + k), bf16)],
        held=before,
        after=after,
    )


def ffn_kernel(p_ref, at_ref, v_ref, wg_ref, wd_ref, mid_ref, gu_ref, f_ref, a_ref, h_ref):
    at = at_ref[...].astype(f32)
    mid = p_ref[...].astype(f32) + row(v_ref, 1) * (at * inv_rms(at))
    mid_ref[...] = mid
    a = (mid * inv_rms(mid) * row(v_ref, 2)).astype(bf16)
    a_ref[...] = a
    g = mm(a, wg_ref[0])
    u = mm(a, wg_ref[1])
    n = g.shape[1]
    gu_ref[:, :n] = g.astype(bf16)
    gu_ref[:, n:] = u.astype(bf16)
    h = (g * jax.nn.sigmoid(g) * u).astype(bf16)
    h_ref[...] = h
    f_ref[...] = mm(h, wd_ref[...]).astype(bf16)


def ffn_call(order, c, patches, at, vec, wg, wd, before):
    t, d = patches.shape
    n = wd.shape[0]
    return chunk_call(
        order,
        ffn_kernel,
        "ffn",
        c,
        (patches, at, vec, wg, wd),
        [part(c, d), alone(d), whole(vec.shape), whole(wg.shape), whole(wd.shape)],
        [(BR, d, f32), (BR, 2 * n, bf16), (BR, d, bf16)],
        [],
        [(t, d, bf16), (t, n, bf16)],
        before,
    )


def ffn_back_kernel(f_ref, mid_ref, c_ref, gu_ref, v_ref, wg_ref, wd_ref, da_ref, cs_ref, y_ref, df_ref, dgu_ref):
    f = f_ref[...].astype(f32)
    cot = c_ref[...].astype(f32)
    r = inv_rms(f)
    fh = f * r
    y_ref[...] = (mid_ref[...] + row(v_ref, 3) * fh).astype(bf16)
    z = cot * row(v_ref, 3)
    df = (r * (z - fh * jnp.mean(z * fh, -1, keepdims=True))).astype(bf16)
    df_ref[...] = df
    cs_ref[...] = col_sum(cot * fh)
    dh = mm_nt(df, wd_ref[...])
    n = dh.shape[1]
    g = gu_ref[:, :n].astype(f32)
    u = gu_ref[:, n:].astype(f32)
    s = jax.nn.sigmoid(g)
    gs = g * s
    dg = (dh * u * (s + gs * (1.0 - s))).astype(bf16)
    du = (dh * gs).astype(bf16)
    dgu_ref[:, :n] = dg
    dgu_ref[:, n:] = du
    da_ref[...] = (mm_nt(dg, wg_ref[0]) + mm_nt(du, wg_ref[1])).astype(bf16)


def ffn_back_call(order, c, f, mid, cot, gu, vec, wg, wd, before):
    t, d = cot.shape
    n = wd.shape[0]
    return chunk_call(
        order,
        ffn_back_kernel,
        "ffn_back",
        c,
        (f, mid, cot, gu, vec, wg, wd),
        [alone(d), alone(d), part(c, d), alone(2 * n), whole(vec.shape), whole(wg.shape), whole(wd.shape)],
        [(BR, d, bf16)],
        [(1, d, f32)],
        [(t, d, bf16), (t, d, bf16), (t, 2 * n, bf16)],
        before,
    )


def out_back_kernel(da_ref, mid_ref, at_ref, c_ref, v_ref, w_ref, o_ref, li_ref, dm_ref, dx_ref, c3_ref, c2_ref, dat_ref, ds_ref):
    da = da_ref[...].astype(f32)
    mid = mid_ref[...]
    r = inv_rms(mid)
    mh = mid * r
    z = da * row(v_ref, 2)
    dm = c_ref[...].astype(f32) + r * (z - mh * jnp.mean(z * mh, -1, keepdims=True))
    dm_ref[...] = dm
    c3_ref[...] = col_sum(da * mh)
    at = at_ref[...].astype(f32)
    ra = inv_rms(at)
    ah = at * ra
    c2_ref[...] = col_sum(dm * ah)
    z = dm * row(v_ref, 1)
    dat = (ra * (z - ah * jnp.mean(z * ah, -1, keepdims=True))).astype(bf16)
    dat_ref[...] = dat
    dx = mm_nt(dat, w_ref[...]).astype(bf16)
    dx_ref[...] = dx
    n = dx.shape[1]
    ds = dx.astype(f32) * li_ref[...]
    ds_ref[:, :n] = ds.astype(bf16)
    hi, lo = split(ds * o_ref[...].astype(f32))
    head = lax.broadcasted_iota(jnp.int32, (n, 128), 0) // HD
    lane = lax.broadcasted_iota(jnp.int32, (n, 128), 1)
    to_lanes = (lane // 3 == head).astype(bf16)
    delta = mm(hi, to_lanes) + mm(lo, to_lanes)
    one = delta.astype(bf16).astype(f32)
    two = (delta - one).astype(bf16).astype(f32)
    which = lax.broadcasted_iota(jnp.int32, (1, 128), 1) % 3
    ds_ref[:, n:] = jnp.where(which == 0, one, jnp.where(which == 1, two, delta - one - two)).astype(bf16)


def out_back_call(order, c, da, mid, at, cot, vec, w, o, li, place, before):
    t, d = cot.shape
    n = w.shape[0]
    return chunk_call(
        order,
        out_back_kernel,
        "out_back",
        c,
        (da, mid, at, cot, vec, w, o, li),
        [alone(d), alone(d), alone(d), part(c, d), whole(vec.shape), whole(w.shape), part(place, n), part(place, n)],
        [(BR, d, f32), (BR, n, bf16)],
        [(1, d, f32), (1, d, f32)],
        [(t, d, bf16), (2 * BR, n + 128, bf16)],
        before,
    )


def dqkv_kernel(pairs, dq_ref, *refs):
    dk_refs, dv_refs = refs[0 : 2 * pairs : 2], refs[1 : 2 * pairs : 2]
    (qr_ref, kr_ref, c_ref, s1_ref, s2_ref, hg_ref, w_ref, p_ref, da_ref, hs_ref, cs_ref, d_ref) = refs[2 * pairs :]
    side = lambda parts: jnp.concatenate([x[...] for x in parts], 1)
    n = dq_ref.shape[1]
    ones = head_ones(n)
    cos, s1, s2 = (tile3(t[...], n) for t in (c_ref, s1_ref, s2_ref))

    def back(dy, x, gain):
        dz = dy * cos - pltpu.roll(dy, 16, 1) * s2 - pltpu.roll(dy, n - 16, 1) * s1
        r = lax.rsqrt(head_sum(x * x, ones) * (1.0 / HD) + EPS)
        xh = x * r
        g = dz * gain
        return r * (g - xh * (head_sum(g * xh, ones) * (1.0 / HD))), col_sum(dz * xh)

    dq, hq = back(dq_ref[...], qr_ref[...], row(hg_ref, 0))
    dk, hk = back(side(dk_refs) * (1.0 / LOG2E), kr_ref[...], row(hg_ref, 1))
    dql, dkl, dvl = dq.astype(bf16), dk.astype(bf16), side(dv_refs).astype(bf16)
    d_ref[:, :n] = dql
    d_ref[:, n : 2 * n] = dkl
    d_ref[:, 2 * n :] = dvl
    da = mm_nt(dql, w_ref[0]) + mm_nt(dkl, w_ref[1]) + mm_nt(dvl, w_ref[2])
    da_ref[...] = da.astype(bf16)
    x = p_ref[...].astype(f32)
    cs_ref[...] = col_sum(da * (x * inv_rms(x)))
    hs_ref[0:1, :] = hq
    hs_ref[1:2, :] = hk


def dqkv_call(order, c, dq, dkv, qr, kr, tabs, hg, w, patches, before):
    t, d = patches.shape
    n = dq.shape[1]
    return chunk_call(
        order,
        functools.partial(dqkv_kernel, len(dkv)),
        "dqkv",
        c,
        (dq, *(x for two in dkv for x in two), qr, kr, *tabs, hg, w, patches),
        [part(c % 2, n)] + [part(c % 2, x.shape[1]) for two in dkv for x in two] + [part(c, n)] * 2 + [part(c, 128)] * 3 + [whole(hg.shape), whole(w.shape), part(c, d)],
        [(BR, d, bf16)],
        [(2, n, f32), (1, d, f32)],
        [(t, 3 * n, bf16)],
        before,
    )


def last_kernel(da_ref, p_ref, dm_ref, v_ref, o_ref):
    x = p_ref[...].astype(f32)
    r = inv_rms(x)
    xh = x * r
    z = da_ref[...].astype(f32) * row(v_ref, 0)
    o_ref[...] = (dm_ref[...] + r * (z - xh * jnp.mean(z * xh, -1, keepdims=True))).astype(bf16)


def last_call(order, c, da, patches, dm, vec, before):
    t, d = patches.shape
    return chunk_call(
        order,
        last_kernel,
        "last",
        c,
        (da, patches, dm, vec),
        [alone(d), part(c, d), alone(d), whole(vec.shape)],
        [],
        [],
        [(t, d, bf16)],
        before,
    )


def caption_grad_kernel(dk_ref, dv_ref, kr_ref, hg_ref, d_ref, hs_ref):
    n = dk_ref.shape[1]
    ones = head_ones(n)
    x = kr_ref[...]
    r = lax.rsqrt(head_sum(x * x, ones) * (1.0 / HD) + EPS)
    xh = x * r
    dy = dk_ref[...]
    g = dy * row(hg_ref, 2)
    d_ref[:, :n] = (r * (g - xh * (head_sum(g * xh, ones) * (1.0 / HD)))).astype(bf16)
    d_ref[:, n:] = dv_ref[...].astype(bf16)
    hs_ref[...] = col_sum(dy * xh)


def caption_norm_kernel(kr_ref, v_ref, hg_ref, o_ref):
    n = kr_ref.shape[1]
    x = kr_ref[...]
    r = lax.rsqrt(head_sum(x * x, head_ones(n)) * (1.0 / HD) + EPS)
    o_ref[:, :n] = (x * r * row(hg_ref, 2)).astype(bf16)
    o_ref[:, n:] = v_ref[...].astype(bf16)


def swap(x, axis, size, m):
    return lax.ppermute(x, axis, [(i, i ^ m) for i in range(size)])


def pick_kernel(count, n_arrays, n_pieces, sc, *refs):
    outs, sem = refs[n_arrays * n_pieces :][:n_arrays], refs[-1]
    for k, out in enumerate(outs):
        pieces = refs[k * n_pieces : (k + 1) * n_pieces]
        rows = pieces[0].shape[0]
        for j in range(count):
            for m in range(n_pieces):

                @pl.when(sc[1 + j] == m)
                def _():
                    pltpu.make_async_copy(pieces[m], out.at[pl.ds(j * rows, rows)], sem.at[k, j]).start()

    for k, out in enumerate(outs):
        first = refs[k * n_pieces]
        rows = first.shape[0]
        for j in range(count):
            pltpu.make_async_copy(first, out.at[pl.ds(j * rows, rows)], sem.at[k, j]).wait()


class Gather:
    def __init__(self, a, b):
        self.all = None
        if lax.axis_size("wide") != 8:
            self.first = self.second = ()
            self.all = [lax.all_gather(x, "wide") for x in (a, b)]
            return
        send = lambda x, pairs: lax.ppermute(x, "wide", pairs)
        over_x = [(i, i ^ 2) for i in range(8)]
        over_y = [(1, 5), (4, 0), (3, 7), (6, 2)]
        a2, a4, b4, b2 = send(a, over_x), send(a, over_y), send(b, over_y), send(b, over_x)
        a6 = send(a2, [(0, 4), (1, 5), (6, 2), (7, 3)])
        b6x, b6y = send(b2, [(0, 4), (7, 3)]), send(b4, [(7, 5), (0, 2)])
        self.first = (a2, a4, b4, b2)
        self.second = (a6, b6x, b6y)
        self.kept = ((a, a2, a4, a6), (b, b2, b4, b6x + b6y))

    def pieces(self):
        if self.all is not None:
            return self.all
        return [[y for x in four for y in (x, swap(x, "wide", 8, 1))] for four in self.kept]


class GatherOne:
    def __init__(self, a):
        self.all = None
        if lax.axis_size("wide") != 8:
            self.first = self.second = ()
            self.all = [lax.all_gather(a, "wide")]
            return
        send = lambda x, pairs: lax.ppermute(x, "wide", pairs)
        a2 = send(a, [(i, i ^ 2) for i in range(8)])
        a4 = send(a, [(1, 5), (4, 0), (3, 7), (6, 2)])
        a6 = send(a2, [(0, 4), (1, 5), (6, 2), (7, 3)])
        self.first, self.second = (a2, a4), (a6,)
        self.kept = ((a, a2, a4, a6),)

    pieces = Gather.pieces


def shift(x, by):
    size = lax.axis_size("wide")
    return lax.ppermute(x, "wide", [(i, i + by) for i in range(size) if 0 <= i + by < size])


def pick(order, sc, pieces, count):
    if not isinstance(pieces[0], list):
        one = lambda x, j: lax.dynamic_index_in_dim(x, sc[1 + SPAN + j], 0, False)
        return [jnp.concatenate([one(x, j) for j in range(count)]) for x in pieces]
    outs = [(count * p[0].shape[0], p[0].shape[1]) for p in pieces]
    return order.run(
        "pick",
        functools.partial(pick_kernel, count, len(pieces), 8),
        (1,),
        [x for p in pieces for x in p],
        loose(8 * len(pieces)),
        [pl.BlockSpec(shape, lambda i, s: (0, 0)) for shape in outs],
        [sds(shape, bf16) for shape in outs],
        [pltpu.SemaphoreType.DMA((len(pieces), count))],
        sc,
    )


def pin_kernel(o_ref):
    pass


def pin(order, x):
    return order.run("pin", pin_kernel, (1,), (), [], loose(1), [sds(x.shape, x.dtype)], held=(x,))[0]


def note_kernel(x_ref, o_ref):
    o_ref[...] = x_ref[...]


def note(order, x):
    n = x.shape[0]
    size = -(-n // 1024) * 8
    x = jnp.pad(x, (0, size * 128 - n)).reshape(size, 128)
    spec = pl.BlockSpec(x.shape, lambda i: (0, 0))
    return order.run("note", note_kernel, (1,), (x,), [spec], [spec], [sds(x.shape, f32)])[0].reshape(-1)[:n]


def gather_small(x, axis):
    n = x.shape[0]
    wide = -(-n // 1024) * 1024
    x = jnp.pad(x, (0, wide - n)).reshape(wide // 128, 128)
    size = lax.axis_size(axis)
    if size > 8:
        return lax.all_gather(x, axis).reshape(size, wide)[:, :n]
    got = jnp.stack([x] + [swap(x, axis, size, m) for m in range(1, size)])
    order = jnp.arange(size, dtype=jnp.int32)
    mine = (order[:, None] ^ lax.axis_index(axis)) == order[None, :]
    out = jnp.sum(jnp.where(mine[:, :, None, None], got[None], 0.0), 1)
    return out.reshape(size, wide)[:, :n]


def gather_now(x, axis):
    n = x.shape[0]
    wide = -(-n // 1024) * 1024
    padded = jnp.pad(x, (0, wide - n)).reshape(1, 8, wide // 8)
    return lax.all_gather(padded, axis, axis=0, tiled=True).reshape(-1, wide)[:, :n]


def hop_kernel(have, sc, *refs):
    ins = dict(zip(have["in"], refs))
    outs = dict(zip(have["out"], refs[len(have["in"]) :]))
    end = sc[0] == 1
    if "total" in outs:
        outs["total"][...] = jnp.where(end, ins["r1"][...], ins["send"][...])
    third = None
    if "second" in ins:
        third = ins["second"][...] + ins["r2"][...]
    if "second" in outs:
        outs["second"][...] = ins["x"][...] + ins["r1"][...]
    if "send" in outs:
        new = ins["new"][...] if "new" in ins else third
        outs["send"][...] = new if third is None else jnp.where(end, new, third)


class Line:
    def __init__(self, order, place):
        self.order = order
        self.end = ((place == 0) | (place == 3)).astype(jnp.int32).reshape(1)
        self.x = self.second = self.send = None
        self.third = False

    def step(self, new, after=()):
        if self.send is None:
            self.x = self.send = new
            return None
        go = lambda x, perm: lax.ppermute(x, "narrow", perm)
        ins = {"r1": go(self.send, [(0, 1), (3, 2), (1, 0), (2, 3)])}
        outs = []
        if self.third:
            ins["send"] = self.send
            outs.append("total")
        if self.second is not None:
            ins["r2"] = go(self.second, [(1, 2), (2, 1)])
            ins["second"] = self.second
        if self.x is not None:
            ins["x"] = self.x
            outs.append("second")
        if new is not None:
            ins["new"] = new
        if new is not None or self.second is not None:
            outs.append("send")
        like = ins["r1"]
        block = pl.BlockSpec((BR // 2, like.shape[1]), lambda i, s: (i, 0))
        got = self.order.run(
            "hop",
            functools.partial(hop_kernel, {"in": list(ins), "out": outs}),
            (2,),
            list(ins.values()),
            [block] * len(ins),
            [block] * len(outs),
            [sds(like.shape, like.dtype)] * len(outs),
            scalar=self.end,
            after=after,
        )
        got = dict(zip(outs, got))
        self.third = self.second is not None
        self.x, self.second, self.send = new, got.get("second"), got.get("send")
        return got.get("total")


class Sums:
    def __init__(self, order, size, place):
        self.line = Line(order, place) if size == 4 else None
        self.names, self.done = [], {}

    def add(self, name, x, after=()):
        if self.line is None:
            self.done[name] = lax.psum(x, "narrow")
            return
        if self.line.send is None:
            self.names = [None]
        self._step(name, x, after)

    def _step(self, name, x, after):
        total = self.line.step(x, after)
        self.names.append(name)
        if total is not None:
            self.done[self.names[-4]] = total

    def get(self, name, after=()):
        while name not in self.done:
            self._step(None, None, after)
            after = ()
        return self.done[name]


def scatter_rows(x):
    return lax.psum_scatter(x.astype(bf16), "wide", scatter_dimension=0, tiled=True)


def rope_tables(position, width):
    lane = jnp.arange(128, dtype=jnp.int32)
    within = lane % HD
    quarter = HD // 4
    frequency = 10000.0 ** (-(within % quarter).astype(f32) / quarter)
    by_row = within < HD // 2
    where = jnp.where(by_row[None, :], (position // width)[:, None], (position % width)[:, None])
    angle = where.astype(f32) * frequency[None, :]
    cos, sin = jnp.cos(angle), jnp.sin(angle)
    former = (within % (HD // 2) < quarter)[None, :]
    return cos, jnp.where(former, -sin, 0.0), jnp.where(former, 0.0, sin)


def local(
    patches,
    cotangent,
    conditioning,
    captions,
    item_lengths,
    grid_widths,
    w_ada,
    norm_gains,
    w_qkv,
    head_gains,
    cross_gate,
    w_caption,
    w_out,
    w_gate_up,
    w_down,
):
    t, d = patches.shape
    n = w_qkv.shape[2]
    heads = n // HD
    ada = w_ada.shape[2]
    ff = w_down.shape[0]
    text = captions.shape[0]
    cd = conditioning.shape[1]
    count = lax.axis_size("wide")
    deep = lax.axis_size("narrow")
    me = lax.axis_index("wide")
    mz = lax.axis_index("narrow")

    slots = item_lengths.shape[0]
    spans = item_lengths // t
    order = jnp.arange(slots, dtype=jnp.int32)
    ends = jnp.sum(jnp.where(order[None, :] <= order[:, None], spans[None, :], 0), 1)
    blocks = jnp.arange(count, dtype=jnp.int32)
    item = jnp.sum((ends[None, :] <= blocks[:, None]).astype(jnp.int32), 1)
    is_item = item[:, None] == order[None, :]
    choose = lambda values: jnp.sum(jnp.where(is_item, values[None, :], 0), 1)
    firsts = choose(ends - spans)
    mine = blocks == me
    of_me = lambda values: jnp.sum(jnp.where(mine, values, 0))
    first = of_me(firsts)
    length = of_me(choose(spans))
    width = of_me(choose(grid_widths))
    position = (me - first) * t + jnp.arange(t, dtype=jnp.int32)
    tabs = rope_tables(position, width)
    steps = first + jnp.minimum(jnp.arange(SPAN, dtype=jnp.int32), length - 1)
    places = steps ^ me if count == 8 else steps
    sc = jnp.concatenate([length.reshape(1), places, steps]).astype(jnp.int32)

    cond = conditioning.astype(f32)[0]
    silu_low = jax.nn.silu(cond).astype(bf16)
    mod = jnp.sum(silu_low.astype(f32)[:, None, None] * w_ada.astype(f32), 0)
    share = cd // deep
    sent = jnp.concatenate([mod.reshape(-1), lax.dynamic_slice_in_dim(cond, mz * share, share)])
    got = gather_now(gather_now(sent, "narrow").reshape(-1), "wide").reshape(count, deep, -1)
    mods = got[:, :, : 4 * ada].reshape(count, deep, 4, ada).transpose(0, 2, 1, 3).reshape(count, 4, d)
    conds = got[:, :, 4 * ada :].reshape(count, cd)
    my_mod = lax.dynamic_index_in_dim(mods, first, 0, False)
    of_block = jnp.sum(jnp.where((firsts[:, None] == blocks[None, :])[:, :, None, None], mods[None], 0.0), 1)
    scales = 1.0 + of_block
    gates = jnp.tanh(of_block)
    factor = jnp.stack([1.0 + my_mod[0], jnp.tanh(my_mod[1]), 1.0 + my_mod[2], jnp.tanh(my_mod[3])])
    vec = norm_gains * factor
    hg = jnp.tile(head_gains, (1, heads))
    tg_heads = jnp.tanh(cross_gate)
    tg = jnp.repeat(tg_heads, HD)[None, :]

    order = Order()
    chunks = range(t // BR)
    pairs_of = range(t // (2 * BR))
    sums = Sums(order, deep, mz)
    cap_raw = jnp.einsum("kd,jde->jke", captions, w_caption, preferred_element_type=f32)
    whole_cap = pl.BlockSpec((text, n), lambda i: (0, 0))
    both_cap = pl.BlockSpec((text, 2 * n), lambda i: (0, 0))
    (cap,) = order.run(
        "caption_norm",
        caption_norm_kernel,
        (1,),
        (cap_raw[0], cap_raw[1], hg),
        [whole_cap, whole_cap, whole(hg.shape)],
        [both_cap],
        [sds((text, 2 * n), bf16)],
    )
    offset = me - first
    own_cap = cap
    got_caps = tuple(shift(own_cap, by) for by in range(1, SPAN))
    for by in range(1, SPAN):
        cap = jnp.where(offset == by, got_caps[by - 1], cap)

    a1, k_raw, k, v = key_call(order, patches, vec, w_qkv, tabs, hg, got_caps)
    kv = Gather(k, v)
    q_raw, q = query_call(order, a1, w_qkv, tabs, hg, kv.first)

    q_all = lax.all_gather(q, "wide", axis=0, tiled=True)
    k_all, v_all = pick(order, sc, kv.pieces(), SPAN)
    heads_out = {}
    for c in chunks[: len(chunks) // 2]:
        heads_out[c] = (*attend_call(order, sc, q, k_all, v_all, cap, tg, c, BR), 0)
        sums.add(("attn", c), mm(heads_out[c][0], w_out).astype(bf16))
    half = (len(chunks) + 1) // 2
    later = attend_call(order, sc, q, k_all, v_all, cap, tg, 1, half * BR)
    for c in chunks[half:]:
        heads_out[c] = (*later, c - half)
        at = (c - half) * BR
        sums.add(("attn", c), mm(later[0][at : at + BR], w_out).astype(bf16))

    mids, gus = {}, {}
    whole_out = ()
    for c in chunks:
        mids[c], gus[c], ffn_part, *whole_out = ffn_call(
            order, c, patches, sums.get(("attn", c)), vec, w_gate_up, w_down, whole_out
        )
        sums.add(("ffn", c), ffn_part)
    a3, hidden = whole_out
    whole_out = ()
    c4 = 0.0
    for c in chunks:
        da3_part, part_sum, *whole_out = ffn_back_call(
            order, c, sums.get(("ffn", c)), mids[c], cotangent, gus[c], vec, w_gate_up, w_down, whole_out
        )
        sums.add(("da3", c), da3_part)
        c4 = c4 + part_sum
    output, d_ffn, d_gu = whole_out

    d_mids, dqs, dq_caps, d_got, d_mixed, d_scaled = {}, {}, {}, {}, {}, {}
    whole_out = ()
    mlp_part = ()
    behind = ()
    c2 = c3 = dck = dcv = gate_sum = 0.0
    for h in pairs_of:
        for c in (2 * h, 2 * h + 1):
            _, o_self, linv, place = heads_out[c]
            if c == 2 * h + 1 and h > 0:
                behind = d_got[h - 1].second
            da3 = sums.get(("da3", c), behind)
            if c == chunks[-1]:
                g_mlp = scatter_rows(pin(order, mlp_part[0]))
            d_mids[c], d_mixed[c], p3, p2, *outs = out_back_call(
                order, c, da3, mids[c], sums.get(("attn", c)), cotangent, vec, w_out, o_self, linv, place, whole_out
            )
            whole_out, d_scaled[h] = (outs if c % 2 == 0 else outs[:1]), outs[1]
            c2, c3 = c2 + p2, c3 + p3
            behind = ()
            if c == 2 * h:
                early = d_got[h - 1].first if h > 0 else ()
                mlp_part = pair_grad_call(order, a3, d_gu, d_ffn, hidden, h, len(pairs_of), mlp_part, early)
        d_got[h] = GatherOne(d_scaled[h])
        dq_caps[h], pk, pv, pg = caption_back_call(order, q, d_mixed[2 * h], d_mixed[2 * h + 1], cap, tg, h)
        dck, dcv, gate_sum = dck + pk, dcv + pv, gate_sum + pg
    d_attn = whole_out[0]
    cap_sum = jnp.concatenate([dck, dcv], 1)
    cap_low = cap_sum.astype(bf16)
    for by in range(1, SPAN):
        cap_sum = cap_sum + jnp.where(by < length, shift(cap_low, -by).astype(f32), 0.0)
    cap_sum = jnp.where(offset == 0, cap_sum, 0.0)
    last_half = pairs_of[-1]

    def make_dq(h, after):
        return dq_call(order, sc, q, d_scaled[h], k_all, v_all, dq_caps[h], h, after)

    for h in pairs_of[:-1]:
        dqs[h] = make_dq(h, ())

    d_cap, hs_c = order.run(
        "caption_grad",
        caption_grad_kernel,
        (1,),
        (cap_sum[:, :n], cap_sum[:, n:], cap_raw[0], hg),
        [whole_cap, whole_cap, whole_cap, whole(hg.shape)],
        [both_cap, pl.BlockSpec((1, n), lambda i: (0, 0))],
        [sds((text, 2 * n), bf16), sds((1, n), f32)],
        after=d_got[last_half].first,
    )
    d_text = (mm_nt(d_cap[:, :n], w_caption[0]) + mm_nt(d_cap[:, n:], w_caption[1])).astype(bf16)
    cap_part = mm_tn(captions, d_cap).astype(bf16)
    pieces = -(-d_text.shape[1] // d)
    padded = jnp.pad(d_text, ((0, 0), (0, pieces * d - d_text.shape[1])))
    text_parts = [padded[:, p * d : (p + 1) * d] for p in range(pieces)]

    sums.add(("text", 0), text_parts[0])
    dqs[last_half] = make_dq(last_half, (*d_got[last_half].second, *text_parts))
    sums.add(("text", 1), text_parts[1], (cap_part,))
    ds = [x for h in pairs_of for x in pick(order, sc, d_got[h].pieces(), SPAN)]
    whole_out = ()
    c1 = hs_qk = 0.0
    mixed = jnp.concatenate([heads_out[c][0] for c in chunks[:half]] + [later[0]])
    pairs = n // 128

    def project(c, dkv, after=()):
        nonlocal whole_out, c1, hs_qk
        da1_part, p_hs, p1, *whole_out = dqkv_call(order, c, dqs[c // 2], dkv, q_raw, k_raw, tabs, hg, w_qkv, patches, whole_out)
        hs_qk, c1 = hs_qk + p_hs, c1 + p1
        return da1_part

    dkv = [dkv_call(order, sc, k, v, q_all, ds, 0, 0, pairs)]
    for p in range(2, pieces):
        sums.add(("text", p), text_parts[p])
    g_cap = scatter_rows(pin(order, cap_part))
    sums.add(("da1", 0), project(0, dkv), (g_mlp,))
    da1_part = project(1, dkv)
    dkv = [dkv_call(order, sc, k, v, q_all, ds, 1, 0, 1)]
    sums.add(("da1", 1), da1_part)
    dkv.append(dkv_call(order, sc, k, v, q_all, ds, 1, 1, pairs - 1))
    for c in chunks[2:]:
        da1_part = project(c, dkv)
        if c == chunks[-1]:
            (d_qkv,) = whole_out
            attn_part = pair_grad_call(order, a1, d_qkv, d_attn, mixed)[0]
        sums.add(("da1", c), da1_part)
    g_attn = scatter_rows(pin(order, attn_part))

    head_part = jnp.concatenate([hs_qk, hs_c]).reshape(3, heads, HD).sum(1)
    gate_part = gate_sum[0, ::HD] * (1.0 - tg_heads * tg_heads)
    got_narrow = gather_small(note(order, jnp.concatenate([c1[0], head_part.reshape(-1), gate_part])), "narrow")
    whole_out = last_call(order, 0, sums.get(("da1", 0)), patches, d_mids[0], vec, ())
    da1 = sums.get(("da1", 1), (g_cap, got_narrow))
    summed = jnp.sum(got_narrow[:, : d + 3 * HD], 0)
    sent = note(order, jnp.concatenate([summed, got_narrow[:, d + 3 * HD :].reshape(-1), c2[0], c3[0], c4[0]]))
    got_wide = gather_small(sent, "wide")
    whole_out = last_call(order, 1, da1, patches, d_mids[1], vec, whole_out)
    da1 = sums.get(("da1", 2), (got_wide,))
    for c in chunks[2:]:
        whole_out = last_call(order, c, da1 if c == 2 else sums.get(("da1", c)), patches, d_mids[c], vec, whole_out)
    (grad_patches,) = whole_out
    grad_captions = jnp.concatenate([sums.get(("text", p)) for p in range(pieces)], 1)[:, : d_text.shape[1]]

    got = got_wide
    one, rest = got[:, :d], got[:, d:]
    grad_head_gains = jnp.sum(rest[:, : 3 * HD], 0).reshape(3, HD)
    grad_cross_gate = jnp.sum(rest[:, 3 * HD : 3 * HD + deep * heads], 0)
    two, three, four = (rest[:, 3 * HD + deep * heads + k * d :][:, :d] for k in range(3))
    cols = jnp.stack([one, two, three, four], 1)
    gain_factor = jnp.stack([scales[:, 0], gates[:, 1], scales[:, 2], gates[:, 3]], 1)
    gain_grads = jnp.sum(gain_factor * cols, 0)
    wide_cols = d // count
    grad_norm_gains = lax.dynamic_slice_in_dim(gain_grads, me * wide_cols, wide_cols, 1)
    ones = jnp.ones_like(one)
    slope = jnp.stack([ones, 1.0 - gates[:, 1] ** 2, ones, 1.0 - gates[:, 3] ** 2], 1)
    d_mod = lax.dynamic_slice_in_dim(slope * norm_gains[None] * cols, mz * ada, ada, 2)
    at_slot = (firsts[None, :] == blocks[:, None]).astype(f32)
    d_slots = jnp.sum(at_slot[:, :, None, None] * d_mod[None], 1).astype(bf16).astype(f32)
    cond_rows = cd // count
    silu_mine = lax.dynamic_slice_in_dim(jax.nn.silu(conds).astype(bf16).astype(f32), me * cond_rows, cond_rows, 1)
    grad_ada = jnp.sum(silu_mine[:, :, None, None] * d_slots[:, None], 0)
    d_mine = lax.dynamic_index_in_dim(d_slots, me, 0, False)
    cond_part = jnp.sum(d_mine[None] * w_ada.astype(f32), (1, 2))
    cond_total = jnp.sum(gather_small(cond_part, "narrow"), 0)
    pull_silu = jax.vjp(jax.nn.silu, cond)[1]
    grad_conditioning = pull_silu(cond_total)[0].reshape(1, -1)

    rows = d // count
    return (
        output,
        grad_patches,
        grad_conditioning,
        grad_captions,
        grad_ada,
        grad_norm_gains,
        g_attn[:, : 3 * n].astype(f32).reshape(rows, 3, n).transpose(1, 0, 2),
        grad_head_gains,
        grad_cross_gate,
        g_cap.astype(f32).reshape(-1, 2, n).transpose(1, 0, 2),
        g_attn[:, 3 * n :].astype(f32).T,
        g_mlp[:, : 2 * ff].astype(f32).reshape(rows, 2, ff).transpose(1, 0, 2),
        g_mlp[:, 2 * ff :].astype(f32).T,
    )


def solution(mesh):
    placed = (
        P("wide", None),
        P("wide", None),
        P("wide", None),
        P("wide", None),
        P(),
        P(),
        P(None, None, "narrow"),
        P(),
        P(None, None, "narrow"),
        P(),
        P("narrow"),
        P(None, None, "narrow"),
        P("narrow", None),
        P(None, None, "narrow"),
        P("narrow", None),
    )
    return jax.shard_map(
        local,
        mesh=mesh,
        in_specs=placed,
        out_specs=(
            P("wide", None),
            P("wide", None),
            P("wide", None),
            P("wide", None),
            P("wide", None, "narrow"),
            P(None, "wide"),
            P(None, "wide", "narrow"),
            P(),
            P(),
            P(None, "wide", "narrow"),
            P("narrow", "wide"),
            P(None, "wide", "narrow"),
            P("narrow", "wide"),
        ),
        check_vma=False,
    )
```

```python
import functools

import jax
import jax.numpy as jnp
from jax import lax
from jax.experimental import pallas as pl
from jax.experimental.pallas import tpu as pltpu
from jax.sharding import PartitionSpec as P

HD = 64
SPAN = 4
EPS = 1e-05
LOG2E = 1.4426950408889634
f32 = jnp.float32
bf16 = jnp.bfloat16
VMEM = 56 * 1024 * 1024
BR = 256
NT = (((1,), (1,)), ((), ()))
TN = (((0,), (0,)), ((), ()))


def params(n):
    return pltpu.CompilerParams(
        dimension_semantics=("arbitrary",) * n, vmem_limit_bytes=VMEM
    )


def sds(shape, dtype):
    return jax.ShapeDtypeStruct(shape, dtype)


COST = {
    "key": 8, "query": 9, "caption_norm": 2, "pick": 5, "attend": 18, "hop": 3, "ffn": 9, "ffn_back": 10, "out_back": 6,
    "pair_grad": 10, "caption_back": 6, "dq": 27, "dkv": 24, "dqkv": 7, "caption_grad": 3, "last": 3, "note": 1, "pin": 1,
}


class Order:
    def __init__(self):
        self.token = ()

    def run(self, name, kernel, grid, ins, in_specs, out_specs, out_shape, scratch=(), scalar=None, held=(), first_held=0, after=()):
        pre = 0 if scalar is None else 1
        given = pre + len(ins)
        extra = [*self.token, *after, *held]

        def body(*refs):
            kernel(*refs[:given], *refs[given + len(extra) :])

        at = given + len(extra) - len(held)
        out = pl.pallas_call(
            body,
            grid_spec=pltpu.PrefetchScalarGridSpec(
                num_scalar_prefetch=pre,
                grid=grid,
                in_specs=list(in_specs) + loose(len(extra)),
                out_specs=out_specs,
                scratch_shapes=list(scratch),
            ),
            out_shape=out_shape,
            input_output_aliases={at + k: first_held + k for k in range(len(held))},
            compiler_params=params(len(grid)),
            cost_estimate=pl.CostEstimate(
                flops=COST[name] * 250_000_000, bytes_accessed=COST[name] * 750_000, transcendentals=0
            ),
            name=name,
        )(*(() if scalar is None else (scalar,)), *ins, *extra)
        self.token = (out[0],)
        return out


def loose(n):
    return [pl.BlockSpec(memory_space=pl.ANY)] * n


def mm(a, b):
    return jnp.dot(a, b, preferred_element_type=f32)


def mm_nt(a, b):
    return lax.dot_general(a, b, NT, preferred_element_type=f32)


def mm_tn(a, b):
    return lax.dot_general(a, b, TN, preferred_element_type=f32)


def split(x):
    hi = x.astype(bf16)
    return hi, (x - hi.astype(f32)).astype(bf16)


def head_sum(x, ones):
    hi, lo = split(x)
    return mm(hi, ones) + mm(lo, ones)


def head_ones(n):
    a = lax.broadcasted_iota(jnp.int32, (n, n), 0) // HD
    b = lax.broadcasted_iota(jnp.int32, (n, n), 1) // HD
    return (a == b).astype(bf16)


def halves(n):
    lane = lax.broadcasted_iota(jnp.int32, (1, n), 1)
    return (lane < HD, lane >= HD)


def keep(x, mask):
    return jnp.where(mask, x, jnp.zeros_like(x))


def inv_rms(x):
    return lax.rsqrt(jnp.mean(x * x, -1, keepdims=True) + EPS)


def row(ref, k):
    return ref[k : k + 1, :]


def whole(shape):
    zeros = (0,) * len(shape)
    return pl.BlockSpec(shape, lambda *_: zeros, pipeline_mode=pl.Buffered(1))


def rows_of(br, width, first=0):
    return pl.BlockSpec((br, width), lambda i, *_: (i, first))


def accumulate(ref, value, first):
    @pl.when(first)
    def _():
        ref[...] = value

    @pl.when(jnp.logical_not(first))
    def _():
        ref[...] += value


def col_sum(x):
    return jnp.sum(x, 0, keepdims=True)


def tile3(t, n):
    return jnp.concatenate([t] * (n // t.shape[1]), 1)


def key_kernel(p_ref, v_ref, w_ref, wv_ref, c_ref, s1_ref, s2_ref, hg_ref, a_ref, kr_ref, k_ref, vv_ref):
    x = p_ref[...].astype(f32)
    a = (x * inv_rms(x) * row(v_ref, 0)).astype(bf16)
    a_ref[...] = a
    k = mm(a, w_ref[0])
    kr_ref[...] = k
    k_ref[...] = turned(k, row(hg_ref, 1), (c_ref, s1_ref, s2_ref)).astype(bf16)
    vv_ref[...] = mm(a, wv_ref[0]).astype(bf16)


def turned(y, gain, tabs):
    n = y.shape[1]
    cos, s1, s2 = (tile3(t[...], n) for t in tabs)
    z = y * lax.rsqrt(head_sum(y * y, head_ones(n)) * (1.0 / HD) + EPS) * gain
    return z * cos + pltpu.roll(z, n - 16, 1) * s1 + pltpu.roll(z, 16, 1) * s2


def query_kernel(a_ref, wq_ref, c_ref, s1_ref, s2_ref, hg_ref, qr_ref, q_ref):
    q = mm(a_ref[...], wq_ref[0])
    qr_ref[...] = q
    q_ref[...] = (turned(q, row(hg_ref, 0), (c_ref, s1_ref, s2_ref)) * (0.125 * LOG2E)).astype(bf16)


def one_weight(w, k):
    return pl.BlockSpec((1, *w.shape[1:]), lambda *_: (k, 0, 0), pipeline_mode=pl.Buffered(1))


def key_call(order, patches, vec, w, tabs, hg, after, br=256):
    t, d = patches.shape
    n = w.shape[2]
    return order.run(
        "key",
        key_kernel,
        (t // br,),
        (patches, vec, w, w, *tabs, hg),
        [rows_of(br, d), whole(vec.shape), one_weight(w, 1), one_weight(w, 2)] + [rows_of(br, 128)] * 3 + [whole(hg.shape)],
        [rows_of(br, d)] + [rows_of(br, n)] * 3,
        [sds((t, d), bf16), sds((t, n), f32), sds((t, n), bf16), sds((t, n), bf16)],
        after=after,
    )


def query_call(order, a, w, tabs, hg, after, br=256):
    t, d = a.shape
    n = w.shape[2]
    return order.run(
        "query",
        query_kernel,
        (t // br,),
        (a, w, *tabs, hg),
        [rows_of(br, d), one_weight(w, 0)] + [rows_of(br, 128)] * 3 + [whole(hg.shape)],
        [rows_of(br, n)] * 2,
        [sds((t, n), f32), sds((t, n), bf16)],
        after=after,
    )


def soft_sums(q, k, v, mask):
    e = jnp.exp2(mm_nt(q, keep(k, mask))).astype(bf16)
    return mm(e, jnp.where(mask, v, jnp.ones_like(v)))


def item_block(j, s):
    return jnp.minimum(j, s[0] - 1)


def attend_kernel(sc, q_ref, k_ref, v_ref, ck_ref, cv_ref, tg_ref, mix_ref, o_ref, li_ref, acc):
    j = pl.program_id(1)
    masks = halves(128)
    keys = 512

    @pl.when(j == 0)
    def _():
        acc[...] = jnp.zeros_like(acc)

    @pl.when(j < sc[0])
    def _():
        q = q_ref[...]
        for h in range(2):
            total = acc[h]
            for c in range(k_ref.shape[0] // keys):
                at = slice(c * keys, (c + 1) * keys)
                total = total + soft_sums(q, k_ref[at, :], v_ref[at, :], masks[h])
            acc[h] = total

    @pl.when(j == SPAN - 1)
    def _():
        q = q_ref[...]

        def finish(a0, a1):
            inverse = 1.0 / jnp.where(masks[0], pltpu.roll(a0, HD, 1), pltpu.roll(a1, HD, 1))
            return jnp.where(masks[0], a0, a1) * inverse, inverse

        o, li = finish(acc[0], acc[1])
        c0, c1 = (soft_sums(q, ck_ref[...], cv_ref[...], m) for m in masks)
        mix_ref[...] = (o + tg_ref[...] * finish(c0, c1)[0]).astype(bf16)
        o_ref[...] = o.astype(bf16)
        li_ref[...] = li


def attend_call(order, sc, q, k, v, cap, text, tg, at, bq):
    n = q.shape[1]
    pairs = n // 128
    block = k.shape[0] // SPAN
    mine = lambda p, j, s: (0, p)
    other = lambda p, j, s: (item_block(j, s), p)
    return order.run(
        "attend",
        attend_kernel,
        (pairs, SPAN),
        (q, k, v, cap, cap, tg),
        [
            pl.BlockSpec((bq, 128), lambda p, j, s: (at, p)),
            pl.BlockSpec((block, 128), other),
            pl.BlockSpec((block, 128), other),
            pl.BlockSpec((text, 128), lambda p, j, s: (s[1 + SPAN], p)),
            pl.BlockSpec((text, 128), lambda p, j, s: (s[1 + SPAN], pairs + p)),
            pl.BlockSpec((1, 128), mine),
        ],
        [pl.BlockSpec((bq, 128), mine)] * 3,
        [sds((bq, n), bf16), sds((bq, n), bf16), sds((bq, n), f32)],
        [pltpu.VMEM((2, bq, 128), f32)],
        sc,
    )


def caption_back_kernel(sc, q_ref, da_ref, db_ref, ck_ref, cv_ref, tg_ref, dq_ref, dk_ref, dv_ref, gs_ref):
    masks = halves(128)
    q, d = q_ref[...], jnp.concatenate([da_ref[...], db_ref[...]], 0)
    dq = jnp.zeros(q.shape, f32)
    dk = jnp.zeros(ck_ref.shape, f32)
    dv = jnp.zeros(ck_ref.shape, f32)
    sums = []
    for h in range(2):
        ck, cv = keep(ck_ref[...], masks[h]), keep(cv_ref[...], masks[h])
        gate = tg_ref[:, h * HD : h * HD + 1]
        e = jnp.exp2(mm_nt(q, ck))
        prob = e * (1.0 / jnp.sum(e, -1, keepdims=True))
        dp = mm_nt(d, cv)
        m = jnp.sum(prob * dp, -1, keepdims=True)
        dc = (prob * (dp - m) * gate).astype(bf16)
        dq = dq + mm(dc, ck)
        dk = dk + mm_tn(dc, keep(q, masks[h]))
        dv = dv + mm_tn(prob.astype(bf16), keep(d, masks[h]))
        sums.append(jnp.sum(m, 0, keepdims=True))
    dq_ref[...] = dq * 0.125
    dk_ref[...] = dk * (1.0 / LOG2E)
    dv_ref[...] = dv * tg_ref[...]
    gs_ref[...] = jnp.where(masks[0], sums[0], sums[1])


def caption_back_call(order, sc, q, da, db, cap, text, tg, h):
    n = q.shape[1]
    pairs = n // 128
    bq = 2 * BR
    mine = lambda p, s: (0, p)
    return order.run(
        "caption_back",
        caption_back_kernel,
        (pairs,),
        (q, da, db, cap, cap, tg),
        [
            pl.BlockSpec((bq, 128), lambda p, s: (h, p)),
            pl.BlockSpec((BR, 128), mine),
            pl.BlockSpec((BR, 128), mine),
            pl.BlockSpec((text, 128), lambda p, s: (s[1 + SPAN], p)),
            pl.BlockSpec((text, 128), lambda p, s: (s[1 + SPAN], pairs + p)),
            pl.BlockSpec((1, 128), mine),
        ],
        [
            pl.BlockSpec((bq, 128), mine),
            pl.BlockSpec((text, 128), mine),
            pl.BlockSpec((text, 128), mine),
            pl.BlockSpec((1, 128), mine),
        ],
        [sds((bq, n), f32), sds((text, n), f32), sds((text, n), f32), sds((1, n), f32)],
        scalar=sc,
    )


def minus_delta(rows, head):
    lane = lax.broadcasted_iota(jnp.int32, (rows, 128), 1)
    return jnp.where((lane >= 3 * head) & (lane < 3 * head + 3), -1.0, 0.0).astype(bf16)


def dq_kernel(sc, q_ref, d_ref, x_ref, k_ref, v_ref, c_ref, dq_ref, acc):
    pair = pl.program_id(0)
    j = pl.program_id(1)
    masks = halves(128)
    keys = 512

    @pl.when(j == 0)
    def _():
        acc[...] = jnp.zeros_like(acc)

    @pl.when(j < sc[0])
    def _():
        q = q_ref[...]
        dx = jnp.concatenate([d_ref[...], x_ref[...]], 1)
        total = acc[...]
        for h in range(2):
            off = minus_delta(keys, 2 * pair + h)
            for c in range(k_ref.shape[0] // keys):
                at = slice(c * keys, (c + 1) * keys)
                k = keep(k_ref[at, :], masks[h])
                e = jnp.exp2(mm_nt(q, k))
                dp = mm_nt(dx, jnp.concatenate([keep(v_ref[at, :], masks[h]), off], 1))
                total = total + mm((e * dp).astype(bf16), k)
        acc[...] = total

    @pl.when(j == SPAN - 1)
    def _():
        dq_ref[...] = acc[...] * 0.125 + c_ref[...]


def dq_call(order, sc, q, d, k, v, cap_dq, h, after=()):
    n = q.shape[1]
    pairs = n // 128
    block = k.shape[0] // SPAN
    bq = 2 * BR
    mine = lambda p, j, s: (0, p)
    extra = lambda p, j, s: (0, pairs)
    other = lambda p, j, s: (item_block(j, s), p)
    return order.run(
        "dq",
        dq_kernel,
        (pairs, SPAN),
        (q, d, d, k, v, cap_dq),
        [
            pl.BlockSpec((bq, 128), lambda p, j, s: (h, p)),
            pl.BlockSpec((bq, 128), mine),
            pl.BlockSpec((bq, 128), extra),
            pl.BlockSpec((block, 128), other),
            pl.BlockSpec((block, 128), other),
            pl.BlockSpec((bq, 128), mine),
        ],
        [pl.BlockSpec((bq, 128), mine)],
        [sds((bq, n), f32)],
        [pltpu.VMEM((bq, 128), f32)],
        sc,
        after=after,
    )[0]


def dkv_kernel(parts, base, sc, k_ref, v_ref, q_ref, *rest):
    d_refs, x_refs = rest[0 : 2 * parts : 2], rest[1 : 2 * parts : 2]
    dk_ref, dv_ref = rest[2 * parts :]
    pair = base + pl.program_id(0)
    j = pl.program_id(1)
    masks = halves(128)
    queries = 2 * BR

    @pl.when(j == 0)
    def _():
        dk_ref[...] = jnp.zeros_like(dk_ref)
        dv_ref[...] = jnp.zeros_like(dv_ref)

    @pl.when(j < sc[0])
    def _():
        dk, dv = dk_ref[...], dv_ref[...]
        for h in range(2):
            vx = jnp.concatenate([keep(v_ref[...], masks[h]), minus_delta(v_ref.shape[0], 2 * pair + h)], 1)
            for r in range(parts):
                q = keep(q_ref[r * queries : (r + 1) * queries, :], masks[h])
                d, x = d_refs[r][...], x_refs[r][...]
                e = jnp.exp2(mm_nt(k_ref[...], q))
                dp = mm_nt(vx, jnp.concatenate([d, x], 1))
                dv = dv + mm(e.astype(bf16), keep(d, masks[h]))
                dk = dk + mm((e * dp).astype(bf16), q)
        dk_ref[...] = dk
        dv_ref[...] = dv


def dkv_call(order, sc, k, v, q_all, ds, half, base, n_pairs):
    t, n = k.shape
    pairs = n // 128
    rows = 2 * BR
    mine = pl.BlockSpec((rows, 128), lambda p, j, s: (half, base + p))
    out = pl.BlockSpec((rows, 128), lambda p, j, s: (0, p))
    other = pl.BlockSpec((rows, 128), lambda p, j, s: (item_block(j, s), base + p))
    extra = pl.BlockSpec((rows, 128), lambda p, j, s: (item_block(j, s), pairs))
    return order.run(
        "dkv",
        functools.partial(dkv_kernel, len(ds), base),
        (n_pairs, SPAN),
        (k, v, q_all, *(x for d in ds for x in (d, d))),
        [mine, mine, pl.BlockSpec((t, 128), lambda p, j, s: (s[1 + SPAN + j], base + p))] + [other, extra] * len(ds),
        [out, out],
        [sds((rows, n_pairs * 128), f32)] * 2,
        scalar=sc,
    )


def chunk_call(order, kernel, name, c, ins, specs, chunk_outs, sum_outs, whole_outs, before):
    one = lambda r, w: pl.BlockSpec((r, w), lambda i: (0, 0))
    own = chunk_outs + sum_outs
    into = [pl.BlockSpec((BR, w), lambda i, at=c % (r // BR): (at, 0)) for r, w, _ in whole_outs]
    return order.run(
        name,
        kernel,
        (1,),
        ins,
        specs,
        [one(r, w) for r, w, _ in own] + into,
        [sds((r, w), k) for r, w, k in own + whole_outs],
        held=tuple(before),
        first_held=len(own),
    )


def part(c, width):
    return pl.BlockSpec((BR, width), lambda i: (c, 0))


def alone(width):
    return pl.BlockSpec((BR, width), lambda i: (0, 0))


def pair_grad_kernel(a_ref, b_ref, c_ref, d_ref, o_ref):
    n = b_ref.shape[1]
    o_ref[:, :n] = mm_tn(a_ref[...], b_ref[...]).astype(bf16)
    o_ref[:, n:] = mm_tn(c_ref[...], d_ref[...]).astype(bf16)


def pair_grad_call(order, a, b, c, d, part=0, parts=1, before=(), after=()):
    t, m = a.shape
    n, k = b.shape[1], d.shape[1]
    blk = 256
    steps = m // blk // parts
    cols = pl.BlockSpec((t, blk), lambda i: (0, part * steps + i))
    return order.run(
        "pair_grad",
        pair_grad_kernel,
        (steps,),
        (a, b, c, d),
        [cols, whole(b.shape), cols, whole(d.shape)],
        [pl.BlockSpec((blk, n + k), lambda i: (part * steps + i, 0))],
        [sds((m, n + k), bf16)],
        held=before,
        after=after,
    )


def ffn_kernel(p_ref, at_ref, v_ref, wg_ref, wd_ref, mid_ref, gu_ref, f_ref, a_ref, h_ref):
    at = at_ref[...].astype(f32)
    mid = p_ref[...].astype(f32) + row(v_ref, 1) * (at * inv_rms(at))
    mid_ref[...] = mid
    a = (mid * inv_rms(mid) * row(v_ref, 2)).astype(bf16)
    a_ref[...] = a
    g = mm(a, wg_ref[0])
    u = mm(a, wg_ref[1])
    n = g.shape[1]
    gu_ref[:, :n] = g.astype(bf16)
    gu_ref[:, n:] = u.astype(bf16)
    h = (g * jax.nn.sigmoid(g) * u).astype(bf16)
    h_ref[...] = h
    f_ref[...] = mm(h, wd_ref[...]).astype(bf16)


def ffn_call(order, c, patches, at, vec, wg, wd, before):
    t, d = patches.shape
    n = wd.shape[0]
    return chunk_call(
        order,
        ffn_kernel,
        "ffn",
        c,
        (patches, at, vec, wg, wd),
        [part(c, d), alone(d), whole(vec.shape), whole(wg.shape), whole(wd.shape)],
        [(BR, d, f32), (BR, 2 * n, bf16), (BR, d, bf16)],
        [],
        [(t, d, bf16), (t, n, bf16)],
        before,
    )


def ffn_back_kernel(f_ref, mid_ref, c_ref, gu_ref, v_ref, wg_ref, wd_ref, da_ref, cs_ref, y_ref, df_ref, dgu_ref):
    f = f_ref[...].astype(f32)
    cot = c_ref[...].astype(f32)
    r = inv_rms(f)
    fh = f * r
    y_ref[...] = (mid_ref[...] + row(v_ref, 3) * fh).astype(bf16)
    z = cot * row(v_ref, 3)
    df = (r * (z - fh * jnp.mean(z * fh, -1, keepdims=True))).astype(bf16)
    df_ref[...] = df
    cs_ref[...] = col_sum(cot * fh)
    dh = mm_nt(df, wd_ref[...])
    n = dh.shape[1]
    g = gu_ref[:, :n].astype(f32)
    u = gu_ref[:, n:].astype(f32)
    s = jax.nn.sigmoid(g)
    gs = g * s
    dg = (dh * u * (s + gs * (1.0 - s))).astype(bf16)
    du = (dh * gs).astype(bf16)
    dgu_ref[:, :n] = dg
    dgu_ref[:, n:] = du
    da_ref[...] = (mm_nt(dg, wg_ref[0]) + mm_nt(du, wg_ref[1])).astype(bf16)


def ffn_back_call(order, c, f, mid, cot, gu, vec, wg, wd, before):
    t, d = cot.shape
    n = wd.shape[0]
    return chunk_call(
        order,
        ffn_back_kernel,
        "ffn_back",
        c,
        (f, mid, cot, gu, vec, wg, wd),
        [alone(d), alone(d), part(c, d), alone(2 * n), whole(vec.shape), whole(wg.shape), whole(wd.shape)],
        [(BR, d, bf16)],
        [(1, d, f32)],
        [(t, d, bf16), (t, d, bf16), (t, 2 * n, bf16)],
        before,
    )


def out_back_kernel(da_ref, mid_ref, at_ref, c_ref, v_ref, w_ref, o_ref, li_ref, dm_ref, dx_ref, c3_ref, c2_ref, dat_ref, ds_ref):
    da = da_ref[...].astype(f32)
    mid = mid_ref[...]
    r = inv_rms(mid)
    mh = mid * r
    z = da * row(v_ref, 2)
    dm = c_ref[...].astype(f32) + r * (z - mh * jnp.mean(z * mh, -1, keepdims=True))
    dm_ref[...] = dm
    c3_ref[...] = col_sum(da * mh)
    at = at_ref[...].astype(f32)
    ra = inv_rms(at)
    ah = at * ra
    c2_ref[...] = col_sum(dm * ah)
    z = dm * row(v_ref, 1)
    dat = (ra * (z - ah * jnp.mean(z * ah, -1, keepdims=True))).astype(bf16)
    dat_ref[...] = dat
    dx = mm_nt(dat, w_ref[...]).astype(bf16)
    dx_ref[...] = dx
    n = dx.shape[1]
    ds = dx.astype(f32) * li_ref[...]
    ds_ref[:, :n] = ds.astype(bf16)
    hi, lo = split(ds * o_ref[...].astype(f32))
    head = lax.broadcasted_iota(jnp.int32, (n, 128), 0) // HD
    lane = lax.broadcasted_iota(jnp.int32, (n, 128), 1)
    to_lanes = (lane // 3 == head).astype(bf16)
    delta = mm(hi, to_lanes) + mm(lo, to_lanes)
    one = delta.astype(bf16).astype(f32)
    two = (delta - one).astype(bf16).astype(f32)
    which = lax.broadcasted_iota(jnp.int32, (1, 128), 1) % 3
    ds_ref[:, n:] = jnp.where(which == 0, one, jnp.where(which == 1, two, delta - one - two)).astype(bf16)


def out_back_call(order, c, da, mid, at, cot, vec, w, o, li, place, before):
    t, d = cot.shape
    n = w.shape[0]
    return chunk_call(
        order,
        out_back_kernel,
        "out_back",
        c,
        (da, mid, at, cot, vec, w, o, li),
        [alone(d), alone(d), alone(d), part(c, d), whole(vec.shape), whole(w.shape), part(place, n), part(place, n)],
        [(BR, d, f32), (BR, n, bf16)],
        [(1, d, f32), (1, d, f32)],
        [(t, d, bf16), (2 * BR, n + 128, bf16)],
        before,
    )


def dqkv_kernel(pairs, dq_ref, *refs):
    dk_refs, dv_refs = refs[0 : 2 * pairs : 2], refs[1 : 2 * pairs : 2]
    (qr_ref, kr_ref, c_ref, s1_ref, s2_ref, hg_ref, w_ref, p_ref, da_ref, hs_ref, cs_ref, d_ref) = refs[2 * pairs :]
    side = lambda parts: jnp.concatenate([x[...] for x in parts], 1)
    n = dq_ref.shape[1]
    ones = head_ones(n)
    cos, s1, s2 = (tile3(t[...], n) for t in (c_ref, s1_ref, s2_ref))

    def back(dy, x, gain):
        dz = dy * cos - pltpu.roll(dy, 16, 1) * s2 - pltpu.roll(dy, n - 16, 1) * s1
        r = lax.rsqrt(head_sum(x * x, ones) * (1.0 / HD) + EPS)
        xh = x * r
        g = dz * gain
        return r * (g - xh * (head_sum(g * xh, ones) * (1.0 / HD))), col_sum(dz * xh)

    dq, hq = back(dq_ref[...], qr_ref[...], row(hg_ref, 0))
    dk, hk = back(side(dk_refs) * (1.0 / LOG2E), kr_ref[...], row(hg_ref, 1))
    dql, dkl, dvl = dq.astype(bf16), dk.astype(bf16), side(dv_refs).astype(bf16)
    d_ref[:, :n] = dql
    d_ref[:, n : 2 * n] = dkl
    d_ref[:, 2 * n :] = dvl
    da = mm_nt(dql, w_ref[0]) + mm_nt(dkl, w_ref[1]) + mm_nt(dvl, w_ref[2])
    da_ref[...] = da.astype(bf16)
    x = p_ref[...].astype(f32)
    cs_ref[...] = col_sum(da * (x * inv_rms(x)))
    hs_ref[0:1, :] = hq
    hs_ref[1:2, :] = hk


def dqkv_call(order, c, dq, dkv, qr, kr, tabs, hg, w, patches, before):
    t, d = patches.shape
    n = dq.shape[1]
    return chunk_call(
        order,
        functools.partial(dqkv_kernel, len(dkv)),
        "dqkv",
        c,
        (dq, *(x for two in dkv for x in two), qr, kr, *tabs, hg, w, patches),
        [part(c % 2, n)] + [part(c % 2, x.shape[1]) for two in dkv for x in two] + [part(c, n)] * 2 + [part(c, 128)] * 3 + [whole(hg.shape), whole(w.shape), part(c, d)],
        [(BR, d, bf16)],
        [(2, n, f32), (1, d, f32)],
        [(t, 3 * n, bf16)],
        before,
    )


def last_kernel(da_ref, p_ref, dm_ref, v_ref, o_ref):
    x = p_ref[...].astype(f32)
    r = inv_rms(x)
    xh = x * r
    z = da_ref[...].astype(f32) * row(v_ref, 0)
    o_ref[...] = (dm_ref[...] + r * (z - xh * jnp.mean(z * xh, -1, keepdims=True))).astype(bf16)


def last_call(order, c, da, patches, dm, vec, before):
    t, d = patches.shape
    return chunk_call(
        order,
        last_kernel,
        "last",
        c,
        (da, patches, dm, vec),
        [alone(d), part(c, d), alone(d), whole(vec.shape)],
        [],
        [],
        [(t, d, bf16)],
        before,
    )


def caption_grad_kernel(dk_ref, dv_ref, kr_ref, hg_ref, d_ref, hs_ref):
    n = dk_ref.shape[1]
    ones = head_ones(n)
    x = kr_ref[...]
    r = lax.rsqrt(head_sum(x * x, ones) * (1.0 / HD) + EPS)
    xh = x * r
    dy = dk_ref[...]
    g = dy * row(hg_ref, 2)
    d_ref[:, :n] = (r * (g - xh * (head_sum(g * xh, ones) * (1.0 / HD)))).astype(bf16)
    d_ref[:, n:] = dv_ref[...].astype(bf16)
    hs_ref[...] = col_sum(dy * xh)


def caption_norm_kernel(kr_ref, v_ref, hg_ref, o_ref):
    n = kr_ref.shape[1]
    x = kr_ref[...]
    r = lax.rsqrt(head_sum(x * x, head_ones(n)) * (1.0 / HD) + EPS)
    o_ref[:, :n] = (x * r * row(hg_ref, 2)).astype(bf16)
    o_ref[:, n:] = v_ref[...].astype(bf16)


def swap(x, axis, size, m):
    return lax.ppermute(x, axis, [(i, i ^ m) for i in range(size)])


def pick_kernel(count, n_arrays, n_pieces, sc, *refs):
    outs, sem = refs[n_arrays * n_pieces :][:n_arrays], refs[-1]
    for k, out in enumerate(outs):
        pieces = refs[k * n_pieces : (k + 1) * n_pieces]
        rows = pieces[0].shape[0]
        for j in range(count):
            for m in range(n_pieces):

                @pl.when(sc[1 + j] == m)
                def _():
                    pltpu.make_async_copy(pieces[m], out.at[pl.ds(j * rows, rows)], sem.at[k, j]).start()

    for k, out in enumerate(outs):
        first = refs[k * n_pieces]
        rows = first.shape[0]
        for j in range(count):
            pltpu.make_async_copy(first, out.at[pl.ds(j * rows, rows)], sem.at[k, j]).wait()


class Gather:
    def __init__(self, a, b):
        self.all = None
        if lax.axis_size("wide") != 8:
            self.first = self.second = ()
            self.all = [lax.all_gather(x, "wide") for x in (a, b)]
            return
        send = lambda x, pairs: lax.ppermute(x, "wide", pairs)
        over_x = [(i, i ^ 2) for i in range(8)]
        over_y = [(1, 5), (4, 0), (3, 7), (6, 2)]
        a2, a4, b4, b2 = send(a, over_x), send(a, over_y), send(b, over_y), send(b, over_x)
        a6 = send(a2, [(0, 4), (1, 5), (6, 2), (7, 3)])
        b6x, b6y = send(b2, [(0, 4), (7, 3)]), send(b4, [(7, 5), (0, 2)])
        self.first = (a2, a4, b4, b2)
        self.second = (a6, b6x, b6y)
        self.kept = ((a, a2, a4, a6), (b, b2, b4, b6x + b6y))

    def pieces(self):
        if self.all is not None:
            return self.all
        return [[y for x in four for y in (x, swap(x, "wide", 8, 1))] for four in self.kept]


class GatherOne:
    def __init__(self, a):
        self.all = None
        if lax.axis_size("wide") != 8:
            self.first = self.second = ()
            self.all = [lax.all_gather(a, "wide")]
            return
        send = lambda x, pairs: lax.ppermute(x, "wide", pairs)
        a2 = send(a, [(i, i ^ 2) for i in range(8)])
        a4 = send(a, [(1, 5), (4, 0), (3, 7), (6, 2)])
        a6 = send(a2, [(0, 4), (1, 5), (6, 2), (7, 3)])
        self.first, self.second = (a2, a4), (a6,)
        self.kept = ((a, a2, a4, a6),)

    pieces = Gather.pieces


def shift(x, by):
    size = lax.axis_size("wide")
    return lax.ppermute(x, "wide", [(i, i + by) for i in range(size) if 0 <= i + by < size])


def pick(order, sc, pieces, count):
    if not isinstance(pieces[0], list):
        one = lambda x, j: lax.dynamic_index_in_dim(x, sc[1 + SPAN + j], 0, False)
        return [jnp.concatenate([one(x, j) for j in range(count)]) for x in pieces]
    outs = [(count * p[0].shape[0], p[0].shape[1]) for p in pieces]
    return order.run(
        "pick",
        functools.partial(pick_kernel, count, len(pieces), 8),
        (1,),
        [x for p in pieces for x in p],
        loose(8 * len(pieces)),
        [pl.BlockSpec(shape, lambda i, s: (0, 0)) for shape in outs],
        [sds(shape, bf16) for shape in outs],
        [pltpu.SemaphoreType.DMA((len(pieces), count))],
        sc,
    )


def pin_kernel(o_ref):
    pass


def pin(order, x, after=()):
    return order.run("pin", pin_kernel, (1,), (), [], loose(1), [sds(x.shape, x.dtype)], held=(x,), after=after)[0]


def note_kernel(x_ref, o_ref):
    o_ref[...] = x_ref[...]


def note(order, x):
    n = x.shape[0]
    size = -(-n // 1024) * 8
    x = jnp.pad(x, (0, size * 128 - n)).reshape(size, 128)
    spec = pl.BlockSpec(x.shape, lambda i: (0, 0))
    return order.run("note", note_kernel, (1,), (x,), [spec], [spec], [sds(x.shape, f32)])[0].reshape(-1)[:n]


def gather_small(x, axis):
    n = x.shape[0]
    wide = -(-n // 1024) * 1024
    x = jnp.pad(x, (0, wide - n)).reshape(wide // 128, 128)
    size = lax.axis_size(axis)
    if size > 8:
        return lax.all_gather(x, axis).reshape(size, wide)[:, :n]
    got = jnp.stack([x] + [swap(x, axis, size, m) for m in range(1, size)])
    order = jnp.arange(size, dtype=jnp.int32)
    mine = (order[:, None] ^ lax.axis_index(axis)) == order[None, :]
    out = jnp.sum(jnp.where(mine[:, :, None, None], got[None], 0.0), 1)
    return out.reshape(size, wide)[:, :n]


def gather_now(x, axis):
    n = x.shape[0]
    wide = -(-n // 1024) * 1024
    padded = jnp.pad(x, (0, wide - n)).reshape(1, 8, wide // 8)
    return lax.all_gather(padded, axis, axis=0, tiled=True).reshape(-1, wide)[:, :n]


def hop_kernel(have, sc, *refs):
    ins = dict(zip(have["in"], refs))
    outs = dict(zip(have["out"], refs[len(have["in"]) :]))
    end = sc[0] == 1
    if "total" in outs:
        outs["total"][...] = jnp.where(end, ins["r1"][...], ins["send"][...])
    third = None
    if "second" in ins:
        third = ins["second"][...] + ins["r2"][...]
    if "second" in outs:
        outs["second"][...] = ins["x"][...] + ins["r1"][...]
    if "send" in outs:
        new = ins["new"][...] if "new" in ins else third
        outs["send"][...] = new if third is None else jnp.where(end, new, third)


class Line:
    def __init__(self, order, place):
        self.order = order
        self.end = ((place == 0) | (place == 3)).astype(jnp.int32).reshape(1)
        self.x = self.second = self.send = None
        self.third = False

    def step(self, new, after=()):
        if self.send is None:
            self.x = self.send = new
            return None
        go = lambda x, perm: lax.ppermute(x, "narrow", perm)
        ins = {"r1": go(self.send, [(0, 1), (3, 2), (1, 0), (2, 3)])}
        outs = []
        if self.third:
            ins["send"] = self.send
            outs.append("total")
        if self.second is not None:
            ins["r2"] = go(self.second, [(1, 2), (2, 1)])
            ins["second"] = self.second
        if self.x is not None:
            ins["x"] = self.x
            outs.append("second")
        if new is not None:
            ins["new"] = new
        if new is not None or self.second is not None:
            outs.append("send")
        like = ins["r1"]
        block = pl.BlockSpec((BR // 2, like.shape[1]), lambda i, s: (i, 0))
        got = self.order.run(
            "hop",
            functools.partial(hop_kernel, {"in": list(ins), "out": outs}),
            (2,),
            list(ins.values()),
            [block] * len(ins),
            [block] * len(outs),
            [sds(like.shape, like.dtype)] * len(outs),
            scalar=self.end,
            after=after,
        )
        got = dict(zip(outs, got))
        self.third = self.second is not None
        self.x, self.second, self.send = new, got.get("second"), got.get("send")
        return got.get("total")


class Sums:
    def __init__(self, order, size, place):
        self.line = Line(order, place) if size == 4 else None
        self.names, self.done = [], {}

    def add(self, name, x, after=()):
        if self.line is None:
            self.done[name] = lax.psum(x, "narrow")
            return
        if self.line.send is None:
            self.names = [None]
        self._step(name, x, after)

    def _step(self, name, x, after):
        total = self.line.step(x, after)
        self.names.append(name)
        if total is not None:
            self.done[self.names[-4]] = total

    def get(self, name, after=()):
        while name not in self.done:
            self._step(None, None, after)
            after = ()
        return self.done[name]


def scatter_rows(x):
    return lax.psum_scatter(x.astype(bf16), "wide", scatter_dimension=0, tiled=True)


def rope_tables(position, width):
    lane = jnp.arange(128, dtype=jnp.int32)
    within = lane % HD
    quarter = HD // 4
    frequency = 10000.0 ** (-(within % quarter).astype(f32) / quarter)
    by_row = within < HD // 2
    where = jnp.where(by_row[None, :], (position // width)[:, None], (position % width)[:, None])
    angle = where.astype(f32) * frequency[None, :]
    cos, sin = jnp.cos(angle), jnp.sin(angle)
    former = (within % (HD // 2) < quarter)[None, :]
    return cos, jnp.where(former, -sin, 0.0), jnp.where(former, 0.0, sin)


def local(
    patches,
    cotangent,
    conditioning,
    captions,
    item_lengths,
    grid_widths,
    w_ada,
    norm_gains,
    w_qkv,
    head_gains,
    cross_gate,
    w_caption,
    w_out,
    w_gate_up,
    w_down,
):
    t, d = patches.shape
    n = w_qkv.shape[2]
    heads = n // HD
    ada = w_ada.shape[2]
    ff = w_down.shape[0]
    text = captions.shape[0]
    cd = conditioning.shape[1]
    count = lax.axis_size("wide")
    deep = lax.axis_size("narrow")
    me = lax.axis_index("wide")
    mz = lax.axis_index("narrow")

    slots = item_lengths.shape[0]
    spans = item_lengths // t
    order = jnp.arange(slots, dtype=jnp.int32)
    ends = jnp.sum(jnp.where(order[None, :] <= order[:, None], spans[None, :], 0), 1)
    blocks = jnp.arange(count, dtype=jnp.int32)
    item = jnp.sum((ends[None, :] <= blocks[:, None]).astype(jnp.int32), 1)
    is_item = item[:, None] == order[None, :]
    choose = lambda values: jnp.sum(jnp.where(is_item, values[None, :], 0), 1)
    firsts = choose(ends - spans)
    mine = blocks == me
    of_me = lambda values: jnp.sum(jnp.where(mine, values, 0))
    first = of_me(firsts)
    length = of_me(choose(spans))
    width = of_me(choose(grid_widths))
    position = (me - first) * t + jnp.arange(t, dtype=jnp.int32)
    tabs = rope_tables(position, width)
    steps = first + jnp.minimum(jnp.arange(SPAN, dtype=jnp.int32), length - 1)
    places = steps ^ me if count == 8 else steps
    sc = jnp.concatenate([length.reshape(1), places, steps]).astype(jnp.int32)

    cond = conditioning.astype(f32)[0]
    silu_low = jax.nn.silu(cond).astype(bf16)
    mod = jnp.sum(silu_low.astype(f32)[:, None, None] * w_ada.astype(f32), 0)
    share = cd // deep
    sent = jnp.concatenate([mod.reshape(-1), lax.dynamic_slice_in_dim(cond, mz * share, share)])
    got = gather_now(gather_now(sent, "narrow").reshape(-1), "wide").reshape(count, deep, -1)
    mods = got[:, :, : 4 * ada].reshape(count, deep, 4, ada).transpose(0, 2, 1, 3).reshape(count, 4, d)
    conds = got[:, :, 4 * ada :].reshape(count, cd)
    my_mod = lax.dynamic_index_in_dim(mods, first, 0, False)
    of_block = jnp.sum(jnp.where((firsts[:, None] == blocks[None, :])[:, :, None, None], mods[None], 0.0), 1)
    scales = 1.0 + of_block
    gates = jnp.tanh(of_block)
    factor = jnp.stack([1.0 + my_mod[0], jnp.tanh(my_mod[1]), 1.0 + my_mod[2], jnp.tanh(my_mod[3])])
    vec = norm_gains * factor
    hg = jnp.tile(head_gains, (1, heads))
    tg_heads = jnp.tanh(cross_gate)
    tg = jnp.repeat(tg_heads, HD)[None, :]

    order = Order()
    chunks = range(t // BR)
    pairs_of = range(t // (2 * BR))
    sums = Sums(order, deep, mz)
    a1, k_raw, k, v = key_call(order, patches, vec, w_qkv, tabs, hg, ())
    kv = Gather(k, v)

    cap_raw = jnp.einsum("kd,jde->jke", captions, w_caption, preferred_element_type=f32)
    whole_cap = pl.BlockSpec((text, n), lambda i: (0, 0))
    both_cap = pl.BlockSpec((text, 2 * n), lambda i: (0, 0))
    (cap,) = order.run(
        "caption_norm",
        caption_norm_kernel,
        (1,),
        (cap_raw[0], cap_raw[1], hg),
        [whole_cap, whole_cap, whole(hg.shape)],
        [both_cap],
        [sds((text, 2 * n), bf16)],
    )
    offset = me - first
    q_raw, q = query_call(order, a1, w_qkv, tabs, hg, ())
    cap = lax.all_gather(pin(order, cap, kv.first), "wide", axis=0, tiled=True)

    q_all = lax.all_gather(q, "wide", axis=0, tiled=True)
    k_all, v_all = pick(order, sc, kv.pieces(), SPAN)
    heads_out = {}
    for c in chunks[: len(chunks) // 2]:
        heads_out[c] = (*attend_call(order, sc, q, k_all, v_all, cap, text, tg, c, BR), 0)
        sums.add(("attn", c), mm(heads_out[c][0], w_out).astype(bf16))
    half = (len(chunks) + 1) // 2
    later = attend_call(order, sc, q, k_all, v_all, cap, text, tg, 1, half * BR)
    for c in chunks[half:]:
        heads_out[c] = (*later, c - half)
        at = (c - half) * BR
        sums.add(("attn", c), mm(later[0][at : at + BR], w_out).astype(bf16))

    mids, gus = {}, {}
    whole_out = ()
    for c in chunks:
        mids[c], gus[c], ffn_part, *whole_out = ffn_call(
            order, c, patches, sums.get(("attn", c)), vec, w_gate_up, w_down, whole_out
        )
        sums.add(("ffn", c), ffn_part)
    a3, hidden = whole_out
    whole_out = ()
    c4 = 0.0
    for c in chunks:
        da3_part, part_sum, *whole_out = ffn_back_call(
            order, c, sums.get(("ffn", c)), mids[c], cotangent, gus[c], vec, w_gate_up, w_down, whole_out
        )
        sums.add(("da3", c), da3_part)
        c4 = c4 + part_sum
    output, d_ffn, d_gu = whole_out

    d_mids, dqs, dq_caps, d_got, d_mixed, d_scaled = {}, {}, {}, {}, {}, {}
    whole_out = ()
    mlp_part = ()
    behind = ()
    c2 = c3 = dck = dcv = gate_sum = 0.0
    for h in pairs_of:
        for c in (2 * h, 2 * h + 1):
            _, o_self, linv, place = heads_out[c]
            if c == 2 * h + 1 and h > 0:
                behind = d_got[h - 1].second
            da3 = sums.get(("da3", c), behind)
            d_mids[c], d_mixed[c], p3, p2, *outs = out_back_call(
                order, c, da3, mids[c], sums.get(("attn", c)), cotangent, vec, w_out, o_self, linv, place, whole_out
            )
            whole_out, d_scaled[h] = (outs if c % 2 == 0 else outs[:1]), outs[1]
            c2, c3 = c2 + p2, c3 + p3
            behind = ()
            if c == 2 * h:
                early = d_got[h - 1].first if h > 0 else ()
                mlp_part = pair_grad_call(order, a3, d_gu, d_ffn, hidden, h, len(pairs_of), mlp_part, early)
        d_got[h] = GatherOne(d_scaled[h])
        dq_caps[h], pk, pv, pg = caption_back_call(order, sc, q, d_mixed[2 * h], d_mixed[2 * h + 1], cap, text, tg, h)
        dck, dcv, gate_sum = dck + pk, dcv + pv, gate_sum + pg
    d_attn = whole_out[0]
    cap_sum = jnp.concatenate([dck, dcv], 1)
    cap_low = cap_sum.astype(bf16)
    for by in range(1, SPAN):
        cap_sum = cap_sum + jnp.where(by < length, shift(cap_low, -by).astype(f32), 0.0)
    cap_sum = jnp.where(offset == 0, cap_sum, 0.0)
    last_half = pairs_of[-1]

    def make_dq(h, after):
        return dq_call(order, sc, q, d_scaled[h], k_all, v_all, dq_caps[h], h, after)

    for h in pairs_of[:-1]:
        dqs[h] = make_dq(h, ())

    d_cap, hs_c = order.run(
        "caption_grad",
        caption_grad_kernel,
        (1,),
        (cap_sum[:, :n], cap_sum[:, n:], cap_raw[0], hg),
        [whole_cap, whole_cap, whole_cap, whole(hg.shape)],
        [both_cap, pl.BlockSpec((1, n), lambda i: (0, 0))],
        [sds((text, 2 * n), bf16), sds((1, n), f32)],
    )
    d_text = (mm_nt(d_cap[:, :n], w_caption[0]) + mm_nt(d_cap[:, n:], w_caption[1])).astype(bf16)
    cap_part = mm_tn(captions, d_cap).astype(bf16)
    pieces = -(-d_text.shape[1] // d)
    padded = jnp.pad(d_text, ((0, 0), (0, pieces * d - d_text.shape[1])))
    text_parts = [padded[:, p * d : (p + 1) * d] for p in range(pieces)]

    sums.add(("text", 0), text_parts[0])
    dqs[last_half] = make_dq(last_half, (*d_got[last_half].first, *text_parts))
    sums.add(("text", 1), text_parts[1], (cap_part, *d_got[last_half].second))
    ds = [x for h in pairs_of for x in pick(order, sc, d_got[h].pieces(), SPAN)]
    g_mlp = scatter_rows(pin(order, mlp_part[0]))
    whole_out = ()
    c1 = hs_qk = 0.0
    mixed = jnp.concatenate([heads_out[c][0] for c in chunks[:half]] + [later[0]])
    pairs = n // 128

    def project(c, dkv, after=()):
        nonlocal whole_out, c1, hs_qk
        da1_part, p_hs, p1, *whole_out = dqkv_call(order, c, dqs[c // 2], dkv, q_raw, k_raw, tabs, hg, w_qkv, patches, whole_out)
        hs_qk, c1 = hs_qk + p_hs, c1 + p1
        return da1_part

    dkv = [dkv_call(order, sc, k, v, q_all, ds, 0, 0, pairs)]
    for p in range(2, pieces):
        sums.add(("text", p), text_parts[p])
    g_cap = scatter_rows(pin(order, cap_part))
    sums.add(("da1", 0), project(0, dkv))
    da1_part = project(1, dkv)
    dkv = [dkv_call(order, sc, k, v, q_all, ds, 1, 0, 1)]
    sums.add(("da1", 1), da1_part)
    dkv.append(dkv_call(order, sc, k, v, q_all, ds, 1, 1, pairs - 1))
    for c in chunks[2:]:
        da1_part = project(c, dkv)
        if c == chunks[-1]:
            (d_qkv,) = whole_out
            attn_part = pair_grad_call(order, a1, d_qkv, d_attn, mixed)[0]
        sums.add(("da1", c), da1_part, (g_mlp,) if c == chunks[-1] else ())
    g_attn = scatter_rows(pin(order, attn_part))

    head_part = jnp.concatenate([hs_qk, hs_c]).reshape(3, heads, HD).sum(1)
    gate_part = gate_sum[0, ::HD] * (1.0 - tg_heads * tg_heads)
    got_narrow = gather_now(note(order, jnp.concatenate([c1[0], head_part.reshape(-1), gate_part])), "narrow")
    whole_out = last_call(order, 0, sums.get(("da1", 0)), patches, d_mids[0], vec, ())
    da1 = sums.get(("da1", 1), (g_cap, got_narrow))
    summed = jnp.sum(got_narrow[:, : d + 3 * HD], 0)
    sent = note(order, jnp.concatenate([summed, got_narrow[:, d + 3 * HD :].reshape(-1), c2[0], c3[0], c4[0]]))
    got_wide = gather_now(sent, "wide")
    whole_out = last_call(order, 1, da1, patches, d_mids[1], vec, whole_out)
    da1 = sums.get(("da1", 2), (got_wide,))
    for c in chunks[2:]:
        whole_out = last_call(order, c, da1 if c == 2 else sums.get(("da1", c), (g_attn,)), patches, d_mids[c], vec, whole_out)
    (grad_patches,) = whole_out
    grad_captions = jnp.concatenate([sums.get(("text", p)) for p in range(pieces)], 1)[:, : d_text.shape[1]]

    got = got_wide
    one, rest = got[:, :d], got[:, d:]
    grad_head_gains = jnp.sum(rest[:, : 3 * HD], 0).reshape(3, HD)
    grad_cross_gate = jnp.sum(rest[:, 3 * HD : 3 * HD + deep * heads], 0)
    two, three, four = (rest[:, 3 * HD + deep * heads + k * d :][:, :d] for k in range(3))
    cols = jnp.stack([one, two, three, four], 1)
    gain_factor = jnp.stack([scales[:, 0], gates[:, 1], scales[:, 2], gates[:, 3]], 1)
    gain_grads = jnp.sum(gain_factor * cols, 0)
    wide_cols = d // count
    grad_norm_gains = lax.dynamic_slice_in_dim(gain_grads, me * wide_cols, wide_cols, 1)
    ones = jnp.ones_like(one)
    slope = jnp.stack([ones, 1.0 - gates[:, 1] ** 2, ones, 1.0 - gates[:, 3] ** 2], 1)
    d_mod = lax.dynamic_slice_in_dim(slope * norm_gains[None] * cols, mz * ada, ada, 2)
    at_slot = (firsts[None, :] == blocks[:, None]).astype(f32)
    d_slots = jnp.sum(at_slot[:, :, None, None] * d_mod[None], 1).astype(bf16).astype(f32)
    cond_rows = cd // count
    silu_mine = lax.dynamic_slice_in_dim(jax.nn.silu(conds).astype(bf16).astype(f32), me * cond_rows, cond_rows, 1)
    grad_ada = jnp.sum(silu_mine[:, :, None, None] * d_slots[:, None], 0)
    d_mine = lax.dynamic_index_in_dim(d_slots, me, 0, False)
    cond_part = jnp.sum(d_mine[None] * w_ada.astype(f32), (1, 2))
    cond_total = jnp.sum(gather_now(cond_part, "narrow"), 0)
    pull_silu = jax.vjp(jax.nn.silu, cond)[1]
    grad_conditioning = pull_silu(cond_total)[0].reshape(1, -1)

    rows = d // count
    return (
        output,
        grad_patches,
        grad_conditioning,
        grad_captions,
        grad_ada,
        grad_norm_gains,
        g_attn[:, : 3 * n].astype(f32).reshape(rows, 3, n).transpose(1, 0, 2),
        grad_head_gains,
        grad_cross_gate,
        g_cap.astype(f32).reshape(-1, 2, n).transpose(1, 0, 2),
        g_attn[:, 3 * n :].astype(f32).T,
        g_mlp[:, : 2 * ff].astype(f32).reshape(rows, 2, ff).transpose(1, 0, 2),
        g_mlp[:, 2 * ff :].astype(f32).T,
    )


def solution(mesh):
    placed = (
        P("wide", None),
        P("wide", None),
        P("wide", None),
        P("wide", None),
        P(),
        P(),
        P(None, None, "narrow"),
        P(),
        P(None, None, "narrow"),
        P(),
        P("narrow"),
        P(None, None, "narrow"),
        P("narrow", None),
        P(None, None, "narrow"),
        P("narrow", None),
    )
    return jax.shard_map(
        local,
        mesh=mesh,
        in_specs=placed,
        out_specs=(
            P("wide", None),
            P("wide", None),
            P("wide", None),
            P("wide", None),
            P("wide", None, "narrow"),
            P(None, "wide"),
            P(None, "wide", "narrow"),
            P(),
            P(),
            P(None, "wide", "narrow"),
            P("narrow", "wide"),
            P(None, "wide", "narrow"),
            P("narrow", "wide"),
        ),
        check_vma=False,
    )
```

```python
import functools

import jax
import jax.numpy as jnp
from jax import lax
from jax.experimental import pallas as pl
from jax.experimental.pallas import tpu as pltpu
from jax.sharding import PartitionSpec as P

HD = 64
SPAN = 4
EPS = 1e-05
LOG2E = 1.4426950408889634
f32 = jnp.float32
bf16 = jnp.bfloat16
VMEM = 56 * 1024 * 1024
BR = 256
NT = (((1,), (1,)), ((), ()))
TN = (((0,), (0,)), ((), ()))


def params(n):
    return pltpu.CompilerParams(
        dimension_semantics=("arbitrary",) * n, vmem_limit_bytes=VMEM
    )


def sds(shape, dtype):
    return jax.ShapeDtypeStruct(shape, dtype)


COST = {
    "key": 8, "query": 9, "caption_norm": 2, "pick": 5, "attend": 18, "hop": 3, "ffn": 9, "ffn_back": 10, "out_back": 6,
    "pair_grad": 10, "caption_back": 6, "dq": 27, "dkv": 24, "dqkv": 7, "caption_grad": 3, "last": 3, "note": 1, "pin": 1,
}


class Order:
    def __init__(self):
        self.token = ()

    def run(self, name, kernel, grid, ins, in_specs, out_specs, out_shape, scratch=(), scalar=None, held=(), first_held=0, after=()):
        pre = 0 if scalar is None else 1
        given = pre + len(ins)
        extra = [*self.token, *after, *held]

        def body(*refs):
            kernel(*refs[:given], *refs[given + len(extra) :])

        at = given + len(extra) - len(held)
        out = pl.pallas_call(
            body,
            grid_spec=pltpu.PrefetchScalarGridSpec(
                num_scalar_prefetch=pre,
                grid=grid,
                in_specs=list(in_specs) + loose(len(extra)),
                out_specs=out_specs,
                scratch_shapes=list(scratch),
            ),
            out_shape=out_shape,
            input_output_aliases={at + k: first_held + k for k in range(len(held))},
            compiler_params=params(len(grid)),
            cost_estimate=pl.CostEstimate(
                flops=COST[name] * 250_000_000, bytes_accessed=COST[name] * 750_000, transcendentals=0
            ),
            name=name,
        )(*(() if scalar is None else (scalar,)), *ins, *extra)
        self.token = (out[0],)
        return out


def loose(n):
    return [pl.BlockSpec(memory_space=pl.ANY)] * n


def mm(a, b):
    return jnp.dot(a, b, preferred_element_type=f32)


def mm_nt(a, b):
    return lax.dot_general(a, b, NT, preferred_element_type=f32)


def mm_tn(a, b):
    return lax.dot_general(a, b, TN, preferred_element_type=f32)


def split(x):
    hi = x.astype(bf16)
    return hi, (x - hi.astype(f32)).astype(bf16)


def head_sum(x, ones):
    hi, lo = split(x)
    return mm(hi, ones) + mm(lo, ones)


def head_ones(n):
    a = lax.broadcasted_iota(jnp.int32, (n, n), 0) // HD
    b = lax.broadcasted_iota(jnp.int32, (n, n), 1) // HD
    return (a == b).astype(bf16)


def halves(n):
    lane = lax.broadcasted_iota(jnp.int32, (1, n), 1)
    return (lane < HD, lane >= HD)


def keep(x, mask):
    return jnp.where(mask, x, jnp.zeros_like(x))


def inv_rms(x):
    return lax.rsqrt(jnp.mean(x * x, -1, keepdims=True) + EPS)


def row(ref, k):
    return ref[k : k + 1, :]


def whole(shape):
    zeros = (0,) * len(shape)
    return pl.BlockSpec(shape, lambda *_: zeros, pipeline_mode=pl.Buffered(1))


def rows_of(br, width, first=0):
    return pl.BlockSpec((br, width), lambda i, *_: (i, first))


def accumulate(ref, value, first):
    @pl.when(first)
    def _():
        ref[...] = value

    @pl.when(jnp.logical_not(first))
    def _():
        ref[...] += value


def col_sum(x):
    return jnp.sum(x, 0, keepdims=True)


def tile3(t, n):
    return jnp.concatenate([t] * (n // t.shape[1]), 1)


def key_kernel(p_ref, v_ref, w_ref, wv_ref, c_ref, s1_ref, s2_ref, hg_ref, a_ref, kr_ref, k_ref, vv_ref):
    x = p_ref[...].astype(f32)
    a = (x * inv_rms(x) * row(v_ref, 0)).astype(bf16)
    a_ref[...] = a
    k = mm(a, w_ref[0])
    kr_ref[...] = k
    k_ref[...] = turned(k, row(hg_ref, 1), (c_ref, s1_ref, s2_ref)).astype(bf16)
    vv_ref[...] = mm(a, wv_ref[0]).astype(bf16)


def turned(y, gain, tabs):
    n = y.shape[1]
    cos, s1, s2 = (tile3(t[...], n) for t in tabs)
    z = y * lax.rsqrt(head_sum(y * y, head_ones(n)) * (1.0 / HD) + EPS) * gain
    return z * cos + pltpu.roll(z, n - 16, 1) * s1 + pltpu.roll(z, 16, 1) * s2


def query_kernel(a_ref, wq_ref, c_ref, s1_ref, s2_ref, hg_ref, qr_ref, q_ref):
    q = mm(a_ref[...], wq_ref[0])
    qr_ref[...] = q
    q_ref[...] = (turned(q, row(hg_ref, 0), (c_ref, s1_ref, s2_ref)) * (0.125 * LOG2E)).astype(bf16)


def one_weight(w, k):
    return pl.BlockSpec((1, *w.shape[1:]), lambda *_: (k, 0, 0), pipeline_mode=pl.Buffered(1))


def key_call(order, patches, vec, w, tabs, hg, after, br=256):
    t, d = patches.shape
    n = w.shape[2]
    return order.run(
        "key",
        key_kernel,
        (t // br,),
        (patches, vec, w, w, *tabs, hg),
        [rows_of(br, d), whole(vec.shape), one_weight(w, 1), one_weight(w, 2)] + [rows_of(br, 128)] * 3 + [whole(hg.shape)],
        [rows_of(br, d)] + [rows_of(br, n)] * 3,
        [sds((t, d), bf16), sds((t, n), f32), sds((t, n), bf16), sds((t, n), bf16)],
        after=after,
    )


def query_call(order, a, w, tabs, hg, after, br=256):
    t, d = a.shape
    n = w.shape[2]
    return order.run(
        "query",
        query_kernel,
        (t // br,),
        (a, w, *tabs, hg),
        [rows_of(br, d), one_weight(w, 0)] + [rows_of(br, 128)] * 3 + [whole(hg.shape)],
        [rows_of(br, n)] * 2,
        [sds((t, n), f32), sds((t, n), bf16)],
        after=after,
    )


def soft_sums(q, k, v, mask):
    e = jnp.exp2(mm_nt(q, keep(k, mask))).astype(bf16)
    return mm(e, jnp.where(mask, v, jnp.ones_like(v)))


def item_block(j, s):
    return jnp.minimum(j, s[0] - 1)


def attend_kernel(sc, q_ref, k_ref, v_ref, ck_ref, cv_ref, tg_ref, mix_ref, o_ref, li_ref, acc):
    j = pl.program_id(1)
    masks = halves(128)
    keys = 512

    @pl.when(j == 0)
    def _():
        acc[...] = jnp.zeros_like(acc)

    @pl.when(j < sc[0])
    def _():
        q = q_ref[...]
        for h in range(2):
            total = acc[h]
            for c in range(k_ref.shape[0] // keys):
                at = slice(c * keys, (c + 1) * keys)
                total = total + soft_sums(q, k_ref[at, :], v_ref[at, :], masks[h])
            acc[h] = total

    @pl.when(j == SPAN - 1)
    def _():
        q = q_ref[...]

        def finish(a0, a1):
            inverse = 1.0 / jnp.where(masks[0], pltpu.roll(a0, HD, 1), pltpu.roll(a1, HD, 1))
            return jnp.where(masks[0], a0, a1) * inverse, inverse

        o, li = finish(acc[0], acc[1])
        c0, c1 = (soft_sums(q, ck_ref[...], cv_ref[...], m) for m in masks)
        mix_ref[...] = (o + tg_ref[...] * finish(c0, c1)[0]).astype(bf16)
        o_ref[...] = o.astype(bf16)
        li_ref[...] = li


def attend_call(order, sc, q, k, v, cap, text, tg, at, bq):
    n = q.shape[1]
    pairs = n // 128
    block = k.shape[0] // SPAN
    mine = lambda p, j, s: (0, p)
    other = lambda p, j, s: (item_block(j, s), p)
    return order.run(
        "attend",
        attend_kernel,
        (pairs, SPAN),
        (q, k, v, cap, cap, tg),
        [
            pl.BlockSpec((bq, 128), lambda p, j, s: (at, p)),
            pl.BlockSpec((block, 128), other),
            pl.BlockSpec((block, 128), other),
            pl.BlockSpec((text, 128), lambda p, j, s: (s[1 + SPAN], p)),
            pl.BlockSpec((text, 128), lambda p, j, s: (s[1 + SPAN], pairs + p)),
            pl.BlockSpec((1, 128), mine),
        ],
        [pl.BlockSpec((bq, 128), mine)] * 3,
        [sds((bq, n), bf16), sds((bq, n), bf16), sds((bq, n), f32)],
        [pltpu.VMEM((2, bq, 128), f32)],
        sc,
    )


def caption_back_kernel(sc, q_ref, da_ref, db_ref, ck_ref, cv_ref, tg_ref, dq_ref, dk_ref, dv_ref, gs_ref):
    masks = halves(128)
    q, d = q_ref[...], jnp.concatenate([da_ref[...], db_ref[...]], 0)
    dq = jnp.zeros(q.shape, f32)
    dk = jnp.zeros(ck_ref.shape, f32)
    dv = jnp.zeros(ck_ref.shape, f32)
    sums = []
    for h in range(2):
        ck, cv = keep(ck_ref[...], masks[h]), keep(cv_ref[...], masks[h])
        gate = tg_ref[:, h * HD : h * HD + 1]
        e = jnp.exp2(mm_nt(q, ck))
        prob = e * (1.0 / jnp.sum(e, -1, keepdims=True))
        dp = mm_nt(d, cv)
        m = jnp.sum(prob * dp, -1, keepdims=True)
        dc = (prob * (dp - m) * gate).astype(bf16)
        dq = dq + mm(dc, ck)
        dk = dk + mm_tn(dc, keep(q, masks[h]))
        dv = dv + mm_tn(prob.astype(bf16), keep(d, masks[h]))
        sums.append(jnp.sum(m, 0, keepdims=True))
    dq_ref[...] = dq * 0.125
    dk_ref[...] = dk * (1.0 / LOG2E)
    dv_ref[...] = dv * tg_ref[...]
    gs_ref[...] = jnp.where(masks[0], sums[0], sums[1])


def caption_back_call(order, sc, q, da, db, cap, text, tg, h):
    n = q.shape[1]
    pairs = n // 128
    bq = 2 * BR
    mine = lambda p, s: (0, p)
    return order.run(
        "caption_back",
        caption_back_kernel,
        (pairs,),
        (q, da, db, cap, cap, tg),
        [
            pl.BlockSpec((bq, 128), lambda p, s: (h, p)),
            pl.BlockSpec((BR, 128), mine),
            pl.BlockSpec((BR, 128), mine),
            pl.BlockSpec((text, 128), lambda p, s: (s[1 + SPAN], p)),
            pl.BlockSpec((text, 128), lambda p, s: (s[1 + SPAN], pairs + p)),
            pl.BlockSpec((1, 128), mine),
        ],
        [
            pl.BlockSpec((bq, 128), mine),
            pl.BlockSpec((text, 128), mine),
            pl.BlockSpec((text, 128), mine),
            pl.BlockSpec((1, 128), mine),
        ],
        [sds((bq, n), f32), sds((text, n), f32), sds((text, n), f32), sds((1, n), f32)],
        scalar=sc,
    )


def minus_delta(rows, head):
    lane = lax.broadcasted_iota(jnp.int32, (rows, 128), 1)
    return jnp.where((lane >= 3 * head) & (lane < 3 * head + 3), -1.0, 0.0).astype(bf16)


def dq_kernel(sc, q_ref, d_ref, x_ref, k_ref, v_ref, c_ref, dq_ref, acc):
    pair = pl.program_id(0)
    j = pl.program_id(1)
    masks = halves(128)
    keys = 512

    @pl.when(j == 0)
    def _():
        acc[...] = jnp.zeros_like(acc)

    @pl.when(j < sc[0])
    def _():
        q = q_ref[...]
        dx = jnp.concatenate([d_ref[...], x_ref[...]], 1)
        total = acc[...]
        for h in range(2):
            off = minus_delta(keys, 2 * pair + h)
            for c in range(k_ref.shape[0] // keys):
                at = slice(c * keys, (c + 1) * keys)
                k = keep(k_ref[at, :], masks[h])
                e = jnp.exp2(mm_nt(q, k))
                dp = mm_nt(dx, jnp.concatenate([keep(v_ref[at, :], masks[h]), off], 1))
                total = total + mm((e * dp).astype(bf16), k)
        acc[...] = total

    @pl.when(j == SPAN - 1)
    def _():
        dq_ref[...] = acc[...] * 0.125 + c_ref[...]


def dq_call(order, sc, q, d, k, v, cap_dq, h, after=()):
    n = q.shape[1]
    pairs = n // 128
    block = k.shape[0] // SPAN
    bq = 2 * BR
    mine = lambda p, j, s: (0, p)
    extra = lambda p, j, s: (0, pairs)
    other = lambda p, j, s: (item_block(j, s), p)
    return order.run(
        "dq",
        dq_kernel,
        (pairs, SPAN),
        (q, d, d, k, v, cap_dq),
        [
            pl.BlockSpec((bq, 128), lambda p, j, s: (h, p)),
            pl.BlockSpec((bq, 128), mine),
            pl.BlockSpec((bq, 128), extra),
            pl.BlockSpec((block, 128), other),
            pl.BlockSpec((block, 128), other),
            pl.BlockSpec((bq, 128), mine),
        ],
        [pl.BlockSpec((bq, 128), mine)],
        [sds((bq, n), f32)],
        [pltpu.VMEM((bq, 128), f32)],
        sc,
        after=after,
    )[0]


def dkv_kernel(parts, base, sc, k_ref, v_ref, q_ref, *rest):
    d_refs, x_refs = rest[0 : 2 * parts : 2], rest[1 : 2 * parts : 2]
    dk_ref, dv_ref = rest[2 * parts :]
    pair = base + pl.program_id(0)
    j = pl.program_id(1)
    masks = halves(128)
    queries = 2 * BR

    @pl.when(j == 0)
    def _():
        dk_ref[...] = jnp.zeros_like(dk_ref)
        dv_ref[...] = jnp.zeros_like(dv_ref)

    @pl.when(j < sc[0])
    def _():
        dk, dv = dk_ref[...], dv_ref[...]
        for h in range(2):
            vx = jnp.concatenate([keep(v_ref[...], masks[h]), minus_delta(v_ref.shape[0], 2 * pair + h)], 1)
            for r in range(parts):
                q = keep(q_ref[r * queries : (r + 1) * queries, :], masks[h])
                d, x = d_refs[r][...], x_refs[r][...]
                e = jnp.exp2(mm_nt(k_ref[...], q))
                dp = mm_nt(vx, jnp.concatenate([d, x], 1))
                dv = dv + mm(e.astype(bf16), keep(d, masks[h]))
                dk = dk + mm((e * dp).astype(bf16), q)
        dk_ref[...] = dk
        dv_ref[...] = dv


def dkv_call(order, sc, k, v, q_all, ds, half, base, n_pairs):
    t, n = k.shape
    pairs = n // 128
    rows = 2 * BR
    mine = pl.BlockSpec((rows, 128), lambda p, j, s: (half, base + p))
    out = pl.BlockSpec((rows, 128), lambda p, j, s: (0, p))
    other = pl.BlockSpec((rows, 128), lambda p, j, s: (item_block(j, s), base + p))
    extra = pl.BlockSpec((rows, 128), lambda p, j, s: (item_block(j, s), pairs))
    return order.run(
        "dkv",
        functools.partial(dkv_kernel, len(ds), base),
        (n_pairs, SPAN),
        (k, v, q_all, *(x for d in ds for x in (d, d))),
        [mine, mine, pl.BlockSpec((t, 128), lambda p, j, s: (s[1 + SPAN + j], base + p))] + [other, extra] * len(ds),
        [out, out],
        [sds((rows, n_pairs * 128), f32)] * 2,
        scalar=sc,
    )


def chunk_call(order, kernel, name, c, ins, specs, chunk_outs, sum_outs, whole_outs, before):
    one = lambda r, w: pl.BlockSpec((r, w), lambda i: (0, 0))
    own = chunk_outs + sum_outs
    into = [pl.BlockSpec((BR, w), lambda i, at=c % (r // BR): (at, 0)) for r, w, _ in whole_outs]
    return order.run(
        name,
        kernel,
        (1,),
        ins,
        specs,
        [one(r, w) for r, w, _ in own] + into,
        [sds((r, w), k) for r, w, k in own + whole_outs],
        held=tuple(before),
        first_held=len(own),
    )


def part(c, width):
    return pl.BlockSpec((BR, width), lambda i: (c, 0))


def alone(width):
    return pl.BlockSpec((BR, width), lambda i: (0, 0))


def pair_grad_kernel(a_ref, b_ref, c_ref, d_ref, o_ref):
    n = b_ref.shape[1]
    o_ref[:, :n] = mm_tn(a_ref[...], b_ref[...]).astype(bf16)
    o_ref[:, n:] = mm_tn(c_ref[...], d_ref[...]).astype(bf16)


def pair_grad_call(order, a, b, c, d, part=0, parts=1, before=(), after=()):
    t, m = a.shape
    n, k = b.shape[1], d.shape[1]
    blk = 256
    steps = m // blk // parts
    cols = pl.BlockSpec((t, blk), lambda i: (0, part * steps + i))
    return order.run(
        "pair_grad",
        pair_grad_kernel,
        (steps,),
        (a, b, c, d),
        [cols, whole(b.shape), cols, whole(d.shape)],
        [pl.BlockSpec((blk, n + k), lambda i: (part * steps + i, 0))],
        [sds((m, n + k), bf16)],
        held=before,
        after=after,
    )


def ffn_kernel(p_ref, at_ref, v_ref, wg_ref, wd_ref, mid_ref, gu_ref, f_ref, a_ref, h_ref):
    at = at_ref[...].astype(f32)
    mid = p_ref[...].astype(f32) + row(v_ref, 1) * (at * inv_rms(at))
    mid_ref[...] = mid
    a = (mid * inv_rms(mid) * row(v_ref, 2)).astype(bf16)
    a_ref[...] = a
    g = mm(a, wg_ref[0])
    u = mm(a, wg_ref[1])
    n = g.shape[1]
    gu_ref[:, :n] = g.astype(bf16)
    gu_ref[:, n:] = u.astype(bf16)
    h = (g * jax.nn.sigmoid(g) * u).astype(bf16)
    h_ref[...] = h
    f_ref[...] = mm(h, wd_ref[...]).astype(bf16)


def ffn_call(order, c, patches, at, vec, wg, wd, before):
    t, d = patches.shape
    n = wd.shape[0]
    return chunk_call(
        order,
        ffn_kernel,
        "ffn",
        c,
        (patches, at, vec, wg, wd),
        [part(c, d), alone(d), whole(vec.shape), whole(wg.shape), whole(wd.shape)],
        [(BR, d, f32), (BR, 2 * n, bf16), (BR, d, bf16)],
        [],
        [(t, d, bf16), (t, n, bf16)],
        before,
    )


def ffn_back_kernel(f_ref, mid_ref, c_ref, gu_ref, v_ref, wg_ref, wd_ref, da_ref, cs_ref, y_ref, df_ref, dgu_ref):
    f = f_ref[...].astype(f32)
    cot = c_ref[...].astype(f32)
    r = inv_rms(f)
    fh = f * r
    y_ref[...] = (mid_ref[...] + row(v_ref, 3) * fh).astype(bf16)
    z = cot * row(v_ref, 3)
    df = (r * (z - fh * jnp.mean(z * fh, -1, keepdims=True))).astype(bf16)
    df_ref[...] = df
    cs_ref[...] = col_sum(cot * fh)
    dh = mm_nt(df, wd_ref[...])
    n = dh.shape[1]
    g = gu_ref[:, :n].astype(f32)
    u = gu_ref[:, n:].astype(f32)
    s = jax.nn.sigmoid(g)
    gs = g * s
    dg = (dh * u * (s + gs * (1.0 - s))).astype(bf16)
    du = (dh * gs).astype(bf16)
    dgu_ref[:, :n] = dg
    dgu_ref[:, n:] = du
    da_ref[...] = (mm_nt(dg, wg_ref[0]) + mm_nt(du, wg_ref[1])).astype(bf16)


def ffn_back_call(order, c, f, mid, cot, gu, vec, wg, wd, before):
    t, d = cot.shape
    n = wd.shape[0]
    return chunk_call(
        order,
        ffn_back_kernel,
        "ffn_back",
        c,
        (f, mid, cot, gu, vec, wg, wd),
        [alone(d), alone(d), part(c, d), alone(2 * n), whole(vec.shape), whole(wg.shape), whole(wd.shape)],
        [(BR, d, bf16)],
        [(1, d, f32)],
        [(t, d, bf16), (t, d, bf16), (t, 2 * n, bf16)],
        before,
    )


def out_back_kernel(da_ref, mid_ref, at_ref, c_ref, v_ref, w_ref, o_ref, li_ref, dm_ref, dx_ref, c3_ref, c2_ref, dat_ref, ds_ref):
    da = da_ref[...].astype(f32)
    mid = mid_ref[...]
    r = inv_rms(mid)
    mh = mid * r
    z = da * row(v_ref, 2)
    dm = c_ref[...].astype(f32) + r * (z - mh * jnp.mean(z * mh, -1, keepdims=True))
    dm_ref[...] = dm
    c3_ref[...] = col_sum(da * mh)
    at = at_ref[...].astype(f32)
    ra = inv_rms(at)
    ah = at * ra
    c2_ref[...] = col_sum(dm * ah)
    z = dm * row(v_ref, 1)
    dat = (ra * (z - ah * jnp.mean(z * ah, -1, keepdims=True))).astype(bf16)
    dat_ref[...] = dat
    dx = mm_nt(dat, w_ref[...]).astype(bf16)
    dx_ref[...] = dx
    n = dx.shape[1]
    ds = dx.astype(f32) * li_ref[...]
    ds_ref[:, :n] = ds.astype(bf16)
    hi, lo = split(ds * o_ref[...].astype(f32))
    head = lax.broadcasted_iota(jnp.int32, (n, 128), 0) // HD
    lane = lax.broadcasted_iota(jnp.int32, (n, 128), 1)
    to_lanes = (lane // 3 == head).astype(bf16)
    delta = mm(hi, to_lanes) + mm(lo, to_lanes)
    one = delta.astype(bf16).astype(f32)
    two = (delta - one).astype(bf16).astype(f32)
    which = lax.broadcasted_iota(jnp.int32, (1, 128), 1) % 3
    ds_ref[:, n:] = jnp.where(which == 0, one, jnp.where(which == 1, two, delta - one - two)).astype(bf16)


def out_back_call(order, c, da, mid, at, cot, vec, w, o, li, place, before):
    t, d = cot.shape
    n = w.shape[0]
    return chunk_call(
        order,
        out_back_kernel,
        "out_back",
        c,
        (da, mid, at, cot, vec, w, o, li),
        [alone(d), alone(d), alone(d), part(c, d), whole(vec.shape), whole(w.shape), part(place, n), part(place, n)],
        [(BR, d, f32), (BR, n, bf16)],
        [(1, d, f32), (1, d, f32)],
        [(t, d, bf16), (2 * BR, n + 128, bf16)],
        before,
    )


def dqkv_kernel(pairs, dq_ref, *refs):
    dk_refs, dv_refs = refs[0 : 2 * pairs : 2], refs[1 : 2 * pairs : 2]
    (qr_ref, kr_ref, c_ref, s1_ref, s2_ref, hg_ref, w_ref, p_ref, da_ref, hs_ref, cs_ref, d_ref) = refs[2 * pairs :]
    side = lambda parts: jnp.concatenate([x[...] for x in parts], 1)
    n = dq_ref.shape[1]
    ones = head_ones(n)
    cos, s1, s2 = (tile3(t[...], n) for t in (c_ref, s1_ref, s2_ref))

    def back(dy, x, gain):
        dz = dy * cos - pltpu.roll(dy, 16, 1) * s2 - pltpu.roll(dy, n - 16, 1) * s1
        r = lax.rsqrt(head_sum(x * x, ones) * (1.0 / HD) + EPS)
        xh = x * r
        g = dz * gain
        return r * (g - xh * (head_sum(g * xh, ones) * (1.0 / HD))), col_sum(dz * xh)

    dq, hq = back(dq_ref[...], qr_ref[...], row(hg_ref, 0))
    dk, hk = back(side(dk_refs) * (1.0 / LOG2E), kr_ref[...], row(hg_ref, 1))
    dql, dkl, dvl = dq.astype(bf16), dk.astype(bf16), side(dv_refs).astype(bf16)
    d_ref[:, :n] = dql
    d_ref[:, n : 2 * n] = dkl
    d_ref[:, 2 * n :] = dvl
    da = mm_nt(dql, w_ref[0]) + mm_nt(dkl, w_ref[1]) + mm_nt(dvl, w_ref[2])
    da_ref[...] = da.astype(bf16)
    x = p_ref[...].astype(f32)
    cs_ref[...] = col_sum(da * (x * inv_rms(x)))
    hs_ref[0:1, :] = hq
    hs_ref[1:2, :] = hk


def dqkv_call(order, c, dq, dkv, qr, kr, tabs, hg, w, patches, before):
    t, d = patches.shape
    n = dq.shape[1]
    return chunk_call(
        order,
        functools.partial(dqkv_kernel, len(dkv)),
        "dqkv",
        c,
        (dq, *(x for two in dkv for x in two), qr, kr, *tabs, hg, w, patches),
        [part(c % 2, n)] + [part(c % 2, x.shape[1]) for two in dkv for x in two] + [part(c, n)] * 2 + [part(c, 128)] * 3 + [whole(hg.shape), whole(w.shape), part(c, d)],
        [(BR, d, bf16)],
        [(2, n, f32), (1, d, f32)],
        [(t, 3 * n, bf16)],
        before,
    )


def last_kernel(da_ref, p_ref, dm_ref, v_ref, o_ref):
    x = p_ref[...].astype(f32)
    r = inv_rms(x)
    xh = x * r
    z = da_ref[...].astype(f32) * row(v_ref, 0)
    o_ref[...] = (dm_ref[...] + r * (z - xh * jnp.mean(z * xh, -1, keepdims=True))).astype(bf16)


def last_call(order, c, da, patches, dm, vec, before):
    t, d = patches.shape
    return chunk_call(
        order,
        last_kernel,
        "last",
        c,
        (da, patches, dm, vec),
        [alone(d), part(c, d), alone(d), whole(vec.shape)],
        [],
        [],
        [(t, d, bf16)],
        before,
    )


def caption_grad_kernel(dk_ref, dv_ref, kr_ref, hg_ref, d_ref, hs_ref):
    n = dk_ref.shape[1]
    ones = head_ones(n)
    x = kr_ref[...]
    r = lax.rsqrt(head_sum(x * x, ones) * (1.0 / HD) + EPS)
    xh = x * r
    dy = dk_ref[...]
    g = dy * row(hg_ref, 2)
    d_ref[:, :n] = (r * (g - xh * (head_sum(g * xh, ones) * (1.0 / HD)))).astype(bf16)
    d_ref[:, n:] = dv_ref[...].astype(bf16)
    hs_ref[...] = col_sum(dy * xh)


def caption_norm_kernel(kr_ref, v_ref, hg_ref, o_ref):
    n = kr_ref.shape[1]
    x = kr_ref[...]
    r = lax.rsqrt(head_sum(x * x, head_ones(n)) * (1.0 / HD) + EPS)
    o_ref[:, :n] = (x * r * row(hg_ref, 2)).astype(bf16)
    o_ref[:, n:] = v_ref[...].astype(bf16)


def swap(x, axis, size, m):
    return lax.ppermute(x, axis, [(i, i ^ m) for i in range(size)])


def pick_kernel(count, n_arrays, n_pieces, sc, *refs):
    outs, sem = refs[n_arrays * n_pieces :][:n_arrays], refs[-1]
    for k, out in enumerate(outs):
        pieces = refs[k * n_pieces : (k + 1) * n_pieces]
        rows = pieces[0].shape[0]
        for j in range(count):
            for m in range(n_pieces):

                @pl.when(sc[1 + j] == m)
                def _():
                    pltpu.make_async_copy(pieces[m], out.at[pl.ds(j * rows, rows)], sem.at[k, j]).start()

    for k, out in enumerate(outs):
        first = refs[k * n_pieces]
        rows = first.shape[0]
        for j in range(count):
            pltpu.make_async_copy(first, out.at[pl.ds(j * rows, rows)], sem.at[k, j]).wait()


class Gather:
    def __init__(self, a, b):
        self.all = None
        if lax.axis_size("wide") != 8:
            self.first = self.second = ()
            self.all = [lax.all_gather(x, "wide") for x in (a, b)]
            return
        send = lambda x, pairs: lax.ppermute(x, "wide", pairs)
        over_x = [(i, i ^ 2) for i in range(8)]
        over_y = [(1, 5), (4, 0), (3, 7), (6, 2)]
        a2, a4, b4, b2 = send(a, over_x), send(a, over_y), send(b, over_y), send(b, over_x)
        a6 = send(a2, [(0, 4), (1, 5), (6, 2), (7, 3)])
        b6x, b6y = send(b2, [(0, 4), (7, 3)]), send(b4, [(7, 5), (0, 2)])
        self.first = (a2, a4, b4, b2)
        self.second = (a6, b6x, b6y)
        self.kept = ((a, a2, a4, a6), (b, b2, b4, b6x + b6y))

    def pieces(self):
        if self.all is not None:
            return self.all
        return [[y for x in four for y in (x, swap(x, "wide", 8, 1))] for four in self.kept]


class GatherOne:
    def __init__(self, a):
        self.all = None
        if lax.axis_size("wide") != 8:
            self.first = self.second = ()
            self.all = [lax.all_gather(a, "wide")]
            return
        send = lambda x, pairs: lax.ppermute(x, "wide", pairs)
        a2 = send(a, [(i, i ^ 2) for i in range(8)])
        a4 = send(a, [(1, 5), (4, 0), (3, 7), (6, 2)])
        a6 = send(a2, [(0, 4), (1, 5), (6, 2), (7, 3)])
        self.first, self.second = (a2, a4), (a6,)
        self.kept = ((a, a2, a4, a6),)

    pieces = Gather.pieces


def pick(order, sc, pieces, count):
    if not isinstance(pieces[0], list):
        one = lambda x, j: lax.dynamic_index_in_dim(x, sc[1 + SPAN + j], 0, False)
        return [jnp.concatenate([one(x, j) for j in range(count)]) for x in pieces]
    outs = [(count * p[0].shape[0], p[0].shape[1]) for p in pieces]
    return order.run(
        "pick",
        functools.partial(pick_kernel, count, len(pieces), 8),
        (1,),
        [x for p in pieces for x in p],
        loose(8 * len(pieces)),
        [pl.BlockSpec(shape, lambda i, s: (0, 0)) for shape in outs],
        [sds(shape, bf16) for shape in outs],
        [pltpu.SemaphoreType.DMA((len(pieces), count))],
        sc,
    )


def tree(parts):
    while len(parts) > 1:
        parts = [a + b for a, b in zip(parts[::2], parts[1::2])]
    return parts[0]


def pack_kernel(count, place, *refs):
    c1, hs = refs[:count], refs[count : 2 * count]
    hc_ref, gs_ref, tg_ref, c2_ref, c3_ref, c4_ref, o_ref = refs[2 * count :]
    n = hc_ref.shape[1]
    o_ref[...] = jnp.zeros_like(o_ref)
    o_ref[0:1, :] = sum(x[...] for x in c1)
    o_ref[1:2, :] = c2_ref[...]
    o_ref[2:3, :] = c3_ref[...]
    o_ref[3:4, :] = c4_ref[...]
    qk = sum(x[...] for x in hs)
    o_ref[4:5, :n] = qk[0:1]
    o_ref[4:5, n : 2 * n] = qk[1:2]
    o_ref[4:5, 2 * n : 3 * n] = hc_ref[...]
    gate = gs_ref[...] * (1.0 - tg_ref[...] * tg_ref[...])
    for z in range(o_ref.shape[1] // n):
        o_ref[5:6, z * n : (z + 1) * n] = jnp.where(place[0] == z, gate, 0.0)


def pack_call(order, c1, hs, hc, gs, tg, c2, c3, c4, place):
    d = c2.shape[1]
    ins = (*c1, *hs, hc, gs, tg, c2, c3, c4)
    spec = lambda x: pl.BlockSpec(x.shape, lambda i, s: (0, 0))

    def kernel(place, *refs):
        pack_kernel(len(c1), place, *refs)

    return order.run(
        "note",
        kernel,
        (1,),
        ins,
        [spec(x) for x in ins],
        [pl.BlockSpec((8, d), lambda i, s: (0, 0))],
        [sds((8, d), f32)],
        scalar=place.astype(jnp.int32).reshape(1),
    )[0]


def fold_kernel(*refs):
    parts, o_ref = refs[:-1], refs[-1]
    total = tree([x[...] for x in parts])
    row_at = lax.broadcasted_iota(jnp.int32, total.shape, 0)
    o_ref[...] = jnp.where((row_at >= 1) & (row_at < 4), parts[0][...], total)


def fold_call(order, parts):
    spec = pl.BlockSpec(parts[0].shape, lambda i: (0, 0))
    return order.run("note", fold_kernel, (1,), parts, [spec] * len(parts), [spec], [sds(parts[0].shape, f32)])


def pin_kernel(o_ref):
    pass


def pin(order, x, after=()):
    return order.run("pin", pin_kernel, (1,), (), [], loose(1), [sds(x.shape, x.dtype)], held=(x,), after=after)[0]


def gather_now(x, axis):
    n = x.shape[0]
    wide = -(-n // 1024) * 1024
    padded = jnp.pad(x, (0, wide - n)).reshape(1, 8, wide // 8)
    return lax.all_gather(padded, axis, axis=0, tiled=True).reshape(-1, wide)[:, :n]


def hop_kernel(have, sc, *refs):
    ins = dict(zip(have["in"], refs))
    outs = dict(zip(have["out"], refs[len(have["in"]) :]))
    end = sc[0] == 1
    if "total" in outs:
        outs["total"][...] = jnp.where(end, ins["r1"][...], ins["send"][...])
    third = None
    if "second" in ins:
        third = ins["second"][...] + ins["r2"][...]
    if "second" in outs:
        outs["second"][...] = ins["x"][...] + ins["r1"][...]
    if "send" in outs:
        new = ins["new"][...] if "new" in ins else third
        outs["send"][...] = new if third is None else jnp.where(end, new, third)


class Line:
    def __init__(self, order, place):
        self.order = order
        self.end = ((place == 0) | (place == 3)).astype(jnp.int32).reshape(1)
        self.x = self.second = self.send = None
        self.third = False

    def step(self, new, after=()):
        if self.send is None:
            self.x = self.send = new
            return None
        go = lambda x, perm: lax.ppermute(x, "narrow", perm)
        ins = {"r1": go(self.send, [(0, 1), (3, 2), (1, 0), (2, 3)])}
        outs = []
        if self.third:
            ins["send"] = self.send
            outs.append("total")
        if self.second is not None:
            ins["r2"] = go(self.second, [(1, 2), (2, 1)])
            ins["second"] = self.second
        if self.x is not None:
            ins["x"] = self.x
            outs.append("second")
        if new is not None:
            ins["new"] = new
        if new is not None or self.second is not None:
            outs.append("send")
        like = ins["r1"]
        block = pl.BlockSpec((BR // 2, like.shape[1]), lambda i, s: (i, 0))
        got = self.order.run(
            "hop",
            functools.partial(hop_kernel, {"in": list(ins), "out": outs}),
            (2,),
            list(ins.values()),
            [block] * len(ins),
            [block] * len(outs),
            [sds(like.shape, like.dtype)] * len(outs),
            scalar=self.end,
            after=after,
        )
        got = dict(zip(outs, got))
        self.third = self.second is not None
        self.x, self.second, self.send = new, got.get("second"), got.get("send")
        return got.get("total")


class Sums:
    def __init__(self, order, size, place):
        self.line = Line(order, place) if size == 4 else None
        self.names, self.done = [], {}

    def add(self, name, x, after=()):
        if self.line is None:
            self.done[name] = lax.psum(x, "narrow")
            return
        if self.line.send is None:
            self.names = [None]
        self._step(name, x, after)

    def _step(self, name, x, after):
        total = self.line.step(x, after)
        self.names.append(name)
        if total is not None:
            self.done[self.names[-4]] = total

    def get(self, name, after=()):
        while name not in self.done:
            self._step(None, None, after)
            after = ()
        return self.done[name]


def scatter_rows(x):
    return lax.psum_scatter(x.astype(bf16), "wide", scatter_dimension=0, tiled=True)


def rope_tables(position, width):
    lane = jnp.arange(128, dtype=jnp.int32)
    within = lane % HD
    quarter = HD // 4
    frequency = 10000.0 ** (-(within % quarter).astype(f32) / quarter)
    by_row = within < HD // 2
    where = jnp.where(by_row[None, :], (position // width)[:, None], (position % width)[:, None])
    angle = where.astype(f32) * frequency[None, :]
    cos, sin = jnp.cos(angle), jnp.sin(angle)
    former = (within % (HD // 2) < quarter)[None, :]
    return cos, jnp.where(former, -sin, 0.0), jnp.where(former, 0.0, sin)


def local(
    patches,
    cotangent,
    conditioning,
    captions,
    item_lengths,
    grid_widths,
    w_ada,
    norm_gains,
    w_qkv,
    head_gains,
    cross_gate,
    w_caption,
    w_out,
    w_gate_up,
    w_down,
):
    t, d = patches.shape
    n = w_qkv.shape[2]
    heads = n // HD
    ada = w_ada.shape[2]
    ff = w_down.shape[0]
    text = captions.shape[0]
    cd = conditioning.shape[1]
    count = lax.axis_size("wide")
    deep = lax.axis_size("narrow")
    me = lax.axis_index("wide")
    mz = lax.axis_index("narrow")

    slots = item_lengths.shape[0]
    spans = item_lengths // t
    order = jnp.arange(slots, dtype=jnp.int32)
    ends = jnp.sum(jnp.where(order[None, :] <= order[:, None], spans[None, :], 0), 1)
    blocks = jnp.arange(count, dtype=jnp.int32)
    item = jnp.sum((ends[None, :] <= blocks[:, None]).astype(jnp.int32), 1)
    is_item = item[:, None] == order[None, :]
    choose = lambda values: jnp.sum(jnp.where(is_item, values[None, :], 0), 1)
    firsts = choose(ends - spans)
    mine = blocks == me
    of_me = lambda values: jnp.sum(jnp.where(mine, values, 0))
    first = of_me(firsts)
    length = of_me(choose(spans))
    width = of_me(choose(grid_widths))
    position = (me - first) * t + jnp.arange(t, dtype=jnp.int32)
    tabs = rope_tables(position, width)
    steps = first + jnp.minimum(jnp.arange(SPAN, dtype=jnp.int32), length - 1)
    places = steps ^ me if count == 8 else steps
    sc = jnp.concatenate([length.reshape(1), places, steps]).astype(jnp.int32)

    cond = conditioning.astype(f32)[0]
    silu_low = jax.nn.silu(cond).astype(bf16)
    mod = jnp.sum(silu_low.astype(f32)[:, None, None] * w_ada.astype(f32), 0)
    share = cd // deep
    sent = jnp.concatenate([mod.reshape(-1), lax.dynamic_slice_in_dim(cond, mz * share, share)])
    got = gather_now(gather_now(sent, "narrow").reshape(-1), "wide").reshape(count, deep, -1)
    mods = got[:, :, : 4 * ada].reshape(count, deep, 4, ada).transpose(0, 2, 1, 3).reshape(count, 4, d)
    conds = got[:, :, 4 * ada :].reshape(count, cd)
    my_mod = lax.dynamic_index_in_dim(mods, first, 0, False)
    of_block = jnp.sum(jnp.where((firsts[:, None] == blocks[None, :])[:, :, None, None], mods[None], 0.0), 1)
    scales = 1.0 + of_block
    gates = jnp.tanh(of_block)
    factor = jnp.stack([1.0 + my_mod[0], jnp.tanh(my_mod[1]), 1.0 + my_mod[2], jnp.tanh(my_mod[3])])
    vec = norm_gains * factor
    hg = jnp.tile(head_gains, (1, heads))
    tg_heads = jnp.tanh(cross_gate)
    tg = jnp.repeat(tg_heads, HD)[None, :]

    order = Order()
    cap_raw = jnp.einsum("kd,jde->jke", captions, w_caption, preferred_element_type=f32)
    whole_cap = pl.BlockSpec((text, n), lambda i: (0, 0))
    both_cap = pl.BlockSpec((text, 2 * n), lambda i: (0, 0))
    (cap,) = order.run(
        "caption_norm",
        caption_norm_kernel,
        (1,),
        (cap_raw[0], cap_raw[1], hg),
        [whole_cap, whole_cap, whole(hg.shape)],
        [both_cap],
        [sds((text, 2 * n), bf16)],
    )
    cap = lax.all_gather(cap, "wide", axis=0, tiled=True)

    chunks = range(t // BR)
    pairs_of = range(t // (2 * BR))
    sums = Sums(order, deep, mz)
    a1, k_raw, k, v = key_call(order, patches, vec, w_qkv, tabs, hg, ())
    kv = Gather(k, v)

    q_raw, q = query_call(order, a1, w_qkv, tabs, hg, ())

    q_all = lax.all_gather(q, "wide", axis=0, tiled=True)
    k_all, v_all = pick(order, sc, kv.pieces(), SPAN)
    heads_out = {}
    for c in chunks[: len(chunks) // 2]:
        heads_out[c] = (*attend_call(order, sc, q, k_all, v_all, cap, text, tg, c, BR), 0)
        sums.add(("attn", c), mm(heads_out[c][0], w_out).astype(bf16))
    half = (len(chunks) + 1) // 2
    later = attend_call(order, sc, q, k_all, v_all, cap, text, tg, 1, half * BR)
    for c in chunks[half:]:
        heads_out[c] = (*later, c - half)
        at = (c - half) * BR
        sums.add(("attn", c), mm(later[0][at : at + BR], w_out).astype(bf16))

    mids, gus = {}, {}
    whole_out = ()
    for c in chunks:
        mids[c], gus[c], ffn_part, *whole_out = ffn_call(
            order, c, patches, sums.get(("attn", c)), vec, w_gate_up, w_down, whole_out
        )
        sums.add(("ffn", c), ffn_part)
    a3, hidden = whole_out
    whole_out = ()
    c4 = 0.0
    for c in chunks:
        da3_part, part_sum, *whole_out = ffn_back_call(
            order, c, sums.get(("ffn", c)), mids[c], cotangent, gus[c], vec, w_gate_up, w_down, whole_out
        )
        sums.add(("da3", c), da3_part)
        c4 = c4 + part_sum
    output, d_ffn, d_gu = whole_out

    d_mids, dqs, dq_caps, d_got, d_mixed, d_scaled = {}, {}, {}, {}, {}, {}
    whole_out = ()
    mlp_part = ()
    behind = ()
    c2 = c3 = dck = dcv = gate_sum = 0.0
    for h in pairs_of:
        for c in (2 * h, 2 * h + 1):
            _, o_self, linv, place = heads_out[c]
            if c == 2 * h + 1 and h > 0:
                behind = d_got[h - 1].second
            da3 = sums.get(("da3", c), behind)
            d_mids[c], d_mixed[c], p3, p2, *outs = out_back_call(
                order, c, da3, mids[c], sums.get(("attn", c)), cotangent, vec, w_out, o_self, linv, place, whole_out
            )
            whole_out, d_scaled[h] = (outs if c % 2 == 0 else outs[:1]), outs[1]
            c2, c3 = c2 + p2, c3 + p3
            behind = ()
            if c == 2 * h:
                early = d_got[h - 1].first if h > 0 else ()
                mlp_part = pair_grad_call(order, a3, d_gu, d_ffn, hidden, h, len(pairs_of), mlp_part, early)
        d_got[h] = GatherOne(d_scaled[h])
        dq_caps[h], pk, pv, pg = caption_back_call(order, sc, q, d_mixed[2 * h], d_mixed[2 * h + 1], cap, text, tg, h)
        dck, dcv, gate_sum = dck + pk, dcv + pv, gate_sum + pg
    d_attn = whole_out[0]
    cap_sum = jnp.concatenate([dck, dcv], 1)
    cap_got = lax.all_gather(cap_sum.astype(bf16), "wide")
    kept = (firsts == me)[:, None, None]
    cap_sum = jnp.sum(jnp.where(kept, cap_got.astype(f32), 0.0), 0)
    last_half = pairs_of[-1]

    def make_dq(h, after):
        return dq_call(order, sc, q, d_scaled[h], k_all, v_all, dq_caps[h], h, after)

    for h in pairs_of[:-1]:
        dqs[h] = make_dq(h, ())

    d_cap, hs_c = order.run(
        "caption_grad",
        caption_grad_kernel,
        (1,),
        (cap_sum[:, :n], cap_sum[:, n:], cap_raw[0], hg),
        [whole_cap, whole_cap, whole_cap, whole(hg.shape)],
        [both_cap, pl.BlockSpec((1, n), lambda i: (0, 0))],
        [sds((text, 2 * n), bf16), sds((1, n), f32)],
    )
    d_text = (mm_nt(d_cap[:, :n], w_caption[0]) + mm_nt(d_cap[:, n:], w_caption[1])).astype(bf16)
    cap_part = mm_tn(captions, d_cap).astype(bf16)
    pieces = -(-d_text.shape[1] // d)
    padded = jnp.pad(d_text, ((0, 0), (0, pieces * d - d_text.shape[1])))
    text_parts = [padded[:, p * d : (p + 1) * d] for p in range(pieces)]

    sums.add(("text", 0), text_parts[0])
    dqs[last_half] = make_dq(last_half, (*d_got[last_half].first, *text_parts))
    sums.add(("text", 1), text_parts[1], (cap_part, *d_got[last_half].second))
    ds = [x for h in pairs_of for x in pick(order, sc, d_got[h].pieces(), SPAN)]
    g_mlp = scatter_rows(pin(order, mlp_part[0]))
    whole_out = ()
    c1_parts, hs_parts = [], []
    mixed = jnp.concatenate([heads_out[c][0] for c in chunks[:half]] + [later[0]])
    pairs = n // 128

    def project(c, dkv, after=()):
        nonlocal whole_out
        da1_part, p_hs, p1, *whole_out = dqkv_call(order, c, dqs[c // 2], dkv, q_raw, k_raw, tabs, hg, w_qkv, patches, whole_out)
        hs_parts.append(p_hs)
        c1_parts.append(p1)
        return da1_part

    dkv = [dkv_call(order, sc, k, v, q_all, ds, 0, 0, pairs)]
    for p in range(2, pieces):
        sums.add(("text", p), text_parts[p])
    g_cap = scatter_rows(pin(order, cap_part))
    first_part = project(0, dkv)
    parts_of = lambda p: dkv_call(order, sc, k, v, q_all, ds, 1, p, 1)
    first_dkv, dkv = dkv, [parts_of(0)]
    sums.add(("da1", 0), first_part)
    da1_part = project(1, first_dkv)
    dkv.append(parts_of(1))
    sums.add(("da1", 1), da1_part)
    dkv += [parts_of(p) for p in range(2, pairs)]
    for c in chunks[2:]:
        da1_part = project(c, dkv)
        if c == chunks[-1]:
            d_qkv = whole_out[0]
            packed = pack_call(order, c1_parts, hs_parts, hs_c, gate_sum, tg, c2, c3, c4, mz)
            from_narrow = [packed] + [swap(packed, "narrow", deep, m) for m in range(1, deep)]
            attn_part = pair_grad_call(order, a1, d_qkv, d_attn, mixed)[0]
            (folded,) = fold_call(order, from_narrow)
            got = lax.all_gather(folded, "wide")
        sums.add(("da1", c), da1_part, (g_mlp, got) if c == chunks[-1] else ())
    g_attn = scatter_rows(pin(order, attn_part))

    whole_out = ()
    for c in chunks:
        whole_out = last_call(order, c, sums.get(("da1", c), (g_cap,) if c < 3 else (g_attn,)), patches, d_mids[c], vec, whole_out)
    (grad_patches,) = whole_out
    grad_captions = jnp.concatenate([sums.get(("text", p)) for p in range(pieces)], 1)[:, : d_text.shape[1]]

    cols = got[:, :4]
    grad_head_gains = jnp.sum(got[:, 4, : 3 * n], 0).reshape(3, heads, HD).sum(1)
    grad_cross_gate = jnp.sum(got[:, 5], 0)[::HD]
    gain_factor = jnp.stack([scales[:, 0], gates[:, 1], scales[:, 2], gates[:, 3]], 1)
    gain_grads = jnp.sum(gain_factor * cols, 0)
    wide_cols = d // count
    grad_norm_gains = lax.dynamic_slice_in_dim(gain_grads, me * wide_cols, wide_cols, 1)
    ones = jnp.ones_like(gates[:, 0])
    slope = jnp.stack([ones, 1.0 - gates[:, 1] ** 2, ones, 1.0 - gates[:, 3] ** 2], 1)
    d_mod = lax.dynamic_slice_in_dim(slope * norm_gains[None] * cols, mz * ada, ada, 2)
    at_slot = (firsts[None, :] == blocks[:, None]).astype(f32)
    d_slots = jnp.sum(at_slot[:, :, None, None] * d_mod[None], 1).astype(bf16).astype(f32)
    cond_rows = cd // count
    silu_mine = lax.dynamic_slice_in_dim(jax.nn.silu(conds).astype(bf16).astype(f32), me * cond_rows, cond_rows, 1)
    grad_ada = jnp.sum(silu_mine[:, :, None, None] * d_slots[:, None], 0)
    d_mine = lax.dynamic_index_in_dim(d_slots, me, 0, False)
    cond_part = jnp.sum(d_mine[None] * w_ada.astype(f32), (1, 2))
    cond_part = cond_part.reshape(-1, 128)
    cond_total = tree([cond_part] + [swap(cond_part, "narrow", deep, m) for m in range(1, deep)]).reshape(-1)
    pull_silu = jax.vjp(jax.nn.silu, cond)[1]
    grad_conditioning = pull_silu(cond_total)[0].reshape(1, -1)

    rows = d // count
    return (
        output,
        grad_patches,
        grad_conditioning,
        grad_captions,
        grad_ada,
        grad_norm_gains,
        g_attn[:, : 3 * n].astype(f32).reshape(rows, 3, n).transpose(1, 0, 2),
        grad_head_gains,
        grad_cross_gate,
        g_cap.astype(f32).reshape(-1, 2, n).transpose(1, 0, 2),
        g_attn[:, 3 * n :].astype(f32).T,
        g_mlp[:, : 2 * ff].astype(f32).reshape(rows, 2, ff).transpose(1, 0, 2),
        g_mlp[:, 2 * ff :].astype(f32).T,
    )


def solution(mesh):
    placed = (
        P("wide", None),
        P("wide", None),
        P("wide", None),
        P("wide", None),
        P(),
        P(),
        P(None, None, "narrow"),
        P(),
        P(None, None, "narrow"),
        P(),
        P("narrow"),
        P(None, None, "narrow"),
        P("narrow", None),
        P(None, None, "narrow"),
        P("narrow", None),
    )
    return jax.shard_map(
        local,
        mesh=mesh,
        in_specs=placed,
        out_specs=(
            P("wide", None),
            P("wide", None),
            P("wide", None),
            P("wide", None),
            P("wide", None, "narrow"),
            P(None, "wide"),
            P(None, "wide", "narrow"),
            P(),
            P(),
            P(None, "wide", "narrow"),
            P("narrow", "wide"),
            P(None, "wide", "narrow"),
            P("narrow", "wide"),
        ),
        check_vma=False,
    )
```

```python
import functools

import jax
import jax.numpy as jnp
from jax import lax
from jax.experimental import pallas as pl
from jax.experimental.pallas import tpu as pltpu
from jax.sharding import PartitionSpec as P

HD = 64
SPAN = 4
EPS = 1e-05
LOG2E = 1.4426950408889634
f32 = jnp.float32
bf16 = jnp.bfloat16
VMEM = 56 * 1024 * 1024
BR = 256
NT = (((1,), (1,)), ((), ()))
TN = (((0,), (0,)), ((), ()))


def params(n):
    return pltpu.CompilerParams(
        dimension_semantics=("arbitrary",) * n, vmem_limit_bytes=VMEM
    )


def sds(shape, dtype):
    return jax.ShapeDtypeStruct(shape, dtype)


COST = {
    "key": 8, "query": 9, "caption_norm": 2, "pick": 5, "attend": 18, "hop": 3, "ffn": 9, "ffn_back": 10, "out_back": 6,
    "pair_grad": 10, "caption_back": 6, "dq": 45, "dkv": 20, "dqkv": 7, "caption_grad": 3, "last": 3, "note": 1, "pin": 1,
}


class Order:
    def __init__(self):
        self.token = ()

    def run(self, name, kernel, grid, ins, in_specs, out_specs, out_shape, scratch=(), scalar=None, held=(), first_held=0, after=()):
        pre = 0 if scalar is None else 1
        given = pre + len(ins)
        extra = [*self.token, *after, *held]

        def body(*refs):
            kernel(*refs[:given], *refs[given + len(extra) :])

        at = given + len(extra) - len(held)
        out = pl.pallas_call(
            body,
            grid_spec=pltpu.PrefetchScalarGridSpec(
                num_scalar_prefetch=pre,
                grid=grid,
                in_specs=list(in_specs) + loose(len(extra)),
                out_specs=out_specs,
                scratch_shapes=list(scratch),
            ),
            out_shape=out_shape,
            input_output_aliases={at + k: first_held + k for k in range(len(held))},
            compiler_params=params(len(grid)),
            cost_estimate=pl.CostEstimate(
                flops=COST[name] * 250_000_000, bytes_accessed=COST[name] * 750_000, transcendentals=0
            ),
            name=name,
        )(*(() if scalar is None else (scalar,)), *ins, *extra)
        self.token = (out[0],)
        return out


def loose(n):
    return [pl.BlockSpec(memory_space=pl.ANY)] * n


def mm(a, b):
    return jnp.dot(a, b, preferred_element_type=f32)


def mm_nt(a, b):
    return lax.dot_general(a, b, NT, preferred_element_type=f32)


def mm_tn(a, b):
    return lax.dot_general(a, b, TN, preferred_element_type=f32)


def split(x):
    hi = x.astype(bf16)
    return hi, (x - hi.astype(f32)).astype(bf16)


def head_sum(x, ones):
    hi, lo = split(x)
    return mm(hi, ones) + mm(lo, ones)


def head_ones(n):
    a = lax.broadcasted_iota(jnp.int32, (n, n), 0) // HD
    b = lax.broadcasted_iota(jnp.int32, (n, n), 1) // HD
    return (a == b).astype(bf16)


def halves(n):
    lane = lax.broadcasted_iota(jnp.int32, (1, n), 1)
    return (lane < HD, lane >= HD)


def keep(x, mask):
    return jnp.where(mask, x, jnp.zeros_like(x))


def inv_rms(x):
    return lax.rsqrt(jnp.mean(x * x, -1, keepdims=True) + EPS)


def row(ref, k):
    return ref[k : k + 1, :]


def whole(shape):
    zeros = (0,) * len(shape)
    return pl.BlockSpec(shape, lambda *_: zeros, pipeline_mode=pl.Buffered(1))


def rows_of(br, width, first=0):
    return pl.BlockSpec((br, width), lambda i, *_: (i, first))


def accumulate(ref, value, first):
    @pl.when(first)
    def _():
        ref[...] = value

    @pl.when(jnp.logical_not(first))
    def _():
        ref[...] += value


def col_sum(x):
    return jnp.sum(x, 0, keepdims=True)


def tile3(t, n):
    return jnp.concatenate([t] * (n // t.shape[1]), 1)


def key_kernel(p_ref, v_ref, w_ref, wv_ref, c_ref, s1_ref, s2_ref, hg_ref, a_ref, kr_ref, k_ref, vv_ref):
    x = p_ref[...].astype(f32)
    a = (x * inv_rms(x) * row(v_ref, 0)).astype(bf16)
    a_ref[...] = a
    k = mm(a, w_ref[0])
    kr_ref[...] = k
    k_ref[...] = turned(k, row(hg_ref, 1), (c_ref, s1_ref, s2_ref)).astype(bf16)
    vv_ref[...] = mm(a, wv_ref[0]).astype(bf16)


def turned(y, gain, tabs):
    n = y.shape[1]
    cos, s1, s2 = (tile3(t[...], n) for t in tabs)
    z = y * lax.rsqrt(head_sum(y * y, head_ones(n)) * (1.0 / HD) + EPS) * gain
    return z * cos + pltpu.roll(z, n - 16, 1) * s1 + pltpu.roll(z, 16, 1) * s2


def query_kernel(a_ref, wq_ref, c_ref, s1_ref, s2_ref, hg_ref, qr_ref, q_ref):
    q = mm(a_ref[...], wq_ref[0])
    qr_ref[...] = q
    q_ref[...] = (turned(q, row(hg_ref, 0), (c_ref, s1_ref, s2_ref)) * (0.125 * LOG2E)).astype(bf16)


def one_weight(w, k):
    return pl.BlockSpec((1, *w.shape[1:]), lambda *_: (k, 0, 0), pipeline_mode=pl.Buffered(1))


def key_call(order, patches, vec, w, tabs, hg, after, br=256):
    t, d = patches.shape
    n = w.shape[2]
    return order.run(
        "key",
        key_kernel,
        (t // br,),
        (patches, vec, w, w, *tabs, hg),
        [rows_of(br, d), whole(vec.shape), one_weight(w, 1), one_weight(w, 2)] + [rows_of(br, 128)] * 3 + [whole(hg.shape)],
        [rows_of(br, d)] + [rows_of(br, n)] * 3,
        [sds((t, d), bf16), sds((t, n), f32), sds((t, n), bf16), sds((t, n), bf16)],
        after=after,
    )


def query_call(order, a, w, tabs, hg, after, br=256):
    t, d = a.shape
    n = w.shape[2]
    return order.run(
        "query",
        query_kernel,
        (t // br,),
        (a, w, *tabs, hg),
        [rows_of(br, d), one_weight(w, 0)] + [rows_of(br, 128)] * 3 + [whole(hg.shape)],
        [rows_of(br, n)] * 2,
        [sds((t, n), f32), sds((t, n), bf16)],
        after=after,
    )


def soft_sums(q, k, v, mask):
    e = jnp.exp2(mm_nt(q, keep(k, mask))).astype(bf16)
    return mm(e, jnp.where(mask, v, jnp.ones_like(v)))


def item_block(j, s):
    return jnp.minimum(j, s[0] - 1)


def attend_kernel(sc, q_ref, k_ref, v_ref, ck_ref, cv_ref, tg_ref, mix_ref, o_ref, li_ref, acc):
    j = pl.program_id(1)
    masks = halves(128)
    keys = 512

    def block_sums(h):
        q = q_ref[...]
        total = 0.0
        for c in range(k_ref.shape[0] // keys):
            at = slice(c * keys, (c + 1) * keys)
            total = total + soft_sums(q, k_ref[at, :], v_ref[at, :], masks[h])
        return total

    @pl.when(j == 0)
    def _():
        for h in range(2):
            acc[2 + h] = soft_sums(q_ref[...], ck_ref[...], cv_ref[...], masks[h])
            acc[h] = block_sums(h)

    @pl.when((j > 0) & (j < sc[0]))
    def _():
        for h in range(2):
            acc[h] += block_sums(h)

    @pl.when(j == SPAN - 1)
    def _():
        def finish(a0, a1):
            inverse = 1.0 / jnp.where(masks[0], pltpu.roll(a0, HD, 1), pltpu.roll(a1, HD, 1))
            return jnp.where(masks[0], a0, a1) * inverse, inverse

        o, li = finish(acc[0], acc[1])
        mix_ref[...] = (o + tg_ref[...] * finish(acc[2], acc[3])[0]).astype(bf16)
        o_ref[...] = o.astype(bf16)
        li_ref[...] = li


def attend_call(order, sc, q, k, v, cap, text, tg, at, bq):
    n = q.shape[1]
    pairs = n // 128
    block = k.shape[0] // SPAN
    mine = lambda p, j, s: (0, p)
    other = lambda p, j, s: (item_block(j, s), p)
    return order.run(
        "attend",
        attend_kernel,
        (pairs, SPAN),
        (q, k, v, cap, cap, tg),
        [
            pl.BlockSpec((bq, 128), lambda p, j, s: (at, p)),
            pl.BlockSpec((block, 128), other),
            pl.BlockSpec((block, 128), other),
            pl.BlockSpec((text, 128), lambda p, j, s: (s[1 + SPAN], p)),
            pl.BlockSpec((text, 128), lambda p, j, s: (s[1 + SPAN], pairs + p)),
            pl.BlockSpec((1, 128), mine),
        ],
        [pl.BlockSpec((bq, 128), mine)] * 3,
        [sds((bq, n), bf16), sds((bq, n), bf16), sds((bq, n), f32)],
        [pltpu.VMEM((4, bq, 128), f32)],
        sc,
    )


def caption_back_kernel(sc, q_ref, da_ref, db_ref, ck_ref, cv_ref, tg_ref, dq_ref, dk_ref, dv_ref, gs_ref):
    masks = halves(128)
    q, d = q_ref[...], jnp.concatenate([da_ref[...], db_ref[...]], 0)
    dq = jnp.zeros(q.shape, f32)
    dk = jnp.zeros(ck_ref.shape, f32)
    dv = jnp.zeros(ck_ref.shape, f32)
    sums = []
    for h in range(2):
        ck, cv = keep(ck_ref[...], masks[h]), keep(cv_ref[...], masks[h])
        gate = tg_ref[:, h * HD : h * HD + 1]
        e = jnp.exp2(mm_nt(q, ck))
        prob = e * (1.0 / jnp.sum(e, -1, keepdims=True))
        dp = mm_nt(d, cv)
        m = jnp.sum(prob * dp, -1, keepdims=True)
        dc = (prob * (dp - m) * gate).astype(bf16)
        dq = dq + mm(dc, ck)
        dk = dk + mm_tn(dc, keep(q, masks[h]))
        dv = dv + mm_tn(prob.astype(bf16), keep(d, masks[h]))
        sums.append(jnp.sum(m, 0, keepdims=True))
    dq_ref[...] = dq * 0.125
    dk_ref[...] = dk * (1.0 / LOG2E)
    dv_ref[...] = dv * tg_ref[...]
    gs_ref[...] = jnp.where(masks[0], sums[0], sums[1])


def caption_back_call(order, sc, q, da, db, cap, text, tg, h):
    n = q.shape[1]
    pairs = n // 128
    bq = 2 * BR
    mine = lambda p, s: (0, p)
    return order.run(
        "caption_back",
        caption_back_kernel,
        (pairs,),
        (q, da, db, cap, cap, tg),
        [
            pl.BlockSpec((bq, 128), lambda p, s: (h, p)),
            pl.BlockSpec((BR, 128), mine),
            pl.BlockSpec((BR, 128), mine),
            pl.BlockSpec((text, 128), lambda p, s: (s[1 + SPAN], p)),
            pl.BlockSpec((text, 128), lambda p, s: (s[1 + SPAN], pairs + p)),
            pl.BlockSpec((1, 128), mine),
        ],
        [
            pl.BlockSpec((bq, 128), mine),
            pl.BlockSpec((text, 128), mine),
            pl.BlockSpec((text, 128), mine),
            pl.BlockSpec((1, 128), mine),
        ],
        [sds((bq, n), f32), sds((text, n), f32), sds((text, n), f32), sds((1, n), f32)],
        scalar=sc,
    )


def minus_delta(rows, head):
    lane = lax.broadcasted_iota(jnp.int32, (rows, 128), 1)
    return jnp.where((lane >= 3 * head) & (lane < 3 * head + 3), -1.0, 0.0).astype(bf16)


def dq_kernel(parts, sc, q_ref, k_ref, v_ref, *refs):
    d_refs, x_refs, c_refs = (refs[k * parts : (k + 1) * parts] for k in range(3))
    dq_ref, acc = refs[3 * parts :]
    pair = pl.program_id(0)
    j = pl.program_id(1)
    masks = halves(128)
    keys = 512
    rows = d_refs[0].shape[0]

    @pl.when(j == 0)
    def _():
        acc[...] = jnp.zeros_like(acc)

    @pl.when(j < sc[0])
    def _():
        for r in range(parts):
            mine = slice(r * rows, (r + 1) * rows)
            q = q_ref[mine, :]
            dx = jnp.concatenate([d_refs[r][...], x_refs[r][...]], 1)
            total = acc[mine, :]
            for h in range(2):
                off = minus_delta(keys, 2 * pair + h)
                for c in range(k_ref.shape[0] // keys):
                    at = slice(c * keys, (c + 1) * keys)
                    k = keep(k_ref[at, :], masks[h])
                    e = jnp.exp2(mm_nt(q, k))
                    dp = mm_nt(dx, jnp.concatenate([keep(v_ref[at, :], masks[h]), off], 1))
                    total = total + mm((e * dp).astype(bf16), k)
            acc[mine, :] = total

    @pl.when(j == SPAN - 1)
    def _():
        for r in range(parts):
            mine = slice(r * rows, (r + 1) * rows)
            dq_ref[mine, :] = acc[mine, :] * 0.125 + c_refs[r][...]


def dq_call(order, sc, q, ds, k, v, cap_dqs, after=()):
    t, n = q.shape
    pairs = n // 128
    parts = len(ds)
    block = k.shape[0] // SPAN
    rows = t // parts
    mine = lambda p, j, s: (0, p)
    other = pl.BlockSpec((block, 128), lambda p, j, s: (item_block(j, s), p))
    return order.run(
        "dq",
        functools.partial(dq_kernel, parts),
        (pairs, SPAN),
        (q, k, v, *ds, *ds, *cap_dqs),
        [pl.BlockSpec((t, 128), mine), other, other]
        + [pl.BlockSpec((rows, 128), mine)] * parts
        + [pl.BlockSpec((rows, 128), lambda p, j, s: (0, pairs))] * parts
        + [pl.BlockSpec((rows, 128), mine)] * parts,
        [pl.BlockSpec((t, 128), mine)],
        [sds((t, n), f32)],
        [pltpu.VMEM((t, 128), f32)],
        sc,
        after=after,
    )[0]


def dkv_kernel(parts, base, sc, k_ref, v_ref, q_ref, *rest):
    d_refs, x_refs = rest[0 : 2 * parts : 2], rest[1 : 2 * parts : 2]
    dk_ref, dv_ref = rest[2 * parts :]
    pair = base + pl.program_id(0)
    j = pl.program_id(1)
    masks = halves(128)
    queries = 2 * BR

    @pl.when(j == 0)
    def _():
        dk_ref[...] = jnp.zeros_like(dk_ref)
        dv_ref[...] = jnp.zeros_like(dv_ref)

    @pl.when(j < sc[0])
    def _():
        keys = 512
        for c in range(k_ref.shape[0] // keys):
            at = slice(c * keys, (c + 1) * keys)
            dk, dv = dk_ref[at, :], dv_ref[at, :]
            for h in range(2):
                vx = jnp.concatenate([keep(v_ref[at, :], masks[h]), minus_delta(keys, 2 * pair + h)], 1)
                for r in range(parts):
                    q = keep(q_ref[r * queries : (r + 1) * queries, :], masks[h])
                    d, x = d_refs[r][...], x_refs[r][...]
                    e = jnp.exp2(mm_nt(k_ref[at, :], q))
                    dp = mm_nt(vx, jnp.concatenate([d, x], 1))
                    dv = dv + mm(e.astype(bf16), keep(d, masks[h]))
                    dk = dk + mm((e * dp).astype(bf16), q)
            dk_ref[at, :] = dk
            dv_ref[at, :] = dv


def dkv_call(order, sc, k, v, q_all, ds, base, n_pairs):
    t, n = k.shape
    pairs = n // 128
    rows = t // len(ds)
    mine = pl.BlockSpec((t, 128), lambda p, j, s: (0, base + p))
    out = pl.BlockSpec((t, 128), lambda p, j, s: (0, p))
    other = pl.BlockSpec((rows, 128), lambda p, j, s: (item_block(j, s), base + p))
    extra = pl.BlockSpec((rows, 128), lambda p, j, s: (item_block(j, s), pairs))
    return order.run(
        "dkv",
        functools.partial(dkv_kernel, len(ds), base),
        (n_pairs, SPAN),
        (k, v, q_all, *(x for d in ds for x in (d, d))),
        [mine, mine, pl.BlockSpec((t, 128), lambda p, j, s: (s[1 + SPAN + j], base + p))] + [other, extra] * len(ds),
        [out, out],
        [sds((t, n_pairs * 128), f32)] * 2,
        scalar=sc,
    )


def chunk_call(order, kernel, name, c, ins, specs, chunk_outs, sum_outs, whole_outs, before):
    one = lambda r, w: pl.BlockSpec((r, w), lambda i: (0, 0))
    own = chunk_outs + sum_outs
    into = [pl.BlockSpec((BR, w), lambda i, at=c % (r // BR): (at, 0)) for r, w, _ in whole_outs]
    return order.run(
        name,
        kernel,
        (1,),
        ins,
        specs,
        [one(r, w) for r, w, _ in own] + into,
        [sds((r, w), k) for r, w, k in own + whole_outs],
        held=tuple(before),
        first_held=len(own),
    )


def part(c, width):
    return pl.BlockSpec((BR, width), lambda i: (c, 0))


def alone(width):
    return pl.BlockSpec((BR, width), lambda i: (0, 0))


def pair_grad_kernel(a_ref, b_ref, c_ref, d_ref, o_ref):
    n = b_ref.shape[1]
    o_ref[:, :n] = mm_tn(a_ref[...], b_ref[...]).astype(bf16)
    o_ref[:, n:] = mm_tn(c_ref[...], d_ref[...]).astype(bf16)


def pair_grad_call(order, a, b, c, d, part=0, parts=1, before=(), after=()):
    t, m = a.shape
    n, k = b.shape[1], d.shape[1]
    blk = 256
    steps = m // blk // parts
    cols = pl.BlockSpec((t, blk), lambda i: (0, part * steps + i))
    return order.run(
        "pair_grad",
        pair_grad_kernel,
        (steps,),
        (a, b, c, d),
        [cols, whole(b.shape), cols, whole(d.shape)],
        [pl.BlockSpec((blk, n + k), lambda i: (part * steps + i, 0))],
        [sds((m, n + k), bf16)],
        held=before,
        after=after,
    )


def ffn_kernel(p_ref, at_ref, v_ref, wg_ref, wd_ref, mid_ref, gu_ref, f_ref, a_ref, h_ref):
    at = at_ref[...].astype(f32)
    mid = p_ref[...].astype(f32) + row(v_ref, 1) * (at * inv_rms(at))
    mid_ref[...] = mid
    a = (mid * inv_rms(mid) * row(v_ref, 2)).astype(bf16)
    a_ref[...] = a
    g = mm(a, wg_ref[0])
    u = mm(a, wg_ref[1])
    n = g.shape[1]
    gu_ref[:, :n] = g.astype(bf16)
    gu_ref[:, n:] = u.astype(bf16)
    h = (g * jax.nn.sigmoid(g) * u).astype(bf16)
    h_ref[...] = h
    f_ref[...] = mm(h, wd_ref[...]).astype(bf16)


def ffn_call(order, c, patches, at, vec, wg, wd, before):
    t, d = patches.shape
    n = wd.shape[0]
    return chunk_call(
        order,
        ffn_kernel,
        "ffn",
        c,
        (patches, at, vec, wg, wd),
        [part(c, d), alone(d), whole(vec.shape), whole(wg.shape), whole(wd.shape)],
        [(BR, d, f32), (BR, 2 * n, bf16), (BR, d, bf16)],
        [],
        [(t, d, bf16), (t, n, bf16)],
        before,
    )


def ffn_back_kernel(f_ref, mid_ref, c_ref, gu_ref, v_ref, wg_ref, wd_ref, da_ref, cs_ref, y_ref, df_ref, dgu_ref):
    f = f_ref[...].astype(f32)
    cot = c_ref[...].astype(f32)
    r = inv_rms(f)
    fh = f * r
    y_ref[...] = (mid_ref[...] + row(v_ref, 3) * fh).astype(bf16)
    z = cot * row(v_ref, 3)
    df = (r * (z - fh * jnp.mean(z * fh, -1, keepdims=True))).astype(bf16)
    df_ref[...] = df
    cs_ref[...] = col_sum(cot * fh)
    dh = mm_nt(df, wd_ref[...])
    n = dh.shape[1]
    g = gu_ref[:, :n].astype(f32)
    u = gu_ref[:, n:].astype(f32)
    s = jax.nn.sigmoid(g)
    gs = g * s
    dg = (dh * u * (s + gs * (1.0 - s))).astype(bf16)
    du = (dh * gs).astype(bf16)
    dgu_ref[:, :n] = dg
    dgu_ref[:, n:] = du
    da_ref[...] = (mm_nt(dg, wg_ref[0]) + mm_nt(du, wg_ref[1])).astype(bf16)


def ffn_back_call(order, c, f, mid, cot, gu, vec, wg, wd, before):
    t, d = cot.shape
    n = wd.shape[0]
    return chunk_call(
        order,
        ffn_back_kernel,
        "ffn_back",
        c,
        (f, mid, cot, gu, vec, wg, wd),
        [alone(d), alone(d), part(c, d), alone(2 * n), whole(vec.shape), whole(wg.shape), whole(wd.shape)],
        [(BR, d, bf16)],
        [(1, d, f32)],
        [(t, d, bf16), (t, d, bf16), (t, 2 * n, bf16)],
        before,
    )


def out_back_kernel(da_ref, mid_ref, at_ref, c_ref, v_ref, w_ref, o_ref, li_ref, dm_ref, dx_ref, c3_ref, c2_ref, dat_ref, ds_ref):
    da = da_ref[...].astype(f32)
    mid = mid_ref[...]
    r = inv_rms(mid)
    mh = mid * r
    z = da * row(v_ref, 2)
    dm = c_ref[...].astype(f32) + r * (z - mh * jnp.mean(z * mh, -1, keepdims=True))
    dm_ref[...] = dm
    c3_ref[...] = col_sum(da * mh)
    at = at_ref[...].astype(f32)
    ra = inv_rms(at)
    ah = at * ra
    c2_ref[...] = col_sum(dm * ah)
    z = dm * row(v_ref, 1)
    dat = (ra * (z - ah * jnp.mean(z * ah, -1, keepdims=True))).astype(bf16)
    dat_ref[...] = dat
    dx = mm_nt(dat, w_ref[...]).astype(bf16)
    dx_ref[...] = dx
    n = dx.shape[1]
    ds = dx.astype(f32) * li_ref[...]
    ds_ref[:, :n] = ds.astype(bf16)
    hi, lo = split(ds * o_ref[...].astype(f32))
    head = lax.broadcasted_iota(jnp.int32, (n, 128), 0) // HD
    lane = lax.broadcasted_iota(jnp.int32, (n, 128), 1)
    to_lanes = (lane // 3 == head).astype(bf16)
    delta = mm(hi, to_lanes) + mm(lo, to_lanes)
    one = delta.astype(bf16).astype(f32)
    two = (delta - one).astype(bf16).astype(f32)
    which = lax.broadcasted_iota(jnp.int32, (1, 128), 1) % 3
    ds_ref[:, n:] = jnp.where(which == 0, one, jnp.where(which == 1, two, delta - one - two)).astype(bf16)


def out_back_call(order, c, da, mid, at, cot, vec, w, o, li, place, before):
    t, d = cot.shape
    n = w.shape[0]
    return chunk_call(
        order,
        out_back_kernel,
        "out_back",
        c,
        (da, mid, at, cot, vec, w, o, li),
        [alone(d), alone(d), alone(d), part(c, d), whole(vec.shape), whole(w.shape), part(place, n), part(place, n)],
        [(BR, d, f32), (BR, n, bf16)],
        [(1, d, f32), (1, d, f32)],
        [(t, d, bf16), (2 * BR, n + 128, bf16)],
        before,
    )


def dqkv_kernel(pairs, dq_ref, *refs):
    dk_refs, dv_refs = refs[0 : 2 * pairs : 2], refs[1 : 2 * pairs : 2]
    (qr_ref, kr_ref, c_ref, s1_ref, s2_ref, hg_ref, w_ref, p_ref, da_ref, hs_ref, cs_ref, d_ref) = refs[2 * pairs :]
    side = lambda parts: jnp.concatenate([x[...] for x in parts], 1)
    n = dq_ref.shape[1]
    ones = head_ones(n)
    cos, s1, s2 = (tile3(t[...], n) for t in (c_ref, s1_ref, s2_ref))

    def back(dy, x, gain):
        dz = dy * cos - pltpu.roll(dy, 16, 1) * s2 - pltpu.roll(dy, n - 16, 1) * s1
        r = lax.rsqrt(head_sum(x * x, ones) * (1.0 / HD) + EPS)
        xh = x * r
        g = dz * gain
        return r * (g - xh * (head_sum(g * xh, ones) * (1.0 / HD))), col_sum(dz * xh)

    dq, hq = back(dq_ref[...], qr_ref[...], row(hg_ref, 0))
    dk, hk = back(side(dk_refs) * (1.0 / LOG2E), kr_ref[...], row(hg_ref, 1))
    dql, dkl, dvl = dq.astype(bf16), dk.astype(bf16), side(dv_refs).astype(bf16)
    d_ref[:, :n] = dql
    d_ref[:, n : 2 * n] = dkl
    d_ref[:, 2 * n :] = dvl
    da = mm_nt(dql, w_ref[0]) + mm_nt(dkl, w_ref[1]) + mm_nt(dvl, w_ref[2])
    da_ref[...] = da.astype(bf16)
    x = p_ref[...].astype(f32)
    cs_ref[...] = col_sum(da * (x * inv_rms(x)))
    hs_ref[0:1, :] = hq
    hs_ref[1:2, :] = hk


def dqkv_call(order, c, dq, dkv, qr, kr, tabs, hg, w, patches, before):
    t, d = patches.shape
    n = dq.shape[1]
    return chunk_call(
        order,
        functools.partial(dqkv_kernel, len(dkv)),
        "dqkv",
        c,
        (dq, *(x for two in dkv for x in two), qr, kr, *tabs, hg, w, patches),
        [part(c, n)] + [part(c, x.shape[1]) for two in dkv for x in two] + [part(c, n)] * 2 + [part(c, 128)] * 3 + [whole(hg.shape), whole(w.shape), part(c, d)],
        [(BR, d, bf16)],
        [(2, n, f32), (1, d, f32)],
        [(t, 3 * n, bf16)],
        before,
    )


def last_kernel(da_ref, p_ref, dm_ref, v_ref, o_ref):
    x = p_ref[...].astype(f32)
    r = inv_rms(x)
    xh = x * r
    z = da_ref[...].astype(f32) * row(v_ref, 0)
    o_ref[...] = (dm_ref[...] + r * (z - xh * jnp.mean(z * xh, -1, keepdims=True))).astype(bf16)


def last_call(order, c, da, patches, dm, vec, before):
    t, d = patches.shape
    return chunk_call(
        order,
        last_kernel,
        "last",
        c,
        (da, patches, dm, vec),
        [alone(d), part(c, d), alone(d), whole(vec.shape)],
        [],
        [],
        [(t, d, bf16)],
        before,
    )


def caption_grad_kernel(dk_ref, dv_ref, kr_ref, hg_ref, d_ref, hs_ref):
    n = dk_ref.shape[1]
    ones = head_ones(n)
    x = kr_ref[...]
    r = lax.rsqrt(head_sum(x * x, ones) * (1.0 / HD) + EPS)
    xh = x * r
    dy = dk_ref[...]
    g = dy * row(hg_ref, 2)
    d_ref[:, :n] = (r * (g - xh * (head_sum(g * xh, ones) * (1.0 / HD)))).astype(bf16)
    d_ref[:, n:] = dv_ref[...].astype(bf16)
    hs_ref[...] = col_sum(dy * xh)


def caption_norm_kernel(kr_ref, v_ref, hg_ref, o_ref):
    n = kr_ref.shape[1]
    x = kr_ref[...]
    r = lax.rsqrt(head_sum(x * x, head_ones(n)) * (1.0 / HD) + EPS)
    o_ref[:, :n] = (x * r * row(hg_ref, 2)).astype(bf16)
    o_ref[:, n:] = v_ref[...].astype(bf16)


def swap(x, axis, size, m):
    return lax.ppermute(x, axis, [(i, i ^ m) for i in range(size)])


def pick_kernel(count, n_arrays, n_pieces, sc, *refs):
    outs, sem = refs[n_arrays * n_pieces :][:n_arrays], refs[-1]
    for k, out in enumerate(outs):
        pieces = refs[k * n_pieces : (k + 1) * n_pieces]
        rows = pieces[0].shape[0]
        for j in range(count):
            for m in range(n_pieces):

                @pl.when(sc[1 + j] == m)
                def _():
                    pltpu.make_async_copy(pieces[m], out.at[pl.ds(j * rows, rows)], sem.at[k, j]).start()

    for k, out in enumerate(outs):
        first = refs[k * n_pieces]
        rows = first.shape[0]
        for j in range(count):
            pltpu.make_async_copy(first, out.at[pl.ds(j * rows, rows)], sem.at[k, j]).wait()


class Gather:
    def __init__(self, order, a, b, between=None):
        self.all = None
        if lax.axis_size("wide") != 8:
            self.all = [lax.all_gather(x, "wide") for x in (a, b)]
            between(None)
            return
        send = lambda x, pairs: lax.ppermute(x, "wide", pairs)
        over_x = [(i, i ^ 2) for i in range(8)]
        over_y = [(1, 5), (4, 0), (3, 7), (6, 2)]
        a2, a4, b4, b2 = send(a, over_x), send(a, over_y), send(b, over_y), send(b, over_x)
        a6 = send(a2, [(0, 4), (1, 5), (6, 2), (7, 3)])
        if between is not None:
            between(a2)
            b2 = pin(order, b2)
        b6x, b6y = send(b2, [(0, 4), (7, 3)]), send(b4, [(7, 5), (0, 2)])
        self.kept = ((a, a2, a4, a6), (b, b2, b4, b6x + b6y))

    def pieces(self):
        if self.all is not None:
            return self.all
        return [[y for x in four for y in (x, swap(x, "wide", 8, 1))] for four in self.kept]


class GatherOne:
    def __init__(self, a):
        self.all, self.first, self.second = None, (), ()
        if lax.axis_size("wide") != 8:
            self.all = [lax.all_gather(a, "wide")]
            return
        a2 = lax.ppermute(a, "wide", [(i, i ^ 2) for i in range(8)])
        a4 = lax.ppermute(a, "wide", [(1, 5), (4, 0), (3, 7), (6, 2)])
        self.first, self.own = (a2, a4), a

    def across(self, order=None):
        if self.all is not None:
            return
        a2, a4 = self.first
        if order is not None:
            a2 = pin(order, a2)
        a6 = lax.ppermute(a2, "wide", [(0, 4), (1, 5), (6, 2), (7, 3)])
        self.second = (a6,)
        self.kept = ((self.own, a2, a4, a6),)

    pieces = Gather.pieces


def pick(order, sc, pieces, count):
    if not isinstance(pieces[0], list):
        one = lambda x, j: lax.dynamic_index_in_dim(x, sc[1 + SPAN + j], 0, False)
        return [jnp.concatenate([one(x, j) for j in range(count)]) for x in pieces]
    outs = [(count * p[0].shape[0], p[0].shape[1]) for p in pieces]
    return order.run(
        "pick",
        functools.partial(pick_kernel, count, len(pieces), 8),
        (1,),
        [x for p in pieces for x in p],
        loose(8 * len(pieces)),
        [pl.BlockSpec(shape, lambda i, s: (0, 0)) for shape in outs],
        [sds(shape, bf16) for shape in outs],
        [pltpu.SemaphoreType.DMA((len(pieces), count))],
        sc,
    )


def tree(parts):
    while len(parts) > 1:
        parts = [a + b for a, b in zip(parts[::2], parts[1::2])]
    return parts[0]


def pack_kernel(count, place, *refs):
    c1, hs = refs[:count], refs[count : 2 * count]
    hc_ref, gs_ref, tg_ref, c2_ref, c3_ref, c4_ref, o_ref = refs[2 * count :]
    n = hc_ref.shape[1]
    o_ref[...] = jnp.zeros_like(o_ref)
    o_ref[0:1, :] = sum(x[...] for x in c1)
    o_ref[1:2, :] = c2_ref[...]
    o_ref[2:3, :] = c3_ref[...]
    o_ref[3:4, :] = c4_ref[...]
    qk = sum(x[...] for x in hs)
    o_ref[4:5, :n] = qk[0:1]
    o_ref[4:5, n : 2 * n] = qk[1:2]
    o_ref[4:5, 2 * n : 3 * n] = hc_ref[...]
    gate = gs_ref[...] * (1.0 - tg_ref[...] * tg_ref[...])
    for z in range(o_ref.shape[1] // n):
        o_ref[5:6, z * n : (z + 1) * n] = jnp.where(place[0] == z, gate, 0.0)


def pack_call(order, c1, hs, hc, gs, tg, c2, c3, c4, place):
    d = c2.shape[1]
    ins = (*c1, *hs, hc, gs, tg, c2, c3, c4)
    spec = lambda x: pl.BlockSpec(x.shape, lambda i, s: (0, 0))

    def kernel(place, *refs):
        pack_kernel(len(c1), place, *refs)

    return order.run(
        "note",
        kernel,
        (1,),
        ins,
        [spec(x) for x in ins],
        [pl.BlockSpec((8, d), lambda i, s: (0, 0))],
        [sds((8, d), f32)],
        scalar=place.astype(jnp.int32).reshape(1),
    )[0]


def fold_kernel(*refs):
    parts, o_ref = refs[:-1], refs[-1]
    total = tree([x[...] for x in parts])
    row_at = lax.broadcasted_iota(jnp.int32, total.shape, 0)
    o_ref[...] = jnp.where((row_at >= 1) & (row_at < 4), parts[0][...], total)


def fold_call(order, parts):
    spec = pl.BlockSpec(parts[0].shape, lambda i: (0, 0))
    return order.run("note", fold_kernel, (1,), parts, [spec] * len(parts), [spec], [sds(parts[0].shape, f32)])


def pin_kernel(o_ref):
    pass


def pin(order, x, after=()):
    return order.run("pin", pin_kernel, (1,), (), [], loose(1), [sds(x.shape, x.dtype)], held=(x,), after=after)[0]


def gather_now(x, axis):
    n = x.shape[0]
    wide = -(-n // 1024) * 1024
    padded = jnp.pad(x, (0, wide - n)).reshape(1, 8, wide // 8)
    return lax.all_gather(padded, axis, axis=0, tiled=True).reshape(-1, wide)[:, :n]


def hop_kernel(have, sc, *refs):
    ins = dict(zip(have["in"], refs))
    outs = dict(zip(have["out"], refs[len(have["in"]) :]))
    end = sc[0] == 1
    if "total" in outs:
        outs["total"][...] = jnp.where(end, ins["r1"][...], ins["send"][...])
    third = None
    if "second" in ins:
        third = ins["second"][...] + ins["r2"][...]
    if "second" in outs:
        outs["second"][...] = ins["x"][...] + ins["r1"][...]
    if "send" in outs:
        new = ins["new"][...] if "new" in ins else third
        outs["send"][...] = new if third is None else jnp.where(end, new, third)


class Line:
    def __init__(self, order, place):
        self.order = order
        self.end = ((place == 0) | (place == 3)).astype(jnp.int32).reshape(1)
        self.x = self.second = self.send = None
        self.third = False

    def step(self, new, after=()):
        if self.send is None:
            self.x = self.send = new
            return None
        go = lambda x, perm: lax.ppermute(x, "narrow", perm)
        ins = {"r1": go(self.send, [(0, 1), (3, 2), (1, 0), (2, 3)])}
        outs = []
        if self.third:
            ins["send"] = self.send
            outs.append("total")
        if self.second is not None:
            ins["r2"] = go(self.second, [(1, 2), (2, 1)])
            ins["second"] = self.second
        if self.x is not None:
            ins["x"] = self.x
            outs.append("second")
        if new is not None:
            ins["new"] = new
        if new is not None or self.second is not None:
            outs.append("send")
        like = ins["r1"]
        block = pl.BlockSpec((BR // 2, like.shape[1]), lambda i, s: (i, 0))
        got = self.order.run(
            "hop",
            functools.partial(hop_kernel, {"in": list(ins), "out": outs}),
            (2,),
            list(ins.values()),
            [block] * len(ins),
            [block] * len(outs),
            [sds(like.shape, like.dtype)] * len(outs),
            scalar=self.end,
            after=after,
        )
        got = dict(zip(outs, got))
        self.third = self.second is not None
        self.x, self.second, self.send = new, got.get("second"), got.get("send")
        return got.get("total")


class Sums:
    def __init__(self, order, size, place):
        self.line = Line(order, place) if size == 4 else None
        self.names, self.done = [], {}

    def add(self, name, x, after=()):
        if self.line is None:
            self.done[name] = lax.psum(x, "narrow")
            return
        if self.line.send is None:
            self.names = [None]
        self._step(name, x, after)

    def _step(self, name, x, after):
        total = self.line.step(x, after)
        self.names.append(name)
        if total is not None:
            self.done[self.names[-4]] = total

    def get(self, name, after=()):
        while name not in self.done:
            self._step(None, None, after)
            after = ()
        return self.done[name]


def scatter_rows(x):
    return lax.psum_scatter(x.astype(bf16), "wide", scatter_dimension=0, tiled=True)


def rope_tables(position, width):
    lane = jnp.arange(128, dtype=jnp.int32)
    within = lane % HD
    quarter = HD // 4
    frequency = 10000.0 ** (-(within % quarter).astype(f32) / quarter)
    by_row = within < HD // 2
    where = jnp.where(by_row[None, :], (position // width)[:, None], (position % width)[:, None])
    angle = where.astype(f32) * frequency[None, :]
    cos, sin = jnp.cos(angle), jnp.sin(angle)
    former = (within % (HD // 2) < quarter)[None, :]
    return cos, jnp.where(former, -sin, 0.0), jnp.where(former, 0.0, sin)


def local(
    patches,
    cotangent,
    conditioning,
    captions,
    item_lengths,
    grid_widths,
    w_ada,
    norm_gains,
    w_qkv,
    head_gains,
    cross_gate,
    w_caption,
    w_out,
    w_gate_up,
    w_down,
):
    t, d = patches.shape
    n = w_qkv.shape[2]
    heads = n // HD
    ada = w_ada.shape[2]
    ff = w_down.shape[0]
    text = captions.shape[0]
    cd = conditioning.shape[1]
    count = lax.axis_size("wide")
    deep = lax.axis_size("narrow")
    me = lax.axis_index("wide")
    mz = lax.axis_index("narrow")

    slots = item_lengths.shape[0]
    spans = item_lengths // t
    order = jnp.arange(slots, dtype=jnp.int32)
    ends = jnp.sum(jnp.where(order[None, :] <= order[:, None], spans[None, :], 0), 1)
    blocks = jnp.arange(count, dtype=jnp.int32)
    item = jnp.sum((ends[None, :] <= blocks[:, None]).astype(jnp.int32), 1)
    is_item = item[:, None] == order[None, :]
    choose = lambda values: jnp.sum(jnp.where(is_item, values[None, :], 0), 1)
    firsts = choose(ends - spans)
    mine = blocks == me
    of_me = lambda values: jnp.sum(jnp.where(mine, values, 0))
    first = of_me(firsts)
    length = of_me(choose(spans))
    width = of_me(choose(grid_widths))
    position = (me - first) * t + jnp.arange(t, dtype=jnp.int32)
    tabs = rope_tables(position, width)
    steps = first + jnp.minimum(jnp.arange(SPAN, dtype=jnp.int32), length - 1)
    places = steps ^ me if count == 8 else steps
    sc = jnp.concatenate([length.reshape(1), places, steps]).astype(jnp.int32)

    cond = conditioning.astype(f32)[0]
    silu_low = jax.nn.silu(cond).astype(bf16)
    mod = jnp.sum(silu_low.astype(f32)[:, None, None] * w_ada.astype(f32), 0)
    share = cd // deep
    sent = jnp.concatenate([mod.reshape(-1), lax.dynamic_slice_in_dim(cond, mz * share, share)])
    got = gather_now(gather_now(sent, "narrow").reshape(-1), "wide").reshape(count, deep, -1)
    mods = got[:, :, : 4 * ada].reshape(count, deep, 4, ada).transpose(0, 2, 1, 3).reshape(count, 4, d)
    conds = got[:, :, 4 * ada :].reshape(count, cd)
    my_mod = lax.dynamic_index_in_dim(mods, first, 0, False)
    of_block = jnp.sum(jnp.where((firsts[:, None] == blocks[None, :])[:, :, None, None], mods[None], 0.0), 1)
    scales = 1.0 + of_block
    gates = jnp.tanh(of_block)
    factor = jnp.stack([1.0 + my_mod[0], jnp.tanh(my_mod[1]), 1.0 + my_mod[2], jnp.tanh(my_mod[3])])
    vec = norm_gains * factor
    hg = jnp.tile(head_gains, (1, heads))
    tg_heads = jnp.tanh(cross_gate)
    tg = jnp.repeat(tg_heads, HD)[None, :]

    order = Order()
    cap_raw = jnp.einsum("kd,jde->jke", captions, w_caption, preferred_element_type=f32)
    whole_cap = pl.BlockSpec((text, n), lambda i: (0, 0))
    both_cap = pl.BlockSpec((text, 2 * n), lambda i: (0, 0))
    (cap,) = order.run(
        "caption_norm",
        caption_norm_kernel,
        (1,),
        (cap_raw[0], cap_raw[1], hg),
        [whole_cap, whole_cap, whole(hg.shape)],
        [both_cap],
        [sds((text, 2 * n), bf16)],
    )
    cap = lax.all_gather(cap, "wide", axis=0, tiled=True)

    chunks = range(t // BR)
    pairs_of = range(t // (2 * BR))
    sums = Sums(order, deep, mz)
    a1, k_raw, k, v = key_call(order, patches, vec, w_qkv, tabs, hg, ())
    made = []

    def queries(done):
        made.extend(query_call(order, a1, w_qkv, tabs, hg, () if done is None else (done,)))

    kv = Gather(order, k, v, queries)
    q_raw, q = made

    q_all = lax.all_gather(q, "wide", axis=0, tiled=True)
    k_all, v_all = pick(order, sc, kv.pieces(), SPAN)
    heads_out = {}
    for c in chunks[: len(chunks) // 2]:
        heads_out[c] = (*attend_call(order, sc, q, k_all, v_all, cap, text, tg, c, BR), 0)
        sums.add(("attn", c), mm(heads_out[c][0], w_out).astype(bf16))
    half = (len(chunks) + 1) // 2
    later = attend_call(order, sc, q, k_all, v_all, cap, text, tg, 1, half * BR)
    for c in chunks[half:]:
        heads_out[c] = (*later, c - half)
        at = (c - half) * BR
        sums.add(("attn", c), mm(later[0][at : at + BR], w_out).astype(bf16))

    mids, gus = {}, {}
    whole_out = ()
    for c in chunks:
        mids[c], gus[c], ffn_part, *whole_out = ffn_call(
            order, c, patches, sums.get(("attn", c)), vec, w_gate_up, w_down, whole_out
        )
        sums.add(("ffn", c), ffn_part)
    a3, hidden = whole_out
    whole_out = ()
    c4 = 0.0
    for c in chunks:
        da3_part, part_sum, *whole_out = ffn_back_call(
            order, c, sums.get(("ffn", c)), mids[c], cotangent, gus[c], vec, w_gate_up, w_down, whole_out
        )
        sums.add(("da3", c), da3_part)
        c4 = c4 + part_sum
    output, d_ffn, d_gu = whole_out

    d_mids, dqs, dq_caps, d_got, d_mixed, d_scaled = {}, {}, {}, {}, {}, {}
    whole_out = ()
    mlp_part = ()
    behind = ()
    c2 = c3 = dck = dcv = gate_sum = 0.0
    for h in pairs_of:
        for c in (2 * h, 2 * h + 1):
            _, o_self, linv, place = heads_out[c]
            if c == 2 * h + 1 and h > 0:
                behind = d_got[h - 1].second
            da3 = sums.get(("da3", c), behind)
            d_mids[c], d_mixed[c], p3, p2, *outs = out_back_call(
                order, c, da3, mids[c], sums.get(("attn", c)), cotangent, vec, w_out, o_self, linv, place, whole_out
            )
            whole_out, d_scaled[h] = (outs if c % 2 == 0 else outs[:1]), outs[1]
            c2, c3 = c2 + p2, c3 + p3
            behind = ()
            if c == 2 * h:
                early = d_got[h - 1].first if h > 0 else ()
                mlp_part = pair_grad_call(order, a3, d_gu, d_ffn, hidden, h, len(pairs_of), mlp_part, early)
        d_got[h] = GatherOne(d_scaled[h])
        if h < pairs_of[-1]:
            d_got[h].across()
        dq_caps[h], pk, pv, pg = caption_back_call(order, sc, q, d_mixed[2 * h], d_mixed[2 * h + 1], cap, text, tg, h)
        dck, dcv, gate_sum = dck + pk, dcv + pv, gate_sum + pg
    d_attn = whole_out[0]
    cap_sum = jnp.concatenate([dck, dcv], 1)
    cap_got = lax.all_gather(cap_sum.astype(bf16), "wide")
    kept = (firsts == me)[:, None, None]
    cap_sum = jnp.sum(jnp.where(kept, cap_got.astype(f32), 0.0), 0)
    halves_of = lambda table: [table[h] for h in pairs_of]
    dq = dq_call(order, sc, q, halves_of(d_scaled), k_all, v_all, halves_of(dq_caps))
    d_got[pairs_of[-1]].across(order)

    d_cap, hs_c = order.run(
        "caption_grad",
        caption_grad_kernel,
        (1,),
        (cap_sum[:, :n], cap_sum[:, n:], cap_raw[0], hg),
        [whole_cap, whole_cap, whole_cap, whole(hg.shape)],
        [both_cap, pl.BlockSpec((1, n), lambda i: (0, 0))],
        [sds((text, 2 * n), bf16), sds((1, n), f32)],
    )
    d_text = (mm_nt(d_cap[:, :n], w_caption[0]) + mm_nt(d_cap[:, n:], w_caption[1])).astype(bf16)
    cap_part = mm_tn(captions, d_cap).astype(bf16)
    pieces = -(-d_text.shape[1] // d)
    padded = jnp.pad(d_text, ((0, 0), (0, pieces * d - d_text.shape[1])))
    text_parts = [padded[:, p * d : (p + 1) * d] for p in range(pieces)]

    sums.add(("text", 0), text_parts[0])
    ds = [x for h in pairs_of for x in pick(order, sc, d_got[h].pieces(), SPAN)]
    g_mlp = scatter_rows(pin(order, mlp_part[0]))
    whole_out = ()
    c1_parts, hs_parts = [], []
    mixed = jnp.concatenate([heads_out[c][0] for c in chunks[:half]] + [later[0]])
    pairs = n // 128

    def project(c, dkv, after=()):
        nonlocal whole_out
        da1_part, p_hs, p1, *whole_out = dqkv_call(order, c, dq, dkv, q_raw, k_raw, tabs, hg, w_qkv, patches, whole_out)
        hs_parts.append(p_hs)
        c1_parts.append(p1)
        return da1_part

    dkv = []
    for p in range(pairs):
        dkv.append(dkv_call(order, sc, k, v, q_all, ds, p, 1))
        if p + 1 < pieces and p + 1 < pairs:
            sums.add(("text", p + 1), text_parts[p + 1])
        if p == 0:
            g_cap = scatter_rows(pin(order, cap_part))
    for p in range(pairs, pieces):
        sums.add(("text", p), text_parts[p])
    for c in chunks:
        da1_part = project(c, dkv)
        if c == chunks[-1]:
            d_qkv = whole_out[0]
            packed = pack_call(order, c1_parts, hs_parts, hs_c, gate_sum, tg, c2, c3, c4, mz)
            from_narrow = [packed] + [swap(packed, "narrow", deep, m) for m in range(1, deep)]
            attn_part = pair_grad_call(order, a1, d_qkv, d_attn, mixed)[0]
            (folded,) = fold_call(order, from_narrow)
            got = lax.all_gather(folded, "wide")
        sums.add(("da1", c), da1_part, (g_mlp, got) if c == chunks[-1] else ())
    g_attn = scatter_rows(pin(order, attn_part))

    whole_out = ()
    for c in chunks:
        whole_out = last_call(order, c, sums.get(("da1", c), (g_cap,) if c < 3 else (g_attn,)), patches, d_mids[c], vec, whole_out)
    (grad_patches,) = whole_out
    grad_captions = jnp.concatenate([sums.get(("text", p)) for p in range(pieces)], 1)[:, : d_text.shape[1]]

    cols = got[:, :4]
    grad_head_gains = jnp.sum(got[:, 4, : 3 * n], 0).reshape(3, heads, HD).sum(1)
    grad_cross_gate = jnp.sum(got[:, 5], 0)[::HD]
    gain_factor = jnp.stack([scales[:, 0], gates[:, 1], scales[:, 2], gates[:, 3]], 1)
    gain_grads = jnp.sum(gain_factor * cols, 0)
    wide_cols = d // count
    grad_norm_gains = lax.dynamic_slice_in_dim(gain_grads, me * wide_cols, wide_cols, 1)
    ones = jnp.ones_like(gates[:, 0])
    slope = jnp.stack([ones, 1.0 - gates[:, 1] ** 2, ones, 1.0 - gates[:, 3] ** 2], 1)
    d_mod = lax.dynamic_slice_in_dim(slope * norm_gains[None] * cols, mz * ada, ada, 2)
    at_slot = (firsts[None, :] == blocks[:, None]).astype(f32)
    d_slots = jnp.sum(at_slot[:, :, None, None] * d_mod[None], 1).astype(bf16).astype(f32)
    cond_rows = cd // count
    silu_mine = lax.dynamic_slice_in_dim(jax.nn.silu(conds).astype(bf16).astype(f32), me * cond_rows, cond_rows, 1)
    grad_ada = jnp.sum(silu_mine[:, :, None, None] * d_slots[:, None], 0)
    d_mine = lax.dynamic_index_in_dim(d_slots, me, 0, False)
    cond_part = jnp.sum(d_mine[None] * w_ada.astype(f32), (1, 2))
    cond_part = cond_part.reshape(-1, 128)
    cond_total = tree([cond_part] + [swap(cond_part, "narrow", deep, m) for m in range(1, deep)]).reshape(-1)
    pull_silu = jax.vjp(jax.nn.silu, cond)[1]
    grad_conditioning = pull_silu(cond_total)[0].reshape(1, -1)

    rows = d // count
    return (
        output,
        grad_patches,
        grad_conditioning,
        grad_captions,
        grad_ada,
        grad_norm_gains,
        g_attn[:, : 3 * n].astype(f32).reshape(rows, 3, n).transpose(1, 0, 2),
        grad_head_gains,
        grad_cross_gate,
        g_cap.astype(f32).reshape(-1, 2, n).transpose(1, 0, 2),
        g_attn[:, 3 * n :].astype(f32).T,
        g_mlp[:, : 2 * ff].astype(f32).reshape(rows, 2, ff).transpose(1, 0, 2),
        g_mlp[:, 2 * ff :].astype(f32).T,
    )


def solution(mesh):
    placed = (
        P("wide", None),
        P("wide", None),
        P("wide", None),
        P("wide", None),
        P(),
        P(),
        P(None, None, "narrow"),
        P(),
        P(None, None, "narrow"),
        P(),
        P("narrow"),
        P(None, None, "narrow"),
        P("narrow", None),
        P(None, None, "narrow"),
        P("narrow", None),
    )
    return jax.shard_map(
        local,
        mesh=mesh,
        in_specs=placed,
        out_specs=(
            P("wide", None),
            P("wide", None),
            P("wide", None),
            P("wide", None),
            P("wide", None, "narrow"),
            P(None, "wide"),
            P(None, "wide", "narrow"),
            P(),
            P(),
            P(None, "wide", "narrow"),
            P("narrow", "wide"),
            P(None, "wide", "narrow"),
            P("narrow", "wide"),
        ),
        check_vma=False,
    )
```

```python
import functools

import jax
import jax.numpy as jnp
from jax import lax
from jax.experimental import pallas as pl
from jax.experimental.pallas import tpu as pltpu
from jax.sharding import PartitionSpec as P

HD = 64
SPAN = 4
EPS = 1e-05
LOG2E = 1.4426950408889634
f32 = jnp.float32
bf16 = jnp.bfloat16
VMEM = 56 * 1024 * 1024
BR = 256
NT = (((1,), (1,)), ((), ()))
TN = (((0,), (0,)), ((), ()))


def params(n):
    return pltpu.CompilerParams(
        dimension_semantics=("arbitrary",) * n, vmem_limit_bytes=VMEM
    )


def sds(shape, dtype):
    return jax.ShapeDtypeStruct(shape, dtype)


COST = {
    "key": 8, "query": 9, "caption_norm": 2, "pick": 5, "attend": 15, "hop": 3, "ffn": 9, "ffn_back": 10, "out_back": 6,
    "pair_grad": 10, "caption_back": 6, "dq": 27, "dkv": 24, "dqkv": 7, "caption_grad": 3, "last": 3, "note": 1, "pin": 1,
}


class Order:
    def __init__(self):
        self.token = ()

    def run(self, name, kernel, grid, ins, in_specs, out_specs, out_shape, scratch=(), scalar=None, held=(), first_held=0, after=()):
        pre = 0 if scalar is None else 1
        given = pre + len(ins)
        extra = [*self.token, *after, *held]

        def body(*refs):
            kernel(*refs[:given], *refs[given + len(extra) :])

        at = given + len(extra) - len(held)
        out = pl.pallas_call(
            body,
            grid_spec=pltpu.PrefetchScalarGridSpec(
                num_scalar_prefetch=pre,
                grid=grid,
                in_specs=list(in_specs) + loose(len(extra)),
                out_specs=out_specs,
                scratch_shapes=list(scratch),
            ),
            out_shape=out_shape,
            input_output_aliases={at + k: first_held + k for k in range(len(held))},
            compiler_params=params(len(grid)),
            cost_estimate=pl.CostEstimate(
                flops=COST[name] * 250_000_000, bytes_accessed=COST[name] * 750_000, transcendentals=0
            ),
            name=name,
        )(*(() if scalar is None else (scalar,)), *ins, *extra)
        self.token = (out[0],)
        return out


def loose(n):
    return [pl.BlockSpec(memory_space=pl.ANY)] * n


def mm(a, b):
    return jnp.dot(a, b, preferred_element_type=f32)


def mm_nt(a, b):
    return lax.dot_general(a, b, NT, preferred_element_type=f32)


def mm_tn(a, b):
    return lax.dot_general(a, b, TN, preferred_element_type=f32)


def split(x):
    hi = x.astype(bf16)
    return hi, (x - hi.astype(f32)).astype(bf16)


def head_sum(x, ones):
    hi, lo = split(x)
    return mm(hi, ones) + mm(lo, ones)


def head_ones(n):
    a = lax.broadcasted_iota(jnp.int32, (n, n), 0) // HD
    b = lax.broadcasted_iota(jnp.int32, (n, n), 1) // HD
    return (a == b).astype(bf16)


def halves(n):
    lane = lax.broadcasted_iota(jnp.int32, (1, n), 1)
    return (lane < HD, lane >= HD)


def keep(x, mask):
    return jnp.where(mask, x, jnp.zeros_like(x))


def inv_rms(x):
    return lax.rsqrt(jnp.mean(x * x, -1, keepdims=True) + EPS)


def row(ref, k):
    return ref[k : k + 1, :]


def whole(shape):
    zeros = (0,) * len(shape)
    return pl.BlockSpec(shape, lambda *_: zeros, pipeline_mode=pl.Buffered(1))


def rows_of(br, width, first=0):
    return pl.BlockSpec((br, width), lambda i, *_: (i, first))


def accumulate(ref, value, first):
    @pl.when(first)
    def _():
        ref[...] = value

    @pl.when(jnp.logical_not(first))
    def _():
        ref[...] += value


def col_sum(x):
    return jnp.sum(x, 0, keepdims=True)


def tile3(t, n):
    return jnp.concatenate([t] * (n // t.shape[1]), 1)


def key_kernel(p_ref, v_ref, w_ref, wv_ref, wq_ref, c_ref, s1_ref, s2_ref, hg_ref, a_ref, kr_ref, k_ref, vv_ref, qr_ref, q_ref):
    x = p_ref[...].astype(f32)
    a = (x * inv_rms(x) * row(v_ref, 0)).astype(bf16)
    a_ref[...] = a
    k = mm(a, w_ref[0])
    kr_ref[...] = k
    k_ref[...] = turned(k, row(hg_ref, 1), (c_ref, s1_ref, s2_ref)).astype(bf16)
    vv_ref[...] = mm(a, wv_ref[0]).astype(bf16)
    q = mm(a, wq_ref[0])
    qr_ref[...] = q
    q_ref[...] = (turned(q, row(hg_ref, 0), (c_ref, s1_ref, s2_ref)) * (0.125 * LOG2E)).astype(bf16)


def turned(y, gain, tabs):
    n = y.shape[1]
    cos, s1, s2 = (tile3(t[...], n) for t in tabs)
    z = y * lax.rsqrt(head_sum(y * y, head_ones(n)) * (1.0 / HD) + EPS) * gain
    return z * cos + pltpu.roll(z, n - 16, 1) * s1 + pltpu.roll(z, 16, 1) * s2


def one_weight(w, k):
    return pl.BlockSpec((1, *w.shape[1:]), lambda *_: (k, 0, 0), pipeline_mode=pl.Buffered(1))


def key_call(order, patches, vec, w, tabs, hg, after, br=256):
    t, d = patches.shape
    n = w.shape[2]
    return order.run(
        "key",
        key_kernel,
        (t // br,),
        (patches, vec, w, w, w, *tabs, hg),
        [rows_of(br, d), whole(vec.shape), one_weight(w, 1), one_weight(w, 2), one_weight(w, 0)] + [rows_of(br, 128)] * 3 + [whole(hg.shape)],
        [rows_of(br, d)] + [rows_of(br, n)] * 5,
        [sds((t, d), bf16), sds((t, n), f32), sds((t, n), bf16), sds((t, n), bf16), sds((t, n), f32), sds((t, n), bf16)],
        after=after,
    )


def soft_sums(q, k, v, mask):
    e = jnp.exp2(mm_nt(q, keep(k, mask))).astype(bf16)
    return mm(e, jnp.where(mask, v, jnp.ones_like(v)))


def item_block(j, s):
    return jnp.minimum(j, s[0] - 1)


def attend_kernel(sc, q_ref, k_ref, v_ref, ck_ref, cv_ref, tg_ref, mix_ref, o_ref, li_ref, acc):
    j = pl.program_id(1)
    masks = halves(128)
    keys = k_ref.shape[0] if q_ref.shape[0] <= BR else 512

    def block_sums(h):
        q = q_ref[...]
        total = 0.0
        for c in range(k_ref.shape[0] // keys):
            at = slice(c * keys, (c + 1) * keys)
            total = total + soft_sums(q, k_ref[at, :], v_ref[at, :], masks[h])
        return total

    @pl.when(j == 0)
    def _():
        for h in range(2):
            acc[2 + h] = soft_sums(q_ref[...], ck_ref[...], cv_ref[...], masks[h])
            acc[h] = block_sums(h)

    @pl.when((j > 0) & (j < sc[0]))
    def _():
        for h in range(2):
            acc[h] += block_sums(h)

    @pl.when(j == SPAN - 1)
    def _():
        def finish(a0, a1):
            inverse = 1.0 / jnp.where(masks[0], pltpu.roll(a0, HD, 1), pltpu.roll(a1, HD, 1))
            return jnp.where(masks[0], a0, a1) * inverse, inverse

        o, li = finish(acc[0], acc[1])
        mix_ref[...] = (o + tg_ref[...] * finish(acc[2], acc[3])[0]).astype(bf16)
        o_ref[...] = o.astype(bf16)
        li_ref[...] = li


def attend_call(order, sc, q, k, v, cap, text, tg, at, bq):
    n = q.shape[1]
    pairs = n // 128
    block = k.shape[0] // SPAN
    mine = lambda p, j, s: (0, p)
    other = lambda p, j, s: (item_block(j, s), p)
    return order.run(
        "attend",
        attend_kernel,
        (pairs, SPAN),
        (q, k, v, cap, cap, tg),
        [
            pl.BlockSpec((bq, 128), lambda p, j, s: (at, p)),
            pl.BlockSpec((block, 128), other),
            pl.BlockSpec((block, 128), other),
            pl.BlockSpec((text, 128), lambda p, j, s: (s[1 + SPAN], p)),
            pl.BlockSpec((text, 128), lambda p, j, s: (s[1 + SPAN], pairs + p)),
            pl.BlockSpec((1, 128), mine),
        ],
        [pl.BlockSpec((bq, 128), mine)] * 3,
        [sds((bq, n), bf16), sds((bq, n), bf16), sds((bq, n), f32)],
        [pltpu.VMEM((4, bq, 128), f32)],
        sc,
    )


def caption_back_kernel(sc, q_ref, da_ref, db_ref, ck_ref, cv_ref, tg_ref, dq_ref, dk_ref, dv_ref, gs_ref):
    masks = halves(128)
    q, d = q_ref[...], jnp.concatenate([da_ref[...], db_ref[...]], 0)
    dq = jnp.zeros(q.shape, f32)
    dk = jnp.zeros(ck_ref.shape, f32)
    dv = jnp.zeros(ck_ref.shape, f32)
    sums = []
    for h in range(2):
        ck, cv = keep(ck_ref[...], masks[h]), keep(cv_ref[...], masks[h])
        gate = tg_ref[:, h * HD : h * HD + 1]
        e = jnp.exp2(mm_nt(q, ck))
        prob = e * (1.0 / jnp.sum(e, -1, keepdims=True))
        dp = mm_nt(d, cv)
        m = jnp.sum(prob * dp, -1, keepdims=True)
        dc = (prob * (dp - m) * gate).astype(bf16)
        dq = dq + mm(dc, ck)
        dk = dk + mm_tn(dc, keep(q, masks[h]))
        dv = dv + mm_tn(prob.astype(bf16), keep(d, masks[h]))
        sums.append(jnp.sum(m, 0, keepdims=True))
    dq_ref[...] = dq * 0.125
    dk_ref[...] = dk * (1.0 / LOG2E)
    dv_ref[...] = dv * tg_ref[...]
    gs_ref[...] = jnp.where(masks[0], sums[0], sums[1])


def caption_back_call(order, sc, q, da, db, cap, text, tg, h):
    n = q.shape[1]
    pairs = n // 128
    bq = 2 * BR
    mine = lambda p, s: (0, p)
    return order.run(
        "caption_back",
        caption_back_kernel,
        (pairs,),
        (q, da, db, cap, cap, tg),
        [
            pl.BlockSpec((bq, 128), lambda p, s: (h, p)),
            pl.BlockSpec((BR, 128), mine),
            pl.BlockSpec((BR, 128), mine),
            pl.BlockSpec((text, 128), lambda p, s: (s[1 + SPAN], p)),
            pl.BlockSpec((text, 128), lambda p, s: (s[1 + SPAN], pairs + p)),
            pl.BlockSpec((1, 128), mine),
        ],
        [
            pl.BlockSpec((bq, 128), mine),
            pl.BlockSpec((text, 128), mine),
            pl.BlockSpec((text, 128), mine),
            pl.BlockSpec((1, 128), mine),
        ],
        [sds((bq, n), f32), sds((text, n), f32), sds((text, n), f32), sds((1, n), f32)],
        scalar=sc,
    )


def minus_delta(rows, head):
    lane = lax.broadcasted_iota(jnp.int32, (rows, 128), 1)
    return jnp.where((lane >= 3 * head) & (lane < 3 * head + 3), -1.0, 0.0).astype(bf16)


def dq_kernel(sc, q_ref, d_ref, x_ref, k_ref, v_ref, c_ref, dq_ref, acc):
    pair = pl.program_id(0)
    j = pl.program_id(1)
    masks = halves(128)
    keys = 512

    @pl.when(j == 0)
    def _():
        acc[...] = jnp.zeros_like(acc)

    @pl.when(j < sc[0])
    def _():
        q = q_ref[...]
        dx = jnp.concatenate([d_ref[...], x_ref[...]], 1)
        total = acc[...]
        for h in range(2):
            off = minus_delta(keys, 2 * pair + h)
            for c in range(k_ref.shape[0] // keys):
                at = slice(c * keys, (c + 1) * keys)
                k = keep(k_ref[at, :], masks[h])
                e = jnp.exp2(mm_nt(q, k))
                dp = mm_nt(dx, jnp.concatenate([keep(v_ref[at, :], masks[h]), off], 1))
                total = total + mm((e * dp).astype(bf16), k)
        acc[...] = total

    @pl.when(j == SPAN - 1)
    def _():
        dq_ref[...] = acc[...] * 0.125 + c_ref[...]


def dq_call(order, sc, q, d, k, v, cap_dq, h, after=()):
    n = q.shape[1]
    pairs = n // 128
    block = k.shape[0] // SPAN
    bq = 2 * BR
    mine = lambda p, j, s: (0, p)
    extra = lambda p, j, s: (0, pairs)
    other = lambda p, j, s: (item_block(j, s), p)
    return order.run(
        "dq",
        dq_kernel,
        (pairs, SPAN),
        (q, d, d, k, v, cap_dq),
        [
            pl.BlockSpec((bq, 128), lambda p, j, s: (h, p)),
            pl.BlockSpec((bq, 128), mine),
            pl.BlockSpec((bq, 128), extra),
            pl.BlockSpec((block, 128), other),
            pl.BlockSpec((block, 128), other),
            pl.BlockSpec((bq, 128), mine),
        ],
        [pl.BlockSpec((bq, 128), mine)],
        [sds((bq, n), f32)],
        [pltpu.VMEM((bq, 128), f32)],
        sc,
        after=after,
    )[0]


def dkv_kernel(parts, base, sc, k_ref, v_ref, q_ref, *rest):
    d_refs, x_refs = rest[0 : 2 * parts : 2], rest[1 : 2 * parts : 2]
    dk_ref, dv_ref = rest[2 * parts :]
    pair = base + pl.program_id(0)
    j = pl.program_id(1)
    masks = halves(128)
    queries = 2 * BR

    @pl.when(j == 0)
    def _():
        dk_ref[...] = jnp.zeros_like(dk_ref)
        dv_ref[...] = jnp.zeros_like(dv_ref)

    @pl.when(j < sc[0])
    def _():
        dk, dv = dk_ref[...], dv_ref[...]
        for h in range(2):
            vx = jnp.concatenate([keep(v_ref[...], masks[h]), minus_delta(v_ref.shape[0], 2 * pair + h)], 1)
            for r in range(parts):
                q = keep(q_ref[r * queries : (r + 1) * queries, :], masks[h])
                d, x = d_refs[r][...], x_refs[r][...]
                e = jnp.exp2(mm_nt(k_ref[...], q))
                dp = mm_nt(vx, jnp.concatenate([d, x], 1))
                dv = dv + mm(e.astype(bf16), keep(d, masks[h]))
                dk = dk + mm((e * dp).astype(bf16), q)
        dk_ref[...] = dk
        dv_ref[...] = dv


def dkv_call(order, sc, k, v, q_all, ds, half, base, n_pairs):
    t, n = k.shape
    pairs = n // 128
    rows = 2 * BR
    mine = pl.BlockSpec((rows, 128), lambda p, j, s: (half, base + p))
    out = pl.BlockSpec((rows, 128), lambda p, j, s: (0, p))
    other = pl.BlockSpec((rows, 128), lambda p, j, s: (item_block(j, s), base + p))
    extra = pl.BlockSpec((rows, 128), lambda p, j, s: (item_block(j, s), pairs))
    return order.run(
        "dkv",
        functools.partial(dkv_kernel, len(ds), base),
        (n_pairs, SPAN),
        (k, v, q_all, *(x for d in ds for x in (d, d))),
        [mine, mine, pl.BlockSpec((t, 128), lambda p, j, s: (s[1 + SPAN + j], base + p))] + [other, extra] * len(ds),
        [out, out],
        [sds((rows, n_pairs * 128), f32)] * 2,
        scalar=sc,
    )


def chunk_call(order, kernel, name, c, ins, specs, chunk_outs, sum_outs, whole_outs, before):
    one = lambda r, w: pl.BlockSpec((r, w), lambda i: (0, 0))
    own = chunk_outs + sum_outs
    into = [pl.BlockSpec((BR, w), lambda i, at=c % (r // BR): (at, 0)) for r, w, _ in whole_outs]
    return order.run(
        name,
        kernel,
        (1,),
        ins,
        specs,
        [one(r, w) for r, w, _ in own] + into,
        [sds((r, w), k) for r, w, k in own + whole_outs],
        held=tuple(before),
        first_held=len(own),
    )


def part(c, width):
    return pl.BlockSpec((BR, width), lambda i: (c, 0))


def alone(width):
    return pl.BlockSpec((BR, width), lambda i: (0, 0))


def pair_grad_kernel(a_ref, b_ref, c_ref, d_ref, o_ref):
    n = b_ref.shape[1]
    o_ref[:, :n] = mm_tn(a_ref[...], b_ref[...]).astype(bf16)
    o_ref[:, n:] = mm_tn(c_ref[...], d_ref[...]).astype(bf16)


def pair_grad_call(order, a, b, c, d, part=0, parts=1, before=(), after=()):
    t, m = a.shape
    n, k = b.shape[1], d.shape[1]
    blk = 256
    steps = m // blk // parts
    cols = pl.BlockSpec((t, blk), lambda i: (0, part * steps + i))
    return order.run(
        "pair_grad",
        pair_grad_kernel,
        (steps,),
        (a, b, c, d),
        [cols, whole(b.shape), cols, whole(d.shape)],
        [pl.BlockSpec((blk, n + k), lambda i: (part * steps + i, 0))],
        [sds((m, n + k), bf16)],
        held=before,
        after=after,
    )


def ffn_kernel(p_ref, at_ref, v_ref, wg_ref, wd_ref, mid_ref, gu_ref, f_ref, a_ref, h_ref):
    at = at_ref[...].astype(f32)
    mid = p_ref[...].astype(f32) + row(v_ref, 1) * (at * inv_rms(at))
    mid_ref[...] = mid
    a = (mid * inv_rms(mid) * row(v_ref, 2)).astype(bf16)
    a_ref[...] = a
    g = mm(a, wg_ref[0])
    u = mm(a, wg_ref[1])
    n = g.shape[1]
    gu_ref[:, :n] = g.astype(bf16)
    gu_ref[:, n:] = u.astype(bf16)
    h = (g * jax.nn.sigmoid(g) * u).astype(bf16)
    h_ref[...] = h
    f_ref[...] = mm(h, wd_ref[...]).astype(bf16)


def ffn_call(order, c, patches, at, vec, wg, wd, before):
    t, d = patches.shape
    n = wd.shape[0]
    return chunk_call(
        order,
        ffn_kernel,
        "ffn",
        c,
        (patches, at, vec, wg, wd),
        [part(c, d), alone(d), whole(vec.shape), whole(wg.shape), whole(wd.shape)],
        [(BR, d, f32), (BR, 2 * n, bf16), (BR, d, bf16)],
        [],
        [(t, d, bf16), (t, n, bf16)],
        before,
    )


def ffn_back_kernel(f_ref, mid_ref, c_ref, gu_ref, v_ref, wg_ref, wd_ref, da_ref, cs_ref, y_ref, df_ref, dgu_ref):
    f = f_ref[...].astype(f32)
    cot = c_ref[...].astype(f32)
    r = inv_rms(f)
    fh = f * r
    y_ref[...] = (mid_ref[...] + row(v_ref, 3) * fh).astype(bf16)
    z = cot * row(v_ref, 3)
    df = (r * (z - fh * jnp.mean(z * fh, -1, keepdims=True))).astype(bf16)
    df_ref[...] = df
    cs_ref[...] = col_sum(cot * fh)
    dh = mm_nt(df, wd_ref[...])
    n = dh.shape[1]
    g = gu_ref[:, :n].astype(f32)
    u = gu_ref[:, n:].astype(f32)
    s = jax.nn.sigmoid(g)
    gs = g * s
    dg = (dh * u * (s + gs * (1.0 - s))).astype(bf16)
    du = (dh * gs).astype(bf16)
    dgu_ref[:, :n] = dg
    dgu_ref[:, n:] = du
    da_ref[...] = (mm_nt(dg, wg_ref[0]) + mm_nt(du, wg_ref[1])).astype(bf16)


def ffn_back_call(order, c, f, mid, cot, gu, vec, wg, wd, before):
    t, d = cot.shape
    n = wd.shape[0]
    return chunk_call(
        order,
        ffn_back_kernel,
        "ffn_back",
        c,
        (f, mid, cot, gu, vec, wg, wd),
        [alone(d), alone(d), part(c, d), alone(2 * n), whole(vec.shape), whole(wg.shape), whole(wd.shape)],
        [(BR, d, bf16)],
        [(1, d, f32)],
        [(t, d, bf16), (t, d, bf16), (t, 2 * n, bf16)],
        before,
    )


def out_back_kernel(da_ref, mid_ref, at_ref, c_ref, v_ref, w_ref, o_ref, li_ref, dm_ref, dx_ref, c3_ref, c2_ref, dat_ref, ds_ref):
    da = da_ref[...].astype(f32)
    mid = mid_ref[...]
    r = inv_rms(mid)
    mh = mid * r
    z = da * row(v_ref, 2)
    dm = c_ref[...].astype(f32) + r * (z - mh * jnp.mean(z * mh, -1, keepdims=True))
    dm_ref[...] = dm
    c3_ref[...] = col_sum(da * mh)
    at = at_ref[...].astype(f32)
    ra = inv_rms(at)
    ah = at * ra
    c2_ref[...] = col_sum(dm * ah)
    z = dm * row(v_ref, 1)
    dat = (ra * (z - ah * jnp.mean(z * ah, -1, keepdims=True))).astype(bf16)
    dat_ref[...] = dat
    dx = mm_nt(dat, w_ref[...]).astype(bf16)
    dx_ref[...] = dx
    n = dx.shape[1]
    ds = dx.astype(f32) * li_ref[...]
    ds_ref[:, :n] = ds.astype(bf16)
    hi, lo = split(ds * o_ref[...].astype(f32))
    head = lax.broadcasted_iota(jnp.int32, (n, 128), 0) // HD
    lane = lax.broadcasted_iota(jnp.int32, (n, 128), 1)
    to_lanes = (lane // 3 == head).astype(bf16)
    delta = mm(hi, to_lanes) + mm(lo, to_lanes)
    one = delta.astype(bf16).astype(f32)
    two = (delta - one).astype(bf16).astype(f32)
    which = lax.broadcasted_iota(jnp.int32, (1, 128), 1) % 3
    ds_ref[:, n:] = jnp.where(which == 0, one, jnp.where(which == 1, two, delta - one - two)).astype(bf16)


def out_back_call(order, c, da, mid, at, cot, vec, w, o, li, place, before):
    t, d = cot.shape
    n = w.shape[0]
    return chunk_call(
        order,
        out_back_kernel,
        "out_back",
        c,
        (da, mid, at, cot, vec, w, o, li),
        [alone(d), alone(d), alone(d), part(c, d), whole(vec.shape), whole(w.shape), part(place, n), part(place, n)],
        [(BR, d, f32), (BR, n, bf16)],
        [(1, d, f32), (1, d, f32)],
        [(t, d, bf16), (2 * BR, n + 128, bf16)],
        before,
    )


def dqkv_kernel(pairs, dq_ref, *refs):
    dk_refs, dv_refs = refs[0 : 2 * pairs : 2], refs[1 : 2 * pairs : 2]
    (qr_ref, kr_ref, c_ref, s1_ref, s2_ref, hg_ref, w_ref, p_ref, da_ref, hs_ref, cs_ref, d_ref) = refs[2 * pairs :]
    side = lambda parts: jnp.concatenate([x[...] for x in parts], 1)
    n = dq_ref.shape[1]
    ones = head_ones(n)
    cos, s1, s2 = (tile3(t[...], n) for t in (c_ref, s1_ref, s2_ref))

    def back(dy, x, gain):
        dz = dy * cos - pltpu.roll(dy, 16, 1) * s2 - pltpu.roll(dy, n - 16, 1) * s1
        r = lax.rsqrt(head_sum(x * x, ones) * (1.0 / HD) + EPS)
        xh = x * r
        g = dz * gain
        return r * (g - xh * (head_sum(g * xh, ones) * (1.0 / HD))), col_sum(dz * xh)

    dq, hq = back(dq_ref[...], qr_ref[...], row(hg_ref, 0))
    dk, hk = back(side(dk_refs) * (1.0 / LOG2E), kr_ref[...], row(hg_ref, 1))
    dql, dkl, dvl = dq.astype(bf16), dk.astype(bf16), side(dv_refs).astype(bf16)
    d_ref[:, :n] = dql
    d_ref[:, n : 2 * n] = dkl
    d_ref[:, 2 * n :] = dvl
    da = mm_nt(dql, w_ref[0]) + mm_nt(dkl, w_ref[1]) + mm_nt(dvl, w_ref[2])
    da_ref[...] = da.astype(bf16)
    x = p_ref[...].astype(f32)
    cs_ref[...] = col_sum(da * (x * inv_rms(x)))
    hs_ref[0:1, :] = hq
    hs_ref[1:2, :] = hk


def dqkv_call(order, c, dq, dkv, qr, kr, tabs, hg, w, patches, before):
    t, d = patches.shape
    n = dq.shape[1]
    return chunk_call(
        order,
        functools.partial(dqkv_kernel, len(dkv)),
        "dqkv",
        c,
        (dq, *(x for two in dkv for x in two), qr, kr, *tabs, hg, w, patches),
        [part(c % 2, n)] + [part(c % 2, x.shape[1]) for two in dkv for x in two] + [part(c, n)] * 2 + [part(c, 128)] * 3 + [whole(hg.shape), whole(w.shape), part(c, d)],
        [(BR, d, bf16)],
        [(2, n, f32), (1, d, f32)],
        [(t, 3 * n, bf16)],
        before,
    )


def last_kernel(da_ref, p_ref, dm_ref, v_ref, o_ref):
    x = p_ref[...].astype(f32)
    r = inv_rms(x)
    xh = x * r
    z = da_ref[...].astype(f32) * row(v_ref, 0)
    o_ref[...] = (dm_ref[...] + r * (z - xh * jnp.mean(z * xh, -1, keepdims=True))).astype(bf16)


def last_call(order, c, da, patches, dm, vec, before):
    t, d = patches.shape
    return chunk_call(
        order,
        last_kernel,
        "last",
        c,
        (da, patches, dm, vec),
        [alone(d), part(c, d), alone(d), whole(vec.shape)],
        [],
        [],
        [(t, d, bf16)],
        before,
    )


def caption_grad_kernel(dk_ref, dv_ref, kr_ref, hg_ref, d_ref, hs_ref):
    n = dk_ref.shape[1]
    ones = head_ones(n)
    x = kr_ref[...]
    r = lax.rsqrt(head_sum(x * x, ones) * (1.0 / HD) + EPS)
    xh = x * r
    dy = dk_ref[...]
    g = dy * row(hg_ref, 2)
    d_ref[:, :n] = (r * (g - xh * (head_sum(g * xh, ones) * (1.0 / HD)))).astype(bf16)
    d_ref[:, n:] = dv_ref[...].astype(bf16)
    hs_ref[...] = col_sum(dy * xh)


def caption_norm_kernel(kr_ref, v_ref, hg_ref, o_ref):
    n = kr_ref.shape[1]
    x = kr_ref[...]
    r = lax.rsqrt(head_sum(x * x, head_ones(n)) * (1.0 / HD) + EPS)
    o_ref[:, :n] = (x * r * row(hg_ref, 2)).astype(bf16)
    o_ref[:, n:] = v_ref[...].astype(bf16)


def swap(x, axis, size, m):
    return lax.ppermute(x, axis, [(i, i ^ m) for i in range(size)])


def pick_kernel(count, n_arrays, n_pieces, sc, *refs):
    outs, sem = refs[n_arrays * n_pieces :][:n_arrays], refs[-1]
    for k, out in enumerate(outs):
        pieces = refs[k * n_pieces : (k + 1) * n_pieces]
        rows = pieces[0].shape[0]
        for j in range(count):
            for m in range(n_pieces):

                @pl.when(sc[1 + j] == m)
                def _():
                    pltpu.make_async_copy(pieces[m], out.at[pl.ds(j * rows, rows)], sem.at[k, j]).start()

    for k, out in enumerate(outs):
        first = refs[k * n_pieces]
        rows = first.shape[0]
        for j in range(count):
            pltpu.make_async_copy(first, out.at[pl.ds(j * rows, rows)], sem.at[k, j]).wait()


class Gather:
    def __init__(self, a, b):
        self.all = None
        if lax.axis_size("wide") != 8:
            self.first = self.second = ()
            self.all = [lax.all_gather(x, "wide") for x in (a, b)]
            return
        send = lambda x, pairs: lax.ppermute(x, "wide", pairs)
        over_x = [(i, i ^ 2) for i in range(8)]
        over_y = [(1, 5), (4, 0), (3, 7), (6, 2)]
        a2, a4, b4, b2 = send(a, over_x), send(a, over_y), send(b, over_y), send(b, over_x)
        a6 = send(a2, [(0, 4), (1, 5), (6, 2), (7, 3)])
        b6x, b6y = send(b2, [(0, 4), (7, 3)]), send(b4, [(7, 5), (0, 2)])
        self.first = (a2, a4, b4, b2)
        self.second = (a6, b6x, b6y)
        self.kept = ((a, a2, a4, a6), (b, b2, b4, b6x + b6y))

    def pieces(self):
        if self.all is not None:
            return self.all
        return [[y for x in four for y in (x, swap(x, "wide", 8, 1))] for four in self.kept]


class GatherOne:
    def __init__(self, a):
        self.all = None
        if lax.axis_size("wide") != 8:
            self.first = self.second = ()
            self.all = [lax.all_gather(a, "wide")]
            return
        send = lambda x, pairs: lax.ppermute(x, "wide", pairs)
        a2 = send(a, [(i, i ^ 2) for i in range(8)])
        a4 = send(a, [(1, 5), (4, 0), (3, 7), (6, 2)])
        a6 = send(a2, [(0, 4), (1, 5), (6, 2), (7, 3)])
        self.first, self.second = (a2, a4), (a6,)
        self.kept = ((a, a2, a4, a6),)

    pieces = Gather.pieces


def pick(order, sc, pieces, count):
    if not isinstance(pieces[0], list):
        one = lambda x, j: lax.dynamic_index_in_dim(x, sc[1 + SPAN + j], 0, False)
        return [jnp.concatenate([one(x, j) for j in range(count)]) for x in pieces]
    outs = [(count * p[0].shape[0], p[0].shape[1]) for p in pieces]
    return order.run(
        "pick",
        functools.partial(pick_kernel, count, len(pieces), 8),
        (1,),
        [x for p in pieces for x in p],
        loose(8 * len(pieces)),
        [pl.BlockSpec(shape, lambda i, s: (0, 0)) for shape in outs],
        [sds(shape, bf16) for shape in outs],
        [pltpu.SemaphoreType.DMA((len(pieces), count))],
        sc,
    )


def tree(parts):
    while len(parts) > 1:
        parts = [a + b for a, b in zip(parts[::2], parts[1::2])]
    return parts[0]


def pack_kernel(count, place, *refs):
    c1, hs = refs[:count], refs[count : 2 * count]
    hc_ref, gs_ref, tg_ref, c2_ref, c3_ref, c4_ref, o_ref = refs[2 * count :]
    n = hc_ref.shape[1]
    o_ref[...] = jnp.zeros_like(o_ref)
    o_ref[0:1, :] = sum(x[...] for x in c1)
    o_ref[1:2, :] = c2_ref[...]
    o_ref[2:3, :] = c3_ref[...]
    o_ref[3:4, :] = c4_ref[...]
    qk = sum(x[...] for x in hs)
    o_ref[4:5, :n] = qk[0:1]
    o_ref[4:5, n : 2 * n] = qk[1:2]
    o_ref[4:5, 2 * n : 3 * n] = hc_ref[...]
    gate = gs_ref[...] * (1.0 - tg_ref[...] * tg_ref[...])
    for z in range(o_ref.shape[1] // n):
        o_ref[5:6, z * n : (z + 1) * n] = jnp.where(place[0] == z, gate, 0.0)


def pack_call(order, c1, hs, hc, gs, tg, c2, c3, c4, place):
    d = c2.shape[1]
    ins = (*c1, *hs, hc, gs, tg, c2, c3, c4)
    spec = lambda x: pl.BlockSpec(x.shape, lambda i, s: (0, 0))

    def kernel(place, *refs):
        pack_kernel(len(c1), place, *refs)

    return order.run(
        "note",
        kernel,
        (1,),
        ins,
        [spec(x) for x in ins],
        [pl.BlockSpec((8, d), lambda i, s: (0, 0))],
        [sds((8, d), f32)],
        scalar=place.astype(jnp.int32).reshape(1),
    )[0]


def fold_kernel(*refs):
    parts, o_ref = refs[:-1], refs[-1]
    total = tree([x[...] for x in parts])
    row_at = lax.broadcasted_iota(jnp.int32, total.shape, 0)
    o_ref[...] = jnp.where((row_at >= 1) & (row_at < 4), parts[0][...], total)


def fold_call(order, parts):
    spec = pl.BlockSpec(parts[0].shape, lambda i: (0, 0))
    return order.run("note", fold_kernel, (1,), parts, [spec] * len(parts), [spec], [sds(parts[0].shape, f32)])


def pin_kernel(o_ref):
    pass


def pin(order, x, after=()):
    return order.run("pin", pin_kernel, (1,), (), [], loose(1), [sds(x.shape, x.dtype)], held=(x,), after=after)[0]


def gather_now(x, axis):
    n = x.shape[0]
    wide = -(-n // 1024) * 1024
    padded = jnp.pad(x, (0, wide - n)).reshape(1, 8, wide // 8)
    return lax.all_gather(padded, axis, axis=0, tiled=True).reshape(-1, wide)[:, :n]


def hop_kernel(have, sc, *refs):
    ins = dict(zip(have["in"], refs))
    outs = dict(zip(have["out"], refs[len(have["in"]) :]))
    end = sc[0] == 1
    if "total" in outs:
        outs["total"][...] = jnp.where(end, ins["r1"][...], ins["send"][...])
    third = None
    if "second" in ins:
        third = ins["second"][...] + ins["r2"][...]
    if "second" in outs:
        outs["second"][...] = ins["x"][...] + ins["r1"][...]
    if "send" in outs:
        new = ins["new"][...] if "new" in ins else third
        outs["send"][...] = new if third is None else jnp.where(end, new, third)


class Line:
    def __init__(self, order, place):
        self.order = order
        self.end = ((place == 0) | (place == 3)).astype(jnp.int32).reshape(1)
        self.x = self.second = self.send = None
        self.third = False

    def step(self, new, after=()):
        if self.send is None:
            self.x = self.send = new
            return None
        go = lambda x, perm: lax.ppermute(x, "narrow", perm)
        ins = {"r1": go(self.send, [(0, 1), (3, 2), (1, 0), (2, 3)])}
        outs = []
        if self.third:
            ins["send"] = self.send
            outs.append("total")
        if self.second is not None:
            ins["r2"] = go(self.second, [(1, 2), (2, 1)])
            ins["second"] = self.second
        if self.x is not None:
            ins["x"] = self.x
            outs.append("second")
        if new is not None:
            ins["new"] = new
        if new is not None or self.second is not None:
            outs.append("send")
        like = ins["r1"]
        block = pl.BlockSpec((BR // 2, like.shape[1]), lambda i, s: (i, 0))
        got = self.order.run(
            "hop",
            functools.partial(hop_kernel, {"in": list(ins), "out": outs}),
            (2,),
            list(ins.values()),
            [block] * len(ins),
            [block] * len(outs),
            [sds(like.shape, like.dtype)] * len(outs),
            scalar=self.end,
            after=after,
        )
        got = dict(zip(outs, got))
        self.third = self.second is not None
        self.x, self.second, self.send = new, got.get("second"), got.get("send")
        return got.get("total")


class Sums:
    def __init__(self, order, size, place):
        self.line = Line(order, place) if size == 4 else None
        self.names, self.done = [], {}

    def add(self, name, x, after=()):
        if self.line is None:
            self.done[name] = lax.psum(x, "narrow")
            return
        if self.line.send is None:
            self.names = [None]
        self._step(name, x, after)

    def _step(self, name, x, after):
        total = self.line.step(x, after)
        self.names.append(name)
        if total is not None:
            self.done[self.names[-4]] = total

    def get(self, name, after=()):
        while name not in self.done:
            self._step(None, None, after)
            after = ()
        return self.done[name]


def scatter_rows(x):
    return lax.psum_scatter(x.astype(bf16), "wide", scatter_dimension=0, tiled=True)


def rope_tables(position, width):
    lane = jnp.arange(128, dtype=jnp.int32)
    within = lane % HD
    quarter = HD // 4
    frequency = 10000.0 ** (-(within % quarter).astype(f32) / quarter)
    by_row = within < HD // 2
    where = jnp.where(by_row[None, :], (position // width)[:, None], (position % width)[:, None])
    angle = where.astype(f32) * frequency[None, :]
    cos, sin = jnp.cos(angle), jnp.sin(angle)
    former = (within % (HD // 2) < quarter)[None, :]
    return cos, jnp.where(former, -sin, 0.0), jnp.where(former, 0.0, sin)


def local(
    patches,
    cotangent,
    conditioning,
    captions,
    item_lengths,
    grid_widths,
    w_ada,
    norm_gains,
    w_qkv,
    head_gains,
    cross_gate,
    w_caption,
    w_out,
    w_gate_up,
    w_down,
):
    t, d = patches.shape
    n = w_qkv.shape[2]
    heads = n // HD
    ada = w_ada.shape[2]
    ff = w_down.shape[0]
    text = captions.shape[0]
    cd = conditioning.shape[1]
    count = lax.axis_size("wide")
    deep = lax.axis_size("narrow")
    me = lax.axis_index("wide")
    mz = lax.axis_index("narrow")

    slots = item_lengths.shape[0]
    spans = item_lengths // t
    order = jnp.arange(slots, dtype=jnp.int32)
    ends = jnp.sum(jnp.where(order[None, :] <= order[:, None], spans[None, :], 0), 1)
    blocks = jnp.arange(count, dtype=jnp.int32)
    item = jnp.sum((ends[None, :] <= blocks[:, None]).astype(jnp.int32), 1)
    is_item = item[:, None] == order[None, :]
    choose = lambda values: jnp.sum(jnp.where(is_item, values[None, :], 0), 1)
    firsts = choose(ends - spans)
    mine = blocks == me
    of_me = lambda values: jnp.sum(jnp.where(mine, values, 0))
    first = of_me(firsts)
    length = of_me(choose(spans))
    width = of_me(choose(grid_widths))
    position = (me - first) * t + jnp.arange(t, dtype=jnp.int32)
    tabs = rope_tables(position, width)
    steps = first + jnp.minimum(jnp.arange(SPAN, dtype=jnp.int32), length - 1)
    places = steps ^ me if count == 8 else steps
    sc = jnp.concatenate([length.reshape(1), places, steps]).astype(jnp.int32)

    cond = conditioning.astype(f32)[0]
    silu_low = jax.nn.silu(cond).astype(bf16)
    mod = jnp.sum(silu_low.astype(f32)[:, None, None] * w_ada.astype(f32), 0)
    share = cd // deep
    sent = jnp.concatenate([mod.reshape(-1), lax.dynamic_slice_in_dim(cond, mz * share, share)])
    got = gather_now(gather_now(sent, "narrow").reshape(-1), "wide").reshape(count, deep, -1)
    mods = got[:, :, : 4 * ada].reshape(count, deep, 4, ada).transpose(0, 2, 1, 3).reshape(count, 4, d)
    conds = got[:, :, 4 * ada :].reshape(count, cd)
    my_mod = lax.dynamic_index_in_dim(mods, first, 0, False)
    of_block = jnp.sum(jnp.where((firsts[:, None] == blocks[None, :])[:, :, None, None], mods[None], 0.0), 1)
    scales = 1.0 + of_block
    gates = jnp.tanh(of_block)
    factor = jnp.stack([1.0 + my_mod[0], jnp.tanh(my_mod[1]), 1.0 + my_mod[2], jnp.tanh(my_mod[3])])
    vec = norm_gains * factor
    hg = jnp.tile(head_gains, (1, heads))
    tg_heads = jnp.tanh(cross_gate)
    tg = jnp.repeat(tg_heads, HD)[None, :]

    order = Order()
    cap_raw = jnp.einsum("kd,jde->jke", captions, w_caption, preferred_element_type=f32)
    whole_cap = pl.BlockSpec((text, n), lambda i: (0, 0))
    both_cap = pl.BlockSpec((text, 2 * n), lambda i: (0, 0))
    (cap,) = order.run(
        "caption_norm",
        caption_norm_kernel,
        (1,),
        (cap_raw[0], cap_raw[1], hg),
        [whole_cap, whole_cap, whole(hg.shape)],
        [both_cap],
        [sds((text, 2 * n), bf16)],
    )
    cap = lax.all_gather(cap, "wide", axis=0, tiled=True)

    chunks = range(t // BR)
    pairs_of = range(t // (2 * BR))
    sums = Sums(order, deep, mz)
    a1, k_raw, k, v, q_raw, q = key_call(order, patches, vec, w_qkv, tabs, hg, ())
    kv = Gather(k, v)


    q_all = lax.all_gather(q, "wide", axis=0, tiled=True)
    k_all, v_all = pick(order, sc, kv.pieces(), SPAN)
    heads_out = {}
    for c in chunks:
        heads_out[c] = (*attend_call(order, sc, q, k_all, v_all, cap, text, tg, c, BR), 0)
        sums.add(("attn", c), mm(heads_out[c][0], w_out).astype(bf16))

    mids, gus = {}, {}
    whole_out = ()
    for c in chunks:
        mids[c], gus[c], ffn_part, *whole_out = ffn_call(
            order, c, patches, sums.get(("attn", c)), vec, w_gate_up, w_down, whole_out
        )
        sums.add(("ffn", c), ffn_part)
    a3, hidden = whole_out
    whole_out = ()
    c4 = 0.0
    for c in chunks:
        da3_part, part_sum, *whole_out = ffn_back_call(
            order, c, sums.get(("ffn", c)), mids[c], cotangent, gus[c], vec, w_gate_up, w_down, whole_out
        )
        sums.add(("da3", c), da3_part)
        c4 = c4 + part_sum
    output, d_ffn, d_gu = whole_out

    d_mids, dqs, dq_caps, d_got, d_mixed, d_scaled = {}, {}, {}, {}, {}, {}
    whole_out = ()
    mlp_part = ()
    behind = ()
    c2 = c3 = dck = dcv = gate_sum = 0.0
    for h in pairs_of:
        for c in (2 * h, 2 * h + 1):
            _, o_self, linv, place = heads_out[c]
            if c == 2 * h + 1 and h > 0:
                behind = d_got[h - 1].second
            da3 = sums.get(("da3", c), behind)
            d_mids[c], d_mixed[c], p3, p2, *outs = out_back_call(
                order, c, da3, mids[c], sums.get(("attn", c)), cotangent, vec, w_out, o_self, linv, place, whole_out
            )
            whole_out, d_scaled[h] = (outs if c % 2 == 0 else outs[:1]), outs[1]
            c2, c3 = c2 + p2, c3 + p3
            behind = ()
            if c == 2 * h:
                early = d_got[h - 1].first if h > 0 else ()
                mlp_part = pair_grad_call(order, a3, d_gu, d_ffn, hidden, h, len(pairs_of), mlp_part, early)
        d_got[h] = GatherOne(d_scaled[h])
        dq_caps[h], pk, pv, pg = caption_back_call(order, sc, q, d_mixed[2 * h], d_mixed[2 * h + 1], cap, text, tg, h)
        dck, dcv, gate_sum = dck + pk, dcv + pv, gate_sum + pg
    d_attn = whole_out[0]
    cap_sum = jnp.concatenate([dck, dcv], 1)
    cap_got = lax.all_gather(cap_sum.astype(bf16), "wide")
    kept = (firsts == me)[:, None, None]
    cap_sum = jnp.sum(jnp.where(kept, cap_got.astype(f32), 0.0), 0)
    last_half = pairs_of[-1]

    def make_dq(h, after):
        return dq_call(order, sc, q, d_scaled[h], k_all, v_all, dq_caps[h], h, after)

    for h in pairs_of:
        dqs[h] = make_dq(h, () if h == 0 else d_got[last_half].first)

    d_cap, hs_c = order.run(
        "caption_grad",
        caption_grad_kernel,
        (1,),
        (cap_sum[:, :n], cap_sum[:, n:], cap_raw[0], hg),
        [whole_cap, whole_cap, whole_cap, whole(hg.shape)],
        [both_cap, pl.BlockSpec((1, n), lambda i: (0, 0))],
        [sds((text, 2 * n), bf16), sds((1, n), f32)],
    )
    d_text = (mm_nt(d_cap[:, :n], w_caption[0]) + mm_nt(d_cap[:, n:], w_caption[1])).astype(bf16)
    cap_part = mm_tn(captions, d_cap).astype(bf16)
    pieces = -(-d_text.shape[1] // d)
    padded = jnp.pad(d_text, ((0, 0), (0, pieces * d - d_text.shape[1])))
    text_parts = [padded[:, p * d : (p + 1) * d] for p in range(pieces)]

    sums.add(("text", 0), text_parts[0])
    ds = [x for h in pairs_of for x in pick(order, sc, d_got[h].pieces(), SPAN)]
    sums.add(("text", 1), text_parts[1], (cap_part,))
    g_mlp = scatter_rows(pin(order, mlp_part[0]))
    whole_out = ()
    c1_parts, hs_parts = [], []
    mixed = jnp.concatenate([heads_out[c][0] for c in chunks])
    pairs = n // 128

    def project(c, dkv, after=()):
        nonlocal whole_out
        da1_part, p_hs, p1, *whole_out = dqkv_call(order, c, dqs[c // 2], dkv, q_raw, k_raw, tabs, hg, w_qkv, patches, whole_out)
        hs_parts.append(p_hs)
        c1_parts.append(p1)
        return da1_part

    dkv = [dkv_call(order, sc, k, v, q_all, ds, 0, 0, pairs)]
    for p in range(2, pieces):
        sums.add(("text", p), text_parts[p])
    g_cap = scatter_rows(pin(order, cap_part))
    first_part = project(0, dkv)
    parts_of = lambda p: dkv_call(order, sc, k, v, q_all, ds, 1, p, 1)
    first_dkv, dkv = dkv, [parts_of(0)]
    sums.add(("da1", 0), first_part)
    da1_part = project(1, first_dkv)
    dkv.append(parts_of(1))
    sums.add(("da1", 1), da1_part)
    dkv += [parts_of(p) for p in range(2, pairs)]
    for c in chunks[2:]:
        da1_part = project(c, dkv)
        if c == chunks[-1]:
            d_qkv = whole_out[0]
            packed = pack_call(order, c1_parts, hs_parts, hs_c, gate_sum, tg, c2, c3, c4, mz)
            from_narrow = [packed] + [swap(packed, "narrow", deep, m) for m in range(1, deep)]
            attn_part = pair_grad_call(order, a1, d_qkv, d_attn, mixed)[0]
        sums.add(("da1", c), da1_part, (g_mlp, *from_narrow) if c == chunks[-1] else ())
    g_attn = scatter_rows(pin(order, attn_part))

    (folded,) = fold_call(order, from_narrow)
    got = lax.all_gather(folded, "wide")
    whole_out = last_call(order, 0, sums.get(("da1", 0)), patches, d_mids[0], vec, ())
    for c in chunks[1:]:
        da1 = sums.get(("da1", c), (g_cap, got) if c == 1 else (g_attn,) if c == chunks[-1] else ())
        if c == 1:
            got = pin(order, got)
        whole_out = last_call(order, c, da1, patches, d_mids[c], vec, whole_out)
    (grad_patches,) = whole_out
    grad_captions = jnp.concatenate([sums.get(("text", p)) for p in range(pieces)], 1)[:, : d_text.shape[1]]

    cols = got[:, :4]
    grad_head_gains = jnp.sum(got[:, 4, : 3 * n], 0).reshape(3, heads, HD).sum(1)
    grad_cross_gate = jnp.sum(got[:, 5], 0)[::HD]
    gain_factor = jnp.stack([scales[:, 0], gates[:, 1], scales[:, 2], gates[:, 3]], 1)
    gain_grads = jnp.sum(gain_factor * cols, 0)
    wide_cols = d // count
    grad_norm_gains = lax.dynamic_slice_in_dim(gain_grads, me * wide_cols, wide_cols, 1)
    ones = jnp.ones_like(gates[:, 0])
    slope = jnp.stack([ones, 1.0 - gates[:, 1] ** 2, ones, 1.0 - gates[:, 3] ** 2], 1)
    d_mod = lax.dynamic_slice_in_dim(slope * norm_gains[None] * cols, mz * ada, ada, 2)
    at_slot = (firsts[None, :] == blocks[:, None]).astype(f32)
    d_slots = jnp.sum(at_slot[:, :, None, None] * d_mod[None], 1).astype(bf16).astype(f32)
    cond_rows = cd // count
    silu_mine = lax.dynamic_slice_in_dim(jax.nn.silu(conds).astype(bf16).astype(f32), me * cond_rows, cond_rows, 1)
    grad_ada = jnp.sum(silu_mine[:, :, None, None] * d_slots[:, None], 0)
    d_mine = lax.dynamic_index_in_dim(d_slots, me, 0, False)
    cond_part = jnp.sum(d_mine[None] * w_ada.astype(f32), (1, 2))
    cond_part = cond_part.reshape(-1, 128)
    cond_total = tree([cond_part] + [swap(cond_part, "narrow", deep, m) for m in range(1, deep)]).reshape(-1)
    pull_silu = jax.vjp(jax.nn.silu, cond)[1]
    grad_conditioning = pull_silu(cond_total)[0].reshape(1, -1)

    rows = d // count
    return (
        output,
        grad_patches,
        grad_conditioning,
        grad_captions,
        grad_ada,
        grad_norm_gains,
        g_attn[:, : 3 * n].astype(f32).reshape(rows, 3, n).transpose(1, 0, 2),
        grad_head_gains,
        grad_cross_gate,
        g_cap.astype(f32).reshape(-1, 2, n).transpose(1, 0, 2),
        g_attn[:, 3 * n :].astype(f32).T,
        g_mlp[:, : 2 * ff].astype(f32).reshape(rows, 2, ff).transpose(1, 0, 2),
        g_mlp[:, 2 * ff :].astype(f32).T,
    )


def solution(mesh):
    placed = (
        P("wide", None),
        P("wide", None),
        P("wide", None),
        P("wide", None),
        P(),
        P(),
        P(None, None, "narrow"),
        P(),
        P(None, None, "narrow"),
        P(),
        P("narrow"),
        P(None, None, "narrow"),
        P("narrow", None),
        P(None, None, "narrow"),
        P("narrow", None),
    )
    return jax.shard_map(
        local,
        mesh=mesh,
        in_specs=placed,
        out_specs=(
            P("wide", None),
            P("wide", None),
            P("wide", None),
            P("wide", None),
            P("wide", None, "narrow"),
            P(None, "wide"),
            P(None, "wide", "narrow"),
            P(),
            P(),
            P(None, "wide", "narrow"),
            P("narrow", "wide"),
            P(None, "wide", "narrow"),
            P("narrow", "wide"),
        ),
        check_vma=False,
    )
```

```python
import functools

import jax
import jax.numpy as jnp
from jax import lax
from jax.experimental import pallas as pl
from jax.experimental.pallas import tpu as pltpu
from jax.sharding import PartitionSpec as P

HD = 64
SPAN = 4
EPS = 1e-05
LOG2E = 1.4426950408889634
f32 = jnp.float32
bf16 = jnp.bfloat16
VMEM = 56 * 1024 * 1024
BR = 256
NT = (((1,), (1,)), ((), ()))
TN = (((0,), (0,)), ((), ()))


def params(n):
    return pltpu.CompilerParams(
        dimension_semantics=("arbitrary",) * n, vmem_limit_bytes=VMEM
    )


def sds(shape, dtype):
    return jax.ShapeDtypeStruct(shape, dtype)


COST = {
    "key": 8, "query": 9, "caption_norm": 2, "pick": 5, "attend": 15, "hop": 3, "ffn": 9, "ffn_back": 10, "out_back": 6,
    "pair_grad": 10, "caption_back": 6, "dq": 27, "dkv": 24, "dqkv": 7, "caption_grad": 3, "last": 3, "note": 1, "pin": 1,
}


class Order:
    def __init__(self):
        self.token = ()

    def run(self, name, kernel, grid, ins, in_specs, out_specs, out_shape, scratch=(), scalar=None, held=(), first_held=0, after=()):
        pre = 0 if scalar is None else 1
        given = pre + len(ins)
        extra = [*self.token, *after, *held]

        def body(*refs):
            kernel(*refs[:given], *refs[given + len(extra) :])

        at = given + len(extra) - len(held)
        out = pl.pallas_call(
            body,
            grid_spec=pltpu.PrefetchScalarGridSpec(
                num_scalar_prefetch=pre,
                grid=grid,
                in_specs=list(in_specs) + loose(len(extra)),
                out_specs=out_specs,
                scratch_shapes=list(scratch),
            ),
            out_shape=out_shape,
            input_output_aliases={at + k: first_held + k for k in range(len(held))},
            compiler_params=params(len(grid)),
            cost_estimate=pl.CostEstimate(
                flops=COST[name] * 250_000_000, bytes_accessed=COST[name] * 750_000, transcendentals=0
            ),
            name=name,
        )(*(() if scalar is None else (scalar,)), *ins, *extra)
        self.token = (out[0],)
        return out


def loose(n):
    return [pl.BlockSpec(memory_space=pl.ANY)] * n


def mm(a, b):
    return jnp.dot(a, b, preferred_element_type=f32)


def mm_nt(a, b):
    return lax.dot_general(a, b, NT, preferred_element_type=f32)


def mm_tn(a, b):
    return lax.dot_general(a, b, TN, preferred_element_type=f32)


def split(x):
    hi = x.astype(bf16)
    return hi, (x - hi.astype(f32)).astype(bf16)


def head_sum(x, ones):
    hi, lo = split(x)
    return mm(hi, ones) + mm(lo, ones)


def head_ones(n):
    a = lax.broadcasted_iota(jnp.int32, (n, n), 0) // HD
    b = lax.broadcasted_iota(jnp.int32, (n, n), 1) // HD
    return (a == b).astype(bf16)


def halves(n):
    lane = lax.broadcasted_iota(jnp.int32, (1, n), 1)
    return (lane < HD, lane >= HD)


def keep(x, mask):
    return jnp.where(mask, x, jnp.zeros_like(x))


def inv_rms(x):
    return lax.rsqrt(jnp.mean(x * x, -1, keepdims=True) + EPS)


def row(ref, k):
    return ref[k : k + 1, :]


def whole(shape):
    zeros = (0,) * len(shape)
    return pl.BlockSpec(shape, lambda *_: zeros, pipeline_mode=pl.Buffered(1))


def rows_of(br, width, first=0):
    return pl.BlockSpec((br, width), lambda i, *_: (i, first))


def accumulate(ref, value, first):
    @pl.when(first)
    def _():
        ref[...] = value

    @pl.when(jnp.logical_not(first))
    def _():
        ref[...] += value


def col_sum(x):
    return jnp.sum(x, 0, keepdims=True)


def tile3(t, n):
    return jnp.concatenate([t] * (n // t.shape[1]), 1)


def key_kernel(p_ref, v_ref, w_ref, wv_ref, wq_ref, c_ref, s1_ref, s2_ref, hg_ref, a_ref, kr_ref, k_ref, vv_ref, qr_ref, q_ref):
    x = p_ref[...].astype(f32)
    a = (x * inv_rms(x) * row(v_ref, 0)).astype(bf16)
    a_ref[...] = a
    k = mm(a, w_ref[0])
    kr_ref[...] = k
    k_ref[...] = turned(k, row(hg_ref, 1), (c_ref, s1_ref, s2_ref)).astype(bf16)
    vv_ref[...] = mm(a, wv_ref[0]).astype(bf16)
    q = mm(a, wq_ref[0])
    qr_ref[...] = q
    q_ref[...] = (turned(q, row(hg_ref, 0), (c_ref, s1_ref, s2_ref)) * (0.125 * LOG2E)).astype(bf16)


def turned(y, gain, tabs):
    n = y.shape[1]
    cos, s1, s2 = (tile3(t[...], n) for t in tabs)
    z = y * lax.rsqrt(head_sum(y * y, head_ones(n)) * (1.0 / HD) + EPS) * gain
    return z * cos + pltpu.roll(z, n - 16, 1) * s1 + pltpu.roll(z, 16, 1) * s2


def one_weight(w, k):
    return pl.BlockSpec((1, *w.shape[1:]), lambda *_: (k, 0, 0), pipeline_mode=pl.Buffered(1))


def key_call(order, patches, vec, w, tabs, hg, after, br=256):
    t, d = patches.shape
    n = w.shape[2]
    return order.run(
        "key",
        key_kernel,
        (t // br,),
        (patches, vec, w, w, w, *tabs, hg),
        [rows_of(br, d), whole(vec.shape), one_weight(w, 1), one_weight(w, 2), one_weight(w, 0)] + [rows_of(br, 128)] * 3 + [whole(hg.shape)],
        [rows_of(br, d)] + [rows_of(br, n)] * 5,
        [sds((t, d), bf16), sds((t, n), f32), sds((t, n), bf16), sds((t, n), bf16), sds((t, n), f32), sds((t, n), bf16)],
        after=after,
    )


def soft_sums(q, k, v, mask):
    e = jnp.exp2(mm_nt(q, keep(k, mask))).astype(bf16)
    return mm(e, jnp.where(mask, v, jnp.ones_like(v)))


def item_block(j, s):
    return jnp.minimum(j, s[0] - 1)


def attend_kernel(sc, q_ref, k_ref, v_ref, ck_ref, cv_ref, tg_ref, mix_ref, o_ref, li_ref, acc):
    j = pl.program_id(1)
    masks = halves(128)
    keys = k_ref.shape[0] if q_ref.shape[0] <= BR else 512

    def block_sums(h):
        q = q_ref[...]
        total = 0.0
        for c in range(k_ref.shape[0] // keys):
            at = slice(c * keys, (c + 1) * keys)
            total = total + soft_sums(q, k_ref[at, :], v_ref[at, :], masks[h])
        return total

    @pl.when(j == 0)
    def _():
        for h in range(2):
            acc[2 + h] = soft_sums(q_ref[...], ck_ref[...], cv_ref[...], masks[h])
            acc[h] = block_sums(h)

    @pl.when((j > 0) & (j < sc[0]))
    def _():
        for h in range(2):
            acc[h] += block_sums(h)

    @pl.when(j == SPAN - 1)
    def _():
        def finish(a0, a1):
            inverse = 1.0 / jnp.where(masks[0], pltpu.roll(a0, HD, 1), pltpu.roll(a1, HD, 1))
            return jnp.where(masks[0], a0, a1) * inverse, inverse

        o, li = finish(acc[0], acc[1])
        mix_ref[...] = (o + tg_ref[...] * finish(acc[2], acc[3])[0]).astype(bf16)
        o_ref[...] = o.astype(bf16)
        li_ref[...] = li


def attend_call(order, sc, q, k, v, cap, text, tg, at, bq):
    n = q.shape[1]
    pairs = n // 128
    block = k.shape[0] // SPAN
    mine = lambda p, j, s: (0, p)
    other = lambda p, j, s: (item_block(j, s), p)
    return order.run(
        "attend",
        attend_kernel,
        (pairs, SPAN),
        (q, k, v, cap, cap, tg),
        [
            pl.BlockSpec((bq, 128), lambda p, j, s: (at, p)),
            pl.BlockSpec((block, 128), other),
            pl.BlockSpec((block, 128), other),
            pl.BlockSpec((text, 128), lambda p, j, s: (s[1 + SPAN], p)),
            pl.BlockSpec((text, 128), lambda p, j, s: (s[1 + SPAN], pairs + p)),
            pl.BlockSpec((1, 128), mine),
        ],
        [pl.BlockSpec((bq, 128), mine)] * 3,
        [sds((bq, n), bf16), sds((bq, n), bf16), sds((bq, n), f32)],
        [pltpu.VMEM((4, bq, 128), f32)],
        sc,
    )


def caption_back_kernel(sc, q_ref, da_ref, db_ref, ck_ref, cv_ref, tg_ref, dq_ref, dk_ref, dv_ref, gs_ref):
    masks = halves(128)
    q, d = q_ref[...], jnp.concatenate([da_ref[...], db_ref[...]], 0)
    dq = jnp.zeros(q.shape, f32)
    dk = jnp.zeros(ck_ref.shape, f32)
    dv = jnp.zeros(ck_ref.shape, f32)
    sums = []
    for h in range(2):
        ck, cv = keep(ck_ref[...], masks[h]), keep(cv_ref[...], masks[h])
        gate = tg_ref[:, h * HD : h * HD + 1]
        e = jnp.exp2(mm_nt(q, ck))
        prob = e * (1.0 / jnp.sum(e, -1, keepdims=True))
        dp = mm_nt(d, cv)
        m = jnp.sum(prob * dp, -1, keepdims=True)
        dc = (prob * (dp - m) * gate).astype(bf16)
        dq = dq + mm(dc, ck)
        dk = dk + mm_tn(dc, keep(q, masks[h]))
        dv = dv + mm_tn(prob.astype(bf16), keep(d, masks[h]))
        sums.append(jnp.sum(m, 0, keepdims=True))
    dq_ref[...] = dq * 0.125
    dk_ref[...] = dk * (1.0 / LOG2E)
    dv_ref[...] = dv * tg_ref[...]
    gs_ref[...] = jnp.where(masks[0], sums[0], sums[1])


def caption_back_call(order, sc, q, da, db, cap, text, tg, h):
    n = q.shape[1]
    pairs = n // 128
    bq = 2 * BR
    mine = lambda p, s: (0, p)
    return order.run(
        "caption_back",
        caption_back_kernel,
        (pairs,),
        (q, da, db, cap, cap, tg),
        [
            pl.BlockSpec((bq, 128), lambda p, s: (h, p)),
            pl.BlockSpec((BR, 128), mine),
            pl.BlockSpec((BR, 128), mine),
            pl.BlockSpec((text, 128), lambda p, s: (s[1 + SPAN], p)),
            pl.BlockSpec((text, 128), lambda p, s: (s[1 + SPAN], pairs + p)),
            pl.BlockSpec((1, 128), mine),
        ],
        [
            pl.BlockSpec((bq, 128), mine),
            pl.BlockSpec((text, 128), mine),
            pl.BlockSpec((text, 128), mine),
            pl.BlockSpec((1, 128), mine),
        ],
        [sds((bq, n), f32), sds((text, n), f32), sds((text, n), f32), sds((1, n), f32)],
        scalar=sc,
    )


def minus_delta(rows, head):
    lane = lax.broadcasted_iota(jnp.int32, (rows, 128), 1)
    return jnp.where((lane >= 3 * head) & (lane < 3 * head + 3), -1.0, 0.0).astype(bf16)


def dq_kernel(sc, q_ref, d_ref, x_ref, k_ref, v_ref, c_ref, dq_ref, acc):
    pair = pl.program_id(0)
    j = pl.program_id(1)
    masks = halves(128)
    keys = 512

    @pl.when(j == 0)
    def _():
        acc[...] = jnp.zeros_like(acc)

    @pl.when(j < sc[0])
    def _():
        q = q_ref[...]
        dx = jnp.concatenate([d_ref[...], x_ref[...]], 1)
        total = acc[...]
        for h in range(2):
            off = minus_delta(keys, 2 * pair + h)
            for c in range(k_ref.shape[0] // keys):
                at = slice(c * keys, (c + 1) * keys)
                k = keep(k_ref[at, :], masks[h])
                e = jnp.exp2(mm_nt(q, k))
                dp = mm_nt(dx, jnp.concatenate([keep(v_ref[at, :], masks[h]), off], 1))
                total = total + mm((e * dp).astype(bf16), k)
        acc[...] = total

    @pl.when(j == SPAN - 1)
    def _():
        dq_ref[...] = acc[...] * 0.125 + c_ref[...]


def dq_call(order, sc, q, d, k, v, cap_dq, h, after=()):
    n = q.shape[1]
    pairs = n // 128
    block = k.shape[0] // SPAN
    bq = 2 * BR
    mine = lambda p, j, s: (0, p)
    extra = lambda p, j, s: (0, pairs)
    other = lambda p, j, s: (item_block(j, s), p)
    return order.run(
        "dq",
        dq_kernel,
        (pairs, SPAN),
        (q, d, d, k, v, cap_dq),
        [
            pl.BlockSpec((bq, 128), lambda p, j, s: (h, p)),
            pl.BlockSpec((bq, 128), mine),
            pl.BlockSpec((bq, 128), extra),
            pl.BlockSpec((block, 128), other),
            pl.BlockSpec((block, 128), other),
            pl.BlockSpec((bq, 128), mine),
        ],
        [pl.BlockSpec((bq, 128), mine)],
        [sds((bq, n), f32)],
        [pltpu.VMEM((bq, 128), f32)],
        sc,
        after=after,
    )[0]


def dkv_kernel(parts, base, sc, k_ref, v_ref, q_ref, *rest):
    d_refs, x_refs = rest[0 : 2 * parts : 2], rest[1 : 2 * parts : 2]
    dk_ref, dv_ref = rest[2 * parts :]
    pair = base + pl.program_id(0)
    j = pl.program_id(1)
    masks = halves(128)
    queries = 2 * BR

    @pl.when(j == 0)
    def _():
        dk_ref[...] = jnp.zeros_like(dk_ref)
        dv_ref[...] = jnp.zeros_like(dv_ref)

    @pl.when(j < sc[0])
    def _():
        dk, dv = dk_ref[...], dv_ref[...]
        for h in range(2):
            vx = jnp.concatenate([keep(v_ref[...], masks[h]), minus_delta(v_ref.shape[0], 2 * pair + h)], 1)
            for r in range(parts):
                q = keep(q_ref[r * queries : (r + 1) * queries, :], masks[h])
                d, x = d_refs[r][...], x_refs[r][...]
                e = jnp.exp2(mm_nt(k_ref[...], q))
                dp = mm_nt(vx, jnp.concatenate([d, x], 1))
                dv = dv + mm(e.astype(bf16), keep(d, masks[h]))
                dk = dk + mm((e * dp).astype(bf16), q)
        dk_ref[...] = dk
        dv_ref[...] = dv


def dkv_call(order, sc, k, v, q_all, ds, half, base, n_pairs):
    t, n = k.shape
    pairs = n // 128
    rows = 2 * BR
    mine = pl.BlockSpec((rows, 128), lambda p, j, s: (half, base + p))
    out = pl.BlockSpec((rows, 128), lambda p, j, s: (0, p))
    other = pl.BlockSpec((rows, 128), lambda p, j, s: (item_block(j, s), base + p))
    extra = pl.BlockSpec((rows, 128), lambda p, j, s: (item_block(j, s), pairs))
    return order.run(
        "dkv",
        functools.partial(dkv_kernel, len(ds), base),
        (n_pairs, SPAN),
        (k, v, q_all, *(x for d in ds for x in (d, d))),
        [mine, mine, pl.BlockSpec((t, 128), lambda p, j, s: (s[1 + SPAN + j], base + p))] + [other, extra] * len(ds),
        [out, out],
        [sds((rows, n_pairs * 128), f32)] * 2,
        scalar=sc,
    )


def chunk_call(order, kernel, name, c, ins, specs, chunk_outs, sum_outs, whole_outs, before):
    one = lambda r, w: pl.BlockSpec((r, w), lambda i: (0, 0))
    own = chunk_outs + sum_outs
    into = [pl.BlockSpec((BR, w), lambda i, at=c % (r // BR): (at, 0)) for r, w, _ in whole_outs]
    return order.run(
        name,
        kernel,
        (1,),
        ins,
        specs,
        [one(r, w) for r, w, _ in own] + into,
        [sds((r, w), k) for r, w, k in own + whole_outs],
        held=tuple(before),
        first_held=len(own),
    )


def part(c, width):
    return pl.BlockSpec((BR, width), lambda i: (c, 0))


def alone(width):
    return pl.BlockSpec((BR, width), lambda i: (0, 0))


def pair_grad_kernel(a_ref, b_ref, c_ref, d_ref, o_ref):
    n = b_ref.shape[1]
    o_ref[:, :n] = mm_tn(a_ref[...], b_ref[...]).astype(bf16)
    o_ref[:, n:] = mm_tn(c_ref[...], d_ref[...]).astype(bf16)


def pair_grad_call(order, a, b, c, d, part=0, parts=1, before=(), after=()):
    t, m = a.shape
    n, k = b.shape[1], d.shape[1]
    blk = 256
    steps = m // blk // parts
    cols = pl.BlockSpec((t, blk), lambda i: (0, part * steps + i))
    return order.run(
        "pair_grad",
        pair_grad_kernel,
        (steps,),
        (a, b, c, d),
        [cols, whole(b.shape), cols, whole(d.shape)],
        [pl.BlockSpec((blk, n + k), lambda i: (part * steps + i, 0))],
        [sds((m, n + k), bf16)],
        held=before,
        after=after,
    )


def ffn_kernel(p_ref, at_ref, v_ref, wg_ref, wd_ref, mid_ref, gu_ref, f_ref, a_ref, h_ref):
    at = at_ref[...].astype(f32)
    mid = p_ref[...].astype(f32) + row(v_ref, 1) * (at * inv_rms(at))
    mid_ref[...] = mid
    a = (mid * inv_rms(mid) * row(v_ref, 2)).astype(bf16)
    a_ref[...] = a
    g = mm(a, wg_ref[0])
    u = mm(a, wg_ref[1])
    n = g.shape[1]
    gu_ref[:, :n] = g.astype(bf16)
    gu_ref[:, n:] = u.astype(bf16)
    h = (g * jax.nn.sigmoid(g) * u).astype(bf16)
    h_ref[...] = h
    f_ref[...] = mm(h, wd_ref[...]).astype(bf16)


def ffn_call(order, c, patches, at, vec, wg, wd, before):
    t, d = patches.shape
    n = wd.shape[0]
    return chunk_call(
        order,
        ffn_kernel,
        "ffn",
        c,
        (patches, at, vec, wg, wd),
        [part(c, d), alone(d), whole(vec.shape), whole(wg.shape), whole(wd.shape)],
        [(BR, d, f32), (BR, 2 * n, bf16), (BR, d, bf16)],
        [],
        [(t, d, bf16), (t, n, bf16)],
        before,
    )


def ffn_back_kernel(f_ref, mid_ref, c_ref, gu_ref, v_ref, wg_ref, wd_ref, da_ref, cs_ref, y_ref, df_ref, dgu_ref):
    f = f_ref[...].astype(f32)
    cot = c_ref[...].astype(f32)
    r = inv_rms(f)
    fh = f * r
    y_ref[...] = (mid_ref[...] + row(v_ref, 3) * fh).astype(bf16)
    z = cot * row(v_ref, 3)
    df = (r * (z - fh * jnp.mean(z * fh, -1, keepdims=True))).astype(bf16)
    df_ref[...] = df
    cs_ref[...] = col_sum(cot * fh)
    dh = mm_nt(df, wd_ref[...])
    n = dh.shape[1]
    g = gu_ref[:, :n].astype(f32)
    u = gu_ref[:, n:].astype(f32)
    s = jax.nn.sigmoid(g)
    gs = g * s
    dg = (dh * u * (s + gs * (1.0 - s))).astype(bf16)
    du = (dh * gs).astype(bf16)
    dgu_ref[:, :n] = dg
    dgu_ref[:, n:] = du
    da_ref[...] = (mm_nt(dg, wg_ref[0]) + mm_nt(du, wg_ref[1])).astype(bf16)


def ffn_back_call(order, c, f, mid, cot, gu, vec, wg, wd, before):
    t, d = cot.shape
    n = wd.shape[0]
    return chunk_call(
        order,
        ffn_back_kernel,
        "ffn_back",
        c,
        (f, mid, cot, gu, vec, wg, wd),
        [alone(d), alone(d), part(c, d), alone(2 * n), whole(vec.shape), whole(wg.shape), whole(wd.shape)],
        [(BR, d, bf16)],
        [(1, d, f32)],
        [(t, d, bf16), (t, d, bf16), (t, 2 * n, bf16)],
        before,
    )


def out_back_kernel(da_ref, mid_ref, at_ref, c_ref, v_ref, w_ref, o_ref, li_ref, dm_ref, dx_ref, c3_ref, c2_ref, dat_ref, ds_ref):
    da = da_ref[...].astype(f32)
    mid = mid_ref[...]
    r = inv_rms(mid)
    mh = mid * r
    z = da * row(v_ref, 2)
    dm = c_ref[...].astype(f32) + r * (z - mh * jnp.mean(z * mh, -1, keepdims=True))
    dm_ref[...] = dm
    c3_ref[...] = col_sum(da * mh)
    at = at_ref[...].astype(f32)
    ra = inv_rms(at)
    ah = at * ra
    c2_ref[...] = col_sum(dm * ah)
    z = dm * row(v_ref, 1)
    dat = (ra * (z - ah * jnp.mean(z * ah, -1, keepdims=True))).astype(bf16)
    dat_ref[...] = dat
    dx = mm_nt(dat, w_ref[...]).astype(bf16)
    dx_ref[...] = dx
    n = dx.shape[1]
    ds = dx.astype(f32) * li_ref[...]
    ds_ref[:, :n] = ds.astype(bf16)
    hi, lo = split(ds * o_ref[...].astype(f32))
    head = lax.broadcasted_iota(jnp.int32, (n, 128), 0) // HD
    lane = lax.broadcasted_iota(jnp.int32, (n, 128), 1)
    to_lanes = (lane // 3 == head).astype(bf16)
    delta = mm(hi, to_lanes) + mm(lo, to_lanes)
    one = delta.astype(bf16).astype(f32)
    two = (delta - one).astype(bf16).astype(f32)
    which = lax.broadcasted_iota(jnp.int32, (1, 128), 1) % 3
    ds_ref[:, n:] = jnp.where(which == 0, one, jnp.where(which == 1, two, delta - one - two)).astype(bf16)


def out_back_call(order, c, da, mid, at, cot, vec, w, o, li, place, before):
    t, d = cot.shape
    n = w.shape[0]
    return chunk_call(
        order,
        out_back_kernel,
        "out_back",
        c,
        (da, mid, at, cot, vec, w, o, li),
        [alone(d), alone(d), alone(d), part(c, d), whole(vec.shape), whole(w.shape), part(place, n), part(place, n)],
        [(BR, d, f32), (BR, n, bf16)],
        [(1, d, f32), (1, d, f32)],
        [(t, d, bf16), (2 * BR, n + 128, bf16)],
        before,
    )


def dqkv_kernel(pairs, dq_ref, *refs):
    dk_refs, dv_refs = refs[0 : 2 * pairs : 2], refs[1 : 2 * pairs : 2]
    (qr_ref, kr_ref, c_ref, s1_ref, s2_ref, hg_ref, w_ref, p_ref, da_ref, hs_ref, cs_ref, d_ref) = refs[2 * pairs :]
    side = lambda parts: jnp.concatenate([x[...] for x in parts], 1)
    n = dq_ref.shape[1]
    ones = head_ones(n)
    cos, s1, s2 = (tile3(t[...], n) for t in (c_ref, s1_ref, s2_ref))

    def back(dy, x, gain):
        dz = dy * cos - pltpu.roll(dy, 16, 1) * s2 - pltpu.roll(dy, n - 16, 1) * s1
        r = lax.rsqrt(head_sum(x * x, ones) * (1.0 / HD) + EPS)
        xh = x * r
        g = dz * gain
        return r * (g - xh * (head_sum(g * xh, ones) * (1.0 / HD))), col_sum(dz * xh)

    dq, hq = back(dq_ref[...], qr_ref[...], row(hg_ref, 0))
    dk, hk = back(side(dk_refs) * (1.0 / LOG2E), kr_ref[...], row(hg_ref, 1))
    dql, dkl, dvl = dq.astype(bf16), dk.astype(bf16), side(dv_refs).astype(bf16)
    d_ref[:, :n] = dql
    d_ref[:, n : 2 * n] = dkl
    d_ref[:, 2 * n :] = dvl
    da = mm_nt(dql, w_ref[0]) + mm_nt(dkl, w_ref[1]) + mm_nt(dvl, w_ref[2])
    da_ref[...] = da.astype(bf16)
    x = p_ref[...].astype(f32)
    cs_ref[...] = col_sum(da * (x * inv_rms(x)))
    hs_ref[0:1, :] = hq
    hs_ref[1:2, :] = hk


def dqkv_call(order, c, dq, dkv, qr, kr, tabs, hg, w, patches, before):
    t, d = patches.shape
    n = dq.shape[1]
    return chunk_call(
        order,
        functools.partial(dqkv_kernel, len(dkv)),
        "dqkv",
        c,
        (dq, *(x for two in dkv for x in two), qr, kr, *tabs, hg, w, patches),
        [part(c % 2, n)] + [part(c % 2, x.shape[1]) for two in dkv for x in two] + [part(c, n)] * 2 + [part(c, 128)] * 3 + [whole(hg.shape), whole(w.shape), part(c, d)],
        [(BR, d, bf16)],
        [(2, n, f32), (1, d, f32)],
        [(t, 3 * n, bf16)],
        before,
    )


def last_kernel(da_ref, p_ref, dm_ref, v_ref, o_ref):
    x = p_ref[...].astype(f32)
    r = inv_rms(x)
    xh = x * r
    z = da_ref[...].astype(f32) * row(v_ref, 0)
    o_ref[...] = (dm_ref[...] + r * (z - xh * jnp.mean(z * xh, -1, keepdims=True))).astype(bf16)


def last_call(order, c, da, patches, dm, vec, before):
    t, d = patches.shape
    return chunk_call(
        order,
        last_kernel,
        "last",
        c,
        (da, patches, dm, vec),
        [alone(d), part(c, d), alone(d), whole(vec.shape)],
        [],
        [],
        [(t, d, bf16)],
        before,
    )


def caption_grad_kernel(dk_ref, dv_ref, kr_ref, hg_ref, d_ref, hs_ref):
    n = dk_ref.shape[1]
    ones = head_ones(n)
    x = kr_ref[...]
    r = lax.rsqrt(head_sum(x * x, ones) * (1.0 / HD) + EPS)
    xh = x * r
    dy = dk_ref[...]
    g = dy * row(hg_ref, 2)
    d_ref[:, :n] = (r * (g - xh * (head_sum(g * xh, ones) * (1.0 / HD)))).astype(bf16)
    d_ref[:, n:] = dv_ref[...].astype(bf16)
    hs_ref[...] = col_sum(dy * xh)


def caption_norm_kernel(kr_ref, v_ref, hg_ref, o_ref):
    n = kr_ref.shape[1]
    x = kr_ref[...]
    r = lax.rsqrt(head_sum(x * x, head_ones(n)) * (1.0 / HD) + EPS)
    o_ref[:, :n] = (x * r * row(hg_ref, 2)).astype(bf16)
    o_ref[:, n:] = v_ref[...].astype(bf16)


def swap(x, axis, size, m):
    return lax.ppermute(x, axis, [(i, i ^ m) for i in range(size)])


def pick_kernel(count, n_arrays, n_pieces, sc, *refs):
    outs, sem = refs[n_arrays * n_pieces :][:n_arrays], refs[-1]
    for k, out in enumerate(outs):
        pieces = refs[k * n_pieces : (k + 1) * n_pieces]
        rows = pieces[0].shape[0]
        for j in range(count):
            for m in range(n_pieces):

                @pl.when(sc[1 + j] == m)
                def _():
                    pltpu.make_async_copy(pieces[m], out.at[pl.ds(j * rows, rows)], sem.at[k, j]).start()

    for k, out in enumerate(outs):
        first = refs[k * n_pieces]
        rows = first.shape[0]
        for j in range(count):
            pltpu.make_async_copy(first, out.at[pl.ds(j * rows, rows)], sem.at[k, j]).wait()


class Gather:
    def __init__(self, a, b):
        self.all = None
        if lax.axis_size("wide") != 8:
            self.first = self.second = ()
            self.all = [lax.all_gather(x, "wide") for x in (a, b)]
            return
        send = lambda x, pairs: lax.ppermute(x, "wide", pairs)
        over_x = [(i, i ^ 2) for i in range(8)]
        over_y = [(1, 5), (4, 0), (3, 7), (6, 2)]
        a2, a4, b4, b2 = send(a, over_x), send(a, over_y), send(b, over_y), send(b, over_x)
        a6 = send(a2, [(0, 4), (1, 5), (6, 2), (7, 3)])
        b6x, b6y = send(b2, [(0, 4), (7, 3)]), send(b4, [(7, 5), (0, 2)])
        self.first = (a2, a4, b4, b2)
        self.second = (a6, b6x, b6y)
        self.kept = ((a, a2, a4, a6), (b, b2, b4, b6x + b6y))

    def pieces(self):
        if self.all is not None:
            return self.all
        return [[y for x in four for y in (x, swap(x, "wide", 8, 1))] for four in self.kept]


class GatherOne:
    def __init__(self, a):
        self.all = None
        if lax.axis_size("wide") != 8:
            self.first = self.second = ()
            self.all = [lax.all_gather(a, "wide")]
            return
        send = lambda x, pairs: lax.ppermute(x, "wide", pairs)
        a2 = send(a, [(i, i ^ 2) for i in range(8)])
        a4 = send(a, [(1, 5), (4, 0), (3, 7), (6, 2)])
        a6 = send(a2, [(0, 4), (1, 5), (6, 2), (7, 3)])
        self.first, self.second = (a2, a4), (a6,)
        self.kept = ((a, a2, a4, a6),)

    pieces = Gather.pieces


def pick(order, sc, pieces, count):
    if not isinstance(pieces[0], list):
        one = lambda x, j: lax.dynamic_index_in_dim(x, sc[1 + SPAN + j], 0, False)
        return [jnp.concatenate([one(x, j) for j in range(count)]) for x in pieces]
    outs = [(count * p[0].shape[0], p[0].shape[1]) for p in pieces]
    return order.run(
        "pick",
        functools.partial(pick_kernel, count, len(pieces), 8),
        (1,),
        [x for p in pieces for x in p],
        loose(8 * len(pieces)),
        [pl.BlockSpec(shape, lambda i, s: (0, 0)) for shape in outs],
        [sds(shape, bf16) for shape in outs],
        [pltpu.SemaphoreType.DMA((len(pieces), count))],
        sc,
    )


def tree(parts):
    while len(parts) > 1:
        parts = [a + b for a, b in zip(parts[::2], parts[1::2])]
    return parts[0]


def pack_kernel(count, place, *refs):
    c1, hs = refs[:count], refs[count : 2 * count]
    hc_ref, gs_ref, tg_ref, c2_ref, c3_ref, c4_ref, o_ref = refs[2 * count :]
    n = hc_ref.shape[1]
    o_ref[...] = jnp.zeros_like(o_ref)
    o_ref[0:1, :] = sum(x[...] for x in c1)
    o_ref[1:2, :] = c2_ref[...]
    o_ref[2:3, :] = c3_ref[...]
    o_ref[3:4, :] = c4_ref[...]
    qk = sum(x[...] for x in hs)
    o_ref[4:5, :n] = qk[0:1]
    o_ref[4:5, n : 2 * n] = qk[1:2]
    o_ref[4:5, 2 * n : 3 * n] = hc_ref[...]
    gate = gs_ref[...] * (1.0 - tg_ref[...] * tg_ref[...])
    for z in range(o_ref.shape[1] // n):
        o_ref[5:6, z * n : (z + 1) * n] = jnp.where(place[0] == z, gate, 0.0)


def pack_call(order, c1, hs, hc, gs, tg, c2, c3, c4, place):
    d = c2.shape[1]
    ins = (*c1, *hs, hc, gs, tg, c2, c3, c4)
    spec = lambda x: pl.BlockSpec(x.shape, lambda i, s: (0, 0))

    def kernel(place, *refs):
        pack_kernel(len(c1), place, *refs)

    return order.run(
        "note",
        kernel,
        (1,),
        ins,
        [spec(x) for x in ins],
        [pl.BlockSpec((8, d), lambda i, s: (0, 0))],
        [sds((8, d), f32)],
        scalar=place.astype(jnp.int32).reshape(1),
    )[0]


def fold_kernel(*refs):
    parts, o_ref = refs[:-1], refs[-1]
    total = tree([x[...] for x in parts])
    row_at = lax.broadcasted_iota(jnp.int32, total.shape, 0)
    o_ref[...] = jnp.where((row_at >= 1) & (row_at < 4), parts[0][...], total)


def fold_call(order, parts):
    spec = pl.BlockSpec(parts[0].shape, lambda i: (0, 0))
    return order.run("note", fold_kernel, (1,), parts, [spec] * len(parts), [spec], [sds(parts[0].shape, f32)])


def pin_kernel(o_ref):
    pass


def pin(order, x, after=()):
    return order.run("pin", pin_kernel, (1,), (), [], loose(1), [sds(x.shape, x.dtype)], held=(x,), after=after)[0]


def gather_now(x, axis):
    n = x.shape[0]
    wide = -(-n // 1024) * 1024
    padded = jnp.pad(x, (0, wide - n)).reshape(1, 8, wide // 8)
    return lax.all_gather(padded, axis, axis=0, tiled=True).reshape(-1, wide)[:, :n]


def hop_kernel(have, sc, *refs):
    ins = dict(zip(have["in"], refs))
    outs = dict(zip(have["out"], refs[len(have["in"]) :]))
    end = sc[0] == 1
    if "total" in outs:
        outs["total"][...] = jnp.where(end, ins["r1"][...], ins["send"][...])
    third = None
    if "second" in ins:
        third = ins["second"][...] + ins["r2"][...]
    if "second" in outs:
        outs["second"][...] = ins["x"][...] + ins["r1"][...]
    if "send" in outs:
        new = ins["new"][...] if "new" in ins else third
        outs["send"][...] = new if third is None else jnp.where(end, new, third)


class Line:
    def __init__(self, order, place):
        self.order = order
        self.end = ((place == 0) | (place == 3)).astype(jnp.int32).reshape(1)
        self.x = self.second = self.send = None
        self.third = False

    def step(self, new, after=()):
        if self.send is None:
            self.x = self.send = new
            return None
        go = lambda x, perm: lax.ppermute(x, "narrow", perm)
        ins = {"r1": go(self.send, [(0, 1), (3, 2), (1, 0), (2, 3)])}
        outs = []
        if self.third:
            ins["send"] = self.send
            outs.append("total")
        if self.second is not None:
            ins["r2"] = go(self.second, [(1, 2), (2, 1)])
            ins["second"] = self.second
        if self.x is not None:
            ins["x"] = self.x
            outs.append("second")
        if new is not None:
            ins["new"] = new
        if new is not None or self.second is not None:
            outs.append("send")
        like = ins["r1"]
        block = pl.BlockSpec((BR // 2, like.shape[1]), lambda i, s: (i, 0))
        got = self.order.run(
            "hop",
            functools.partial(hop_kernel, {"in": list(ins), "out": outs}),
            (2,),
            list(ins.values()),
            [block] * len(ins),
            [block] * len(outs),
            [sds(like.shape, like.dtype)] * len(outs),
            scalar=self.end,
            after=after,
        )
        got = dict(zip(outs, got))
        self.third = self.second is not None
        self.x, self.second, self.send = new, got.get("second"), got.get("send")
        return got.get("total")


class Sums:
    def __init__(self, order, size, place):
        self.line = Line(order, place) if size == 4 else None
        self.names, self.done = [], {}

    def add(self, name, x, after=()):
        if self.line is None:
            self.done[name] = lax.psum(x, "narrow")
            return
        if self.line.send is None:
            self.names = [None]
        self._step(name, x, after)

    def _step(self, name, x, after):
        total = self.line.step(x, after)
        self.names.append(name)
        if total is not None:
            self.done[self.names[-4]] = total

    def get(self, name, after=()):
        while name not in self.done:
            self._step(None, None, after)
            after = ()
        return self.done[name]


def scatter_rows(x):
    return lax.psum_scatter(x.astype(bf16), "wide", scatter_dimension=0, tiled=True)


def rope_tables(position, width):
    lane = jnp.arange(128, dtype=jnp.int32)
    within = lane % HD
    quarter = HD // 4
    frequency = 10000.0 ** (-(within % quarter).astype(f32) / quarter)
    by_row = within < HD // 2
    where = jnp.where(by_row[None, :], (position // width)[:, None], (position % width)[:, None])
    angle = where.astype(f32) * frequency[None, :]
    cos, sin = jnp.cos(angle), jnp.sin(angle)
    former = (within % (HD // 2) < quarter)[None, :]
    return cos, jnp.where(former, -sin, 0.0), jnp.where(former, 0.0, sin)


def local(
    patches,
    cotangent,
    conditioning,
    captions,
    item_lengths,
    grid_widths,
    w_ada,
    norm_gains,
    w_qkv,
    head_gains,
    cross_gate,
    w_caption,
    w_out,
    w_gate_up,
    w_down,
):
    t, d = patches.shape
    n = w_qkv.shape[2]
    heads = n // HD
    ada = w_ada.shape[2]
    ff = w_down.shape[0]
    text = captions.shape[0]
    cd = conditioning.shape[1]
    count = lax.axis_size("wide")
    deep = lax.axis_size("narrow")
    me = lax.axis_index("wide")
    mz = lax.axis_index("narrow")

    slots = item_lengths.shape[0]
    spans = item_lengths // t
    order = jnp.arange(slots, dtype=jnp.int32)
    ends = jnp.sum(jnp.where(order[None, :] <= order[:, None], spans[None, :], 0), 1)
    blocks = jnp.arange(count, dtype=jnp.int32)
    item = jnp.sum((ends[None, :] <= blocks[:, None]).astype(jnp.int32), 1)
    is_item = item[:, None] == order[None, :]
    choose = lambda values: jnp.sum(jnp.where(is_item, values[None, :], 0), 1)
    firsts = choose(ends - spans)
    mine = blocks == me
    of_me = lambda values: jnp.sum(jnp.where(mine, values, 0))
    first = of_me(firsts)
    length = of_me(choose(spans))
    width = of_me(choose(grid_widths))
    position = (me - first) * t + jnp.arange(t, dtype=jnp.int32)
    tabs = rope_tables(position, width)
    steps = first + jnp.minimum(jnp.arange(SPAN, dtype=jnp.int32), length - 1)
    places = steps ^ me if count == 8 else steps
    sc = jnp.concatenate([length.reshape(1), places, steps]).astype(jnp.int32)

    cond = conditioning.astype(f32)[0]
    silu_low = jax.nn.silu(cond).astype(bf16)
    mod = jnp.sum(silu_low.astype(f32)[:, None, None] * w_ada.astype(f32), 0)
    share = cd // deep
    sent = jnp.concatenate([mod.reshape(-1), lax.dynamic_slice_in_dim(cond, mz * share, share)])
    got = gather_now(gather_now(sent, "narrow").reshape(-1), "wide").reshape(count, deep, -1)
    mods = got[:, :, : 4 * ada].reshape(count, deep, 4, ada).transpose(0, 2, 1, 3).reshape(count, 4, d)
    conds = got[:, :, 4 * ada :].reshape(count, cd)
    my_mod = lax.dynamic_index_in_dim(mods, first, 0, False)
    of_block = jnp.sum(jnp.where((firsts[:, None] == blocks[None, :])[:, :, None, None], mods[None], 0.0), 1)
    scales = 1.0 + of_block
    gates = jnp.tanh(of_block)
    factor = jnp.stack([1.0 + my_mod[0], jnp.tanh(my_mod[1]), 1.0 + my_mod[2], jnp.tanh(my_mod[3])])
    vec = norm_gains * factor
    hg = jnp.tile(head_gains, (1, heads))
    tg_heads = jnp.tanh(cross_gate)
    tg = jnp.repeat(tg_heads, HD)[None, :]

    order = Order()
    cap_raw = jnp.einsum("kd,jde->jke", captions, w_caption, preferred_element_type=f32)
    whole_cap = pl.BlockSpec((text, n), lambda i: (0, 0))
    both_cap = pl.BlockSpec((text, 2 * n), lambda i: (0, 0))
    (cap,) = order.run(
        "caption_norm",
        caption_norm_kernel,
        (1,),
        (cap_raw[0], cap_raw[1], hg),
        [whole_cap, whole_cap, whole(hg.shape)],
        [both_cap],
        [sds((text, 2 * n), bf16)],
    )
    cap = lax.all_gather(cap, "wide", axis=0, tiled=True)

    chunks = range(t // BR)
    pairs_of = range(t // (2 * BR))
    sums = Sums(order, deep, mz)
    a1, k_raw, k, v, q_raw, q = key_call(order, patches, vec, w_qkv, tabs, hg, ())
    kv = Gather(k, v)


    k_all, v_all = pick(order, sc, kv.pieces(), SPAN)
    heads_out = {}
    for c in chunks:
        heads_out[c] = (*attend_call(order, sc, q, k_all, v_all, cap, text, tg, c, BR), 0)
        sums.add(("attn", c), mm(heads_out[c][0], w_out).astype(bf16))
        if c == 1:
            q_all = lax.all_gather(pin(order, q), "wide", axis=0, tiled=True)

    mids, gus = {}, {}
    whole_out = ()
    for c in chunks:
        mids[c], gus[c], ffn_part, *whole_out = ffn_call(
            order, c, patches, sums.get(("attn", c)), vec, w_gate_up, w_down, whole_out
        )
        sums.add(("ffn", c), ffn_part, (q_all,) if c == 1 else ())
    a3, hidden = whole_out
    whole_out = ()
    c4 = 0.0
    for c in chunks:
        da3_part, part_sum, *whole_out = ffn_back_call(
            order, c, sums.get(("ffn", c)), mids[c], cotangent, gus[c], vec, w_gate_up, w_down, whole_out
        )
        sums.add(("da3", c), da3_part)
        c4 = c4 + part_sum
    output, d_ffn, d_gu = whole_out

    d_mids, dqs, dq_caps, d_got, d_mixed, d_scaled = {}, {}, {}, {}, {}, {}
    whole_out = ()
    mlp_part = ()
    behind = ()
    c2 = c3 = dck = dcv = gate_sum = 0.0
    for h in pairs_of:
        for c in (2 * h, 2 * h + 1):
            _, o_self, linv, place = heads_out[c]
            if c == 2 * h + 1 and h > 0:
                behind = d_got[h - 1].second
            da3 = sums.get(("da3", c), behind)
            d_mids[c], d_mixed[c], p3, p2, *outs = out_back_call(
                order, c, da3, mids[c], sums.get(("attn", c)), cotangent, vec, w_out, o_self, linv, place, whole_out
            )
            whole_out, d_scaled[h] = (outs if c % 2 == 0 else outs[:1]), outs[1]
            c2, c3 = c2 + p2, c3 + p3
            behind = ()
            if c == 2 * h:
                early = d_got[h - 1].first if h > 0 else ()
                mlp_part = pair_grad_call(order, a3, d_gu, d_ffn, hidden, h, len(pairs_of), mlp_part, early)
        d_got[h] = GatherOne(d_scaled[h])
        dq_caps[h], pk, pv, pg = caption_back_call(order, sc, q, d_mixed[2 * h], d_mixed[2 * h + 1], cap, text, tg, h)
        dck, dcv, gate_sum = dck + pk, dcv + pv, gate_sum + pg
    d_attn = whole_out[0]
    cap_sum = jnp.concatenate([dck, dcv], 1)
    cap_got = lax.all_gather(cap_sum.astype(bf16), "wide")
    kept = (firsts == me)[:, None, None]
    cap_sum = jnp.sum(jnp.where(kept, cap_got.astype(f32), 0.0), 0)
    last_half = pairs_of[-1]

    def make_dq(h, after):
        return dq_call(order, sc, q, d_scaled[h], k_all, v_all, dq_caps[h], h, after)

    for h in pairs_of:
        dqs[h] = make_dq(h, () if h == 0 else d_got[last_half].first)
        if h == 0:
            g_mlp = scatter_rows(pin(order, mlp_part[0], d_got[last_half].first))

    d_cap, hs_c = order.run(
        "caption_grad",
        caption_grad_kernel,
        (1,),
        (cap_sum[:, :n], cap_sum[:, n:], cap_raw[0], hg),
        [whole_cap, whole_cap, whole_cap, whole(hg.shape)],
        [both_cap, pl.BlockSpec((1, n), lambda i: (0, 0))],
        [sds((text, 2 * n), bf16), sds((1, n), f32)],
    )
    d_text = (mm_nt(d_cap[:, :n], w_caption[0]) + mm_nt(d_cap[:, n:], w_caption[1])).astype(bf16)
    cap_part = mm_tn(captions, d_cap).astype(bf16)
    grad_captions = lax.psum(d_text, "narrow")

    ds = [x for h in pairs_of for x in pick(order, sc, d_got[h].pieces(), SPAN)]
    whole_out = ()
    c1_parts, hs_parts = [], []
    mixed = jnp.concatenate([heads_out[c][0] for c in chunks])
    pairs = n // 128

    def project(c, dkv, after=()):
        nonlocal whole_out
        da1_part, p_hs, p1, *whole_out = dqkv_call(order, c, dqs[c // 2], dkv, q_raw, k_raw, tabs, hg, w_qkv, patches, whole_out)
        hs_parts.append(p_hs)
        c1_parts.append(p1)
        return da1_part

    first_dkv = [dkv_call(order, sc, k, v, q_all, ds, 0, 0, pairs)]
    parts_of = lambda p: dkv_call(order, sc, k, v, q_all, ds, 1, p, 1)
    sums.add(("da1", 0), project(0, first_dkv))
    da1_part = project(1, first_dkv)
    dkv = [parts_of(0)]
    sums.add(("da1", 1), da1_part, (g_mlp,))
    g_cap = scatter_rows(pin(order, cap_part))
    dkv.append(parts_of(1))
    dkv += [parts_of(p) for p in range(2, pairs)]
    for c in chunks[2:]:
        da1_part = project(c, dkv)
        if c == chunks[-1]:
            d_qkv = whole_out[0]
            packed = pack_call(order, c1_parts, hs_parts, hs_c, gate_sum, tg, c2, c3, c4, mz)
            from_narrow = [packed] + [swap(packed, "narrow", deep, m) for m in range(1, deep)]
            attn_part = pair_grad_call(order, a1, d_qkv, d_attn, mixed)[0]
        sums.add(("da1", c), da1_part, (*from_narrow, grad_captions) if c == chunks[-1] else ())
    g_attn = scatter_rows(pin(order, attn_part))

    (folded,) = fold_call(order, from_narrow)
    got = lax.all_gather(folded, "wide")
    whole_out = last_call(order, 0, sums.get(("da1", 0)), patches, d_mids[0], vec, ())
    for c in chunks[1:]:
        da1 = sums.get(("da1", c), (got,) if c == 1 else (g_cap,) if c == 2 else ())
        if c == 1:
            got = pin(order, got)
        whole_out = last_call(order, c, da1, patches, d_mids[c], vec, whole_out)
    (grad_patches,) = whole_out

    cols = got[:, :4]
    grad_head_gains = jnp.sum(got[:, 4, : 3 * n], 0).reshape(3, heads, HD).sum(1)
    grad_cross_gate = jnp.sum(got[:, 5], 0)[::HD]
    gain_factor = jnp.stack([scales[:, 0], gates[:, 1], scales[:, 2], gates[:, 3]], 1)
    gain_grads = jnp.sum(gain_factor * cols, 0)
    wide_cols = d // count
    grad_norm_gains = lax.dynamic_slice_in_dim(gain_grads, me * wide_cols, wide_cols, 1)
    ones = jnp.ones_like(gates[:, 0])
    slope = jnp.stack([ones, 1.0 - gates[:, 1] ** 2, ones, 1.0 - gates[:, 3] ** 2], 1)
    d_mod = lax.dynamic_slice_in_dim(slope * norm_gains[None] * cols, mz * ada, ada, 2)
    at_slot = (firsts[None, :] == blocks[:, None]).astype(f32)
    d_slots = jnp.sum(at_slot[:, :, None, None] * d_mod[None], 1).astype(bf16).astype(f32)
    cond_rows = cd // count
    silu_mine = lax.dynamic_slice_in_dim(jax.nn.silu(conds).astype(bf16).astype(f32), me * cond_rows, cond_rows, 1)
    grad_ada = jnp.sum(silu_mine[:, :, None, None] * d_slots[:, None], 0)
    d_mine = lax.dynamic_index_in_dim(d_slots, me, 0, False)
    cond_part = jnp.sum(d_mine[None] * w_ada.astype(f32), (1, 2))
    cond_part = cond_part.reshape(-1, 128)
    cond_total = tree([cond_part] + [swap(cond_part, "narrow", deep, m) for m in range(1, deep)]).reshape(-1)
    pull_silu = jax.vjp(jax.nn.silu, cond)[1]
    grad_conditioning = pull_silu(cond_total)[0].reshape(1, -1)

    rows = d // count
    return (
        output,
        grad_patches,
        grad_conditioning,
        grad_captions,
        grad_ada,
        grad_norm_gains,
        g_attn[:, : 3 * n].astype(f32).reshape(rows, 3, n).transpose(1, 0, 2),
        grad_head_gains,
        grad_cross_gate,
        g_cap.astype(f32).reshape(-1, 2, n).transpose(1, 0, 2),
        g_attn[:, 3 * n :].astype(f32).T,
        g_mlp[:, : 2 * ff].astype(f32).reshape(rows, 2, ff).transpose(1, 0, 2),
        g_mlp[:, 2 * ff :].astype(f32).T,
    )


def solution(mesh):
    placed = (
        P("wide", None),
        P("wide", None),
        P("wide", None),
        P("wide", None),
        P(),
        P(),
        P(None, None, "narrow"),
        P(),
        P(None, None, "narrow"),
        P(),
        P("narrow"),
        P(None, None, "narrow"),
        P("narrow", None),
        P(None, None, "narrow"),
        P("narrow", None),
    )
    return jax.shard_map(
        local,
        mesh=mesh,
        in_specs=placed,
        out_specs=(
            P("wide", None),
            P("wide", None),
            P("wide", None),
            P("wide", None),
            P("wide", None, "narrow"),
            P(None, "wide"),
            P(None, "wide", "narrow"),
            P(),
            P(),
            P(None, "wide", "narrow"),
            P("narrow", "wide"),
            P(None, "wide", "narrow"),
            P("narrow", "wide"),
        ),
        check_vma=False,
    )
```

```python
import functools

import jax
import jax.numpy as jnp
from jax import lax
from jax.experimental import pallas as pl
from jax.experimental.pallas import tpu as pltpu
from jax.sharding import PartitionSpec as P

HD = 64
SPAN = 4
EPS = 1e-05
LOG2E = 1.4426950408889634
f32 = jnp.float32
bf16 = jnp.bfloat16
VMEM = 56 * 1024 * 1024
BR = 256
NT = (((1,), (1,)), ((), ()))
TN = (((0,), (0,)), ((), ()))


def params(n):
    return pltpu.CompilerParams(
        dimension_semantics=("arbitrary",) * n, vmem_limit_bytes=VMEM
    )


def sds(shape, dtype):
    return jax.ShapeDtypeStruct(shape, dtype)


COST = {
    "key": 8, "query": 9, "caption_norm": 2, "pick": 5, "attend": 15, "hop": 3, "ffn": 9, "ffn_back": 10, "out_back": 6,
    "pair_grad": 10, "caption_back": 6, "dq": 45, "dkv": 24, "dqkv": 7, "caption_grad": 3, "last": 3, "note": 1, "pin": 1,
}


class Order:
    def __init__(self):
        self.token = ()

    def run(self, name, kernel, grid, ins, in_specs, out_specs, out_shape, scratch=(), scalar=None, held=(), first_held=0, after=()):
        pre = 0 if scalar is None else 1
        given = pre + len(ins)
        extra = [*self.token, *after, *held]

        def body(*refs):
            kernel(*refs[:given], *refs[given + len(extra) :])

        at = given + len(extra) - len(held)
        out = pl.pallas_call(
            body,
            grid_spec=pltpu.PrefetchScalarGridSpec(
                num_scalar_prefetch=pre,
                grid=grid,
                in_specs=list(in_specs) + loose(len(extra)),
                out_specs=out_specs,
                scratch_shapes=list(scratch),
            ),
            out_shape=out_shape,
            input_output_aliases={at + k: first_held + k for k in range(len(held))},
            compiler_params=params(len(grid)),
            cost_estimate=pl.CostEstimate(
                flops=COST[name] * 250_000_000, bytes_accessed=COST[name] * 750_000, transcendentals=0
            ),
            name=name,
        )(*(() if scalar is None else (scalar,)), *ins, *extra)
        self.token = (out[0],)
        return out


def loose(n):
    return [pl.BlockSpec(memory_space=pl.ANY)] * n


def mm(a, b):
    return jnp.dot(a, b, preferred_element_type=f32)


def mm_nt(a, b):
    return lax.dot_general(a, b, NT, preferred_element_type=f32)


def mm_tn(a, b):
    return lax.dot_general(a, b, TN, preferred_element_type=f32)


def split(x):
    hi = x.astype(bf16)
    return hi, (x - hi.astype(f32)).astype(bf16)


def head_sum(x, ones):
    hi, lo = split(x)
    return mm(hi, ones) + mm(lo, ones)


def head_ones(n):
    a = lax.broadcasted_iota(jnp.int32, (n, n), 0) // HD
    b = lax.broadcasted_iota(jnp.int32, (n, n), 1) // HD
    return (a == b).astype(bf16)


def halves(n):
    lane = lax.broadcasted_iota(jnp.int32, (1, n), 1)
    return (lane < HD, lane >= HD)


def keep(x, mask):
    return jnp.where(mask, x, jnp.zeros_like(x))


def inv_rms(x):
    return lax.rsqrt(jnp.mean(x * x, -1, keepdims=True) + EPS)


def row(ref, k):
    return ref[k : k + 1, :]


def whole(shape):
    zeros = (0,) * len(shape)
    return pl.BlockSpec(shape, lambda *_: zeros, pipeline_mode=pl.Buffered(1))


def rows_of(br, width, first=0):
    return pl.BlockSpec((br, width), lambda i, *_: (i, first))


def accumulate(ref, value, first):
    @pl.when(first)
    def _():
        ref[...] = value

    @pl.when(jnp.logical_not(first))
    def _():
        ref[...] += value


def col_sum(x):
    return jnp.sum(x, 0, keepdims=True)


def tile3(t, n):
    return jnp.concatenate([t] * (n // t.shape[1]), 1)


def key_kernel(p_ref, v_ref, w_ref, wv_ref, wq_ref, c_ref, s1_ref, s2_ref, hg_ref, a_ref, kr_ref, k_ref, vv_ref, qr_ref, q_ref):
    x = p_ref[...].astype(f32)
    a = (x * inv_rms(x) * row(v_ref, 0)).astype(bf16)
    a_ref[...] = a
    k = mm(a, w_ref[0])
    kr_ref[...] = k
    k_ref[...] = turned(k, row(hg_ref, 1), (c_ref, s1_ref, s2_ref)).astype(bf16)
    vv_ref[...] = mm(a, wv_ref[0]).astype(bf16)
    q = mm(a, wq_ref[0])
    qr_ref[...] = q
    q_ref[...] = (turned(q, row(hg_ref, 0), (c_ref, s1_ref, s2_ref)) * (0.125 * LOG2E)).astype(bf16)


def turned(y, gain, tabs):
    n = y.shape[1]
    cos, s1, s2 = (tile3(t[...], n) for t in tabs)
    z = y * lax.rsqrt(head_sum(y * y, head_ones(n)) * (1.0 / HD) + EPS) * gain
    return z * cos + pltpu.roll(z, n - 16, 1) * s1 + pltpu.roll(z, 16, 1) * s2


def one_weight(w, k):
    return pl.BlockSpec((1, *w.shape[1:]), lambda *_: (k, 0, 0), pipeline_mode=pl.Buffered(1))


def key_call(order, patches, vec, w, tabs, hg, after, br=256):
    t, d = patches.shape
    n = w.shape[2]
    return order.run(
        "key",
        key_kernel,
        (t // br,),
        (patches, vec, w, w, w, *tabs, hg),
        [rows_of(br, d), whole(vec.shape), one_weight(w, 1), one_weight(w, 2), one_weight(w, 0)] + [rows_of(br, 128)] * 3 + [whole(hg.shape)],
        [rows_of(br, d)] + [rows_of(br, n)] * 5,
        [sds((t, d), bf16), sds((t, n), f32), sds((t, n), bf16), sds((t, n), bf16), sds((t, n), f32), sds((t, n), bf16)],
        after=after,
    )


def soft_sums(q, k, v, mask):
    e = jnp.exp2(mm_nt(q, keep(k, mask))).astype(bf16)
    return mm(e, jnp.where(mask, v, jnp.ones_like(v)))


def item_block(j, s):
    return jnp.minimum(j, s[0] - 1)


def attend_kernel(sc, q_ref, k_ref, v_ref, ck_ref, cv_ref, tg_ref, mix_ref, o_ref, li_ref, acc):
    j = pl.program_id(1)
    masks = halves(128)
    keys = k_ref.shape[0] if q_ref.shape[0] <= BR else 512

    def block_sums(h):
        q = q_ref[...]
        total = 0.0
        for c in range(k_ref.shape[0] // keys):
            at = slice(c * keys, (c + 1) * keys)
            total = total + soft_sums(q, k_ref[at, :], v_ref[at, :], masks[h])
        return total

    @pl.when(j == 0)
    def _():
        for h in range(2):
            acc[2 + h] = soft_sums(q_ref[...], ck_ref[...], cv_ref[...], masks[h])
            acc[h] = block_sums(h)

    @pl.when((j > 0) & (j < sc[0]))
    def _():
        for h in range(2):
            acc[h] += block_sums(h)

    @pl.when(j == SPAN - 1)
    def _():
        def finish(a0, a1):
            inverse = 1.0 / jnp.where(masks[0], pltpu.roll(a0, HD, 1), pltpu.roll(a1, HD, 1))
            return jnp.where(masks[0], a0, a1) * inverse, inverse

        o, li = finish(acc[0], acc[1])
        mix_ref[...] = (o + tg_ref[...] * finish(acc[2], acc[3])[0]).astype(bf16)
        o_ref[...] = o.astype(bf16)
        li_ref[...] = li


def attend_call(order, sc, q, k, v, cap, text, tg, at, bq):
    n = q.shape[1]
    pairs = n // 128
    block = k.shape[0] // SPAN
    mine = lambda p, j, s: (0, p)
    other = lambda p, j, s: (item_block(j, s), p)
    return order.run(
        "attend",
        attend_kernel,
        (pairs, SPAN),
        (q, k, v, cap, cap, tg),
        [
            pl.BlockSpec((bq, 128), lambda p, j, s: (at, p)),
            pl.BlockSpec((block, 128), other),
            pl.BlockSpec((block, 128), other),
            pl.BlockSpec((text, 128), lambda p, j, s: (s[1 + SPAN], p)),
            pl.BlockSpec((text, 128), lambda p, j, s: (s[1 + SPAN], pairs + p)),
            pl.BlockSpec((1, 128), mine),
        ],
        [pl.BlockSpec((bq, 128), mine)] * 3,
        [sds((bq, n), bf16), sds((bq, n), bf16), sds((bq, n), f32)],
        [pltpu.VMEM((4, bq, 128), f32)],
        sc,
    )


def caption_back_kernel(sc, q_ref, da_ref, db_ref, ck_ref, cv_ref, tg_ref, dq_ref, dk_ref, dv_ref, gs_ref):
    masks = halves(128)
    q, d = q_ref[...], jnp.concatenate([da_ref[...], db_ref[...]], 0)
    dq = jnp.zeros(q.shape, f32)
    dk = jnp.zeros(ck_ref.shape, f32)
    dv = jnp.zeros(ck_ref.shape, f32)
    sums = []
    for h in range(2):
        ck, cv = keep(ck_ref[...], masks[h]), keep(cv_ref[...], masks[h])
        gate = tg_ref[:, h * HD : h * HD + 1]
        e = jnp.exp2(mm_nt(q, ck))
        prob = e * (1.0 / jnp.sum(e, -1, keepdims=True))
        dp = mm_nt(d, cv)
        m = jnp.sum(prob * dp, -1, keepdims=True)
        dc = (prob * (dp - m) * gate).astype(bf16)
        dq = dq + mm(dc, ck)
        dk = dk + mm_tn(dc, keep(q, masks[h]))
        dv = dv + mm_tn(prob.astype(bf16), keep(d, masks[h]))
        sums.append(jnp.sum(m, 0, keepdims=True))
    dq_ref[...] = dq * 0.125
    dk_ref[...] = dk * (1.0 / LOG2E)
    dv_ref[...] = dv * tg_ref[...]
    gs_ref[...] = jnp.where(masks[0], sums[0], sums[1])


def caption_back_call(order, sc, q, da, db, cap, text, tg, h):
    n = q.shape[1]
    pairs = n // 128
    bq = 2 * BR
    mine = lambda p, s: (0, p)
    return order.run(
        "caption_back",
        caption_back_kernel,
        (pairs,),
        (q, da, db, cap, cap, tg),
        [
            pl.BlockSpec((bq, 128), lambda p, s: (h, p)),
            pl.BlockSpec((BR, 128), mine),
            pl.BlockSpec((BR, 128), mine),
            pl.BlockSpec((text, 128), lambda p, s: (s[1 + SPAN], p)),
            pl.BlockSpec((text, 128), lambda p, s: (s[1 + SPAN], pairs + p)),
            pl.BlockSpec((1, 128), mine),
        ],
        [
            pl.BlockSpec((bq, 128), mine),
            pl.BlockSpec((text, 128), mine),
            pl.BlockSpec((text, 128), mine),
            pl.BlockSpec((1, 128), mine),
        ],
        [sds((bq, n), f32), sds((text, n), f32), sds((text, n), f32), sds((1, n), f32)],
        scalar=sc,
    )


def minus_delta(rows, head):
    lane = lax.broadcasted_iota(jnp.int32, (rows, 128), 1)
    return jnp.where((lane >= 3 * head) & (lane < 3 * head + 3), -1.0, 0.0).astype(bf16)


def dq_kernel(parts, sc, q_ref, k_ref, v_ref, *refs):
    d_refs, x_refs, c_refs = (refs[k * parts : (k + 1) * parts] for k in range(3))
    dq_ref, acc = refs[3 * parts :]
    pair = pl.program_id(0)
    j = pl.program_id(1)
    masks = halves(128)
    keys = 512
    rows = d_refs[0].shape[0]

    @pl.when(j == 0)
    def _():
        acc[...] = jnp.zeros_like(acc)

    @pl.when(j < sc[0])
    def _():
        for r in range(parts):
            mine = slice(r * rows, (r + 1) * rows)
            q = q_ref[mine, :]
            dx = jnp.concatenate([d_refs[r][...], x_refs[r][...]], 1)
            total = acc[mine, :]
            for h in range(2):
                off = minus_delta(keys, 2 * pair + h)
                for c in range(k_ref.shape[0] // keys):
                    at = slice(c * keys, (c + 1) * keys)
                    k = keep(k_ref[at, :], masks[h])
                    e = jnp.exp2(mm_nt(q, k))
                    dp = mm_nt(dx, jnp.concatenate([keep(v_ref[at, :], masks[h]), off], 1))
                    total = total + mm((e * dp).astype(bf16), k)
            acc[mine, :] = total

    @pl.when(j == SPAN - 1)
    def _():
        for r in range(parts):
            mine = slice(r * rows, (r + 1) * rows)
            dq_ref[mine, :] = acc[mine, :] * 0.125 + c_refs[r][...]


def dq_call(order, sc, q, ds, k, v, cap_dqs, after=()):
    t, n = q.shape
    pairs = n // 128
    parts = len(ds)
    block = k.shape[0] // SPAN
    rows = t // parts
    mine = lambda p, j, s: (0, p)
    other = pl.BlockSpec((block, 128), lambda p, j, s: (item_block(j, s), p))
    return order.run(
        "dq",
        functools.partial(dq_kernel, parts),
        (pairs, SPAN),
        (q, k, v, *ds, *ds, *cap_dqs),
        [pl.BlockSpec((t, 128), mine), other, other]
        + [pl.BlockSpec((rows, 128), mine)] * parts
        + [pl.BlockSpec((rows, 128), lambda p, j, s: (0, pairs))] * parts
        + [pl.BlockSpec((rows, 128), mine)] * parts,
        [pl.BlockSpec((t, 128), mine)],
        [sds((t, n), f32)],
        [pltpu.VMEM((t, 128), f32)],
        sc,
        after=after,
    )[0]


def dkv_kernel(parts, base, sc, k_ref, v_ref, q_ref, *rest):
    d_refs, x_refs = rest[0 : 2 * parts : 2], rest[1 : 2 * parts : 2]
    dk_ref, dv_ref = rest[2 * parts :]
    pair = base + pl.program_id(0)
    j = pl.program_id(1)
    masks = halves(128)
    queries = 2 * BR

    @pl.when(j == 0)
    def _():
        dk_ref[...] = jnp.zeros_like(dk_ref)
        dv_ref[...] = jnp.zeros_like(dv_ref)

    @pl.when(j < sc[0])
    def _():
        dk, dv = dk_ref[...], dv_ref[...]
        for h in range(2):
            vx = jnp.concatenate([keep(v_ref[...], masks[h]), minus_delta(v_ref.shape[0], 2 * pair + h)], 1)
            for r in range(parts):
                q = keep(q_ref[r * queries : (r + 1) * queries, :], masks[h])
                d, x = d_refs[r][...], x_refs[r][...]
                e = jnp.exp2(mm_nt(k_ref[...], q))
                dp = mm_nt(vx, jnp.concatenate([d, x], 1))
                dv = dv + mm(e.astype(bf16), keep(d, masks[h]))
                dk = dk + mm((e * dp).astype(bf16), q)
        dk_ref[...] = dk
        dv_ref[...] = dv


def dkv_call(order, sc, k, v, q_all, ds, half, base, n_pairs):
    t, n = k.shape
    pairs = n // 128
    rows = 2 * BR
    mine = pl.BlockSpec((rows, 128), lambda p, j, s: (half, base + p))
    out = pl.BlockSpec((rows, 128), lambda p, j, s: (0, p))
    other = pl.BlockSpec((rows, 128), lambda p, j, s: (item_block(j, s), base + p))
    extra = pl.BlockSpec((rows, 128), lambda p, j, s: (item_block(j, s), pairs))
    return order.run(
        "dkv",
        functools.partial(dkv_kernel, len(ds), base),
        (n_pairs, SPAN),
        (k, v, q_all, *(x for d in ds for x in (d, d))),
        [mine, mine, pl.BlockSpec((t, 128), lambda p, j, s: (s[1 + SPAN + j], base + p))] + [other, extra] * len(ds),
        [out, out],
        [sds((rows, n_pairs * 128), f32)] * 2,
        scalar=sc,
    )


def chunk_call(order, kernel, name, c, ins, specs, chunk_outs, sum_outs, whole_outs, before):
    one = lambda r, w: pl.BlockSpec((r, w), lambda i: (0, 0))
    own = chunk_outs + sum_outs
    into = [pl.BlockSpec((BR, w), lambda i, at=c % (r // BR): (at, 0)) for r, w, _ in whole_outs]
    return order.run(
        name,
        kernel,
        (1,),
        ins,
        specs,
        [one(r, w) for r, w, _ in own] + into,
        [sds((r, w), k) for r, w, k in own + whole_outs],
        held=tuple(before),
        first_held=len(own),
    )


def part(c, width):
    return pl.BlockSpec((BR, width), lambda i: (c, 0))


def alone(width):
    return pl.BlockSpec((BR, width), lambda i: (0, 0))


def pair_grad_kernel(a_ref, b_ref, c_ref, d_ref, o_ref):
    n = b_ref.shape[1]
    o_ref[:, :n] = mm_tn(a_ref[...], b_ref[...]).astype(bf16)
    o_ref[:, n:] = mm_tn(c_ref[...], d_ref[...]).astype(bf16)


def pair_grad_call(order, a, b, c, d, part=0, parts=1, before=(), after=()):
    t, m = a.shape
    n, k = b.shape[1], d.shape[1]
    blk = 256
    steps = m // blk // parts
    cols = pl.BlockSpec((t, blk), lambda i: (0, part * steps + i))
    return order.run(
        "pair_grad",
        pair_grad_kernel,
        (steps,),
        (a, b, c, d),
        [cols, whole(b.shape), cols, whole(d.shape)],
        [pl.BlockSpec((blk, n + k), lambda i: (part * steps + i, 0))],
        [sds((m, n + k), bf16)],
        held=before,
        after=after,
    )


def ffn_kernel(p_ref, at_ref, v_ref, wg_ref, wd_ref, mid_ref, gu_ref, f_ref, a_ref, h_ref):
    at = at_ref[...].astype(f32)
    mid = p_ref[...].astype(f32) + row(v_ref, 1) * (at * inv_rms(at))
    mid_ref[...] = mid
    a = (mid * inv_rms(mid) * row(v_ref, 2)).astype(bf16)
    a_ref[...] = a
    g = mm(a, wg_ref[0])
    u = mm(a, wg_ref[1])
    n = g.shape[1]
    gu_ref[:, :n] = g.astype(bf16)
    gu_ref[:, n:] = u.astype(bf16)
    h = (g * jax.nn.sigmoid(g) * u).astype(bf16)
    h_ref[...] = h
    f_ref[...] = mm(h, wd_ref[...]).astype(bf16)


def ffn_call(order, c, patches, at, vec, wg, wd, before):
    t, d = patches.shape
    n = wd.shape[0]
    return chunk_call(
        order,
        ffn_kernel,
        "ffn",
        c,
        (patches, at, vec, wg, wd),
        [part(c, d), alone(d), whole(vec.shape), whole(wg.shape), whole(wd.shape)],
        [(BR, d, f32), (BR, 2 * n, bf16), (BR, d, bf16)],
        [],
        [(t, d, bf16), (t, n, bf16)],
        before,
    )


def ffn_back_kernel(f_ref, mid_ref, c_ref, gu_ref, v_ref, wg_ref, wd_ref, da_ref, cs_ref, y_ref, df_ref, dgu_ref):
    f = f_ref[...].astype(f32)
    cot = c_ref[...].astype(f32)
    r = inv_rms(f)
    fh = f * r
    y_ref[...] = (mid_ref[...] + row(v_ref, 3) * fh).astype(bf16)
    z = cot * row(v_ref, 3)
    df = (r * (z - fh * jnp.mean(z * fh, -1, keepdims=True))).astype(bf16)
    df_ref[...] = df
    cs_ref[...] = col_sum(cot * fh)
    dh = mm_nt(df, wd_ref[...])
    n = dh.shape[1]
    g = gu_ref[:, :n].astype(f32)
    u = gu_ref[:, n:].astype(f32)
    s = jax.nn.sigmoid(g)
    gs = g * s
    dg = (dh * u * (s + gs * (1.0 - s))).astype(bf16)
    du = (dh * gs).astype(bf16)
    dgu_ref[:, :n] = dg
    dgu_ref[:, n:] = du
    da_ref[...] = (mm_nt(dg, wg_ref[0]) + mm_nt(du, wg_ref[1])).astype(bf16)


def ffn_back_call(order, c, f, mid, cot, gu, vec, wg, wd, before):
    t, d = cot.shape
    n = wd.shape[0]
    return chunk_call(
        order,
        ffn_back_kernel,
        "ffn_back",
        c,
        (f, mid, cot, gu, vec, wg, wd),
        [alone(d), alone(d), part(c, d), alone(2 * n), whole(vec.shape), whole(wg.shape), whole(wd.shape)],
        [(BR, d, bf16)],
        [(1, d, f32)],
        [(t, d, bf16), (t, d, bf16), (t, 2 * n, bf16)],
        before,
    )


def out_back_kernel(da_ref, mid_ref, at_ref, c_ref, v_ref, w_ref, o_ref, li_ref, dm_ref, dx_ref, c3_ref, c2_ref, dat_ref, ds_ref):
    da = da_ref[...].astype(f32)
    mid = mid_ref[...]
    r = inv_rms(mid)
    mh = mid * r
    z = da * row(v_ref, 2)
    dm = c_ref[...].astype(f32) + r * (z - mh * jnp.mean(z * mh, -1, keepdims=True))
    dm_ref[...] = dm
    c3_ref[...] = col_sum(da * mh)
    at = at_ref[...].astype(f32)
    ra = inv_rms(at)
    ah = at * ra
    c2_ref[...] = col_sum(dm * ah)
    z = dm * row(v_ref, 1)
    dat = (ra * (z - ah * jnp.mean(z * ah, -1, keepdims=True))).astype(bf16)
    dat_ref[...] = dat
    dx = mm_nt(dat, w_ref[...]).astype(bf16)
    dx_ref[...] = dx
    n = dx.shape[1]
    ds = dx.astype(f32) * li_ref[...]
    ds_ref[:, :n] = ds.astype(bf16)
    hi, lo = split(ds * o_ref[...].astype(f32))
    head = lax.broadcasted_iota(jnp.int32, (n, 128), 0) // HD
    lane = lax.broadcasted_iota(jnp.int32, (n, 128), 1)
    to_lanes = (lane // 3 == head).astype(bf16)
    delta = mm(hi, to_lanes) + mm(lo, to_lanes)
    one = delta.astype(bf16).astype(f32)
    two = (delta - one).astype(bf16).astype(f32)
    which = lax.broadcasted_iota(jnp.int32, (1, 128), 1) % 3
    ds_ref[:, n:] = jnp.where(which == 0, one, jnp.where(which == 1, two, delta - one - two)).astype(bf16)


def out_back_call(order, c, da, mid, at, cot, vec, w, o, li, place, before):
    t, d = cot.shape
    n = w.shape[0]
    return chunk_call(
        order,
        out_back_kernel,
        "out_back",
        c,
        (da, mid, at, cot, vec, w, o, li),
        [alone(d), alone(d), alone(d), part(c, d), whole(vec.shape), whole(w.shape), part(place, n), part(place, n)],
        [(BR, d, f32), (BR, n, bf16)],
        [(1, d, f32), (1, d, f32)],
        [(t, d, bf16), (2 * BR, n + 128, bf16)],
        before,
    )


def dqkv_kernel(pairs, dq_ref, *refs):
    dk_refs, dv_refs = refs[0 : 2 * pairs : 2], refs[1 : 2 * pairs : 2]
    (qr_ref, kr_ref, c_ref, s1_ref, s2_ref, hg_ref, w_ref, p_ref, da_ref, hs_ref, cs_ref, d_ref) = refs[2 * pairs :]
    side = lambda parts: jnp.concatenate([x[...] for x in parts], 1)
    n = dq_ref.shape[1]
    ones = head_ones(n)
    cos, s1, s2 = (tile3(t[...], n) for t in (c_ref, s1_ref, s2_ref))

    def back(dy, x, gain):
        dz = dy * cos - pltpu.roll(dy, 16, 1) * s2 - pltpu.roll(dy, n - 16, 1) * s1
        r = lax.rsqrt(head_sum(x * x, ones) * (1.0 / HD) + EPS)
        xh = x * r
        g = dz * gain
        return r * (g - xh * (head_sum(g * xh, ones) * (1.0 / HD))), col_sum(dz * xh)

    dq, hq = back(dq_ref[...], qr_ref[...], row(hg_ref, 0))
    dk, hk = back(side(dk_refs) * (1.0 / LOG2E), kr_ref[...], row(hg_ref, 1))
    dql, dkl, dvl = dq.astype(bf16), dk.astype(bf16), side(dv_refs).astype(bf16)
    d_ref[:, :n] = dql
    d_ref[:, n : 2 * n] = dkl
    d_ref[:, 2 * n :] = dvl
    da = mm_nt(dql, w_ref[0]) + mm_nt(dkl, w_ref[1]) + mm_nt(dvl, w_ref[2])
    da_ref[...] = da.astype(bf16)
    x = p_ref[...].astype(f32)
    cs_ref[...] = col_sum(da * (x * inv_rms(x)))
    hs_ref[0:1, :] = hq
    hs_ref[1:2, :] = hk


def dqkv_call(order, c, dq, dkv, qr, kr, tabs, hg, w, patches, before):
    t, d = patches.shape
    n = dq.shape[1]
    return chunk_call(
        order,
        functools.partial(dqkv_kernel, len(dkv)),
        "dqkv",
        c,
        (dq, *(x for two in dkv for x in two), qr, kr, *tabs, hg, w, patches),
        [part(c, n)] + [part(c % 2, x.shape[1]) for two in dkv for x in two] + [part(c, n)] * 2 + [part(c, 128)] * 3 + [whole(hg.shape), whole(w.shape), part(c, d)],
        [(BR, d, bf16)],
        [(2, n, f32), (1, d, f32)],
        [(t, 3 * n, bf16)],
        before,
    )


def last_kernel(da_ref, p_ref, dm_ref, v_ref, o_ref):
    x = p_ref[...].astype(f32)
    r = inv_rms(x)
    xh = x * r
    z = da_ref[...].astype(f32) * row(v_ref, 0)
    o_ref[...] = (dm_ref[...] + r * (z - xh * jnp.mean(z * xh, -1, keepdims=True))).astype(bf16)


def last_call(order, c, da, patches, dm, vec, before):
    t, d = patches.shape
    return chunk_call(
        order,
        last_kernel,
        "last",
        c,
        (da, patches, dm, vec),
        [alone(d), part(c, d), alone(d), whole(vec.shape)],
        [],
        [],
        [(t, d, bf16)],
        before,
    )


def caption_grad_kernel(dk_ref, dv_ref, kr_ref, hg_ref, d_ref, hs_ref):
    n = dk_ref.shape[1]
    ones = head_ones(n)
    x = kr_ref[...]
    r = lax.rsqrt(head_sum(x * x, ones) * (1.0 / HD) + EPS)
    xh = x * r
    dy = dk_ref[...]
    g = dy * row(hg_ref, 2)
    d_ref[:, :n] = (r * (g - xh * (head_sum(g * xh, ones) * (1.0 / HD)))).astype(bf16)
    d_ref[:, n:] = dv_ref[...].astype(bf16)
    hs_ref[...] = col_sum(dy * xh)


def caption_norm_kernel(kr_ref, v_ref, hg_ref, o_ref):
    n = kr_ref.shape[1]
    x = kr_ref[...]
    r = lax.rsqrt(head_sum(x * x, head_ones(n)) * (1.0 / HD) + EPS)
    o_ref[:, :n] = (x * r * row(hg_ref, 2)).astype(bf16)
    o_ref[:, n:] = v_ref[...].astype(bf16)


def swap(x, axis, size, m):
    return lax.ppermute(x, axis, [(i, i ^ m) for i in range(size)])


def pick_kernel(count, n_arrays, n_pieces, sc, *refs):
    outs, sem = refs[n_arrays * n_pieces :][:n_arrays], refs[-1]
    for k, out in enumerate(outs):
        pieces = refs[k * n_pieces : (k + 1) * n_pieces]
        rows = pieces[0].shape[0]
        for j in range(count):
            for m in range(n_pieces):

                @pl.when(sc[1 + j] == m)
                def _():
                    pltpu.make_async_copy(pieces[m], out.at[pl.ds(j * rows, rows)], sem.at[k, j]).start()

    for k, out in enumerate(outs):
        first = refs[k * n_pieces]
        rows = first.shape[0]
        for j in range(count):
            pltpu.make_async_copy(first, out.at[pl.ds(j * rows, rows)], sem.at[k, j]).wait()


class Gather:
    def __init__(self, a, b):
        self.all = None
        if lax.axis_size("wide") != 8:
            self.first = self.second = ()
            self.all = [lax.all_gather(x, "wide") for x in (a, b)]
            return
        send = lambda x, pairs: lax.ppermute(x, "wide", pairs)
        over_x = [(i, i ^ 2) for i in range(8)]
        over_y = [(1, 5), (4, 0), (3, 7), (6, 2)]
        a2, a4, b4, b2 = send(a, over_x), send(a, over_y), send(b, over_y), send(b, over_x)
        a6 = send(a2, [(0, 4), (1, 5), (6, 2), (7, 3)])
        b6x, b6y = send(b2, [(0, 4), (7, 3)]), send(b4, [(7, 5), (0, 2)])
        self.first = (a2, a4, b4, b2)
        self.second = (a6, b6x, b6y)
        self.kept = ((a, a2, a4, a6), (b, b2, b4, b6x + b6y))

    def pieces(self):
        if self.all is not None:
            return self.all
        return [[y for x in four for y in (x, swap(x, "wide", 8, 1))] for four in self.kept]


class GatherOne:
    def __init__(self, a):
        self.all, self.first, self.second = None, (), ()
        if lax.axis_size("wide") != 8:
            self.all = [lax.all_gather(a, "wide")]
            return
        a2 = lax.ppermute(a, "wide", [(i, i ^ 2) for i in range(8)])
        a4 = lax.ppermute(a, "wide", [(1, 5), (4, 0), (3, 7), (6, 2)])
        self.first, self.own = (a2, a4), a

    def across(self, order=None):
        if self.all is not None:
            return
        a2, a4 = self.first
        if order is not None:
            a2 = pin(order, a2)
        a6 = lax.ppermute(a2, "wide", [(0, 4), (1, 5), (6, 2), (7, 3)])
        self.second = (a6,)
        self.kept = ((self.own, a2, a4, a6),)

    pieces = Gather.pieces


def pick(order, sc, pieces, count):
    if not isinstance(pieces[0], list):
        one = lambda x, j: lax.dynamic_index_in_dim(x, sc[1 + SPAN + j], 0, False)
        return [jnp.concatenate([one(x, j) for j in range(count)]) for x in pieces]
    outs = [(count * p[0].shape[0], p[0].shape[1]) for p in pieces]
    return order.run(
        "pick",
        functools.partial(pick_kernel, count, len(pieces), 8),
        (1,),
        [x for p in pieces for x in p],
        loose(8 * len(pieces)),
        [pl.BlockSpec(shape, lambda i, s: (0, 0)) for shape in outs],
        [sds(shape, bf16) for shape in outs],
        [pltpu.SemaphoreType.DMA((len(pieces), count))],
        sc,
    )


def tree(parts):
    while len(parts) > 1:
        parts = [a + b for a, b in zip(parts[::2], parts[1::2])]
    return parts[0]


def pack_kernel(count, place, *refs):
    c1, hs = refs[:count], refs[count : 2 * count]
    hc_ref, gs_ref, tg_ref, c2_ref, c3_ref, c4_ref, o_ref = refs[2 * count :]
    n = hc_ref.shape[1]
    o_ref[...] = jnp.zeros_like(o_ref)
    o_ref[0:1, :] = sum(x[...] for x in c1)
    o_ref[1:2, :] = c2_ref[...]
    o_ref[2:3, :] = c3_ref[...]
    o_ref[3:4, :] = c4_ref[...]
    qk = sum(x[...] for x in hs)
    o_ref[4:5, :n] = qk[0:1]
    o_ref[4:5, n : 2 * n] = qk[1:2]
    o_ref[4:5, 2 * n : 3 * n] = hc_ref[...]
    gate = gs_ref[...] * (1.0 - tg_ref[...] * tg_ref[...])
    for z in range(o_ref.shape[1] // n):
        o_ref[5:6, z * n : (z + 1) * n] = jnp.where(place[0] == z, gate, 0.0)


def pack_call(order, c1, hs, hc, gs, tg, c2, c3, c4, place):
    d = c2.shape[1]
    ins = (*c1, *hs, hc, gs, tg, c2, c3, c4)
    spec = lambda x: pl.BlockSpec(x.shape, lambda i, s: (0, 0))

    def kernel(place, *refs):
        pack_kernel(len(c1), place, *refs)

    return order.run(
        "note",
        kernel,
        (1,),
        ins,
        [spec(x) for x in ins],
        [pl.BlockSpec((8, d), lambda i, s: (0, 0))],
        [sds((8, d), f32)],
        scalar=place.astype(jnp.int32).reshape(1),
    )[0]


def fold_kernel(*refs):
    parts, o_ref = refs[:-1], refs[-1]
    total = tree([x[...] for x in parts])
    row_at = lax.broadcasted_iota(jnp.int32, total.shape, 0)
    o_ref[...] = jnp.where((row_at >= 1) & (row_at < 4), parts[0][...], total)


def fold_call(order, parts):
    spec = pl.BlockSpec(parts[0].shape, lambda i: (0, 0))
    return order.run("note", fold_kernel, (1,), parts, [spec] * len(parts), [spec], [sds(parts[0].shape, f32)])


def pin_kernel(o_ref):
    pass


def pin(order, x, after=()):
    return order.run("pin", pin_kernel, (1,), (), [], loose(1), [sds(x.shape, x.dtype)], held=(x,), after=after)[0]


def gather_now(x, axis):
    n = x.shape[0]
    wide = -(-n // 1024) * 1024
    padded = jnp.pad(x, (0, wide - n)).reshape(1, 8, wide // 8)
    return lax.all_gather(padded, axis, axis=0, tiled=True).reshape(-1, wide)[:, :n]


def hop_kernel(have, sc, *refs):
    ins = dict(zip(have["in"], refs))
    outs = dict(zip(have["out"], refs[len(have["in"]) :]))
    end = sc[0] == 1
    if "total" in outs:
        outs["total"][...] = jnp.where(end, ins["r1"][...], ins["send"][...])
    third = None
    if "second" in ins:
        third = ins["second"][...] + ins["r2"][...]
    if "second" in outs:
        outs["second"][...] = ins["x"][...] + ins["r1"][...]
    if "send" in outs:
        new = ins["new"][...] if "new" in ins else third
        outs["send"][...] = new if third is None else jnp.where(end, new, third)


class Line:
    def __init__(self, order, place):
        self.order = order
        self.end = ((place == 0) | (place == 3)).astype(jnp.int32).reshape(1)
        self.x = self.second = self.send = None
        self.third = False

    def step(self, new, after=()):
        if self.send is None:
            self.x = self.send = new
            return None
        go = lambda x, perm: lax.ppermute(x, "narrow", perm)
        ins = {"r1": go(self.send, [(0, 1), (3, 2), (1, 0), (2, 3)])}
        outs = []
        if self.third:
            ins["send"] = self.send
            outs.append("total")
        if self.second is not None:
            ins["r2"] = go(self.second, [(1, 2), (2, 1)])
            ins["second"] = self.second
        if self.x is not None:
            ins["x"] = self.x
            outs.append("second")
        if new is not None:
            ins["new"] = new
        if new is not None or self.second is not None:
            outs.append("send")
        like = ins["r1"]
        block = pl.BlockSpec((BR // 2, like.shape[1]), lambda i, s: (i, 0))
        got = self.order.run(
            "hop",
            functools.partial(hop_kernel, {"in": list(ins), "out": outs}),
            (2,),
            list(ins.values()),
            [block] * len(ins),
            [block] * len(outs),
            [sds(like.shape, like.dtype)] * len(outs),
            scalar=self.end,
            after=after,
        )
        got = dict(zip(outs, got))
        self.third = self.second is not None
        self.x, self.second, self.send = new, got.get("second"), got.get("send")
        return got.get("total")


class Sums:
    def __init__(self, order, size, place):
        self.line = Line(order, place) if size == 4 else None
        self.names, self.done = [], {}

    def add(self, name, x, after=()):
        if self.line is None:
            self.done[name] = lax.psum(x, "narrow")
            return
        if self.line.send is None:
            self.names = [None]
        self._step(name, x, after)

    def _step(self, name, x, after):
        total = self.line.step(x, after)
        self.names.append(name)
        if total is not None:
            self.done[self.names[-4]] = total

    def get(self, name, after=()):
        while name not in self.done:
            self._step(None, None, after)
            after = ()
        return self.done[name]


def scatter_rows(x):
    return lax.psum_scatter(x.astype(bf16), "wide", scatter_dimension=0, tiled=True)


def rope_tables(position, width):
    lane = jnp.arange(128, dtype=jnp.int32)
    within = lane % HD
    quarter = HD // 4
    frequency = 10000.0 ** (-(within % quarter).astype(f32) / quarter)
    by_row = within < HD // 2
    where = jnp.where(by_row[None, :], (position // width)[:, None], (position % width)[:, None])
    angle = where.astype(f32) * frequency[None, :]
    cos, sin = jnp.cos(angle), jnp.sin(angle)
    former = (within % (HD // 2) < quarter)[None, :]
    return cos, jnp.where(former, -sin, 0.0), jnp.where(former, 0.0, sin)


def local(
    patches,
    cotangent,
    conditioning,
    captions,
    item_lengths,
    grid_widths,
    w_ada,
    norm_gains,
    w_qkv,
    head_gains,
    cross_gate,
    w_caption,
    w_out,
    w_gate_up,
    w_down,
):
    t, d = patches.shape
    n = w_qkv.shape[2]
    heads = n // HD
    ada = w_ada.shape[2]
    ff = w_down.shape[0]
    text = captions.shape[0]
    cd = conditioning.shape[1]
    count = lax.axis_size("wide")
    deep = lax.axis_size("narrow")
    me = lax.axis_index("wide")
    mz = lax.axis_index("narrow")

    slots = item_lengths.shape[0]
    spans = item_lengths // t
    order = jnp.arange(slots, dtype=jnp.int32)
    ends = jnp.sum(jnp.where(order[None, :] <= order[:, None], spans[None, :], 0), 1)
    blocks = jnp.arange(count, dtype=jnp.int32)
    item = jnp.sum((ends[None, :] <= blocks[:, None]).astype(jnp.int32), 1)
    is_item = item[:, None] == order[None, :]
    choose = lambda values: jnp.sum(jnp.where(is_item, values[None, :], 0), 1)
    firsts = choose(ends - spans)
    mine = blocks == me
    of_me = lambda values: jnp.sum(jnp.where(mine, values, 0))
    first = of_me(firsts)
    length = of_me(choose(spans))
    width = of_me(choose(grid_widths))
    position = (me - first) * t + jnp.arange(t, dtype=jnp.int32)
    tabs = rope_tables(position, width)
    steps = first + jnp.minimum(jnp.arange(SPAN, dtype=jnp.int32), length - 1)
    places = steps ^ me if count == 8 else steps
    sc = jnp.concatenate([length.reshape(1), places, steps]).astype(jnp.int32)

    cond = conditioning.astype(f32)[0]
    silu_low = jax.nn.silu(cond).astype(bf16)
    mod = jnp.sum(silu_low.astype(f32)[:, None, None] * w_ada.astype(f32), 0)
    share = cd // deep
    sent = jnp.concatenate([mod.reshape(-1), lax.dynamic_slice_in_dim(cond, mz * share, share)])
    got = gather_now(gather_now(sent, "narrow").reshape(-1), "wide").reshape(count, deep, -1)
    mods = got[:, :, : 4 * ada].reshape(count, deep, 4, ada).transpose(0, 2, 1, 3).reshape(count, 4, d)
    conds = got[:, :, 4 * ada :].reshape(count, cd)
    my_mod = lax.dynamic_index_in_dim(mods, first, 0, False)
    of_block = jnp.sum(jnp.where((firsts[:, None] == blocks[None, :])[:, :, None, None], mods[None], 0.0), 1)
    scales = 1.0 + of_block
    gates = jnp.tanh(of_block)
    factor = jnp.stack([1.0 + my_mod[0], jnp.tanh(my_mod[1]), 1.0 + my_mod[2], jnp.tanh(my_mod[3])])
    vec = norm_gains * factor
    hg = jnp.tile(head_gains, (1, heads))
    tg_heads = jnp.tanh(cross_gate)
    tg = jnp.repeat(tg_heads, HD)[None, :]

    order = Order()
    cap_raw = jnp.einsum("kd,jde->jke", captions, w_caption, preferred_element_type=f32)
    whole_cap = pl.BlockSpec((text, n), lambda i: (0, 0))
    both_cap = pl.BlockSpec((text, 2 * n), lambda i: (0, 0))
    (cap,) = order.run(
        "caption_norm",
        caption_norm_kernel,
        (1,),
        (cap_raw[0], cap_raw[1], hg),
        [whole_cap, whole_cap, whole(hg.shape)],
        [both_cap],
        [sds((text, 2 * n), bf16)],
    )
    cap = lax.all_gather(cap, "wide", axis=0, tiled=True)

    chunks = range(t // BR)
    pairs_of = range(t // (2 * BR))
    sums = Sums(order, deep, mz)
    a1, k_raw, k, v, q_raw, q = key_call(order, patches, vec, w_qkv, tabs, hg, ())
    kv = Gather(k, v)


    q_all = lax.all_gather(q, "wide", axis=0, tiled=True)
    k_all, v_all = pick(order, sc, kv.pieces(), SPAN)
    heads_out = {}
    for c in chunks:
        heads_out[c] = (*attend_call(order, sc, q, k_all, v_all, cap, text, tg, c, BR), 0)
        sums.add(("attn", c), mm(heads_out[c][0], w_out).astype(bf16))

    mids, gus = {}, {}
    whole_out = ()
    for c in chunks:
        mids[c], gus[c], ffn_part, *whole_out = ffn_call(
            order, c, patches, sums.get(("attn", c)), vec, w_gate_up, w_down, whole_out
        )
        sums.add(("ffn", c), ffn_part)
    a3, hidden = whole_out
    whole_out = ()
    c4 = 0.0
    for c in chunks:
        da3_part, part_sum, *whole_out = ffn_back_call(
            order, c, sums.get(("ffn", c)), mids[c], cotangent, gus[c], vec, w_gate_up, w_down, whole_out
        )
        sums.add(("da3", c), da3_part)
        c4 = c4 + part_sum
    output, d_ffn, d_gu = whole_out

    d_mids, dqs, dq_caps, d_got, d_mixed, d_scaled = {}, {}, {}, {}, {}, {}
    whole_out = ()
    mlp_part = ()
    behind = ()
    c2 = c3 = dck = dcv = gate_sum = 0.0
    for h in pairs_of:
        for c in (2 * h, 2 * h + 1):
            _, o_self, linv, place = heads_out[c]
            if c == 2 * h + 1 and h > 0:
                behind = d_got[h - 1].second
            da3 = sums.get(("da3", c), behind)
            d_mids[c], d_mixed[c], p3, p2, *outs = out_back_call(
                order, c, da3, mids[c], sums.get(("attn", c)), cotangent, vec, w_out, o_self, linv, place, whole_out
            )
            whole_out, d_scaled[h] = (outs if c % 2 == 0 else outs[:1]), outs[1]
            c2, c3 = c2 + p2, c3 + p3
            behind = ()
            if c == 2 * h:
                early = d_got[h - 1].first if h > 0 else ()
                mlp_part = pair_grad_call(order, a3, d_gu, d_ffn, hidden, h, len(pairs_of), mlp_part, early)
        d_got[h] = GatherOne(d_scaled[h])
        if h < pairs_of[-1]:
            d_got[h].across()
        dq_caps[h], pk, pv, pg = caption_back_call(order, sc, q, d_mixed[2 * h], d_mixed[2 * h + 1], cap, text, tg, h)
        dck, dcv, gate_sum = dck + pk, dcv + pv, gate_sum + pg
    d_attn = whole_out[0]
    cap_sum = jnp.concatenate([dck, dcv], 1)
    cap_got = lax.all_gather(cap_sum.astype(bf16), "wide")
    kept = (firsts == me)[:, None, None]
    cap_sum = jnp.sum(jnp.where(kept, cap_got.astype(f32), 0.0), 0)
    last_half = pairs_of[-1]

    halves_of = lambda table: [table[h] for h in pairs_of]
    dq = dq_call(order, sc, q, halves_of(d_scaled), k_all, v_all, halves_of(dq_caps))

    d_cap, hs_c = order.run(
        "caption_grad",
        caption_grad_kernel,
        (1,),
        (cap_sum[:, :n], cap_sum[:, n:], cap_raw[0], hg),
        [whole_cap, whole_cap, whole_cap, whole(hg.shape)],
        [both_cap, pl.BlockSpec((1, n), lambda i: (0, 0))],
        [sds((text, 2 * n), bf16), sds((1, n), f32)],
    )
    d_got[last_half].across(order)
    d_text = (mm_nt(d_cap[:, :n], w_caption[0]) + mm_nt(d_cap[:, n:], w_caption[1])).astype(bf16)
    cap_part = mm_tn(captions, d_cap).astype(bf16)
    pieces = -(-d_text.shape[1] // d)
    padded = jnp.pad(d_text, ((0, 0), (0, pieces * d - d_text.shape[1])))
    text_parts = [padded[:, p * d : (p + 1) * d] for p in range(pieces)]

    sums.add(("text", 0), text_parts[0])
    ds = [x for h in pairs_of for x in pick(order, sc, d_got[h].pieces(), SPAN)]
    sums.add(("text", 1), text_parts[1], (cap_part,))
    g_mlp = scatter_rows(pin(order, mlp_part[0]))
    whole_out = ()
    c1_parts, hs_parts = [], []
    mixed = jnp.concatenate([heads_out[c][0] for c in chunks])
    pairs = n // 128

    def project(c, dkv, after=()):
        nonlocal whole_out
        da1_part, p_hs, p1, *whole_out = dqkv_call(order, c, dq, dkv, q_raw, k_raw, tabs, hg, w_qkv, patches, whole_out)
        hs_parts.append(p_hs)
        c1_parts.append(p1)
        return da1_part

    dkv = [dkv_call(order, sc, k, v, q_all, ds, 0, 0, pairs)]
    for p in range(2, pieces):
        sums.add(("text", p), text_parts[p])
    g_cap = scatter_rows(pin(order, cap_part))
    first_part = project(0, dkv)
    parts_of = lambda p: dkv_call(order, sc, k, v, q_all, ds, 1, p, 1)
    first_dkv, dkv = dkv, [parts_of(0)]
    sums.add(("da1", 0), first_part)
    da1_part = project(1, first_dkv)
    dkv.append(parts_of(1))
    sums.add(("da1", 1), da1_part)
    dkv += [parts_of(p) for p in range(2, pairs)]
    for c in chunks[2:]:
        da1_part = project(c, dkv)
        if c == chunks[-1]:
            d_qkv = whole_out[0]
            packed = pack_call(order, c1_parts, hs_parts, hs_c, gate_sum, tg, c2, c3, c4, mz)
            from_narrow = [packed] + [swap(packed, "narrow", deep, m) for m in range(1, deep)]
            attn_part = pair_grad_call(order, a1, d_qkv, d_attn, mixed)[0]
        sums.add(("da1", c), da1_part, (g_mlp, *from_narrow) if c == chunks[-1] else ())
    g_attn = scatter_rows(pin(order, attn_part))

    (folded,) = fold_call(order, from_narrow)
    got = lax.all_gather(folded, "wide")
    whole_out = last_call(order, 0, sums.get(("da1", 0)), patches, d_mids[0], vec, ())
    for c in chunks[1:]:
        da1 = sums.get(("da1", c), (g_cap, got) if c == 1 else (g_attn,) if c == chunks[-1] else ())
        if c == 1:
            got = pin(order, got)
        whole_out = last_call(order, c, da1, patches, d_mids[c], vec, whole_out)
    (grad_patches,) = whole_out
    grad_captions = jnp.concatenate([sums.get(("text", p)) for p in range(pieces)], 1)[:, : d_text.shape[1]]

    cols = got[:, :4]
    grad_head_gains = jnp.sum(got[:, 4, : 3 * n], 0).reshape(3, heads, HD).sum(1)
    grad_cross_gate = jnp.sum(got[:, 5], 0)[::HD]
    gain_factor = jnp.stack([scales[:, 0], gates[:, 1], scales[:, 2], gates[:, 3]], 1)
    gain_grads = jnp.sum(gain_factor * cols, 0)
    wide_cols = d // count
    grad_norm_gains = lax.dynamic_slice_in_dim(gain_grads, me * wide_cols, wide_cols, 1)
    ones = jnp.ones_like(gates[:, 0])
    slope = jnp.stack([ones, 1.0 - gates[:, 1] ** 2, ones, 1.0 - gates[:, 3] ** 2], 1)
    d_mod = lax.dynamic_slice_in_dim(slope * norm_gains[None] * cols, mz * ada, ada, 2)
    at_slot = (firsts[None, :] == blocks[:, None]).astype(f32)
    d_slots = jnp.sum(at_slot[:, :, None, None] * d_mod[None], 1).astype(bf16).astype(f32)
    cond_rows = cd // count
    silu_mine = lax.dynamic_slice_in_dim(jax.nn.silu(conds).astype(bf16).astype(f32), me * cond_rows, cond_rows, 1)
    grad_ada = jnp.sum(silu_mine[:, :, None, None] * d_slots[:, None], 0)
    d_mine = lax.dynamic_index_in_dim(d_slots, me, 0, False)
    cond_part = jnp.sum(d_mine[None] * w_ada.astype(f32), (1, 2))
    cond_part = cond_part.reshape(-1, 128)
    cond_total = tree([cond_part] + [swap(cond_part, "narrow", deep, m) for m in range(1, deep)]).reshape(-1)
    pull_silu = jax.vjp(jax.nn.silu, cond)[1]
    grad_conditioning = pull_silu(cond_total)[0].reshape(1, -1)

    rows = d // count
    return (
        output,
        grad_patches,
        grad_conditioning,
        grad_captions,
        grad_ada,
        grad_norm_gains,
        g_attn[:, : 3 * n].astype(f32).reshape(rows, 3, n).transpose(1, 0, 2),
        grad_head_gains,
        grad_cross_gate,
        g_cap.astype(f32).reshape(-1, 2, n).transpose(1, 0, 2),
        g_attn[:, 3 * n :].astype(f32).T,
        g_mlp[:, : 2 * ff].astype(f32).reshape(rows, 2, ff).transpose(1, 0, 2),
        g_mlp[:, 2 * ff :].astype(f32).T,
    )


def solution(mesh):
    placed = (
        P("wide", None),
        P("wide", None),
        P("wide", None),
        P("wide", None),
        P(),
        P(),
        P(None, None, "narrow"),
        P(),
        P(None, None, "narrow"),
        P(),
        P("narrow"),
        P(None, None, "narrow"),
        P("narrow", None),
        P(None, None, "narrow"),
        P("narrow", None),
    )
    return jax.shard_map(
        local,
        mesh=mesh,
        in_specs=placed,
        out_specs=(
            P("wide", None),
            P("wide", None),
            P("wide", None),
            P("wide", None),
            P("wide", None, "narrow"),
            P(None, "wide"),
            P(None, "wide", "narrow"),
            P(),
            P(),
            P(None, "wide", "narrow"),
            P("narrow", "wide"),
            P(None, "wide", "narrow"),
            P("narrow", "wide"),
        ),
        check_vma=False,
    )
```

```python
import functools

import jax
import jax.numpy as jnp
from jax import lax
from jax.experimental import pallas as pl
from jax.experimental.pallas import tpu as pltpu
from jax.sharding import PartitionSpec as P

HD = 64
SPAN = 4
EPS = 1e-05
LOG2E = 1.4426950408889634
f32 = jnp.float32
bf16 = jnp.bfloat16
VMEM = 56 * 1024 * 1024
BR = 256
NT = (((1,), (1,)), ((), ()))
TN = (((0,), (0,)), ((), ()))


def params(n):
    return pltpu.CompilerParams(
        dimension_semantics=("arbitrary",) * n, vmem_limit_bytes=VMEM
    )


def sds(shape, dtype):
    return jax.ShapeDtypeStruct(shape, dtype)


COST = {
    "key": 8, "query": 9, "caption_norm": 2, "pick": 5, "attend": 15, "hop": 3, "ffn": 9, "ffn_back": 10, "out_back": 6,
    "pair_grad": 10, "caption_back": 6, "dq": 27, "dkv": 24, "dqkv": 7, "caption_grad": 3, "last": 3, "note": 1, "pin": 1,
}


class Order:
    def __init__(self):
        self.token = ()

    def run(self, name, kernel, grid, ins, in_specs, out_specs, out_shape, scratch=(), scalar=None, held=(), first_held=0, after=()):
        pre = 0 if scalar is None else 1
        given = pre + len(ins)
        extra = [*self.token, *after, *held]

        def body(*refs):
            kernel(*refs[:given], *refs[given + len(extra) :])

        at = given + len(extra) - len(held)
        out = pl.pallas_call(
            body,
            grid_spec=pltpu.PrefetchScalarGridSpec(
                num_scalar_prefetch=pre,
                grid=grid,
                in_specs=list(in_specs) + loose(len(extra)),
                out_specs=out_specs,
                scratch_shapes=list(scratch),
            ),
            out_shape=out_shape,
            input_output_aliases={at + k: first_held + k for k in range(len(held))},
            compiler_params=params(len(grid)),
            cost_estimate=pl.CostEstimate(
                flops=COST[name] * 250_000_000, bytes_accessed=COST[name] * 750_000, transcendentals=0
            ),
            name=name,
        )(*(() if scalar is None else (scalar,)), *ins, *extra)
        self.token = (out[0],)
        return out


def loose(n):
    return [pl.BlockSpec(memory_space=pl.ANY)] * n


def mm(a, b):
    return jnp.dot(a, b, preferred_element_type=f32)


def mm_nt(a, b):
    return lax.dot_general(a, b, NT, preferred_element_type=f32)


def mm_tn(a, b):
    return lax.dot_general(a, b, TN, preferred_element_type=f32)


def split(x):
    hi = x.astype(bf16)
    return hi, (x - hi.astype(f32)).astype(bf16)


def head_sum(x, ones):
    hi, lo = split(x)
    return mm(hi, ones) + mm(lo, ones)


def head_ones(n):
    a = lax.broadcasted_iota(jnp.int32, (n, n), 0) // HD
    b = lax.broadcasted_iota(jnp.int32, (n, n), 1) // HD
    return (a == b).astype(bf16)


def halves(n):
    lane = lax.broadcasted_iota(jnp.int32, (1, n), 1)
    return (lane < HD, lane >= HD)


def keep(x, mask):
    return jnp.where(mask, x, jnp.zeros_like(x))


def inv_rms(x):
    return lax.rsqrt(jnp.mean(x * x, -1, keepdims=True) + EPS)


def row(ref, k):
    return ref[k : k + 1, :]


def whole(shape):
    zeros = (0,) * len(shape)
    return pl.BlockSpec(shape, lambda *_: zeros, pipeline_mode=pl.Buffered(1))


def rows_of(br, width, first=0):
    return pl.BlockSpec((br, width), lambda i, *_: (i, first))


def accumulate(ref, value, first):
    @pl.when(first)
    def _():
        ref[...] = value

    @pl.when(jnp.logical_not(first))
    def _():
        ref[...] += value


def col_sum(x):
    return jnp.sum(x, 0, keepdims=True)


def tile3(t, n):
    return jnp.concatenate([t] * (n // t.shape[1]), 1)


def key_kernel(p_ref, v_ref, w_ref, wv_ref, wq_ref, c_ref, s1_ref, s2_ref, hg_ref, a_ref, kr_ref, k_ref, vv_ref, qr_ref, q_ref):
    x = p_ref[...].astype(f32)
    a = (x * inv_rms(x) * row(v_ref, 0)).astype(bf16)
    a_ref[...] = a
    k = mm(a, w_ref[0])
    kr_ref[...] = k
    k_ref[...] = turned(k, row(hg_ref, 1), (c_ref, s1_ref, s2_ref)).astype(bf16)
    vv_ref[...] = mm(a, wv_ref[0]).astype(bf16)
    q = mm(a, wq_ref[0])
    qr_ref[...] = q
    q_ref[...] = (turned(q, row(hg_ref, 0), (c_ref, s1_ref, s2_ref)) * (0.125 * LOG2E)).astype(bf16)


def turned(y, gain, tabs):
    n = y.shape[1]
    cos, s1, s2 = (tile3(t[...], n) for t in tabs)
    z = y * lax.rsqrt(head_sum(y * y, head_ones(n)) * (1.0 / HD) + EPS) * gain
    return z * cos + pltpu.roll(z, n - 16, 1) * s1 + pltpu.roll(z, 16, 1) * s2


def one_weight(w, k):
    return pl.BlockSpec((1, *w.shape[1:]), lambda *_: (k, 0, 0), pipeline_mode=pl.Buffered(1))


def key_call(order, patches, vec, w, tabs, hg, after, br=256):
    t, d = patches.shape
    n = w.shape[2]
    return order.run(
        "key",
        key_kernel,
        (t // br,),
        (patches, vec, w, w, w, *tabs, hg),
        [rows_of(br, d), whole(vec.shape), one_weight(w, 1), one_weight(w, 2), one_weight(w, 0)] + [rows_of(br, 128)] * 3 + [whole(hg.shape)],
        [rows_of(br, d)] + [rows_of(br, n)] * 5,
        [sds((t, d), bf16), sds((t, n), f32), sds((t, n), bf16), sds((t, n), bf16), sds((t, n), f32), sds((t, n), bf16)],
        after=after,
    )


def soft_sums(q, k, v, mask):
    e = jnp.exp2(mm_nt(q, keep(k, mask))).astype(bf16)
    return mm(e, jnp.where(mask, v, jnp.ones_like(v)))


def item_block(j, s):
    return jnp.minimum(j, s[0] - 1)


def attend_kernel(sc, q_ref, k_ref, v_ref, ck_ref, cv_ref, tg_ref, mix_ref, o_ref, li_ref, acc):
    j = pl.program_id(1)
    masks = halves(128)
    keys = k_ref.shape[0] if q_ref.shape[0] <= BR else 512

    def block_sums(h):
        q = q_ref[...]
        total = 0.0
        for c in range(k_ref.shape[0] // keys):
            at = slice(c * keys, (c + 1) * keys)
            total = total + soft_sums(q, k_ref[at, :], v_ref[at, :], masks[h])
        return total

    @pl.when(j == 0)
    def _():
        for h in range(2):
            acc[2 + h] = soft_sums(q_ref[...], ck_ref[...], cv_ref[...], masks[h])
            acc[h] = block_sums(h)

    @pl.when((j > 0) & (j < sc[0]))
    def _():
        for h in range(2):
            acc[h] += block_sums(h)

    @pl.when(j == SPAN - 1)
    def _():
        def finish(a0, a1):
            inverse = 1.0 / jnp.where(masks[0], pltpu.roll(a0, HD, 1), pltpu.roll(a1, HD, 1))
            return jnp.where(masks[0], a0, a1) * inverse, inverse

        o, li = finish(acc[0], acc[1])
        mix_ref[...] = (o + tg_ref[...] * finish(acc[2], acc[3])[0]).astype(bf16)
        o_ref[...] = o.astype(bf16)
        li_ref[...] = li


def attend_call(order, sc, q, k, v, cap, text, tg, at, bq):
    n = q.shape[1]
    pairs = n // 128
    block = k.shape[0] // SPAN
    mine = lambda p, j, s: (0, p)
    other = lambda p, j, s: (item_block(j, s), p)
    return order.run(
        "attend",
        attend_kernel,
        (pairs, SPAN),
        (q, k, v, cap, cap, tg),
        [
            pl.BlockSpec((bq, 128), lambda p, j, s: (at, p)),
            pl.BlockSpec((block, 128), other),
            pl.BlockSpec((block, 128), other),
            pl.BlockSpec((text, 128), lambda p, j, s: (s[1 + SPAN], p)),
            pl.BlockSpec((text, 128), lambda p, j, s: (s[1 + SPAN], pairs + p)),
            pl.BlockSpec((1, 128), mine),
        ],
        [pl.BlockSpec((bq, 128), mine)] * 3,
        [sds((bq, n), bf16), sds((bq, n), bf16), sds((bq, n), f32)],
        [pltpu.VMEM((4, bq, 128), f32)],
        sc,
    )


def caption_back_kernel(sc, q_ref, da_ref, db_ref, ck_ref, cv_ref, tg_ref, dq_ref, dk_ref, dv_ref, gs_ref):
    masks = halves(128)
    q, d = q_ref[...], jnp.concatenate([da_ref[...], db_ref[...]], 0)
    dq = jnp.zeros(q.shape, f32)
    dk = jnp.zeros(ck_ref.shape, f32)
    dv = jnp.zeros(ck_ref.shape, f32)
    sums = []
    for h in range(2):
        ck, cv = keep(ck_ref[...], masks[h]), keep(cv_ref[...], masks[h])
        gate = tg_ref[:, h * HD : h * HD + 1]
        e = jnp.exp2(mm_nt(q, ck))
        prob = e * (1.0 / jnp.sum(e, -1, keepdims=True))
        dp = mm_nt(d, cv)
        m = jnp.sum(prob * dp, -1, keepdims=True)
        dc = (prob * (dp - m) * gate).astype(bf16)
        dq = dq + mm(dc, ck)
        dk = dk + mm_tn(dc, keep(q, masks[h]))
        dv = dv + mm_tn(prob.astype(bf16), keep(d, masks[h]))
        sums.append(jnp.sum(m, 0, keepdims=True))
    dq_ref[...] = dq * 0.125
    dk_ref[...] = dk * (1.0 / LOG2E)
    dv_ref[...] = dv * tg_ref[...]
    gs_ref[...] = jnp.where(masks[0], sums[0], sums[1])


def caption_back_call(order, sc, q, da, db, cap, text, tg, h):
    n = q.shape[1]
    pairs = n // 128
    bq = 2 * BR
    mine = lambda p, s: (0, p)
    return order.run(
        "caption_back",
        caption_back_kernel,
        (pairs,),
        (q, da, db, cap, cap, tg),
        [
            pl.BlockSpec((bq, 128), lambda p, s: (h, p)),
            pl.BlockSpec((BR, 128), mine),
            pl.BlockSpec((BR, 128), mine),
            pl.BlockSpec((text, 128), lambda p, s: (s[1 + SPAN], p)),
            pl.BlockSpec((text, 128), lambda p, s: (s[1 + SPAN], pairs + p)),
            pl.BlockSpec((1, 128), mine),
        ],
        [
            pl.BlockSpec((bq, 128), mine),
            pl.BlockSpec((text, 128), mine),
            pl.BlockSpec((text, 128), mine),
            pl.BlockSpec((1, 128), mine),
        ],
        [sds((bq, n), f32), sds((text, n), f32), sds((text, n), f32), sds((1, n), f32)],
        scalar=sc,
    )


def minus_delta(rows, head):
    lane = lax.broadcasted_iota(jnp.int32, (rows, 128), 1)
    return jnp.where((lane >= 3 * head) & (lane < 3 * head + 3), -1.0, 0.0).astype(bf16)


def dq_kernel(sc, q_ref, d_ref, x_ref, k_ref, v_ref, c_ref, dq_ref, acc):
    pair = pl.program_id(0)
    j = pl.program_id(1)
    masks = halves(128)
    keys = 512

    @pl.when(j == 0)
    def _():
        acc[...] = jnp.zeros_like(acc)

    @pl.when(j < sc[0])
    def _():
        q = q_ref[...]
        dx = jnp.concatenate([d_ref[...], x_ref[...]], 1)
        total = acc[...]
        for h in range(2):
            off = minus_delta(keys, 2 * pair + h)
            for c in range(k_ref.shape[0] // keys):
                at = slice(c * keys, (c + 1) * keys)
                k = keep(k_ref[at, :], masks[h])
                e = jnp.exp2(mm_nt(q, k))
                dp = mm_nt(dx, jnp.concatenate([keep(v_ref[at, :], masks[h]), off], 1))
                total = total + mm((e * dp).astype(bf16), k)
        acc[...] = total

    @pl.when(j == SPAN - 1)
    def _():
        dq_ref[...] = acc[...] * 0.125 + c_ref[...]


def dq_call(order, sc, q, d, k, v, cap_dq, h, after=()):
    n = q.shape[1]
    pairs = n // 128
    block = k.shape[0] // SPAN
    bq = 2 * BR
    mine = lambda p, j, s: (0, p)
    extra = lambda p, j, s: (0, pairs)
    other = lambda p, j, s: (item_block(j, s), p)
    return order.run(
        "dq",
        dq_kernel,
        (pairs, SPAN),
        (q, d, d, k, v, cap_dq),
        [
            pl.BlockSpec((bq, 128), lambda p, j, s: (h, p)),
            pl.BlockSpec((bq, 128), mine),
            pl.BlockSpec((bq, 128), extra),
            pl.BlockSpec((block, 128), other),
            pl.BlockSpec((block, 128), other),
            pl.BlockSpec((bq, 128), mine),
        ],
        [pl.BlockSpec((bq, 128), mine)],
        [sds((bq, n), f32)],
        [pltpu.VMEM((bq, 128), f32)],
        sc,
        after=after,
    )[0]


def dkv_kernel(parts, base, sc, k_ref, v_ref, q_ref, *rest):
    d_refs, x_refs = rest[0 : 2 * parts : 2], rest[1 : 2 * parts : 2]
    dk_ref, dv_ref = rest[2 * parts :]
    pair = base + pl.program_id(0)
    j = pl.program_id(1)
    masks = halves(128)
    queries = 2 * BR

    @pl.when(j == 0)
    def _():
        dk_ref[...] = jnp.zeros_like(dk_ref)
        dv_ref[...] = jnp.zeros_like(dv_ref)

    @pl.when(j < sc[0])
    def _():
        dk, dv = dk_ref[...], dv_ref[...]
        for h in range(2):
            vx = jnp.concatenate([keep(v_ref[...], masks[h]), minus_delta(v_ref.shape[0], 2 * pair + h)], 1)
            for r in range(parts):
                q = keep(q_ref[r * queries : (r + 1) * queries, :], masks[h])
                d, x = d_refs[r][...], x_refs[r][...]
                e = jnp.exp2(mm_nt(k_ref[...], q))
                dp = mm_nt(vx, jnp.concatenate([d, x], 1))
                dv = dv + mm(e.astype(bf16), keep(d, masks[h]))
                dk = dk + mm((e * dp).astype(bf16), q)
        dk_ref[...] = dk
        dv_ref[...] = dv


def dkv_call(order, sc, k, v, q_all, ds, half, base, n_pairs):
    t, n = k.shape
    pairs = n // 128
    rows = 2 * BR
    mine = pl.BlockSpec((rows, 128), lambda p, j, s: (half, base + p))
    out = pl.BlockSpec((rows, 128), lambda p, j, s: (0, p))
    other = pl.BlockSpec((rows, 128), lambda p, j, s: (item_block(j, s), base + p))
    extra = pl.BlockSpec((rows, 128), lambda p, j, s: (item_block(j, s), pairs))
    return order.run(
        "dkv",
        functools.partial(dkv_kernel, len(ds), base),
        (n_pairs, SPAN),
        (k, v, q_all, *(x for d in ds for x in (d, d))),
        [mine, mine, pl.BlockSpec((t, 128), lambda p, j, s: (s[1 + SPAN + j], base + p))] + [other, extra] * len(ds),
        [out, out],
        [sds((rows, n_pairs * 128), f32)] * 2,
        scalar=sc,
    )


def chunk_call(order, kernel, name, c, ins, specs, chunk_outs, sum_outs, whole_outs, before):
    one = lambda r, w: pl.BlockSpec((r, w), lambda i: (0, 0))
    own = chunk_outs + sum_outs
    into = [pl.BlockSpec((BR, w), lambda i, at=c % (r // BR): (at, 0)) for r, w, _ in whole_outs]
    return order.run(
        name,
        kernel,
        (1,),
        ins,
        specs,
        [one(r, w) for r, w, _ in own] + into,
        [sds((r, w), k) for r, w, k in own + whole_outs],
        held=tuple(before),
        first_held=len(own),
    )


def part(c, width):
    return pl.BlockSpec((BR, width), lambda i: (c, 0))


def alone(width):
    return pl.BlockSpec((BR, width), lambda i: (0, 0))


def pair_grad_kernel(a_ref, b_ref, c_ref, d_ref, o_ref):
    n = b_ref.shape[1]
    o_ref[:, :n] = mm_tn(a_ref[...], b_ref[...]).astype(bf16)
    o_ref[:, n:] = mm_tn(c_ref[...], d_ref[...]).astype(bf16)


def pair_grad_call(order, a, b, c, d, part=0, parts=1, before=(), after=()):
    t, m = a.shape
    n, k = b.shape[1], d.shape[1]
    blk = 256
    steps = m // blk // parts
    cols = pl.BlockSpec((t, blk), lambda i: (0, part * steps + i))
    return order.run(
        "pair_grad",
        pair_grad_kernel,
        (steps,),
        (a, b, c, d),
        [cols, whole(b.shape), cols, whole(d.shape)],
        [pl.BlockSpec((blk, n + k), lambda i: (part * steps + i, 0))],
        [sds((m, n + k), bf16)],
        held=before,
        after=after,
    )


def ffn_kernel(p_ref, at_ref, v_ref, wg_ref, wd_ref, mid_ref, gu_ref, f_ref, a_ref, h_ref):
    at = at_ref[...].astype(f32)
    mid = p_ref[...].astype(f32) + row(v_ref, 1) * (at * inv_rms(at))
    mid_ref[...] = mid
    a = (mid * inv_rms(mid) * row(v_ref, 2)).astype(bf16)
    a_ref[...] = a
    g = mm(a, wg_ref[0])
    u = mm(a, wg_ref[1])
    n = g.shape[1]
    gu_ref[:, :n] = g.astype(bf16)
    gu_ref[:, n:] = u.astype(bf16)
    h = (g * jax.nn.sigmoid(g) * u).astype(bf16)
    h_ref[...] = h
    f_ref[...] = mm(h, wd_ref[...]).astype(bf16)


def ffn_call(order, c, patches, at, vec, wg, wd, before):
    t, d = patches.shape
    n = wd.shape[0]
    return chunk_call(
        order,
        ffn_kernel,
        "ffn",
        c,
        (patches, at, vec, wg, wd),
        [part(c, d), alone(d), whole(vec.shape), whole(wg.shape), whole(wd.shape)],
        [(BR, d, f32), (BR, 2 * n, bf16), (BR, d, bf16)],
        [],
        [(t, d, bf16), (t, n, bf16)],
        before,
    )


def ffn_back_kernel(f_ref, mid_ref, c_ref, gu_ref, v_ref, wg_ref, wd_ref, da_ref, cs_ref, y_ref, df_ref, dgu_ref):
    f = f_ref[...].astype(f32)
    cot = c_ref[...].astype(f32)
    r = inv_rms(f)
    fh = f * r
    y_ref[...] = (mid_ref[...] + row(v_ref, 3) * fh).astype(bf16)
    z = cot * row(v_ref, 3)
    df = (r * (z - fh * jnp.mean(z * fh, -1, keepdims=True))).astype(bf16)
    df_ref[...] = df
    cs_ref[...] = col_sum(cot * fh)
    dh = mm_nt(df, wd_ref[...])
    n = dh.shape[1]
    g = gu_ref[:, :n].astype(f32)
    u = gu_ref[:, n:].astype(f32)
    s = jax.nn.sigmoid(g)
    gs = g * s
    dg = (dh * u * (s + gs * (1.0 - s))).astype(bf16)
    du = (dh * gs).astype(bf16)
    dgu_ref[:, :n] = dg
    dgu_ref[:, n:] = du
    da_ref[...] = (mm_nt(dg, wg_ref[0]) + mm_nt(du, wg_ref[1])).astype(bf16)


def ffn_back_call(order, c, f, mid, cot, gu, vec, wg, wd, before):
    t, d = cot.shape
    n = wd.shape[0]
    return chunk_call(
        order,
        ffn_back_kernel,
        "ffn_back",
        c,
        (f, mid, cot, gu, vec, wg, wd),
        [alone(d), alone(d), part(c, d), alone(2 * n), whole(vec.shape), whole(wg.shape), whole(wd.shape)],
        [(BR, d, bf16)],
        [(1, d, f32)],
        [(t, d, bf16), (t, d, bf16), (t, 2 * n, bf16)],
        before,
    )


def out_back_kernel(da_ref, mid_ref, at_ref, c_ref, v_ref, w_ref, o_ref, li_ref, dm_ref, dx_ref, c3_ref, c2_ref, dat_ref, ds_ref):
    da = da_ref[...].astype(f32)
    mid = mid_ref[...]
    r = inv_rms(mid)
    mh = mid * r
    z = da * row(v_ref, 2)
    dm = c_ref[...].astype(f32) + r * (z - mh * jnp.mean(z * mh, -1, keepdims=True))
    dm_ref[...] = dm
    c3_ref[...] = col_sum(da * mh)
    at = at_ref[...].astype(f32)
    ra = inv_rms(at)
    ah = at * ra
    c2_ref[...] = col_sum(dm * ah)
    z = dm * row(v_ref, 1)
    dat = (ra * (z - ah * jnp.mean(z * ah, -1, keepdims=True))).astype(bf16)
    dat_ref[...] = dat
    dx = mm_nt(dat, w_ref[...]).astype(bf16)
    dx_ref[...] = dx
    n = dx.shape[1]
    ds = dx.astype(f32) * li_ref[...]
    ds_ref[:, :n] = ds.astype(bf16)
    hi, lo = split(ds * o_ref[...].astype(f32))
    head = lax.broadcasted_iota(jnp.int32, (n, 128), 0) // HD
    lane = lax.broadcasted_iota(jnp.int32, (n, 128), 1)
    to_lanes = (lane // 3 == head).astype(bf16)
    delta = mm(hi, to_lanes) + mm(lo, to_lanes)
    one = delta.astype(bf16).astype(f32)
    two = (delta - one).astype(bf16).astype(f32)
    which = lax.broadcasted_iota(jnp.int32, (1, 128), 1) % 3
    ds_ref[:, n:] = jnp.where(which == 0, one, jnp.where(which == 1, two, delta - one - two)).astype(bf16)


def out_back_call(order, c, da, mid, at, cot, vec, w, o, li, place, before):
    t, d = cot.shape
    n = w.shape[0]
    return chunk_call(
        order,
        out_back_kernel,
        "out_back",
        c,
        (da, mid, at, cot, vec, w, o, li),
        [alone(d), alone(d), alone(d), part(c, d), whole(vec.shape), whole(w.shape), part(place, n), part(place, n)],
        [(BR, d, f32), (BR, n, bf16)],
        [(1, d, f32), (1, d, f32)],
        [(t, d, bf16), (2 * BR, n + 128, bf16)],
        before,
    )


def dqkv_kernel(pairs, dq_ref, *refs):
    dk_refs, dv_refs = refs[0 : 2 * pairs : 2], refs[1 : 2 * pairs : 2]
    (qr_ref, kr_ref, c_ref, s1_ref, s2_ref, hg_ref, w_ref, p_ref, da_ref, hs_ref, cs_ref, d_ref) = refs[2 * pairs :]
    side = lambda parts: jnp.concatenate([x[...] for x in parts], 1)
    n = dq_ref.shape[1]
    ones = head_ones(n)
    cos, s1, s2 = (tile3(t[...], n) for t in (c_ref, s1_ref, s2_ref))

    def back(dy, x, gain):
        dz = dy * cos - pltpu.roll(dy, 16, 1) * s2 - pltpu.roll(dy, n - 16, 1) * s1
        r = lax.rsqrt(head_sum(x * x, ones) * (1.0 / HD) + EPS)
        xh = x * r
        g = dz * gain
        return r * (g - xh * (head_sum(g * xh, ones) * (1.0 / HD))), col_sum(dz * xh)

    dq, hq = back(dq_ref[...], qr_ref[...], row(hg_ref, 0))
    dk, hk = back(side(dk_refs) * (1.0 / LOG2E), kr_ref[...], row(hg_ref, 1))
    dql, dkl, dvl = dq.astype(bf16), dk.astype(bf16), side(dv_refs).astype(bf16)
    d_ref[:, :n] = dql
    d_ref[:, n : 2 * n] = dkl
    d_ref[:, 2 * n :] = dvl
    da = mm_nt(dql, w_ref[0]) + mm_nt(dkl, w_ref[1]) + mm_nt(dvl, w_ref[2])
    da_ref[...] = da.astype(bf16)
    x = p_ref[...].astype(f32)
    cs_ref[...] = col_sum(da * (x * inv_rms(x)))
    hs_ref[0:1, :] = hq
    hs_ref[1:2, :] = hk


def dqkv_call(order, c, dq, dkv, qr, kr, tabs, hg, w, patches, before):
    t, d = patches.shape
    n = dq.shape[1]
    return chunk_call(
        order,
        functools.partial(dqkv_kernel, len(dkv)),
        "dqkv",
        c,
        (dq, *(x for two in dkv for x in two), qr, kr, *tabs, hg, w, patches),
        [part(c % 2, n)] + [part(c % 2, x.shape[1]) for two in dkv for x in two] + [part(c, n)] * 2 + [part(c, 128)] * 3 + [whole(hg.shape), whole(w.shape), part(c, d)],
        [(BR, d, bf16)],
        [(2, n, f32), (1, d, f32)],
        [(t, 3 * n, bf16)],
        before,
    )


def last_kernel(da_ref, p_ref, dm_ref, v_ref, o_ref):
    x = p_ref[...].astype(f32)
    r = inv_rms(x)
    xh = x * r
    z = da_ref[...].astype(f32) * row(v_ref, 0)
    o_ref[...] = (dm_ref[...] + r * (z - xh * jnp.mean(z * xh, -1, keepdims=True))).astype(bf16)


def last_call(order, c, da, patches, dm, vec, before):
    t, d = patches.shape
    return chunk_call(
        order,
        last_kernel,
        "last",
        c,
        (da, patches, dm, vec),
        [alone(d), part(c, d), alone(d), whole(vec.shape)],
        [],
        [],
        [(t, d, bf16)],
        before,
    )


def caption_grad_kernel(dk_ref, dv_ref, kr_ref, hg_ref, d_ref, hs_ref):
    n = dk_ref.shape[1]
    ones = head_ones(n)
    x = kr_ref[...]
    r = lax.rsqrt(head_sum(x * x, ones) * (1.0 / HD) + EPS)
    xh = x * r
    dy = dk_ref[...]
    g = dy * row(hg_ref, 2)
    d_ref[:, :n] = (r * (g - xh * (head_sum(g * xh, ones) * (1.0 / HD)))).astype(bf16)
    d_ref[:, n:] = dv_ref[...].astype(bf16)
    hs_ref[...] = col_sum(dy * xh)


def caption_norm_kernel(kr_ref, v_ref, hg_ref, o_ref):
    n = kr_ref.shape[1]
    x = kr_ref[...]
    r = lax.rsqrt(head_sum(x * x, head_ones(n)) * (1.0 / HD) + EPS)
    o_ref[:, :n] = (x * r * row(hg_ref, 2)).astype(bf16)
    o_ref[:, n:] = v_ref[...].astype(bf16)


def swap(x, axis, size, m):
    return lax.ppermute(x, axis, [(i, i ^ m) for i in range(size)])


def pick_kernel(count, n_pieces, sc, *refs):
    total = sum(n_pieces)
    outs, sem = refs[total : total + len(n_pieces)], refs[-1]
    begin = 0
    for k, out in enumerate(outs):
        pieces = refs[begin : begin + n_pieces[k]]
        begin += n_pieces[k]
        rows = pieces[0].shape[0]
        for j in range(count):
            for m, piece in enumerate(pieces):

                @pl.when(sc[1 + j if k == 0 else 1 + 2 * SPAN + j] == m)
                def _():
                    pltpu.make_async_copy(piece, out.at[pl.ds(j * rows, rows)], sem.at[k, j]).start()

    begin = 0
    for k, out in enumerate(outs):
        first = refs[begin]
        begin += n_pieces[k]
        rows = first.shape[0]
        for j in range(count):
            pltpu.make_async_copy(first, out.at[pl.ds(j * rows, rows)], sem.at[k, j]).wait()


class Gather:
    def __init__(self, a, b):
        self.all = None
        if lax.axis_size("wide") != 8:
            self.first = self.second = ()
            self.all = [lax.all_gather(x, "wide") for x in (a, b)]
            return
        send = lambda x, pairs: lax.ppermute(x, "wide", pairs)
        over_x = [(i, i ^ 2) for i in range(8)]
        over_y = [(1, 5), (4, 0), (3, 7), (6, 2)]
        a2, a4, b4, b2 = send(a, over_x), send(a, over_y), send(b, over_y), send(b, over_x)
        a6 = send(a2, [(0, 4), (1, 5), (6, 2), (7, 3)])
        b6x, b6y = send(b2, [(0, 4), (7, 3)]), send(b4, [(7, 5), (0, 2)])
        self.first = (a2, a4, b4, b2)
        self.second = (a6, b6x, b6y)
        self.kept = ((a, a2, a4, a6), (b, b2, b4, b6x, b6y))

    def pieces(self):
        if self.all is not None:
            return self.all
        return [[y for x in four for y in (x, swap(x, "wide", 8, 1))] for four in self.kept]


class GatherOne:
    def __init__(self, a):
        self.all = None
        if lax.axis_size("wide") != 8:
            self.first = self.second = ()
            self.all = [lax.all_gather(a, "wide")]
            return
        send = lambda x, pairs: lax.ppermute(x, "wide", pairs)
        a2 = send(a, [(i, i ^ 2) for i in range(8)])
        a4 = send(a, [(1, 5), (4, 0), (3, 7), (6, 2)])
        a6 = send(a2, [(0, 4), (1, 5), (6, 2), (7, 3)])
        self.first, self.second = (a2, a4), (a6,)
        self.kept = ((a, a2, a4, a6),)

    pieces = Gather.pieces


def pick(order, sc, pieces, count):
    if not isinstance(pieces[0], list):
        one = lambda x, j: lax.dynamic_index_in_dim(x, sc[1 + SPAN + j], 0, False)
        return [jnp.concatenate([one(x, j) for j in range(count)]) for x in pieces]
    outs = [(count * p[0].shape[0], p[0].shape[1]) for p in pieces]
    return order.run(
        "pick",
        functools.partial(pick_kernel, count, [len(p) for p in pieces]),
        (1,),
        [x for p in pieces for x in p],
        loose(sum(len(p) for p in pieces)),
        [pl.BlockSpec(shape, lambda i, s: (0, 0)) for shape in outs],
        [sds(shape, bf16) for shape in outs],
        [pltpu.SemaphoreType.DMA((len(pieces), count))],
        sc,
    )


def tree(parts):
    while len(parts) > 1:
        parts = [a + b for a, b in zip(parts[::2], parts[1::2])]
    return parts[0]


def pack_kernel(count, place, *refs):
    c1, hs = refs[:count], refs[count : 2 * count]
    hc_ref, gs_ref, tg_ref, c2_ref, c3_ref, c4_ref, o_ref = refs[2 * count :]
    n = hc_ref.shape[1]
    o_ref[...] = jnp.zeros_like(o_ref)
    o_ref[0:1, :] = sum(x[...] for x in c1)
    o_ref[1:2, :] = c2_ref[...]
    o_ref[2:3, :] = c3_ref[...]
    o_ref[3:4, :] = c4_ref[...]
    qk = sum(x[...] for x in hs)
    o_ref[4:5, :n] = qk[0:1]
    o_ref[4:5, n : 2 * n] = qk[1:2]
    o_ref[4:5, 2 * n : 3 * n] = hc_ref[...]
    gate = gs_ref[...] * (1.0 - tg_ref[...] * tg_ref[...])
    for z in range(o_ref.shape[1] // n):
        o_ref[5:6, z * n : (z + 1) * n] = jnp.where(place[0] == z, gate, 0.0)


def pack_call(order, c1, hs, hc, gs, tg, c2, c3, c4, place):
    d = c2.shape[1]
    ins = (*c1, *hs, hc, gs, tg, c2, c3, c4)
    spec = lambda x: pl.BlockSpec(x.shape, lambda i, s: (0, 0))

    def kernel(place, *refs):
        pack_kernel(len(c1), place, *refs)

    return order.run(
        "note",
        kernel,
        (1,),
        ins,
        [spec(x) for x in ins],
        [pl.BlockSpec((8, d), lambda i, s: (0, 0))],
        [sds((8, d), f32)],
        scalar=place.astype(jnp.int32).reshape(1),
    )[0]


def fold_kernel(*refs):
    parts, o_ref = refs[:-1], refs[-1]
    total = tree([x[...] for x in parts])
    row_at = lax.broadcasted_iota(jnp.int32, total.shape, 0)
    o_ref[...] = jnp.where((row_at >= 1) & (row_at < 4), parts[0][...], total)


def fold_call(order, parts):
    spec = pl.BlockSpec(parts[0].shape, lambda i: (0, 0))
    return order.run("note", fold_kernel, (1,), parts, [spec] * len(parts), [spec], [sds(parts[0].shape, f32)])


def pin_kernel(o_ref):
    pass


def pin(order, x, after=()):
    return order.run("pin", pin_kernel, (1,), (), [], loose(1), [sds(x.shape, x.dtype)], held=(x,), after=after)[0]


def gather_now(x, axis):
    n = x.shape[0]
    wide = -(-n // 1024) * 1024
    padded = jnp.pad(x, (0, wide - n)).reshape(1, 8, wide // 8)
    return lax.all_gather(padded, axis, axis=0, tiled=True).reshape(-1, wide)[:, :n]


def hop_kernel(have, sc, *refs):
    ins = dict(zip(have["in"], refs))
    outs = dict(zip(have["out"], refs[len(have["in"]) :]))
    end = sc[0] == 1
    if "total" in outs:
        outs["total"][...] = jnp.where(end, ins["r1"][...], ins["send"][...])
    third = None
    if "second" in ins:
        third = ins["second"][...] + ins["r2"][...]
    if "second" in outs:
        outs["second"][...] = ins["x"][...] + ins["r1"][...]
    if "send" in outs:
        new = ins["new"][...] if "new" in ins else third
        outs["send"][...] = new if third is None else jnp.where(end, new, third)


class Line:
    def __init__(self, order, place):
        self.order = order
        self.end = ((place == 0) | (place == 3)).astype(jnp.int32).reshape(1)
        self.x = self.second = self.send = None
        self.third = False

    def step(self, new, after=()):
        if self.send is None:
            self.x = self.send = new
            return None
        go = lambda x, perm: lax.ppermute(x, "narrow", perm)
        ins = {"r1": go(self.send, [(0, 1), (3, 2), (1, 0), (2, 3)])}
        outs = []
        if self.third:
            ins["send"] = self.send
            outs.append("total")
        if self.second is not None:
            ins["r2"] = go(self.second, [(1, 2), (2, 1)])
            ins["second"] = self.second
        if self.x is not None:
            ins["x"] = self.x
            outs.append("second")
        if new is not None:
            ins["new"] = new
        if new is not None or self.second is not None:
            outs.append("send")
        like = ins["r1"]
        block = pl.BlockSpec((BR // 2, like.shape[1]), lambda i, s: (i, 0))
        got = self.order.run(
            "hop",
            functools.partial(hop_kernel, {"in": list(ins), "out": outs}),
            (2,),
            list(ins.values()),
            [block] * len(ins),
            [block] * len(outs),
            [sds(like.shape, like.dtype)] * len(outs),
            scalar=self.end,
            after=after,
        )
        got = dict(zip(outs, got))
        self.third = self.second is not None
        self.x, self.second, self.send = new, got.get("second"), got.get("send")
        return got.get("total")


class Sums:
    def __init__(self, order, size, place):
        self.line = Line(order, place) if size == 4 else None
        self.names, self.done = [], {}

    def add(self, name, x, after=()):
        if self.line is None:
            self.done[name] = lax.psum(x, "narrow")
            return
        if self.line.send is None:
            self.names = [None]
        self._step(name, x, after)

    def _step(self, name, x, after):
        total = self.line.step(x, after)
        self.names.append(name)
        if total is not None:
            self.done[self.names[-4]] = total

    def get(self, name, after=()):
        while name not in self.done:
            self._step(None, None, after)
            after = ()
        return self.done[name]


def scatter_rows(x):
    return lax.psum_scatter(x.astype(bf16), "wide", scatter_dimension=0, tiled=True)


def rope_tables(position, width):
    lane = jnp.arange(128, dtype=jnp.int32)
    within = lane % HD
    quarter = HD // 4
    frequency = 10000.0 ** (-(within % quarter).astype(f32) / quarter)
    by_row = within < HD // 2
    where = jnp.where(by_row[None, :], (position // width)[:, None], (position % width)[:, None])
    angle = where.astype(f32) * frequency[None, :]
    cos, sin = jnp.cos(angle), jnp.sin(angle)
    former = (within % (HD // 2) < quarter)[None, :]
    return cos, jnp.where(former, -sin, 0.0), jnp.where(former, 0.0, sin)


def local(
    patches,
    cotangent,
    conditioning,
    captions,
    item_lengths,
    grid_widths,
    w_ada,
    norm_gains,
    w_qkv,
    head_gains,
    cross_gate,
    w_caption,
    w_out,
    w_gate_up,
    w_down,
):
    t, d = patches.shape
    n = w_qkv.shape[2]
    heads = n // HD
    ada = w_ada.shape[2]
    ff = w_down.shape[0]
    text = captions.shape[0]
    cd = conditioning.shape[1]
    count = lax.axis_size("wide")
    deep = lax.axis_size("narrow")
    me = lax.axis_index("wide")
    mz = lax.axis_index("narrow")

    slots = item_lengths.shape[0]
    spans = item_lengths // t
    order = jnp.arange(slots, dtype=jnp.int32)
    ends = jnp.sum(jnp.where(order[None, :] <= order[:, None], spans[None, :], 0), 1)
    blocks = jnp.arange(count, dtype=jnp.int32)
    item = jnp.sum((ends[None, :] <= blocks[:, None]).astype(jnp.int32), 1)
    is_item = item[:, None] == order[None, :]
    choose = lambda values: jnp.sum(jnp.where(is_item, values[None, :], 0), 1)
    firsts = choose(ends - spans)
    mine = blocks == me
    of_me = lambda values: jnp.sum(jnp.where(mine, values, 0))
    first = of_me(firsts)
    length = of_me(choose(spans))
    width = of_me(choose(grid_widths))
    position = (me - first) * t + jnp.arange(t, dtype=jnp.int32)
    tabs = rope_tables(position, width)
    steps = first + jnp.minimum(jnp.arange(SPAN, dtype=jnp.int32), length - 1)
    places = steps ^ me if count == 8 else steps
    second = jnp.where((places == 6) & ((me == 2) | (me == 5)), 8, places)
    second = jnp.where((places == 7) & ((me == 3) | (me == 4)), 9, second)
    sc = jnp.concatenate([length.reshape(1), places, steps, second]).astype(jnp.int32)

    cond = conditioning.astype(f32)[0]
    silu_low = jax.nn.silu(cond).astype(bf16)
    mod = jnp.sum(silu_low.astype(f32)[:, None, None] * w_ada.astype(f32), 0)
    share = cd // deep
    sent = jnp.concatenate([mod.reshape(-1), lax.dynamic_slice_in_dim(cond, mz * share, share)])
    got = gather_now(gather_now(sent, "narrow").reshape(-1), "wide").reshape(count, deep, -1)
    mods = got[:, :, : 4 * ada].reshape(count, deep, 4, ada).transpose(0, 2, 1, 3).reshape(count, 4, d)
    conds = got[:, :, 4 * ada :].reshape(count, cd)
    my_mod = lax.dynamic_index_in_dim(mods, first, 0, False)
    of_block = jnp.sum(jnp.where((firsts[:, None] == blocks[None, :])[:, :, None, None], mods[None], 0.0), 1)
    scales = 1.0 + of_block
    gates = jnp.tanh(of_block)
    factor = jnp.stack([1.0 + my_mod[0], jnp.tanh(my_mod[1]), 1.0 + my_mod[2], jnp.tanh(my_mod[3])])
    vec = norm_gains * factor
    hg = jnp.tile(head_gains, (1, heads))
    tg_heads = jnp.tanh(cross_gate)
    tg = jnp.repeat(tg_heads, HD)[None, :]

    order = Order()
    cap_raw = jnp.einsum("kd,jde->jke", captions, w_caption, preferred_element_type=f32)
    whole_cap = pl.BlockSpec((text, n), lambda i: (0, 0))
    both_cap = pl.BlockSpec((text, 2 * n), lambda i: (0, 0))
    (cap,) = order.run(
        "caption_norm",
        caption_norm_kernel,
        (1,),
        (cap_raw[0], cap_raw[1], hg),
        [whole_cap, whole_cap, whole(hg.shape)],
        [both_cap],
        [sds((text, 2 * n), bf16)],
    )
    cap = lax.all_gather(cap, "wide", axis=0, tiled=True)

    chunks = range(t // BR)
    pairs_of = range(t // (2 * BR))
    sums = Sums(order, deep, mz)
    a1, k_raw, k, v, q_raw, q = key_call(order, patches, vec, w_qkv, tabs, hg, ())
    kv = Gather(k, v)


    q_all = lax.all_gather(q, "wide", axis=0, tiled=True)
    k_all, v_all = pick(order, sc, kv.pieces(), SPAN)
    heads_out = {}
    for c in chunks:
        heads_out[c] = (*attend_call(order, sc, q, k_all, v_all, cap, text, tg, c, BR), 0)
        sums.add(("attn", c), mm(heads_out[c][0], w_out).astype(bf16))

    mids, gus = {}, {}
    whole_out = ()
    for c in chunks:
        mids[c], gus[c], ffn_part, *whole_out = ffn_call(
            order, c, patches, sums.get(("attn", c)), vec, w_gate_up, w_down, whole_out
        )
        sums.add(("ffn", c), ffn_part)
    a3, hidden = whole_out
    whole_out = ()
    c4 = 0.0
    for c in chunks:
        da3_part, part_sum, *whole_out = ffn_back_call(
            order, c, sums.get(("ffn", c)), mids[c], cotangent, gus[c], vec, w_gate_up, w_down, whole_out
        )
        sums.add(("da3", c), da3_part)
        c4 = c4 + part_sum
    output, d_ffn, d_gu = whole_out

    d_mids, dqs, dq_caps, d_got, d_mixed, d_scaled = {}, {}, {}, {}, {}, {}
    whole_out = ()
    mlp_part = ()
    behind = ()
    c2 = c3 = dck = dcv = gate_sum = 0.0
    for h in pairs_of:
        for c in (2 * h, 2 * h + 1):
            _, o_self, linv, place = heads_out[c]
            if c == 2 * h + 1 and h > 0:
                behind = d_got[h - 1].second
            da3 = sums.get(("da3", c), behind)
            d_mids[c], d_mixed[c], p3, p2, *outs = out_back_call(
                order, c, da3, mids[c], sums.get(("attn", c)), cotangent, vec, w_out, o_self, linv, place, whole_out
            )
            whole_out, d_scaled[h] = (outs if c % 2 == 0 else outs[:1]), outs[1]
            c2, c3 = c2 + p2, c3 + p3
            behind = ()
            if c == 2 * h:
                early = d_got[h - 1].first if h > 0 else ()
                mlp_part = pair_grad_call(order, a3, d_gu, d_ffn, hidden, h, len(pairs_of), mlp_part, early)
        d_got[h] = GatherOne(d_scaled[h])
        dq_caps[h], pk, pv, pg = caption_back_call(order, sc, q, d_mixed[2 * h], d_mixed[2 * h + 1], cap, text, tg, h)
        dck, dcv, gate_sum = dck + pk, dcv + pv, gate_sum + pg
    d_attn = whole_out[0]
    cap_sum = jnp.concatenate([dck, dcv], 1)
    cap_got = lax.all_gather(cap_sum.astype(bf16), "wide")
    kept = (firsts == me)[:, None, None]
    cap_sum = jnp.sum(jnp.where(kept, cap_got.astype(f32), 0.0), 0)
    last_half = pairs_of[-1]

    def make_dq(h, after):
        return dq_call(order, sc, q, d_scaled[h], k_all, v_all, dq_caps[h], h, after)

    for h in pairs_of:
        dqs[h] = make_dq(h, () if h == 0 else d_got[last_half].first)

    d_cap, hs_c = order.run(
        "caption_grad",
        caption_grad_kernel,
        (1,),
        (cap_sum[:, :n], cap_sum[:, n:], cap_raw[0], hg),
        [whole_cap, whole_cap, whole_cap, whole(hg.shape)],
        [both_cap, pl.BlockSpec((1, n), lambda i: (0, 0))],
        [sds((text, 2 * n), bf16), sds((1, n), f32)],
    )
    d_text = (mm_nt(d_cap[:, :n], w_caption[0]) + mm_nt(d_cap[:, n:], w_caption[1])).astype(bf16)
    cap_part = mm_tn(captions, d_cap).astype(bf16)
    pieces = -(-d_text.shape[1] // d)
    padded = jnp.pad(d_text, ((0, 0), (0, pieces * d - d_text.shape[1])))
    text_parts = [padded[:, p * d : (p + 1) * d] for p in range(pieces)]

    sums.add(("text", 0), text_parts[0])
    ds = [x for h in pairs_of for x in pick(order, sc, d_got[h].pieces(), SPAN)]
    sums.add(("text", 1), text_parts[1], (cap_part,))
    g_mlp = scatter_rows(pin(order, mlp_part[0]))
    whole_out = ()
    c1_parts, hs_parts = [], []
    mixed = jnp.concatenate([heads_out[c][0] for c in chunks])
    pairs = n // 128

    def project(c, dkv, after=()):
        nonlocal whole_out
        da1_part, p_hs, p1, *whole_out = dqkv_call(order, c, dqs[c // 2], dkv, q_raw, k_raw, tabs, hg, w_qkv, patches, whole_out)
        hs_parts.append(p_hs)
        c1_parts.append(p1)
        return da1_part

    dkv = [dkv_call(order, sc, k, v, q_all, ds, 0, 0, pairs)]
    for p in range(2, pieces):
        sums.add(("text", p), text_parts[p])
    g_cap = scatter_rows(pin(order, cap_part))
    first_part = project(0, dkv)
    parts_of = lambda p: dkv_call(order, sc, k, v, q_all, ds, 1, p, 1)
    first_dkv, dkv = dkv, [parts_of(0)]
    sums.add(("da1", 0), first_part)
    da1_part = project(1, first_dkv)
    dkv.append(parts_of(1))
    sums.add(("da1", 1), da1_part)
    dkv += [parts_of(p) for p in range(2, pairs)]
    for c in chunks[2:]:
        da1_part = project(c, dkv)
        if c == chunks[-1]:
            d_qkv = whole_out[0]
            packed = pack_call(order, c1_parts, hs_parts, hs_c, gate_sum, tg, c2, c3, c4, mz)
            from_narrow = [packed] + [swap(packed, "narrow", deep, m) for m in range(1, deep)]
            attn_part = pair_grad_call(order, a1, d_qkv, d_attn, mixed)[0]
        sums.add(("da1", c), da1_part, (g_mlp, *from_narrow) if c == chunks[-1] else ())
    g_attn = scatter_rows(pin(order, attn_part))

    (folded,) = fold_call(order, from_narrow)
    got = lax.all_gather(folded, "wide")
    whole_out = last_call(order, 0, sums.get(("da1", 0)), patches, d_mids[0], vec, ())
    for c in chunks[1:]:
        da1 = sums.get(("da1", c), (g_cap, got) if c == 1 else (g_attn,) if c == chunks[-1] else ())
        if c == 1:
            got = pin(order, got)
        whole_out = last_call(order, c, da1, patches, d_mids[c], vec, whole_out)
    (grad_patches,) = whole_out
    grad_captions = jnp.concatenate([sums.get(("text", p)) for p in range(pieces)], 1)[:, : d_text.shape[1]]

    cols = got[:, :4]
    grad_head_gains = jnp.sum(got[:, 4, : 3 * n], 0).reshape(3, heads, HD).sum(1)
    grad_cross_gate = jnp.sum(got[:, 5], 0)[::HD]
    gain_factor = jnp.stack([scales[:, 0], gates[:, 1], scales[:, 2], gates[:, 3]], 1)
    gain_grads = jnp.sum(gain_factor * cols, 0)
    wide_cols = d // count
    grad_norm_gains = lax.dynamic_slice_in_dim(gain_grads, me * wide_cols, wide_cols, 1)
    ones = jnp.ones_like(gates[:, 0])
    slope = jnp.stack([ones, 1.0 - gates[:, 1] ** 2, ones, 1.0 - gates[:, 3] ** 2], 1)
    d_mod = lax.dynamic_slice_in_dim(slope * norm_gains[None] * cols, mz * ada, ada, 2)
    at_slot = (firsts[None, :] == blocks[:, None]).astype(f32)
    d_slots = jnp.sum(at_slot[:, :, None, None] * d_mod[None], 1).astype(bf16).astype(f32)
    cond_rows = cd // count
    silu_mine = lax.dynamic_slice_in_dim(jax.nn.silu(conds).astype(bf16).astype(f32), me * cond_rows, cond_rows, 1)
    grad_ada = jnp.sum(silu_mine[:, :, None, None] * d_slots[:, None], 0)
    d_mine = lax.dynamic_index_in_dim(d_slots, me, 0, False)
    cond_part = jnp.sum(d_mine[None] * w_ada.astype(f32), (1, 2))
    cond_part = cond_part.reshape(-1, 128)
    cond_total = tree([cond_part] + [swap(cond_part, "narrow", deep, m) for m in range(1, deep)]).reshape(-1)
    pull_silu = jax.vjp(jax.nn.silu, cond)[1]
    grad_conditioning = pull_silu(cond_total)[0].reshape(1, -1)

    rows = d // count
    return (
        output,
        grad_patches,
        grad_conditioning,
        grad_captions,
        grad_ada,
        grad_norm_gains,
        g_attn[:, : 3 * n].astype(f32).reshape(rows, 3, n).transpose(1, 0, 2),
        grad_head_gains,
        grad_cross_gate,
        g_cap.astype(f32).reshape(-1, 2, n).transpose(1, 0, 2),
        g_attn[:, 3 * n :].astype(f32).T,
        g_mlp[:, : 2 * ff].astype(f32).reshape(rows, 2, ff).transpose(1, 0, 2),
        g_mlp[:, 2 * ff :].astype(f32).T,
    )


def solution(mesh):
    placed = (
        P("wide", None),
        P("wide", None),
        P("wide", None),
        P("wide", None),
        P(),
        P(),
        P(None, None, "narrow"),
        P(),
        P(None, None, "narrow"),
        P(),
        P("narrow"),
        P(None, None, "narrow"),
        P("narrow", None),
        P(None, None, "narrow"),
        P("narrow", None),
    )
    return jax.shard_map(
        local,
        mesh=mesh,
        in_specs=placed,
        out_specs=(
            P("wide", None),
            P("wide", None),
            P("wide", None),
            P("wide", None),
            P("wide", None, "narrow"),
            P(None, "wide"),
            P(None, "wide", "narrow"),
            P(),
            P(),
            P(None, "wide", "narrow"),
            P("narrow", "wide"),
            P(None, "wide", "narrow"),
            P("narrow", "wide"),
        ),
        check_vma=False,
    )
```
